32 devices in a mesh: spot: 16 (over z, y, x), gene: 2 (over core).
Axes of the slice: x: 2, y: 2, z: 4, core: 2. Of those that a mesh axis runs over, the one named last changes fastest.
Arguments:
- logits: bfloat16 [4096, 4096], P(('spot', 'gene')), may hold values from -8 to 8
- filt: float32 [4096], P('spot'), may hold values from -8 to 8
- expr: bfloat16 [4096, 2048], P('spot', 'gene'), may hold values from -8 to 8
- target: bfloat16 [4096, 2048], P('spot', 'gene'), may hold values from -9 to 9
- gene_mask: int32 [4, 2048], P(None, 'gene'), may hold values from 0 to 1, as said below
- density: int32 [4096], P('spot'), may hold values from 1 to 2
Outputs:
- loss: float32 [], replicated
- grad_logits: float32 [4096, 4096], P(('spot', 'gene'))
- grad_filt: float32 [4096], P('spot')
- grad_expr: float32 [4096, 2048], P('spot', 'gene')
The draws below stay inside these ranges and needn't reach their ends.
Inputs may be any that keep to these rules, and one draw needn't show every extreme that they name: `gene_mask`: 0 or 1; a slide may measure no gene at all.
All inputs are finite; a program needn't handle non-finite values.
Results may differ from the reference program's by a relative error of at most 0.005.
Values may be sent and summed in bfloat16 or wider, within the bound.
A program may use at most 64 MiB of HBM per device.

```python
import jax
import jax.numpy as jnp
from jax import lax

SPOTS = 4096
GENES = 2048
SLIDES = 4
CELLS = 4096


def gene_signs(key):
    bits = jax.random.randint(jax.random.fold_in(key, 53), (GENES,), 0, 2)
    return 2.0 * bits.astype(jnp.float32) - 1.0


def draw_gene_mask(key, part):
    key_bits, key_slide = jax.random.split(jax.random.fold_in(key, 17))
    measured = (jax.random.randint(key_bits, (SLIDES, GENES), 0, 4) < 3).astype(jnp.int32)
    silent = jax.random.randint(key_slide, (), 0, SLIDES)
    kept_rows = (jnp.arange(SLIDES, dtype=jnp.int32) != silent).astype(jnp.int32)
    return measured * kept_rows[:, None]


def draw_filt(key, part):
    key = jax.random.fold_in(key, 29)
    ramp = 1.5 * (2.0 * jnp.arange(CELLS, dtype=jnp.float32) / (CELLS - 1) - 1.0)
    noise = jnp.clip(1.2 * jax.random.normal(key, (CELLS,), jnp.float32), -6.0, 6.0)
    return ramp + noise


def draw_expr(key, part):
    signs = gene_signs(key)
    key = jax.random.fold_in(key, 41)
    rising = 0.3 * 10.0 ** (jnp.arange(GENES, dtype=jnp.float32) / (GENES - 1))
    center = 3.0 * rising * signs / jnp.sqrt(jnp.float32(CELLS))
    noise = jnp.clip(jax.random.normal(key, (CELLS, GENES), jnp.float32), -6.0, 6.0)
    return (noise + center[None, :]).astype(jnp.bfloat16)


def draw_target(key, part):
    signs = gene_signs(key)
    key = jax.random.fold_in(key, 43)
    place = jnp.arange(SPOTS, dtype=jnp.float32) / (SPOTS - 1)
    rising = 0.3 * 10.0 ** place
    noise = jnp.clip(jax.random.normal(key, (SPOTS, GENES), jnp.float32), -6.0, 6.0)
    return (noise + 0.7 * rising[:, None] * signs[None, :]).astype(jnp.bfloat16)


def touch_ends(values, rng, low, high):
    longest = values.shape.index(max(values.shape))
    spots = []
    for shift in (0, 1):
        where = [jax.random.randint(jax.random.fold_in(rng, axis), (), 0, length) for axis, length in enumerate(values.shape)]
        where[longest] = (where[longest] + shift) % values.shape[longest]
        spots.append(tuple(where))
    return values.at[spots[0]].set(low).at[spots[1]].set(high)


def levels(key, extent, shards, least, largest):
    gain = 1.0
    for dim, blocks in shards:
        draws = jax.random.uniform(jax.random.fold_in(jax.random.fold_in(key, 6), dim), (blocks,), jnp.float32, least / len(shards), largest / len(shards))
        gain = gain * jnp.repeat(jnp.exp(draws), extent[dim] // blocks).reshape((-1,) + (1,) * (len(extent) - 1 - dim))
    return gain


def gaussian(stream_key, dims, spread, bound, cuts=(), kind=jnp.bfloat16):
    values = spread * jax.random.normal(stream_key, dims, jnp.float32)
    if cuts:
        values = values * levels(stream_key, dims, cuts, -0.22, 0.18)
    return jnp.clip(values, -bound, bound).astype(kind)


def setup_inputs(seed: int = 0) -> dict:
    key_of = jax.random.split(jax.random.key(seed), 7)
    logits = gaussian(key_of[0], (SPOTS, CELLS), 1.5, 8.0, ((0, 32),))
    filt = draw_filt(jax.random.fold_in(key_of[6], 71), 0)
    expr = draw_expr(jax.random.fold_in(key_of[6], 71), 0)
    target = draw_target(jax.random.fold_in(key_of[6], 71), 0)
    gene_mask = draw_gene_mask(jax.random.fold_in(key_of[6], 71), 0)
    density = touch_ends(jax.random.randint(key_of[5], (SPOTS,), 1, max(2, 2 * CELLS // SPOTS) + 1), jax.random.fold_in(key_of[5], 1), 1, (max(2, 2 * CELLS // SPOTS) + 1) - 1).astype(jnp.int32)
    return dict(logits=logits, filt=filt, expr=expr, target=target, gene_mask=gene_mask, density=density)


@jax.custom_vjp
def low(v):
    return lax.optimization_barrier(v.astype(jnp.bfloat16)).astype(jnp.float32)

@jax.custom_vjp
def low_back(v):
    return v

def low_keep(v):
    return (low(v), None)

def low_pass(kept, grad):
    return (grad,)

def back_keep(v):
    return (v, None)

def back_low(kept, grad):
    return (low(grad),)
low.defvjp(low_keep, low_pass)
low_back.defvjp(back_keep, back_low)
eps_norm = 1e-06
spot_block = 256

def forward(logit_full, filt_full, expr_full, truth, maskf, dens):
    hi = lax.Precision.HIGHEST
    gate = jax.nn.sigmoid(filt_full)

    def block(rows):
        probs = jax.nn.softmax(rows, axis=1)
        sent = low(low_back(probs))
        weighted = low(gate[None, :] * sent)
        pred_rows = jnp.dot(weighted, expr_full, precision=hi)
        return (pred_rows, lax.optimization_barrier(jnp.sum(weighted, axis=1)))
    pred, mass = lax.map(jax.checkpoint(block), logit_full.reshape(SPOTS // spot_block, spot_block, CELLS))
    pred = low_back(pred.reshape(SPOTS, GENES))
    mass = low_back(mass.reshape(SPOTS))
    pred_s = pred.reshape(SLIDES, SPOTS // SLIDES, GENES)
    truth_s = truth.reshape(SLIDES, SPOTS // SLIDES, GENES)
    dots = lax.optimization_barrier(jnp.sum(pred_s * truth_s, axis=1))
    slide_a = lax.rsqrt(lax.optimization_barrier(jnp.sum(pred_s * pred_s, axis=1)) + eps_norm)
    slide_b = lax.rsqrt(lax.optimization_barrier(jnp.sum(truth_s * truth_s, axis=1)) + eps_norm)
    cos_gene = dots * slide_a * slide_b
    genes_kept = jnp.maximum(lax.optimization_barrier(jnp.sum(maskf, axis=1)), 1.0)
    gene_term = jnp.mean(lax.optimization_barrier(jnp.sum(maskf * cos_gene, axis=1)) / genes_kept)
    spot_dot = lax.optimization_barrier(jnp.sum(pred * truth, axis=1))
    spot_a = lax.rsqrt(lax.optimization_barrier(jnp.sum(pred * pred, axis=1)) + eps_norm)
    spot_b = lax.rsqrt(lax.optimization_barrier(jnp.sum(truth * truth, axis=1)) + eps_norm)
    spot_term = jnp.mean(spot_dot * spot_a * spot_b)
    mass_total = jnp.sum(mass)
    count_total = jnp.sum(dens)
    share = dens / count_total
    kl_value = jnp.sum(share * (jnp.log(share) - jnp.log(mass) + jnp.log(mass_total)))
    excess = jnp.sum(gate) / count_total - 1.0
    return -gene_term - spot_term + kl_value + excess * excess

def reference(logits, filt, expr, target, gene_mask, density):
    logit_full = logits.astype(jnp.float32)
    expr_full = expr.astype(jnp.float32)
    truth = target.astype(jnp.float32)
    maskf = gene_mask.astype(jnp.float32)
    dens = density.astype(jnp.float32)

    def wrapped(a, b, c):
        return forward(a, b, c, truth, maskf, dens)
    loss, pull = jax.vjp(wrapped, logit_full, filt, expr_full)
    grad_logits, grad_filt, grad_expr = pull(jnp.ones_like(loss))
    return (loss, grad_logits, grad_filt, grad_expr)
```

```python
import functools

import jax
import jax.numpy as jnp
from jax import lax
from jax.experimental import pallas as pl
from jax.experimental.pallas import tpu as pltpu
from jax.sharding import PartitionSpec as P

SPOTS = 4096
SLIDES = 4


eps_norm = 1e-06


def slide_moments(onehot, pred, truth):
    hi = lax.Precision.HIGHEST
    return jnp.stack(
        [
            jnp.dot(onehot.T, pred * truth, precision=hi),
            jnp.dot(onehot.T, pred * pred, precision=hi),
            jnp.dot(onehot.T, truth * truth, precision=hi),
        ]
    )


def spot_moments(pred, truth):
    return jnp.stack(
        [
            jnp.sum(pred * truth, axis=1),
            jnp.sum(pred * pred, axis=1),
            jnp.sum(truth * truth, axis=1),
        ]
    )


def cosine_parts(slide_stats):
    dots = slide_stats[0]
    slide_a = lax.rsqrt(slide_stats[1] + eps_norm)
    slide_b = lax.rsqrt(slide_stats[2] + eps_norm)
    return (dots, slide_a, slide_b, dots * slide_a * slide_b)


def pred_gradient(onehot, weight_slide, dots, slide_a, slide_b, spot_stats, pred, truth):
    hi = lax.Precision.HIGHEST
    spot_a = lax.rsqrt(spot_stats[1] + eps_norm)
    spot_b = lax.rsqrt(spot_stats[2] + eps_norm)
    coef_truth = -weight_slide * slide_a * slide_b
    coef_pred = weight_slide * dots * slide_a**3 * slide_b
    grad_pred = (
        jnp.dot(onehot, coef_truth, precision=hi) * truth
        + jnp.dot(onehot, coef_pred, precision=hi) * pred
    )
    grad_pred = (
        grad_pred
        + (
            -(spot_a * spot_b)[:, None] * truth
            + (spot_stats[0] * spot_a**3 * spot_b)[:, None] * pred
        )
        / SPOTS
    )
    return (grad_pred, spot_stats[0] * spot_a * spot_b)


def streamed(logits, filt, expr, target, gene_mask, density):
    f32 = jnp.float32
    bf16 = jnp.bfloat16
    nspot = lax.axis_size("spot")
    ngene = lax.axis_size("gene")
    spot_dev = logits.shape[0]
    cells = logits.shape[1]
    cell_dev = filt.shape[0]
    owned = target.shape[0]
    half = target.shape[1]
    spots_all = owned * nspot
    slide_len = SPOTS // SLIDES
    scores = logits.astype(f32)
    shifted = jnp.exp(scores - jnp.max(scores, axis=1, keepdims=True))
    probs = shifted / jnp.sum(shifted, axis=1, keepdims=True)
    moved = lax.all_to_all(probs.astype(bf16), "spot", split_axis=1, concat_axis=0, tiled=True)
    paired = lax.all_gather(moved.reshape(nspot, 1, spot_dev, cell_dev), "gene", axis=1, tiled=True)
    paired = paired.reshape(spots_all, cell_dev)
    gate = jax.nn.sigmoid(filt)
    weighted = (paired.astype(f32) * gate[None, :]).astype(bf16)
    partial_pred = jnp.dot(weighted, expr, preferred_element_type=f32)
    partial_mass = jnp.sum(weighted.astype(f32), axis=1)
    gate_part = jnp.sum(gate)
    maskf = gene_mask.astype(f32)
    mask_part = jnp.sum(maskf, axis=1)
    pred_three, mass_two = (
        lax.psum_scatter(
            partial_pred.reshape(nspot, owned, half), "spot", scatter_dimension=0, tiled=True
        ),
        lax.psum_scatter(
            partial_mass.reshape(nspot, owned), "spot", scatter_dimension=0, tiled=True
        ),
    )
    pred = pred_three.reshape(owned, half)
    mass = mass_two.reshape(owned)
    truth = target.astype(f32)
    dens = density.astype(f32)
    spot_ids = lax.axis_index("spot") * owned + jnp.arange(owned, dtype=jnp.int32)
    onehot = (
        spot_ids[:, None] // slide_len == jnp.arange(SLIDES, dtype=jnp.int32)[None, :]
    ).astype(f32)
    slide_stats, mass_total, gate_total, count_total = lax.psum(
        (slide_moments(onehot, pred, truth), jnp.sum(mass), gate_part, jnp.sum(dens)), "spot"
    )
    dots, slide_a, slide_b, cos_gene = cosine_parts(slide_stats)
    spot_stats, kept_genes, gene_numer = lax.psum(
        (spot_moments(pred, truth), mask_part, jnp.sum(maskf * cos_gene, axis=1)), "gene"
    )
    genes_kept = jnp.maximum(kept_genes, 1.0)
    weight_slide = maskf / genes_kept[:, None] / SLIDES
    grad_pred, cos_spot = pred_gradient(
        onehot, weight_slide, dots, slide_a, slide_b, spot_stats, pred, truth
    )
    share = dens / count_total
    kl_local = jnp.sum(share * (jnp.log(share) - jnp.log(mass) + jnp.log(mass_total)))
    cos_total, kl_total = lax.psum((jnp.sum(cos_spot), kl_local), "spot")
    grad_mass = 1.0 / mass_total - share / mass
    spread_three, spread_two = (
        lax.all_gather(grad_pred.astype(bf16).reshape(1, owned, half), "spot", axis=0, tiled=True),
        lax.all_gather(grad_mass.astype(bf16).reshape(1, owned), "spot", axis=0, tiled=True),
    )
    spread_pred = spread_three.reshape(spots_all, half)
    spread_mass = spread_two.reshape(spots_all)
    gene_term = jnp.mean(gene_numer / genes_kept)
    excess = gate_total / count_total - 1.0
    loss = -gene_term - cos_total / SPOTS + kl_total + excess * excess
    grad_expr = lax.dot_general(
        weighted, spread_pred, (((0,), (0,)), ((), ())), preferred_element_type=f32
    )
    first_half = (lax.axis_index("gene") == 0).astype(f32)
    grad_weighted = lax.dot_general(
        spread_pred, expr, (((1,), (1,)), ((), ())), preferred_element_type=f32
    )
    grad_weighted = grad_weighted + first_half * spread_mass.astype(f32)[:, None]
    filter_part = jnp.sum(grad_weighted * paired.astype(f32), axis=0)
    filter_total = lax.psum(filter_part, "gene")
    grad_filt = (filter_total + 2.0 * excess / count_total) * gate * (1.0 - gate)
    terms = (grad_weighted * gate[None, :]).reshape(nspot, ngene, spot_dev, cell_dev)
    moved_back = lax.all_to_all(terms, "spot", split_axis=0, concat_axis=3, tiled=True)
    folded = lax.psum_scatter(moved_back, "gene", scatter_dimension=1, tiled=True)
    rounded = lax.optimization_barrier(folded.reshape(spot_dev, cells).astype(bf16))
    grad_probs = rounded.astype(f32)
    grad_logits = probs * (grad_probs - jnp.sum(probs * grad_probs, axis=1, keepdims=True))
    return (loss, grad_logits, grad_filt, grad_expr)


GROUP = 4
MESH = pl.DeviceIdType.MESH
VMEM_BYTES = 60 << 20
POS = {0: 0, 1: 1, 3: 2, 2: 3}


def remote(src, dst, send, recv, dev):
    return pltpu.make_async_remote_copy(
        src_ref=src, dst_ref=dst, send_sem=send, recv_sem=recv, device_id=dev, device_id_type=MESH
    )


def dot_nt(a, b):
    return lax.dot_general(a, b, (((1,), (1,)), ((), ())), preferred_element_type=jnp.float32)


def column(row, length):
    return jnp.transpose(jnp.broadcast_to(row, (128, length)))


def lanes_to_row(values):
    folded = values[:, 0:128]
    for i in range(1, values.shape[1] // 128):
        folded = folded + values[:, i * 128 : (i + 1) * 128]
    return jnp.sum(jnp.transpose(folded), axis=0, keepdims=True)


def group_kernel(
    nspot, logits, filt, expr, target, mask, dens,
    loss_o, gl_o, gf_o, ge_o,
    probs, gateb, wbuf, ebuf, tbuf, pbuf, dpb, dps, dpt,
    small, massb, lossb, pair_s, pair_r, stat_s, stat_r,
    sendx, recvx, sendy, recvy, send2x, recv2x, send2y, recv2y, gwr, held,
    grad, dsend, dright, dleft, fins, finr, fsend, frecv, fpart,
    lc, ea_s, ea_r, ez_s, ez_r, es_s, es_r, w_s, w_r, wd_s, wd_r, t_s, t_r,
    sm_s, sm_r, ma_s, ma_r, lo_s, lo_r, fi_s, fi_r, pr_s, pr_r, st_s, st_r,
    x_s, x_r, y_s, y_r, x2_s, x2_r, y2_s, y2_r, dr_s, dr_r, dl_s, dl_r, fn_s, fn_r, dp_s, dp_r,
):
    f32, bf16 = jnp.float32, jnp.bfloat16
    rows, cells = logits.shape
    cd = expr.shape[0]
    gq = expr.shape[1] // GROUP
    nz = nspot // GROUP
    grp = GROUP * rows
    half = cells // 2
    cc = half // 4
    spots_all = nspot * 2 * rows
    me, j = lax.axis_index("spot"), lax.axis_index("gene")
    sib = 1 - j
    z, q = me // GROUP, me % GROUP
    x, y = q % 2, q // 2
    nbr = [me, me + 1 - 2 * x, me + 2 - 4 * y, me + 3 - 2 * x - 4 * y]
    nq = [n % GROUP for n in nbr]
    here = (me, sib)

    barrier = pltpu.get_barrier_semaphore()

    @pl.loop(1, nspot)
    def _(r):
        pl.semaphore_signal(barrier, inc=1, device_id=((me + r) % nspot, j), device_id_type=MESH)

    for k in range(GROUP):
        pl.semaphore_signal(barrier, inc=1, device_id=(nbr[k], sib), device_id_type=MESH)

    def eblock(h, o):
        return ebuf.at[h, pl.ds(pl.multiple_of(o * cd, cd), cd), :]

    def ecols(ref, k):
        return ref.at[:, pl.ds(pl.multiple_of(nq[k] * gq, gq), gq)]

    own_e = pltpu.make_async_copy(ecols(expr, 0), eblock(0, me), lc.at[0])
    own_e.start()
    own_t = pltpu.make_async_copy(
        target.at[pl.ds(pl.multiple_of(j * rows, rows), rows), pl.ds(pl.multiple_of(q * gq, gq), gq)],
        tbuf.at[0, pl.ds(0, rows), :],
        lc.at[1],
    )
    own_t.start()
    small[pl.ds(me, 1), 0:2, :] = filt[...][None]
    small[pl.ds(me, 1), 2:4, :] = dens[...].astype(f32)[None]
    small[pl.ds(me, 1), 4:8, :] = jnp.zeros((1, 4, 128), f32)
    mrow = mask[pl.ds(z, 1), :].astype(f32)
    mine_mask = mask[pl.ds(z, 1), pl.ds(pl.multiple_of(q * gq, gq), gq)].astype(f32)
    kept_mine = jnp.sum(mrow)
    pair_s[0, :, 0:gq] = jnp.broadcast_to(mine_mask, (8, gq))
    pair_s[0, :, gq : 2 * gq] = jnp.broadcast_to(kept_mine, (8, gq))
    pl.semaphore_wait(barrier, nspot - 1 + GROUP)

    ea = [
        remote(ecols(expr, k), eblock(0, me), ea_s.at[k], ea_r.at[k], (nbr[k], j))
        for k in range(1, GROUP)
    ]
    for c in ea:
        c.start()

    def zsend(way, o):
        return remote(
            eblock(0, o), eblock(0, o), ez_s.at[way, o], ez_r.at[o], (me + (GROUP if way == 0 else -GROUP), j)
        )

    def ezwait(o):
        remote(eblock(0, o), eblock(0, o), ez_s.at[0, o], ez_r.at[o], here).wait_recv()

    def esib(o):
        return remote(eblock(0, o), eblock(1, o), es_s.at[o], es_r.at[o], here)

    own_e.wait()

    def spread(o):
        @pl.when(z < nz - 1)
        def _():
            zsend(0, o).start()

        @pl.when(z > 0)
        def _():
            zsend(1, o).start()

        esib(o).start()

    spread(me)

    def gather(buf, r, ss, rs):
        return remote(buf.at[me], buf.at[me], ss.at[r], rs.at[r], ((me + r) % nspot, j))

    def gather_start(buf, ss, rs):
        @pl.loop(1, nspot)
        def _(r):
            gather(buf, r, ss, rs).start()

    def gather_wait(buf, ss, rs):
        @pl.loop(1, nspot)
        def _(r):
            o = (me + nspot - r) % nspot
            remote(buf.at[o], buf.at[o], ss.at[r], rs.at[r], here).wait_recv()

    def gather_sent(buf, ss, rs):
        @pl.loop(1, nspot)
        def _(r):
            gather(buf, r, ss, rs).wait_send()

    gather_start(small, sm_s, sm_r)

    def pair(i):
        return remote(pair_s.at[i], pair_r.at[i], pr_s.at[i], pr_r.at[i], here)

    pair(0).start()

    def tcopy(k, h):
        jj = j if h == 0 else sib
        src = target.at[
            pl.ds(pl.multiple_of(jj * rows, rows), rows), pl.ds(pl.multiple_of(nq[k] * gq, gq), gq)
        ]
        i = k * 2 + h
        return remote(
            src, tbuf.at[h, pl.ds(POS[k] * rows, rows), :], t_s.at[i], t_r.at[i], (nbr[k], jj)
        )

    tlist = [(k, h) for k in (1, 2, 3, 0) for h in (0, 1) if (k, h) != (0, 0)]
    for k, h in tlist:
        tcopy(k, h).start()

    for k in range(1, GROUP):
        remote(eblock(0, nbr[k]), eblock(0, nbr[k]), ea_s.at[k], ea_r.at[k], here).wait_recv()
        spread(nbr[k])

    step = 16

    @pl.loop(0, rows // step)
    def _(i):
        at = pl.ds(pl.multiple_of(i * step, step), step)
        s = logits[at, :].astype(f32)
        e = jnp.exp(s - jnp.max(s, axis=1, keepdims=True))
        probs[at, :] = e / jnp.sum(e, axis=1, keepdims=True)

    gather_wait(small, sm_s, sm_r)
    for o in range(nspot):
        for h in range(cd // 128):
            g = jax.nn.sigmoid(small[o, h : h + 1, :])
            gateb[:, o * cd + h * 128 : o * cd + (h + 1) * 128] = jnp.broadcast_to(g, (8, 128))

    @pl.loop(0, rows // step)
    def _(i):
        at = pl.ds(pl.multiple_of(i * step, step), step)
        sent = probs[at, :].astype(bf16).astype(f32)
        wbuf[0, at, :] = (gateb[0:1, :] * sent).astype(bf16)

    lo, hi = pl.ds(0, half), pl.ds(half, half)

    def wrows(h, k):
        return wbuf.at[h, pl.ds(POS[k] * rows, rows), :]

    def wcopy(i):
        src_k, dst_k, cols, to = (
            (0, 1, lo, 1), (0, 1, hi, 1), (0, 2, hi, 2), (0, 2, lo, 2), (1, 3, lo, 2), (2, 3, hi, 1),
        )[i]
        return remote(
            wbuf.at[0, pl.ds(POS[src_k] * rows, rows), cols],
            wbuf.at[0, pl.ds(POS[dst_k] * rows, rows), cols],
            w_s.at[i],
            w_r.at[i],
            (nbr[to], j),
        )

    def wsib(k):
        return remote(wrows(0, k), wrows(1, k), wd_s.at[k], wd_r.at[k], here)

    for i in (0, 2, 1, 3):
        wcopy(i).start()
    wsib(0).start()

    massb[pl.ds(me, 1), :, :] = dot_nt(jnp.ones((8, cells), bf16), wbuf[0, 0:rows, :])[None]
    gather_start(massb, ma_s, ma_r)

    for s in range(1, nz):
        for k in range(GROUP):

            @pl.when(z >= s)
            def _():
                o = nbr[k] - GROUP * s
                ezwait(o)

                @pl.when(z < nz - 1)
                def _():
                    zsend(0, o).start()

                esib(o).start()

            @pl.when(z + s <= nz - 1)
            def _():
                o = nbr[k] + GROUP * s
                ezwait(o)

                @pl.when(z > 0)
                def _():
                    zsend(1, o).start()

                esib(o).start()

        if s == max(nz - 2, 1):
            wcopy(0).wait_recv()
            wcopy(4).start()
            wcopy(2).wait_recv()
            wcopy(5).start()
    wcopy(1).wait_recv()
    wsib(1).start()
    wcopy(3).wait_recv()
    wsib(2).start()

    gather_wait(massb, ma_s, ma_r)
    count_total = jnp.zeros((1, 128), f32)
    gate_sum = jnp.zeros((1, 128), f32)
    for o in range(nspot):
        count_total = count_total + small[o, 2:3, :] + small[o, 3:4, :]
    for o in range(cells // 128):
        gate_sum = gate_sum + gateb[0:1, o * 128 : (o + 1) * 128]
    count_total = jnp.sum(count_total)
    gate_total = jnp.sum(gate_sum)
    mass_sum = jnp.zeros((1, 128), f32)
    kl_sum = jnp.zeros((1, 128), f32)
    share_sum = jnp.zeros((1, 128), f32)
    for o in range(nspot):
        m = massb[o, 0:1, :]
        share = jnp.where(j == 0, small[o, 2:3, :], small[o, 3:4, :]) / count_total
        mass_sum = mass_sum + m
        share_sum = share_sum + share
        kl_sum = kl_sum + share * (jnp.log(share) - jnp.log(m))
    pair_s[1, 0:1, 0:128] = mass_sum
    pair_s[1, 1:2, 0:128] = kl_sum
    pair_s[1, 2:3, 0:128] = share_sum
    pair(1).start()
    pair(0).wait_recv()
    kept = jnp.maximum(kept_mine + jnp.sum(pair_r[0, 0:1, gq : gq + 1]), 1.0)
    pair(1).wait_recv()
    mass_total = jnp.sum(mass_sum + pair_r[1, 0:1, 0:128])
    kl_all = jnp.sum(kl_sum + pair_r[1, 1:2, 0:128])
    share_all = jnp.sum(share_sum + pair_r[1, 2:3, 0:128])
    log_total = jnp.log(jnp.full((1, 128), mass_total))
    excess = gate_total / count_total - 1.0
    my_dens = small[pl.ds(me, 1), pl.ds(2 + j, 1), :].reshape(1, 128)
    my_mass = massb[pl.ds(me, 1), 0:1, :].reshape(1, 128)
    gm_row = (1.0 / mass_total - my_dens / count_total / my_mass).astype(bf16).astype(f32)
    gm = column(gm_row, rows)

    wcopy(4).wait_recv()
    wcopy(5).wait_recv()
    wsib(3).start()

    @pl.loop(0, nspot)
    def _(o):
        esib(o).wait_recv()

    own_t.wait()
    for k, h in tlist:
        tcopy(k, h).wait_recv()
    kb = 512
    for h in range(2):
        pbuf[:, h * gq : (h + 1) * gq] = jnp.dot(
            wbuf[0, :, 0:kb], ebuf[h, 0:kb, :], preferred_element_type=f32
        )

    @pl.loop(1, cells // kb)
    def _(i):
        at = pl.ds(pl.multiple_of(i * kb, kb), kb)
        for h in range(2):
            pbuf[:, h * gq : (h + 1) * gq] += jnp.dot(
                wbuf[0, :, at], ebuf[h, at, :], preferred_element_type=f32
            )

    for h in range(2):
        p = pbuf[:, h * gq : (h + 1) * gq]
        t = tbuf[h].astype(f32)
        for i, v in enumerate((p * t, p * p, t * t)):
            stat_s[0, i : i + 1, h * gq : (h + 1) * gq] = jnp.sum(v, axis=0, keepdims=True)
            r = lanes_to_row(v)
            if h == 0:
                stat_s[1, i : i + 1, 0:grp] = r
            else:
                stat_s[1, i : i + 1, 0:grp] += r

    def stat(k):
        if k == 0:
            return remote(stat_s.at[0], stat_r.at[0], st_s.at[0], st_r.at[0], here)
        return remote(stat_s.at[1], stat_r.at[k], st_s.at[k], st_r.at[k], (nbr[k], j))

    for k in (3, 1, 2, 0):
        stat(k).start()
    stat(0).wait_recv()
    order = (slice(gq, 2 * gq), slice(0, gq))
    slide = [
        jnp.concatenate([stat_r[0, i : i + 1, c] for c in order], axis=1) + stat_s[0, i : i + 1, :]
        for i in range(3)
    ]
    dots = slide[0]
    slide_a = lax.rsqrt(slide[1] + eps_norm)
    slide_b = lax.rsqrt(slide[2] + eps_norm)
    maskf = jnp.concatenate([mine_mask, pair_r[0, 0:1, 0:gq]], axis=1)
    weight = maskf / kept / SLIDES
    coef_t = -weight * slide_a * slide_b
    coef_p = weight * dots * slide_a**3 * slide_b
    cos_gene = (dots * slide_a * slide_b)[:, 0:gq]
    gene_part = jnp.sum(mine_mask * cos_gene / kept)
    for k in (1, 2, 3):
        stat(k).wait_recv()
    at_pos = {0: 0, 1: 1, 2: 3, 3: 2}
    spot = []
    for i in range(3):
        parts = []
        for p in range(GROUP):
            k = at_pos[p]
            v = stat_s[1, i : i + 1, p * rows : (p + 1) * rows]
            there = [
                stat_r[m, i : i + 1, POS[k ^ m] * rows : (POS[k ^ m] + 1) * rows] for m in (1, 2, 3)
            ]
            parts.append((v + there[0]) + (there[1] + there[2]))
        spot.append(jnp.concatenate(parts, axis=1))
    spot_a = lax.rsqrt(spot[1] + eps_norm)
    spot_b = lax.rsqrt(spot[2] + eps_norm)
    cos_spot = (spot[0] * spot_a * spot_b)[:, 0:rows]
    col_t = column(-(spot_a * spot_b) / spots_all, grp)
    col_p = column(spot[0] * spot_a**3 * spot_b / spots_all, grp)

    for g in range(2 * gq // 128):
        at = slice(g * 128, (g + 1) * 128)
        t = tbuf[g * 128 // gq, :, (g * 128) % gq : (g * 128) % gq + 128].astype(f32)
        dpb[:, at] = ((coef_t[:, at] + col_t) * t + (coef_p[:, at] + col_p) * pbuf[:, at]).astype(bf16)
    dps_copy = remote(dpb.at[:, pl.ds(gq, gq)], dps, dp_s.at[0], dp_r.at[0], here)
    dps_copy.start()
    lossb[pl.ds(me, 1), :, :] = jnp.broadcast_to(
        (-gene_part / SLIDES - jnp.sum(cos_spot) / spots_all), (1, 8, 128)
    )
    gather_start(lossb, lo_s, lo_r)

    def xcopy(c):
        return remote(sendx.at[c], recvx.at[c], x_s.at[c], x_r.at[c], (nbr[1], j))

    def ycopy(c):
        return remote(sendy.at[c], recvy.at[c], y_s.at[c], y_r.at[c], (nbr[2], j))

    def x2copy(c):
        return remote(send2x.at[c], recv2x.at[c], x2_s.at[c], x2_r.at[c], (nbr[1], j))

    def y2copy(c):
        return remote(send2y.at[c], recv2y.at[c], y2_s.at[c], y2_r.at[c], (nbr[2], j))

    def weight_grad(at):
        return dot_nt(dpb[:, 0:gq], ebuf[0, at, :]) + dot_nt(dpb[:, gq : 2 * gq], ebuf[1, at, :])

    dpt[:, 0:grp] = jnp.transpose(dpb[:, 0:gq].astype(f32)).astype(bf16)
    wsib_pos = [wsib(k) for k in range(GROUP)]
    for w in wsib_pos:
        w.wait_recv()
    dps_copy.wait_recv()
    dpt[:, grp : 2 * grp] = jnp.transpose(dps[...].astype(f32)).astype(bf16)

    def dsend_to(way, o):
        if way == 0:
            return remote(dsend.at[o], dright.at[o], dr_s.at[o], dr_r.at[o], (me + GROUP, j))
        return remote(dsend.at[o], dleft.at[o], dl_s.at[o], dl_r.at[o], (me - GROUP, j))

    up = z // (nz // 2)

    @pl.loop(0, 4)
    def _(c):
        lo_at = pl.ds(pl.multiple_of(c * cc, cc), cc)
        d = weight_grad(lo_at)
        gwr[:, lo_at] = d[0:rows]
        sendx[c] = d[rows : 3 * rows].astype(bf16)
        held[0, :, lo_at] = d[3 * rows : 4 * rows]
        xcopy(c).start()
        hi_at = pl.ds(pl.multiple_of(half + c * cc, cc), cc)
        d = weight_grad(hi_at)
        gwr[:, hi_at] = d[0:rows]
        sendy[c] = d[2 * rows : 4 * rows].astype(bf16)
        held[1, :, lo_at] = d[rows : 2 * rows]
        ycopy(c).start()
        k = 3 - c
        kx, ky = k % 2, k // 2
        kq = (x + kx - 2 * x * kx) + 2 * (y + ky - 2 * y * ky)

        @pl.loop(0, nz)
        def _(u):
            to = up * u + (1 - up) * (nz - 1 - u)
            o = to * GROUP + kq
            at = pl.ds(pl.multiple_of(o * cd, cd), cd)
            v = jnp.dot(dpt[:, 0:grp], wbuf[0, :, at], preferred_element_type=f32) + jnp.dot(
                dpt[:, grp : 2 * grp], wbuf[1, :, at], preferred_element_type=f32
            )
            grad[o] = v

            @pl.when((z == 0) & (to > 0))
            def _():
                dsend[o] = v.astype(bf16)
                dsend_to(0, o).start()

            @pl.when((z == nz - 1) & (to < nz - 1))
            def _():
                dsend[o] = v.astype(bf16)
                dsend_to(1, o).start()

    def fin(k):
        return remote(fins.at[k - 1], finr.at[k - 1], fn_s.at[k], fn_r.at[k], (nbr[k], j))

    def relay(c):
        lo_at = pl.ds(c * cc, cc)
        xcopy(c).wait_recv()
        send2y[c] = (held[0, :, lo_at] + recvx[c, rows : 2 * rows].astype(f32)).astype(bf16)
        y2copy(c).start()
        gwr[:, lo_at] += recvx[c, 0:rows].astype(f32)
        ycopy(c).wait_recv()
        send2x[c] = (held[1, :, lo_at] + recvy[c, 0:rows].astype(f32)).astype(bf16)
        x2copy(c).start()
        gwr[:, pl.ds(half + c * cc, cc)] += recvy[c, rows : 2 * rows].astype(f32)

    for n, k in enumerate((3, 2, 1, 0)):
        for s in range(nz - 1, 0, -1):

            @pl.when((z > 0) & (z + s <= nz - 1))
            def _():
                o = nbr[k] + GROUP * s
                dsend_to(0, o).wait_recv()
                dsend[o] = (grad[o] + dright[o].astype(f32)).astype(bf16)
                dsend_to(0, o).start()

            @pl.when((z < nz - 1) & (z >= s))
            def _():
                o = nbr[k] - GROUP * s
                dsend_to(1, o).wait_recv()
                dsend[o] = (grad[o] + dleft[o].astype(f32)).astype(bf16)
                dsend_to(1, o).start()

        relay(n)
        o = nbr[k]

        @pl.when(z > 0)
        def _():
            dsend_to(0, o).wait_recv()
            grad[o] += dright[o].astype(f32)

        @pl.when(z < nz - 1)
        def _():
            dsend_to(1, o).wait_recv()
            grad[o] += dleft[o].astype(f32)

        v = jnp.transpose(grad[o])
        if k:
            fins[k - 1] = v.astype(bf16)
            fin(k).start()
        else:
            ge_o[:, pl.ds(pl.multiple_of(q * gq, gq), gq)] = v

    gather_wait(lossb, lo_s, lo_r)
    total = jnp.zeros((8, 128), f32)
    for o in range(nspot):
        total = total + lossb[o]
    pair_s[2, :, 0:128] = total
    pair(2).start()

    fpart[...] = jnp.zeros_like(fpart)
    rowsum = jnp.zeros((rows, 128), f32)

    def whole(base, got, rowsum):
        def one(c, rowsum):
            at = pl.ds(pl.multiple_of(base + c * cc, cc), cc)
            got(c).wait_recv()
            piece = (recv2y if base == 0 else recv2x)[c]
            p = probs[:, at]
            gw = gwr[:, at] + piece.astype(f32) + jnp.concatenate([gm] * (cc // 128), axis=1)
            fpart[:, at] = jnp.sum(gw * p.astype(bf16).astype(f32), axis=0, keepdims=True)
            gp = (gateb[0:1, at] * gw).astype(bf16).astype(f32)
            gwr[:, at] = gp
            v = p * gp
            for i in range(cc // 128):
                rowsum = rowsum + v[:, i * 128 : (i + 1) * 128]
            return rowsum

        return lax.fori_loop(0, 4, one, rowsum)

    rowsum = whole(0, y2copy, rowsum)
    rowsum = whole(half, x2copy, rowsum)

    for o in range(nspot):
        fsend[o] = fpart[:, o * cd : (o + 1) * cd]
    frecv[pl.ds(me, 1)] = fsend[pl.ds(me, 1)]

    def fcopy(r):
        o = (me + r) % nspot
        return remote(fsend.at[o], frecv.at[me], fi_s.at[r], fi_r.at[r], (o, j))

    @pl.loop(1, nspot)
    def _(r):
        fcopy(r).start()

    total_row = jnp.sum(rowsum, axis=1, keepdims=True)

    @pl.loop(0, cells // cc)
    def _(c):
        at = pl.ds(pl.multiple_of(c * cc, cc), cc)
        gl_o[:, at] = probs[:, at] * (gwr[:, at] - total_row)

    for k in (3, 2, 1):
        fin(k).wait_recv()
        ge_o[:, pl.ds(pl.multiple_of(nq[k] * gq, gq), gq)] = finr[k - 1].astype(f32)

    @pl.loop(1, nspot)
    def _(r):
        o = (me + nspot - r) % nspot
        remote(fsend.at[o], frecv.at[o], fi_s.at[r], fi_r.at[r], here).wait_recv()

    ftotal = frecv[0]
    for o in range(1, nspot):
        ftotal = ftotal + frecv[o]
    pair_s[3, 0:1, 0:cd] = ftotal
    pair(3).start()
    pair(2).wait_recv()
    loss_sum = jnp.sum(total[0:1, 0:1] + pair_r[2, 0:1, 0:1])
    log_all = jnp.sum(log_total[:, 0:1])
    loss_o[0, 0] = loss_sum + kl_all + share_all * log_all + excess * excess
    pair(3).wait_recv()
    my_gate = jax.nn.sigmoid(
        jnp.concatenate([small[pl.ds(me, 1), h : h + 1, :].reshape(1, 128) for h in range(cd // 128)], axis=1)
    )
    gf_o[...] = (ftotal + pair_r[3, 0:1, 0:cd] + 2.0 * excess / count_total) * my_gate * (1.0 - my_gate)

    for c in ea:
        c.wait_send()
    gather_sent(small, sm_s, sm_r)
    gather_sent(massb, ma_s, ma_r)
    gather_sent(lossb, lo_s, lo_r)

    @pl.loop(1, nspot)
    def _(r):
        fcopy(r).wait_send()

    for i in range(4):
        pair(i).wait_send()
        stat(i).wait_send()
        wsib(i).wait_send()
    for k, h in tlist:
        tcopy(k, h).wait_send()
    for i in range(6):
        wcopy(i).wait_send()
    for k in range(1, GROUP):
        fin(k).wait_send()
    dps_copy.wait_send()

    @pl.loop(0, 4)
    def _(c):
        xcopy(c).wait_send()
        ycopy(c).wait_send()
        x2copy(c).wait_send()
        y2copy(c).wait_send()

    @pl.loop(0, nspot)
    def _(o):
        esib(o).wait_send()
        at = o // GROUP

        @pl.when((z < nz - 1) & (at <= z))
        def _():
            zsend(0, o).wait_send()

        @pl.when((z > 0) & (at >= z))
        def _():
            zsend(1, o).wait_send()

        @pl.when((z < nz - 1) & (at > z))
        def _():
            dsend_to(0, o).wait_send()

        @pl.when((z > 0) & (at < z))
        def _():
            dsend_to(1, o).wait_send()


def grouped(logits, filt, expr, target, gene_mask, density):
    f32, bf16 = jnp.float32, jnp.bfloat16
    nspot = lax.axis_size("spot")
    rows, cells = logits.shape
    cd, half = expr.shape
    gq = half // GROUP
    grp = GROUP * rows
    hc = cells // 2
    cc = hc // 4
    wide = max(2 * gq, grp, cd, 128)
    dma = pltpu.SemaphoreType.DMA

    def vmem(*shape, dtype=f32):
        return pltpu.VMEM(shape, dtype)

    buffers = [
        vmem(rows, cells), vmem(8, cells), vmem(2, grp, cells, dtype=bf16), vmem(2, cells, gq, dtype=bf16),
        vmem(2, grp, gq, dtype=bf16), vmem(grp, 2 * gq), vmem(grp, 2 * gq, dtype=bf16),
        vmem(grp, gq, dtype=bf16), vmem(gq, 2 * grp, dtype=bf16),
        vmem(nspot, 8, 128), vmem(nspot, 8, 128), vmem(nspot, 8, 128),
        vmem(4, 8, wide), vmem(4, 8, wide), vmem(2, 8, wide), vmem(4, 8, wide),
        vmem(4, 2 * rows, cc, dtype=bf16), vmem(4, 2 * rows, cc, dtype=bf16),
        vmem(4, 2 * rows, cc, dtype=bf16), vmem(4, 2 * rows, cc, dtype=bf16),
        vmem(4, rows, cc, dtype=bf16), vmem(4, rows, cc, dtype=bf16),
        vmem(4, rows, cc, dtype=bf16), vmem(4, rows, cc, dtype=bf16),
        vmem(rows, cells), vmem(2, rows, hc),
        vmem(nspot, gq, cd), vmem(nspot, gq, cd, dtype=bf16),
        vmem(nspot, gq, cd, dtype=bf16), vmem(nspot, gq, cd, dtype=bf16),
        vmem(3, cd, gq, dtype=bf16), vmem(3, cd, gq, dtype=bf16),
        vmem(nspot, 1, cd), vmem(nspot, 1, cd), vmem(1, cells),
    ]
    sems = [
        dma((2,)), dma((4,)), dma((4,)), dma((2, nspot)), dma((nspot,)), dma((nspot,)), dma((nspot,)),
        dma((6,)), dma((6,)), dma((4,)), dma((4,)), dma((8,)), dma((8,)),
        dma((nspot,)), dma((nspot,)), dma((nspot,)), dma((nspot,)),
        dma((nspot,)), dma((nspot,)), dma((nspot,)), dma((nspot,)),
        dma((4,)), dma((4,)), dma((4,)), dma((4,)),
        dma((4,)), dma((4,)), dma((4,)), dma((4,)), dma((4,)), dma((4,)), dma((4,)), dma((4,)),
        dma((nspot,)), dma((nspot,)), dma((nspot,)), dma((nspot,)), dma((4,)), dma((4,)), dma((1,)), dma((1,)),
    ]
    v, a = pl.BlockSpec(memory_space=pltpu.VMEM), pl.BlockSpec(memory_space=pl.ANY)
    loss, grad_logits, grad_filt, grad_expr = pl.pallas_call(
        functools.partial(group_kernel, nspot),
        out_shape=[
            jax.ShapeDtypeStruct((1, 1), f32),
            jax.ShapeDtypeStruct((rows, cells), f32),
            jax.ShapeDtypeStruct((1, cd), f32),
            jax.ShapeDtypeStruct((cd, half), f32),
        ],
        in_specs=[v, v, a, a, v, v],
        out_specs=[pl.BlockSpec(memory_space=pltpu.SMEM), v, v, v],
        scratch_shapes=buffers + sems,
        compiler_params=pltpu.CompilerParams(
            collective_id=0, has_side_effects=True, vmem_limit_bytes=VMEM_BYTES
        ),
        name="group_step",
    )(logits, filt.reshape(-1, 128), expr, target, gene_mask, density.reshape(-1, 128))
    return (loss.reshape(()), grad_logits, grad_filt.reshape(-1), grad_expr)


def fits(logits, filt, expr):
    nspot = lax.axis_size("spot")
    rows, cells = logits.shape
    held = cells * (expr.shape[1] // GROUP) * 2 * 2 + 2 * GROUP * rows * cells * 2
    return (
        nspot == GROUP * SLIDES
        and lax.axis_size("gene") == 2
        and rows == 128
        and filt.shape[0] == 256
        and held <= 16 << 20
    )


def per_device(logits, filt, expr, target, gene_mask, density):
    plan = grouped if fits(logits, filt, expr) else streamed
    return plan(logits, filt, expr, target, gene_mask, density)


def solution(mesh):
    in_specs = (
        P(("spot", "gene"), None),
        P("spot"),
        P("spot", "gene"),
        P("spot", "gene"),
        P(None, "gene"),
        P("spot"),
    )
    out_specs = (P(), P(("spot", "gene"), None), P("spot"), P("spot", "gene"))
    return jax.shard_map(
        per_device, mesh=mesh, in_specs=in_specs, out_specs=out_specs, check_vma=False
    )
```

```python
import functools

import jax
import jax.numpy as jnp
from jax import lax
from jax.experimental import pallas as pl
from jax.experimental.pallas import tpu as pltpu
from jax.sharding import PartitionSpec as P

SPOTS = 4096
SLIDES = 4


eps_norm = 1e-06


def slide_moments(onehot, pred, truth):
    hi = lax.Precision.HIGHEST
    return jnp.stack(
        [
            jnp.dot(onehot.T, pred * truth, precision=hi),
            jnp.dot(onehot.T, pred * pred, precision=hi),
            jnp.dot(onehot.T, truth * truth, precision=hi),
        ]
    )


def spot_moments(pred, truth):
    return jnp.stack(
        [
            jnp.sum(pred * truth, axis=1),
            jnp.sum(pred * pred, axis=1),
            jnp.sum(truth * truth, axis=1),
        ]
    )


def cosine_parts(slide_stats):
    dots = slide_stats[0]
    slide_a = lax.rsqrt(slide_stats[1] + eps_norm)
    slide_b = lax.rsqrt(slide_stats[2] + eps_norm)
    return (dots, slide_a, slide_b, dots * slide_a * slide_b)


def pred_gradient(onehot, weight_slide, dots, slide_a, slide_b, spot_stats, pred, truth):
    hi = lax.Precision.HIGHEST
    spot_a = lax.rsqrt(spot_stats[1] + eps_norm)
    spot_b = lax.rsqrt(spot_stats[2] + eps_norm)
    coef_truth = -weight_slide * slide_a * slide_b
    coef_pred = weight_slide * dots * slide_a**3 * slide_b
    grad_pred = (
        jnp.dot(onehot, coef_truth, precision=hi) * truth
        + jnp.dot(onehot, coef_pred, precision=hi) * pred
    )
    grad_pred = (
        grad_pred
        + (
            -(spot_a * spot_b)[:, None] * truth
            + (spot_stats[0] * spot_a**3 * spot_b)[:, None] * pred
        )
        / SPOTS
    )
    return (grad_pred, spot_stats[0] * spot_a * spot_b)


def streamed(logits, filt, expr, target, gene_mask, density):
    f32 = jnp.float32
    bf16 = jnp.bfloat16
    nspot = lax.axis_size("spot")
    ngene = lax.axis_size("gene")
    spot_dev = logits.shape[0]
    cells = logits.shape[1]
    cell_dev = filt.shape[0]
    owned = target.shape[0]
    half = target.shape[1]
    spots_all = owned * nspot
    slide_len = SPOTS // SLIDES
    scores = logits.astype(f32)
    shifted = jnp.exp(scores - jnp.max(scores, axis=1, keepdims=True))
    probs = shifted / jnp.sum(shifted, axis=1, keepdims=True)
    moved = lax.all_to_all(probs.astype(bf16), "spot", split_axis=1, concat_axis=0, tiled=True)
    paired = lax.all_gather(moved.reshape(nspot, 1, spot_dev, cell_dev), "gene", axis=1, tiled=True)
    paired = paired.reshape(spots_all, cell_dev)
    gate = jax.nn.sigmoid(filt)
    weighted = (paired.astype(f32) * gate[None, :]).astype(bf16)
    partial_pred = jnp.dot(weighted, expr, preferred_element_type=f32)
    partial_mass = jnp.sum(weighted.astype(f32), axis=1)
    gate_part = jnp.sum(gate)
    maskf = gene_mask.astype(f32)
    mask_part = jnp.sum(maskf, axis=1)
    pred_three, mass_two = (
        lax.psum_scatter(
            partial_pred.reshape(nspot, owned, half), "spot", scatter_dimension=0, tiled=True
        ),
        lax.psum_scatter(
            partial_mass.reshape(nspot, owned), "spot", scatter_dimension=0, tiled=True
        ),
    )
    pred = pred_three.reshape(owned, half)
    mass = mass_two.reshape(owned)
    truth = target.astype(f32)
    dens = density.astype(f32)
    spot_ids = lax.axis_index("spot") * owned + jnp.arange(owned, dtype=jnp.int32)
    onehot = (
        spot_ids[:, None] // slide_len == jnp.arange(SLIDES, dtype=jnp.int32)[None, :]
    ).astype(f32)
    slide_stats, mass_total, gate_total, count_total = lax.psum(
        (slide_moments(onehot, pred, truth), jnp.sum(mass), gate_part, jnp.sum(dens)), "spot"
    )
    dots, slide_a, slide_b, cos_gene = cosine_parts(slide_stats)
    spot_stats, kept_genes, gene_numer = lax.psum(
        (spot_moments(pred, truth), mask_part, jnp.sum(maskf * cos_gene, axis=1)), "gene"
    )
    genes_kept = jnp.maximum(kept_genes, 1.0)
    weight_slide = maskf / genes_kept[:, None] / SLIDES
    grad_pred, cos_spot = pred_gradient(
        onehot, weight_slide, dots, slide_a, slide_b, spot_stats, pred, truth
    )
    share = dens / count_total
    kl_local = jnp.sum(share * (jnp.log(share) - jnp.log(mass) + jnp.log(mass_total)))
    cos_total, kl_total = lax.psum((jnp.sum(cos_spot), kl_local), "spot")
    grad_mass = 1.0 / mass_total - share / mass
    spread_three, spread_two = (
        lax.all_gather(grad_pred.astype(bf16).reshape(1, owned, half), "spot", axis=0, tiled=True),
        lax.all_gather(grad_mass.astype(bf16).reshape(1, owned), "spot", axis=0, tiled=True),
    )
    spread_pred = spread_three.reshape(spots_all, half)
    spread_mass = spread_two.reshape(spots_all)
    gene_term = jnp.mean(gene_numer / genes_kept)
    excess = gate_total / count_total - 1.0
    loss = -gene_term - cos_total / SPOTS + kl_total + excess * excess
    grad_expr = lax.dot_general(
        weighted, spread_pred, (((0,), (0,)), ((), ())), preferred_element_type=f32
    )
    first_half = (lax.axis_index("gene") == 0).astype(f32)
    grad_weighted = lax.dot_general(
        spread_pred, expr, (((1,), (1,)), ((), ())), preferred_element_type=f32
    )
    grad_weighted = grad_weighted + first_half * spread_mass.astype(f32)[:, None]
    filter_part = jnp.sum(grad_weighted * paired.astype(f32), axis=0)
    filter_total = lax.psum(filter_part, "gene")
    grad_filt = (filter_total + 2.0 * excess / count_total) * gate * (1.0 - gate)
    terms = (grad_weighted * gate[None, :]).reshape(nspot, ngene, spot_dev, cell_dev)
    moved_back = lax.all_to_all(terms, "spot", split_axis=0, concat_axis=3, tiled=True)
    folded = lax.psum_scatter(moved_back, "gene", scatter_dimension=1, tiled=True)
    rounded = lax.optimization_barrier(folded.reshape(spot_dev, cells).astype(bf16))
    grad_probs = rounded.astype(f32)
    grad_logits = probs * (grad_probs - jnp.sum(probs * grad_probs, axis=1, keepdims=True))
    return (loss, grad_logits, grad_filt, grad_expr)


GROUP = 4
MESH = pl.DeviceIdType.MESH
VMEM_BYTES = 48 << 20
LAST_BYTES = 16 << 20
POS = {0: 0, 1: 1, 3: 2, 2: 3}


def remote(src, dst, send, recv, dev):
    return pltpu.make_async_remote_copy(
        src_ref=src, dst_ref=dst, send_sem=send, recv_sem=recv, device_id=dev, device_id_type=MESH
    )


def dot_nt(a, b):
    return lax.dot_general(a, b, (((1,), (1,)), ((), ())), preferred_element_type=jnp.float32)


def column(row, length):
    return jnp.transpose(jnp.broadcast_to(row, (128, length)))


def fold(values):
    total = values[:, 0:128]
    for i in range(1, values.shape[1] // 128):
        total = total + values[:, i * 128 : (i + 1) * 128]
    return total


def lanes_to_row(values):
    return jnp.sum(jnp.transpose(fold(values)), axis=0, keepdims=True)


def group_kernel(
    nspot, logits_h, filt_h, expr, target, mask_h, dens_h,
    loss_o, probs, gpb, tot_o, gf_o, ge_o,
    logits, filt, mask, dens, gateb, raw, wbuf, ebuf, tbuf, pbuf, dpb, dps, dpt,
    small, massb, pair_s, pair_r, stat_s, stat_r,
    sendx, recvx, sendy, recvy, send2x, recv2x, send2y, recv2y, gwr, held, rowsum,
    grad, dsend, dright, dleft, fins, gexpr, fsend, frecv,
    lc, ea_s, ea_r, ez_s, ez_r, es_s, es_r, wx_s, wx_r, wy_s, wy_r, wd_s, wd_r, t_s, t_r,
    sm_s, sm_r, sz_s, sz_r, ma_s, ma_r, fi_s, fi_r, pr_s, pr_r, st_s, st_r,
    x_s, x_r, y_s, y_r, x2_s, x2_r, y2_s, y2_r, dr_s, dr_r, dl_s, dl_r, fn_s, fn_r, dp_s, dp_r,
):
    f32, bf16 = jnp.float32, jnp.bfloat16
    rows, cells = probs.shape
    cd = expr.shape[0]
    gq = expr.shape[1] // GROUP
    nz = nspot // GROUP
    grp = GROUP * rows
    half = cells // 2
    cc = half // 4
    spots_all = nspot * 2 * rows
    me, j = lax.axis_index("spot"), lax.axis_index("gene")
    sib = 1 - j
    z, q = me // GROUP, me % GROUP
    x, y = q % 2, q // 2
    nbr = [me, me + 1 - 2 * x, me + 2 - 4 * y, me + 3 - 2 * x - 4 * y]
    nq = [n % GROUP for n in nbr]
    here = (me, sib)
    has_right, has_left = z < nz - 1, z > 0

    barrier = pltpu.get_barrier_semaphore()

    def greet(dev):
        pl.semaphore_signal(barrier, inc=1, device_id=dev, device_id_type=MESH)

    for k in (1, 2, 3):
        greet((nbr[k], j))

    @pl.when(has_right)
    def _():
        greet((me + GROUP, j))

    @pl.when(has_left)
    def _():
        greet((me - GROUP, j))

    for k in (3, 1, 2, 0):
        greet((nbr[k], sib))

    def eblock(h, o):
        return ebuf.at[h, pl.ds(pl.multiple_of(o * cd, cd), cd), :]

    def ecols(ref, k):
        return ref.at[:, pl.ds(pl.multiple_of(nq[k] * gq, gq), gq)]

    step = 32
    loads = [
        pltpu.make_async_copy(logits_h, logits, lc.at[0]),
        pltpu.make_async_copy(filt_h, filt, lc.at[1]),
        pltpu.make_async_copy(mask_h, mask, lc.at[2]),
        pltpu.make_async_copy(dens_h, dens, lc.at[3]),
        pltpu.make_async_copy(ecols(expr, 0), eblock(0, me), lc.at[4]),
        pltpu.make_async_copy(
            target.at[
                pl.ds(pl.multiple_of(j * rows, rows), rows), pl.ds(pl.multiple_of(q * gq, gq), gq)
            ],
            tbuf.at[0, pl.ds(0, rows), :],
            lc.at[5],
        ),
    ]
    for c in loads:
        c.start()
    loads[0].wait()

    @pl.loop(0, rows // step)
    def _(i):
        at = pl.ds(pl.multiple_of(i * step, step), step)
        s = logits[at, :].astype(f32)
        top = jnp.max(s, axis=1, keepdims=True)
        e = jnp.exp(s - top)
        total = jnp.sum(e, axis=1, keepdims=True)
        p = e * (1.0 / total)
        probs[at, :] = p
        raw[at, :] = p.astype(bf16)

    for c in loads[1:4]:
        c.wait()
    small[pl.ds(me, 1), 0:2, :] = filt[...][None]
    small[pl.ds(me, 1), 2:4, :] = dens[...].astype(f32)[None]
    small[pl.ds(me, 1), 4:8, :] = jnp.zeros((1, 4, 128), f32)
    mine_mask = mask[pl.ds(z, 1), pl.ds(pl.multiple_of(q * gq, gq), gq)].astype(f32)
    kept_mine = jnp.sum(mask[pl.ds(z, 1), :].astype(f32))
    pair_s[0, :, 0:gq] = jnp.broadcast_to(mine_mask, (8, gq))
    pair_s[0, :, gq : 2 * gq] = jnp.broadcast_to(kept_mine, (8, gq))
    for c in loads[4:]:
        c.wait()
    pl.semaphore_wait(barrier, 7 + has_right.astype(jnp.int32) + has_left.astype(jnp.int32))

    def smalls(k):
        return remote(small.at[me], small.at[me], sm_s.at[k], sm_r.at[k], (nbr[k], j))

    for k in (3, 1, 2):
        smalls(k).start()
    ea = [
        remote(ecols(expr, k), eblock(0, me), ea_s.at[k], ea_r.at[k], (nbr[k], j))
        for k in range(1, GROUP)
    ]
    for c in ea:
        c.start()

    def zsend(way, o):
        return remote(
            eblock(0, o), eblock(0, o), ez_s.at[way, o], ez_r.at[o], (me + (GROUP if way == 0 else -GROUP), j)
        )

    def ezwait(o):
        remote(eblock(0, o), eblock(0, o), ez_s.at[0, o], ez_r.at[o], here).wait_recv()

    def esib(o):
        return remote(eblock(0, o), eblock(1, o), es_s.at[o], es_r.at[o], here)

    def spread(o):
        @pl.when(has_right)
        def _():
            zsend(0, o).start()

        @pl.when(has_left)
        def _():
            zsend(1, o).start()

        esib(o).start()

    spread(me)

    def plane(at):
        return small.at[pl.ds(at * GROUP, GROUP)]

    def zsmall(way, at):
        return remote(
            plane(at), plane(at), sz_s.at[way, at], sz_r.at[at], (me + (GROUP if way == 0 else -GROUP), j)
        )

    def pair(i):
        return remote(pair_s.at[i], pair_r.at[i], pr_s.at[i], pr_r.at[i], here)

    pair(0).start()

    def tcopy(k, h):
        jj = j if h == 0 else sib
        src = target.at[
            pl.ds(pl.multiple_of(jj * rows, rows), rows), pl.ds(pl.multiple_of(nq[k] * gq, gq), gq)
        ]
        i = k * 2 + h
        return remote(
            src, tbuf.at[h, pl.ds(POS[k] * rows, rows), :], t_s.at[i], t_r.at[i], (nbr[k], jj)
        )

    tlist = [(k, h) for k in (3, 1, 2, 0) for h in (0, 1) if (k, h) != (0, 0)]
    for k, h in tlist:
        tcopy(k, h).start()

    def wcols(way, u):
        u = u if way == 0 else (u + 4) % 8
        return pl.ds(u * cc, cc)

    def wrows(p):
        return pl.ds(p * rows, rows)

    def wown(way, u):
        to, ss, rs = ((1, wx_s, wx_r), (2, wy_s, wy_r))[way]
        at = wcols(way, u)
        return remote(
            raw.at[wrows(0), at], raw.at[wrows(POS[to]), at], ss.at[u], rs.at[u], (nbr[to], j)
        )

    def wpass(way, m):
        to, ss, rs = ((1, wx_s, wx_r), (2, wy_s, wy_r))[way]
        at = wcols(1 - way, m)
        return remote(
            raw.at[wrows(POS[3 - to]), at], raw.at[wrows(2), at], ss.at[8 + m], rs.at[8 + m], (nbr[to], j)
        )

    def wsib(p, i, at):
        return remote(wbuf.at[0, wrows(p), at], wbuf.at[1, wrows(p), at], wd_s.at[i], wd_r.at[i], here)

    every = pl.ds(0, cells)
    for u in range(8):
        wown(0, u).start()
        wown(1, u).start()

    for k in (1, 2, 3):
        remote(small.at[nbr[k]], small.at[nbr[k]], sm_s.at[k], sm_r.at[k], here).wait_recv()

    @pl.when(has_right)
    def _():
        zsmall(0, z).start()

    @pl.when(has_left)
    def _():
        zsmall(1, z).start()

    def small_hop(s):
        @pl.when(z >= s)
        def _():
            zsmall(0, z - s).wait_recv()

            @pl.when(has_right)
            def _():
                zsmall(0, z - s).start()

        @pl.when(z + s <= nz - 1)
        def _():
            zsmall(1, z + s).wait_recv()

            @pl.when(has_left)
            def _():
                zsmall(1, z + s).start()

    for k in (1, 2, 3):
        remote(eblock(0, nbr[k]), eblock(0, nbr[k]), ea_s.at[k], ea_r.at[k], here).wait_recv()
        spread(nbr[k])
        if k < nz:
            small_hop(k)

    def gated(p, at):
        wbuf[0, wrows(p), at] = (gateb[0:1, at] * raw[wrows(p), at].astype(f32)).astype(bf16)

    def gates():
        for o in range(nspot):
            for h in range(cd // 128):
                g = jax.nn.sigmoid(small[o, h : h + 1, :])
                gateb[:, o * cd + h * 128 : o * cd + (h + 1) * 128] = jnp.broadcast_to(g, (8, 128))

        @pl.loop(0, 8)
        def _(u):
            gated(0, pl.ds(pl.multiple_of(u * cc, cc), cc))

        wsib(0, 0, every).start()
        massb[pl.ds(me, 1), :, :] = dot_nt(jnp.ones((8, cells), bf16), wbuf[0, 0:rows, :])[None]

    n = 0
    for s in range(1, nz):
        for k in range(GROUP):

            @pl.when(z >= s)
            def _():
                o = nbr[k] - GROUP * s
                ezwait(o)

                @pl.when(has_right)
                def _():
                    zsend(0, o).start()

                esib(o).start()

            @pl.when(z + s <= nz - 1)
            def _():
                o = nbr[k] + GROUP * s
                ezwait(o)

                @pl.when(has_left)
                def _():
                    zsend(1, o).start()

                esib(o).start()

            if n == 0:
                gates()
            if n >= 4:
                u = n - 4
                wown(0, u).wait_recv()
                wown(1, u).wait_recv()
                if u < 4:
                    wpass(0, u).start()
                    wpass(1, u).start()
                gated(1, wcols(0, u))
                gated(3, wcols(1, u))
            n += 1
    wsib(1, 1, every).start()
    wsib(3, 2, every).start()

    @pl.loop(0, nspot)
    def _(o):
        esib(o).wait_recv()

    kb = cc

    def project(at, span, first):
        for h in range(2):
            v = jnp.dot(wbuf[0, span, at], ebuf[h, at, :], preferred_element_type=f32)
            to = (span, slice(h * gq, (h + 1) * gq))
            if first:
                pbuf[to] = v
            else:
                pbuf[to] += v

    early = (slice(0, 2 * rows), slice(3 * rows, 4 * rows))
    late = slice(2 * rows, 3 * rows)
    for span in early:
        project(pl.ds(0, kb), span, True)

    @pl.loop(1, cells // kb)
    def _(i):
        for span in early:
            project(pl.ds(pl.multiple_of(i * kb, kb), kb), span, False)

    for k, h in tlist:
        tcopy(k, h).wait_recv()

    def moments(p, which):
        span = slice(p * rows, (p + 1) * rows)
        for h in range(2):
            at = slice(h * gq, (h + 1) * gq)
            t = tbuf[h, span, :].astype(f32)
            v = pbuf[span, at]
            for i in which:
                w = (v * t, v * v, t * t)[i]
                by_gene = jnp.sum(w, axis=0, keepdims=True)
                if p == 0:
                    stat_s[0, i : i + 1, at] = by_gene
                else:
                    stat_s[0, i : i + 1, at] += by_gene
                by_spot = lanes_to_row(w)
                if h == 0:
                    stat_s[1, i : i + 1, span] = by_spot
                else:
                    stat_s[1, i : i + 1, span] += by_spot

    for p in (0, 1, 3):
        moments(p, (0, 1, 2))
    moments(2, (2,))
    pair(0).wait_recv()
    kept = jnp.maximum(kept_mine + jnp.sum(pair_r[0, 0:1, gq : gq + 1]), 1.0)
    weight = jnp.concatenate([mine_mask, pair_r[0, 0:1, 0:gq]], axis=1) / kept / SLIDES

    def gather(buf, r, ss, rs):
        return remote(buf.at[me], buf.at[me], ss.at[r], rs.at[r], ((me + r) % nspot, j))

    def gather_start(buf, ss, rs):
        @pl.loop(1, nspot)
        def _(r):
            gather(buf, r, ss, rs).start()

    def gather_wait(buf, ss, rs):
        @pl.loop(1, nspot)
        def _(r):
            o = (me + nspot - r) % nspot
            remote(buf.at[o], buf.at[o], ss.at[r], rs.at[r], here).wait_recv()

    def gather_sent(buf, ss, rs):
        @pl.loop(1, nspot)
        def _(r):
            gather(buf, r, ss, rs).wait_send()

    gather_start(massb, ma_s, ma_r)

    for m in range(4):
        wpass(0, m).wait_recv()
        wpass(1, m).wait_recv()
        for way in (0, 1):
            at = wcols(1 - way, m)
            gated(2, at)
            project(at, late, m == 0 and way == 0)
    wsib(2, 3, every).start()
    moments(2, (0, 1))

    def stat(k):
        if k == 0:
            return remote(stat_s.at[0], stat_r.at[0], st_s.at[0], st_r.at[0], here)
        return remote(stat_s.at[1], stat_r.at[k], st_s.at[k], st_r.at[k], (nbr[k], j))

    for k in (3, 1, 2, 0):
        stat(k).start()
    stat(0).wait_recv()
    order = (slice(gq, 2 * gq), slice(0, gq))
    slide = [
        jnp.concatenate([stat_r[0, i : i + 1, c] for c in order], axis=1) + stat_s[0, i : i + 1, :]
        for i in range(3)
    ]
    dots = slide[0]
    slide_a = lax.rsqrt(slide[1] + eps_norm)
    slide_b = lax.rsqrt(slide[2] + eps_norm)
    coef_t = -weight * slide_a * slide_b
    coef_p = weight * dots * slide_a**3 * slide_b
    cos_gene = (dots * slide_a * slide_b)[:, 0:gq]
    gene_part = jnp.sum(mine_mask * cos_gene / kept)
    for k in (1, 2, 3):
        stat(k).wait_recv()
    at_pos = {0: 0, 1: 1, 2: 3, 3: 2}
    spot = []
    for i in range(3):
        parts = []
        for p in range(GROUP):
            k = at_pos[p]
            v = stat_s[1, i : i + 1, p * rows : (p + 1) * rows]
            there = [
                stat_r[m, i : i + 1, POS[k ^ m] * rows : (POS[k ^ m] + 1) * rows] for m in (1, 2, 3)
            ]
            parts.append((v + there[0]) + (there[1] + there[2]))
        spot.append(jnp.concatenate(parts, axis=1))
    spot_a = lax.rsqrt(spot[1] + eps_norm)
    spot_b = lax.rsqrt(spot[2] + eps_norm)
    cos_spot = (spot[0] * spot_a * spot_b)[:, 0:rows]
    col_t = column(-(spot_a * spot_b) / spots_all, grp)
    col_p = column(spot[0] * spot_a**3 * spot_b / spots_all, grp)

    for g in range(2 * gq // 128):
        at = slice(g * 128, (g + 1) * 128)
        t = tbuf[g * 128 // gq, :, (g * 128) % gq : (g * 128) % gq + 128].astype(f32)
        dpb[:, at] = ((coef_t[:, at] + col_t) * t + (coef_p[:, at] + col_p) * pbuf[:, at]).astype(bf16)
    dps_copy = remote(dpb.at[:, pl.ds(gq, gq)], dps, dp_s.at[0], dp_r.at[0], here)
    dps_copy.start()

    def xcopy(c):
        return remote(sendx.at[c], recvx.at[c], x_s.at[c], x_r.at[c], (nbr[1], j))

    def ycopy(c):
        return remote(sendy.at[c], recvy.at[c], y_s.at[c], y_r.at[c], (nbr[2], j))

    def x2copy(c):
        return remote(send2x.at[c], recv2x.at[c], x2_s.at[c], x2_r.at[c], (nbr[1], j))

    def y2copy(c):
        return remote(send2y.at[c], recv2y.at[c], y2_s.at[c], y2_r.at[c], (nbr[2], j))

    def weight_grad(at):
        return dot_nt(dpb[:, 0:gq], ebuf[0, at, :]) + dot_nt(dpb[:, gq : 2 * gq], ebuf[1, at, :])

    def dsend_to(way, o):
        if way == 0:
            return remote(dsend.at[o], dright.at[o], dr_s.at[o], dr_r.at[o], (me + GROUP, j))
        return remote(dsend.at[o], dleft.at[o], dl_s.at[o], dl_r.at[o], (me - GROUP, j))

    up = z // (nz // 2)

    def weight_chunk(c):
        lo_at = pl.ds(pl.multiple_of(c * cc, cc), cc)
        d = weight_grad(lo_at)
        gwr[:, lo_at] = d[0:rows]
        sendx[c] = d[rows : 3 * rows].astype(bf16)
        held[0, :, lo_at] = d[3 * rows : 4 * rows]
        xcopy(c).start()
        hi_at = pl.ds(pl.multiple_of(half + c * cc, cc), cc)
        d = weight_grad(hi_at)
        gwr[:, hi_at] = d[0:rows]
        sendy[c] = d[2 * rows : 4 * rows].astype(bf16)
        held[1, :, lo_at] = d[rows : 2 * rows]
        ycopy(c).start()

    def expr_block(k, u):
        kx, ky = k % 2, k // 2
        kq = (x + kx - 2 * x * kx) + 2 * (y + ky - 2 * y * ky)
        to = up * u + (1 - up) * (nz - 1 - u)
        o = to * GROUP + kq
        at = pl.ds(pl.multiple_of(o * cd, cd), cd)
        v = jnp.dot(dpt[:, 0:grp], wbuf[0, :, at], preferred_element_type=f32) + jnp.dot(
            dpt[:, grp : 2 * grp], wbuf[1, :, at], preferred_element_type=f32
        )
        grad[o] = v

        @pl.when((z == 0) & (to > 0))
        def _():
            dsend[o] = v.astype(bf16)
            dsend_to(0, o).start()

        @pl.when((z == nz - 1) & (to < nz - 1))
        def _():
            dsend[o] = v.astype(bf16)
            dsend_to(1, o).start()

    @pl.loop(0, GROUP + nz - 1)
    def _(w):
        @pl.when(w < 4)
        def _():
            weight_chunk(w)

        @pl.when(w == 0)
        def _():
            dpt[:, 0:grp] = jnp.transpose(dpb[:, 0:gq].astype(f32)).astype(bf16)
            for i, p in enumerate((0, 1, 3, 2)):
                wsib(p, i, every).wait_recv()
            dps_copy.wait_recv()
            dpt[:, grp : 2 * grp] = jnp.transpose(dps[...].astype(f32)).astype(bf16)

        @pl.loop(0, nz)
        def _(u):
            @pl.when((w >= u) & (w - u < GROUP))
            def _():
                expr_block(GROUP - 1 - (w - u), u)

    def chain(hops, u, k):
        @pl.when((z == hops) & (z < nz - 1 - u))
        def _():
            o = nbr[k] + GROUP * (nz - 1 - u - z)
            dsend_to(0, o).wait_recv()
            dsend[o] = (grad[o] + dright[o].astype(f32)).astype(bf16)
            dsend_to(0, o).start()

        @pl.when((nz - 1 - z == hops) & (z > u))
        def _():
            o = nbr[k] - GROUP * (z - u)
            dsend_to(1, o).wait_recv()
            dsend[o] = (grad[o] + dleft[o].astype(f32)).astype(bf16)
            dsend_to(1, o).start()

    mine_cols = pl.ds(pl.multiple_of(q * gq, gq), gq)

    def fin(k):
        return remote(fins.at[k - 1], gexpr.at[:, mine_cols], fn_s.at[k], fn_r.at[k], (nbr[k], j))

    def fin_wait(k):
        remote(fins.at[k - 1], gexpr.at[:, pl.ds(pl.multiple_of(nq[k] * gq, gq), gq)],
               fn_s.at[k], fn_r.at[k], here).wait_recv()

    def finish(k):
        o = nbr[k]

        @pl.when(has_left)
        def _():
            dsend_to(0, o).wait_recv()
            grad[o] += dright[o].astype(f32)

        @pl.when(has_right)
        def _():
            dsend_to(1, o).wait_recv()
            grad[o] += dleft[o].astype(f32)

        v = jnp.transpose(grad[o]).astype(bf16)
        if k:
            fins[k - 1] = v
            fin(k).start()
        else:
            gexpr[:, mine_cols] = v

    def relay(c):
        lo_at = pl.ds(c * cc, cc)
        xcopy(c).wait_recv()
        send2y[c] = (held[0, :, lo_at] + recvx[c, rows : 2 * rows].astype(f32)).astype(bf16)
        y2copy(c).start()
        ycopy(c).wait_recv()
        send2x[c] = (held[1, :, lo_at] + recvy[c, 0:rows].astype(f32)).astype(bf16)
        x2copy(c).start()
        gwr[:, lo_at] += recvx[c, 0:rows].astype(f32)
        gwr[:, pl.ds(half + c * cc, cc)] += recvy[c, rows : 2 * rows].astype(f32)

    def fcopy(o):
        return remote(fsend.at[o], frecv.at[me], fi_s.at[o], fi_r.at[me], (o, j))

    def whole(c, gm):
        for base, got, pieces in ((0, y2copy, recv2y), (half, x2copy, recv2x)):
            got(c).wait_recv()
            start = base + c * cc
            at = slice(start, start + cc)
            p = probs[:, at]
            gw = gwr[:, at] + pieces[c].astype(f32) + jnp.concatenate([gm] * (cc // 128), axis=1)
            part = jnp.sum(gw * p.astype(bf16).astype(f32), axis=0, keepdims=True)
            for i in range(cc // cd):
                o = start // cd + i
                fsend[o, 0:1] = part[:, i * cd : (i + 1) * cd]
                fsend[o, 1:2] = loss_part

                @pl.when(me != o)
                def _():
                    fcopy(o).start()

            gp = (gateb[0:1, at] * gw).astype(bf16)
            gpb[:, at] = gp
            v = fold(p * gp.astype(f32))
            if c == 0 and base == 0:
                rowsum[...] = v
            else:
                rowsum[...] += v

    def mass_parts():
        gather_wait(massb, ma_s, ma_r)
        count_total = jnp.zeros((1, 128), f32)
        gate_sum = jnp.zeros((1, 128), f32)
        for o in range(nspot):
            count_total = count_total + small[o, 2:3, :] + small[o, 3:4, :]
        for o in range(cells // 128):
            gate_sum = gate_sum + gateb[0:1, o * 128 : (o + 1) * 128]
        count_total = jnp.sum(count_total)
        gate_total = jnp.sum(gate_sum)
        mass_sum = jnp.zeros((1, 128), f32)
        kl_sum = jnp.zeros((1, 128), f32)
        share_sum = jnp.zeros((1, 128), f32)
        for o in range(nspot):
            m = massb[o, 0:1, :]
            share = jnp.where(j == 0, small[o, 2:3, :], small[o, 3:4, :]) / count_total
            mass_sum = mass_sum + m
            share_sum = share_sum + share
            kl_sum = kl_sum + share * (jnp.log(share) - jnp.log(m))
        pair_s[1, 0:1, 0:128] = mass_sum
        pair_s[1, 1:2, 0:128] = kl_sum
        pair_s[1, 2:3, 0:128] = share_sum
        pair(1).start()
        return count_total, gate_total, mass_sum, kl_sum, share_sum

    def mass_totals(count_total, gate_total, mass_sum, kl_sum, share_sum):
        pair(1).wait_recv()
        mass_total = jnp.sum(mass_sum + pair_r[1, 0:1, 0:128])
        kl_all = jnp.sum(kl_sum + pair_r[1, 1:2, 0:128])
        share_all = jnp.sum(share_sum + pair_r[1, 2:3, 0:128])
        log_total = jnp.sum(jnp.log(jnp.full((1, 128), mass_total))[:, 0:1])
        excess = gate_total / count_total - 1.0
        my_dens = small[pl.ds(me, 1), pl.ds(2 + j, 1), :].reshape(1, 128)
        my_mass = massb[pl.ds(me, 1), 0:1, :].reshape(1, 128)
        gm_row = (1.0 / mass_total - my_dens / count_total / my_mass).astype(bf16).astype(f32)
        return kl_all + share_all * log_total + excess * excess, excess, column(gm_row, rows)

    def forward_sent():
        for c in ea:
            c.wait_send()
        for k, h in tlist:
            tcopy(k, h).wait_send()
        for k in (1, 2, 3):
            smalls(k).wait_send()
        for way in (0, 1):
            for u in range(8):
                wown(way, u).wait_send()
            for m in range(4):
                wpass(way, m).wait_send()
        for i, p in enumerate((0, 1, 3, 2)):
            wsib(p, i, every).wait_send()
        for i in range(4):
            stat(i).wait_send()
        dps_copy.wait_send()

    def along_sent():
        @pl.loop(0, nspot)
        def _(o):
            esib(o).wait_send()
            at = o // GROUP

            @pl.when(has_right & (at <= z))
            def _():
                zsend(0, o).wait_send()

            @pl.when(has_left & (at >= z))
            def _():
                zsend(1, o).wait_send()

        @pl.loop(0, nz)
        def _(at):
            @pl.when(has_right & (at <= z))
            def _():
                zsmall(0, at).wait_send()

            @pl.when(has_left & (at >= z))
            def _():
                zsmall(1, at).wait_send()

    relay(0)
    chain(1, 0, 3)
    chain(1, 1, 3)
    totals = mass_parts()
    chain(1, 0, 2)
    rest, excess, gm = mass_totals(*totals)
    relay(1)
    chain(2, 0, 3)
    forward_sent()
    chain(2, 0, 2)
    chain(1, 1, 2)
    relay(2)
    chain(1, 0, 1)
    along_sent()
    gather_sent(massb, ma_s, ma_r)
    relay(3)
    finish(3)
    finish(2)
    chain(2, 0, 1)
    chain(1, 1, 1)
    loss_part = jnp.broadcast_to(-gene_part / SLIDES - jnp.sum(cos_spot) / spots_all, (1, cd))
    whole(0, gm)
    chain(1, 0, 0)
    whole(1, gm)
    finish(1)
    chain(2, 0, 0)
    chain(1, 1, 0)
    whole(2, gm)
    whole(3, gm)

    frecv[pl.ds(me, 1)] = fsend[pl.ds(me, 1)]

    def others(act):
        @pl.loop(0, nspot)
        def _(o):
            @pl.when(o != me)
            def _():
                act(o)

    tot_o[...] = jnp.broadcast_to(jnp.sum(rowsum[...], axis=1, keepdims=True), (rows, 128))
    finish(0)
    others(lambda o: remote(fsend.at[o], frecv.at[o], fi_s.at[o], fi_r.at[o], here).wait_recv())
    ftotal = frecv[0]
    for o in range(1, nspot):
        ftotal = ftotal + frecv[o]
    pair_s[2, 0:2, 0:cd] = ftotal
    pair(2).start()
    count_total = totals[0]
    my_gate = jax.nn.sigmoid(filt[...])

    others(lambda o: fcopy(o).wait_send())
    for k in range(1, GROUP):
        fin(k).wait_send()

    @pl.loop(0, 4)
    def _(c):
        xcopy(c).wait_send()
        ycopy(c).wait_send()
        x2copy(c).wait_send()
        y2copy(c).wait_send()

    @pl.loop(0, nspot)
    def _(o):
        at = o // GROUP

        @pl.when(has_right & (at > z))
        def _():
            dsend_to(0, o).wait_send()

        @pl.when(has_left & (at < z))
        def _():
            dsend_to(1, o).wait_send()

    for i in range(3):
        pair(i).wait_send()
    pair(2).wait_recv()
    fsum = ftotal + pair_r[2, 0:2, 0:cd]
    loss_o[0, 0] = jnp.sum(fsum[1:2, 0:1]) + rest
    fsum = fsum[0:1] + 2.0 * excess / count_total
    for h in range(cd // 128):
        g = my_gate[h : h + 1, :]
        gf_o[h : h + 1, :] = fsum[:, h * 128 : (h + 1) * 128] * g * (1.0 - g)
    for k in (3, 2, 1):
        fin_wait(k)
    ge_o[...] = gexpr[...]


def finish_kernel(probs, gp, tot, ge, loss, gf, gl_o, ge_o, loss_o, gf_o, gl, gx, out_s):
    f32 = jnp.float32
    parts = 4
    cc = probs.shape[1] // parts
    copies = []
    for i in range(parts):
        for c in range(i * cc, (i + 1) * cc, 128):
            at = slice(c, c + 128)
            gl[:, at] = probs[:, at] * (gp[:, at].astype(f32) - tot[...])
        at = pl.ds(i * cc, cc)
        copies.append(pltpu.make_async_copy(gl.at[:, at], gl_o.at[:, at], out_s.at[i]))
        copies[-1].start()
    gx[...] = ge[...].astype(f32)
    copies.append(pltpu.make_async_copy(gx, ge_o, out_s.at[parts]))
    copies[-1].start()
    gf_o[...] = gf[...]
    loss_o[0, 0] = loss[0, 0]
    for c in copies:
        c.wait()


def grouped(logits, filt, expr, target, gene_mask, density):
    f32, bf16, i32 = jnp.float32, jnp.bfloat16, jnp.int32
    nspot = lax.axis_size("spot")
    rows, cells = logits.shape
    cd, half = expr.shape
    gq = half // GROUP
    grp = GROUP * rows
    hc = cells // 2
    cc = hc // 4
    nz = nspot // GROUP
    wide = max(2 * gq, grp, cd, 128)

    def vmem(*shape, dtype=f32):
        return pltpu.VMEM(shape, dtype)

    def dma(*shape):
        return pltpu.SemaphoreType.DMA(shape)

    buffers = [
        vmem(rows, cells, dtype=bf16), vmem(cd // 128, 128), vmem(*gene_mask.shape, dtype=i32),
        vmem(2 * rows // 128, 128, dtype=i32),
        vmem(8, cells), vmem(grp, cells, dtype=bf16), vmem(2, grp, cells, dtype=bf16),
        vmem(2, cells, gq, dtype=bf16),
        vmem(2, grp, gq, dtype=bf16), vmem(grp, 2 * gq), vmem(grp, 2 * gq, dtype=bf16),
        vmem(grp, gq, dtype=bf16), vmem(gq, 2 * grp, dtype=bf16),
        vmem(nspot, 8, 128), vmem(nspot, 8, 128),
        vmem(4, 8, wide), vmem(4, 8, wide), vmem(2, 8, wide), vmem(4, 8, wide),
        vmem(4, 2 * rows, cc, dtype=bf16), vmem(4, 2 * rows, cc, dtype=bf16),
        vmem(4, 2 * rows, cc, dtype=bf16), vmem(4, 2 * rows, cc, dtype=bf16),
        vmem(4, rows, cc, dtype=bf16), vmem(4, rows, cc, dtype=bf16),
        vmem(4, rows, cc, dtype=bf16), vmem(4, rows, cc, dtype=bf16),
        vmem(rows, cells), vmem(2, rows, hc), vmem(rows, 128),
        vmem(nspot, gq, cd), vmem(nspot, gq, cd, dtype=bf16),
        vmem(nspot, gq, cd, dtype=bf16), vmem(nspot, gq, cd, dtype=bf16),
        vmem(3, cd, gq, dtype=bf16), vmem(cd, half, dtype=bf16),
        vmem(nspot, 2, cd), vmem(nspot, 2, cd),
    ]
    sems = [
        dma(6), dma(4), dma(4), dma(2, nspot), dma(nspot), dma(nspot), dma(nspot),
        dma(12), dma(12), dma(12), dma(12), dma(4), dma(4), dma(8), dma(8),
        dma(4), dma(4), dma(2, nz), dma(nz), dma(nspot), dma(nspot),
        dma(nspot), dma(nspot),
        dma(4), dma(4), dma(4), dma(4),
        dma(4), dma(4), dma(4), dma(4), dma(4), dma(4), dma(4), dma(4),
        dma(nspot), dma(nspot), dma(nspot), dma(nspot), dma(4), dma(4), dma(1), dma(1),
    ]
    v, a = pl.BlockSpec(memory_space=pltpu.VMEM), pl.BlockSpec(memory_space=pl.ANY)
    s, hbm = pl.BlockSpec(memory_space=pltpu.SMEM), pl.BlockSpec(memory_space=pltpu.HBM)
    shape = jax.ShapeDtypeStruct
    fparts = (cd // 128, 128)
    given = (logits, filt.reshape(-1, 128), expr, target, gene_mask, density.reshape(-1, 128))
    loss, probs, gp, tot, grad_filt, grad_expr = pl.pallas_call(
        functools.partial(group_kernel, nspot),
        out_shape=[
            shape((1, 1), f32),
            vmem(rows, cells),
            vmem(rows, cells, dtype=bf16),
            vmem(rows, 128),
            vmem(*fparts),
            vmem(cd, half, dtype=bf16),
        ],
        in_specs=[hbm] * 6,
        out_specs=[s, v, v, v, v, v],
        scratch_shapes=buffers + sems,
        compiler_params=pltpu.CompilerParams(
            collective_id=0, has_side_effects=True, vmem_limit_bytes=VMEM_BYTES
        ),
        name="group_step",
    )(*(pltpu.with_memory_space_constraint(v, pltpu.HBM) for v in given))
    grad_logits, grad_expr, loss, grad_filt = pl.pallas_call(
        finish_kernel,
        out_shape=[shape((rows, cells), f32), shape((cd, half), f32), shape((1, 1), f32), shape(fparts, f32)],
        in_specs=[v, v, v, v, s, v],
        out_specs=[a, a, s, v],
        scratch_shapes=[vmem(rows, cells), vmem(cd, half), dma(5)],
        compiler_params=pltpu.CompilerParams(vmem_limit_bytes=LAST_BYTES),
        name="finish_step",
    )(probs, gp, tot, grad_expr, loss, grad_filt)
    return (loss.reshape(()), grad_logits, grad_filt.reshape(-1), grad_expr)


def fits(logits, filt, expr):
    nspot = lax.axis_size("spot")
    rows, cells = logits.shape
    held = cells * (expr.shape[1] // GROUP) * 2 * 2 + 2 * GROUP * rows * cells * 2
    return (
        nspot == GROUP * SLIDES
        and lax.axis_size("gene") == 2
        and rows == 128
        and filt.shape[0] == 256
        and held <= 16 << 20
    )


def per_device(logits, filt, expr, target, gene_mask, density):
    plan = grouped if fits(logits, filt, expr) else streamed
    return plan(logits, filt, expr, target, gene_mask, density)


def solution(mesh):
    in_specs = (
        P(("spot", "gene"), None),
        P("spot"),
        P("spot", "gene"),
        P("spot", "gene"),
        P(None, "gene"),
        P("spot"),
    )
    out_specs = (P(), P(("spot", "gene"), None), P("spot"), P("spot", "gene"))
    return jax.shard_map(
        per_device, mesh=mesh, in_specs=in_specs, out_specs=out_specs, check_vma=False
    )
```

```python
import functools

import jax
import jax.numpy as jnp
from jax import lax
from jax.experimental import pallas as pl
from jax.experimental.pallas import tpu as pltpu
from jax.sharding import PartitionSpec as P

SPOTS = 4096
SLIDES = 4


eps_norm = 1e-06


def slide_moments(onehot, pred, truth):
    hi = lax.Precision.HIGHEST
    return jnp.stack(
        [
            jnp.dot(onehot.T, pred * truth, precision=hi),
            jnp.dot(onehot.T, pred * pred, precision=hi),
            jnp.dot(onehot.T, truth * truth, precision=hi),
        ]
    )


def spot_moments(pred, truth):
    return jnp.stack(
        [
            jnp.sum(pred * truth, axis=1),
            jnp.sum(pred * pred, axis=1),
            jnp.sum(truth * truth, axis=1),
        ]
    )


def cosine_parts(slide_stats):
    dots = slide_stats[0]
    slide_a = lax.rsqrt(slide_stats[1] + eps_norm)
    slide_b = lax.rsqrt(slide_stats[2] + eps_norm)
    return (dots, slide_a, slide_b, dots * slide_a * slide_b)


def pred_gradient(onehot, weight_slide, dots, slide_a, slide_b, spot_stats, pred, truth):
    hi = lax.Precision.HIGHEST
    spot_a = lax.rsqrt(spot_stats[1] + eps_norm)
    spot_b = lax.rsqrt(spot_stats[2] + eps_norm)
    coef_truth = -weight_slide * slide_a * slide_b
    coef_pred = weight_slide * dots * slide_a**3 * slide_b
    grad_pred = (
        jnp.dot(onehot, coef_truth, precision=hi) * truth
        + jnp.dot(onehot, coef_pred, precision=hi) * pred
    )
    grad_pred = (
        grad_pred
        + (
            -(spot_a * spot_b)[:, None] * truth
            + (spot_stats[0] * spot_a**3 * spot_b)[:, None] * pred
        )
        / SPOTS
    )
    return (grad_pred, spot_stats[0] * spot_a * spot_b)


def streamed(logits, filt, expr, target, gene_mask, density):
    f32 = jnp.float32
    bf16 = jnp.bfloat16
    nspot = lax.axis_size("spot")
    ngene = lax.axis_size("gene")
    spot_dev = logits.shape[0]
    cells = logits.shape[1]
    cell_dev = filt.shape[0]
    owned = target.shape[0]
    half = target.shape[1]
    spots_all = owned * nspot
    slide_len = SPOTS // SLIDES
    scores = logits.astype(f32)
    shifted = jnp.exp(scores - jnp.max(scores, axis=1, keepdims=True))
    probs = shifted / jnp.sum(shifted, axis=1, keepdims=True)
    moved = lax.all_to_all(probs.astype(bf16), "spot", split_axis=1, concat_axis=0, tiled=True)
    paired = lax.all_gather(moved.reshape(nspot, 1, spot_dev, cell_dev), "gene", axis=1, tiled=True)
    paired = paired.reshape(spots_all, cell_dev)
    gate = jax.nn.sigmoid(filt)
    weighted = (paired.astype(f32) * gate[None, :]).astype(bf16)
    partial_pred = jnp.dot(weighted, expr, preferred_element_type=f32)
    partial_mass = jnp.sum(weighted.astype(f32), axis=1)
    gate_part = jnp.sum(gate)
    maskf = gene_mask.astype(f32)
    mask_part = jnp.sum(maskf, axis=1)
    pred_three, mass_two = (
        lax.psum_scatter(
            partial_pred.reshape(nspot, owned, half), "spot", scatter_dimension=0, tiled=True
        ),
        lax.psum_scatter(
            partial_mass.reshape(nspot, owned), "spot", scatter_dimension=0, tiled=True
        ),
    )
    pred = pred_three.reshape(owned, half)
    mass = mass_two.reshape(owned)
    truth = target.astype(f32)
    dens = density.astype(f32)
    spot_ids = lax.axis_index("spot") * owned + jnp.arange(owned, dtype=jnp.int32)
    onehot = (
        spot_ids[:, None] // slide_len == jnp.arange(SLIDES, dtype=jnp.int32)[None, :]
    ).astype(f32)
    slide_stats, mass_total, gate_total, count_total = lax.psum(
        (slide_moments(onehot, pred, truth), jnp.sum(mass), gate_part, jnp.sum(dens)), "spot"
    )
    dots, slide_a, slide_b, cos_gene = cosine_parts(slide_stats)
    spot_stats, kept_genes, gene_numer = lax.psum(
        (spot_moments(pred, truth), mask_part, jnp.sum(maskf * cos_gene, axis=1)), "gene"
    )
    genes_kept = jnp.maximum(kept_genes, 1.0)
    weight_slide = maskf / genes_kept[:, None] / SLIDES
    grad_pred, cos_spot = pred_gradient(
        onehot, weight_slide, dots, slide_a, slide_b, spot_stats, pred, truth
    )
    share = dens / count_total
    kl_local = jnp.sum(share * (jnp.log(share) - jnp.log(mass) + jnp.log(mass_total)))
    cos_total, kl_total = lax.psum((jnp.sum(cos_spot), kl_local), "spot")
    grad_mass = 1.0 / mass_total - share / mass
    spread_three, spread_two = (
        lax.all_gather(grad_pred.astype(bf16).reshape(1, owned, half), "spot", axis=0, tiled=True),
        lax.all_gather(grad_mass.astype(bf16).reshape(1, owned), "spot", axis=0, tiled=True),
    )
    spread_pred = spread_three.reshape(spots_all, half)
    spread_mass = spread_two.reshape(spots_all)
    gene_term = jnp.mean(gene_numer / genes_kept)
    excess = gate_total / count_total - 1.0
    loss = -gene_term - cos_total / SPOTS + kl_total + excess * excess
    grad_expr = lax.dot_general(
        weighted, spread_pred, (((0,), (0,)), ((), ())), preferred_element_type=f32
    )
    first_half = (lax.axis_index("gene") == 0).astype(f32)
    grad_weighted = lax.dot_general(
        spread_pred, expr, (((1,), (1,)), ((), ())), preferred_element_type=f32
    )
    grad_weighted = grad_weighted + first_half * spread_mass.astype(f32)[:, None]
    filter_part = jnp.sum(grad_weighted * paired.astype(f32), axis=0)
    filter_total = lax.psum(filter_part, "gene")
    grad_filt = (filter_total + 2.0 * excess / count_total) * gate * (1.0 - gate)
    terms = (grad_weighted * gate[None, :]).reshape(nspot, ngene, spot_dev, cell_dev)
    moved_back = lax.all_to_all(terms, "spot", split_axis=0, concat_axis=3, tiled=True)
    folded = lax.psum_scatter(moved_back, "gene", scatter_dimension=1, tiled=True)
    rounded = lax.optimization_barrier(folded.reshape(spot_dev, cells).astype(bf16))
    grad_probs = rounded.astype(f32)
    grad_logits = probs * (grad_probs - jnp.sum(probs * grad_probs, axis=1, keepdims=True))
    return (loss, grad_logits, grad_filt, grad_expr)


GROUP = 4
MESH = pl.DeviceIdType.MESH
VMEM_BYTES = 48 << 20
LAST_BYTES = 16 << 20


def remote(src, dst, send, recv, dev):
    return pltpu.make_async_remote_copy(
        src_ref=src, dst_ref=dst, send_sem=send, recv_sem=recv, device_id=dev, device_id_type=MESH
    )


def dot_nt(a, b):
    return lax.dot_general(a, b, (((1,), (1,)), ((), ())), preferred_element_type=jnp.float32)


def column(row, length):
    return jnp.transpose(jnp.broadcast_to(row, (128, length)))


def fold(values):
    total = values[:, 0:128]
    for i in range(1, values.shape[1] // 128):
        total = total + values[:, i * 128 : (i + 1) * 128]
    return total


def lanes_to_row(values):
    return jnp.sum(jnp.transpose(fold(values)), axis=0, keepdims=True)


def group_kernel(
    nspot, logits_h, filt_h, expr, target, mask_h, dens_h,
    probs, gpb, tot_o, last_o, ge_o,
    logits, filt, mask, dens, gateb, raw, wbuf, ebuf, tbuf, pbuf, dpb, dps, dpt,
    small, massb, pair_s, pair_r, stat_s, stat_r,
    sendx, recvx, sendy, recvy, send2x, recv2x, send2y, recv2y, gwr, held, rowsum,
    grad, dsend, dright, dleft, fins, gexpr, fsend, frecv,
    lc, ea_s, ea_r, ez_s, ez_r, es_s, es_r, wx_s, wx_r, wy_s, wy_r, wd_s, wd_r, t_s, t_r,
    sm_s, sm_r, sz_s, sz_r, ma_s, ma_r, fi_s, fi_r, pr_s, pr_r, st_s, st_r,
    x_s, x_r, y_s, y_r, x2_s, x2_r, y2_s, y2_r, dr_s, dr_r, dl_s, dl_r, fn_s, fn_r, dp_s, dp_r,
):
    f32, bf16 = jnp.float32, jnp.bfloat16
    rows, cells = probs.shape
    cd = expr.shape[0]
    gq = expr.shape[1] // GROUP
    nz = nspot // GROUP
    grp = GROUP * rows
    half = cells // 2
    cc = half // 4
    spots_all = nspot * 2 * rows
    me, j = lax.axis_index("spot"), lax.axis_index("gene")
    sib = 1 - j
    z, q = me // GROUP, me % GROUP
    x, y = q % 2, q // 2
    nbr = [me, me + 1 - 2 * x, me + 2 - 4 * y, me + 3 - 2 * x - 4 * y]
    nq = [n % GROUP for n in nbr]
    here = (me, sib)
    has_right, has_left = z < nz - 1, z > 0

    barrier = pltpu.get_barrier_semaphore()

    def greet(dev):
        pl.semaphore_signal(barrier, inc=1, device_id=dev, device_id_type=MESH)

    greet((nbr[1], j))
    greet((nbr[2], j))

    @pl.when(has_right)
    def _():
        greet((me + GROUP, j))

    @pl.when(has_left)
    def _():
        greet((me - GROUP, j))

    greet(here)

    def eblock(h, o):
        return ebuf.at[h, pl.ds(pl.multiple_of(o * cd, cd), cd), :]

    def ecols(ref, k):
        return ref.at[:, pl.ds(pl.multiple_of(nq[k] * gq, gq), gq)]

    step = 32
    loads = [
        pltpu.make_async_copy(logits_h, logits, lc.at[0]),
        pltpu.make_async_copy(filt_h, filt, lc.at[1]),
        pltpu.make_async_copy(mask_h, mask, lc.at[2]),
        pltpu.make_async_copy(dens_h, dens, lc.at[3]),
        pltpu.make_async_copy(ecols(expr, 0), eblock(0, me), lc.at[4]),
        pltpu.make_async_copy(
            target.at[
                pl.ds(pl.multiple_of(j * rows, rows), rows), pl.ds(pl.multiple_of(q * gq, gq), gq)
            ],
            tbuf.at[0, pl.ds(0, rows), :],
            lc.at[5],
        ),
    ]
    for c in loads:
        c.start()
    loads[0].wait()

    @pl.loop(0, rows // step)
    def _(i):
        at = pl.ds(pl.multiple_of(i * step, step), step)
        s = logits[at, :].astype(f32)
        top = jnp.max(s, axis=1, keepdims=True)
        e = jnp.exp(s - top)
        total = jnp.sum(e, axis=1, keepdims=True)
        p = e * (1.0 / total)
        probs[at, :] = p
        raw[at, :] = p.astype(bf16)

    for c in loads[1:4]:
        c.wait()
    small[pl.ds(me, 1), 0:2, :] = filt[...][None]
    small[pl.ds(me, 1), 2:4, :] = dens[...].astype(f32)[None]
    small[pl.ds(me, 1), 4:8, :] = jnp.zeros((1, 4, 128), f32)
    mine_mask = mask[pl.ds(z, 1), pl.ds(pl.multiple_of(q * gq, gq), gq)].astype(f32)
    kept_mine = jnp.sum(mask[pl.ds(z, 1), :].astype(f32))
    pair_s[0, :, 0:gq] = jnp.broadcast_to(mine_mask, (8, gq))
    pair_s[0, :, gq : 2 * gq] = jnp.broadcast_to(kept_mine, (8, gq))
    for c in loads[4:]:
        c.wait()
    pl.semaphore_wait(barrier, 3 + has_right.astype(jnp.int32) + has_left.astype(jnp.int32))

    def smalls(k):
        return remote(small.at[me], small.at[me], sm_s.at[k], sm_r.at[k], (nbr[k], j))

    ea = {
        k: remote(ecols(expr, k), eblock(0, me), ea_s.at[k], ea_r.at[k], (nbr[k], j)) for k in (1, 2, 3)
    }
    for k in (1, 2):
        smalls(k).start()
        ea[k].start()

    def zsend(way, o):
        return remote(
            eblock(0, o), eblock(0, o), ez_s.at[way, o], ez_r.at[o], (me + (GROUP if way == 0 else -GROUP), j)
        )

    def ezwait(o):
        remote(eblock(0, o), eblock(0, o), ez_s.at[0, o], ez_r.at[o], here).wait_recv()

    def esib(o):
        return remote(eblock(0, o), eblock(1, o), es_s.at[o], es_r.at[o], here)

    def spread(o):
        @pl.when(has_right)
        def _():
            zsend(0, o).start()

        @pl.when(has_left)
        def _():
            zsend(1, o).start()

        esib(o).start()

    spread(me)

    def plane(at):
        return small.at[pl.ds(at * GROUP, GROUP)]

    def zsmall(way, at):
        return remote(
            plane(at), plane(at), sz_s.at[way, at], sz_r.at[at], (me + (GROUP if way == 0 else -GROUP), j)
        )

    def pair(i):
        return remote(pair_s.at[i], pair_r.at[i], pr_s.at[i], pr_r.at[i], here)

    pair(0).start()

    def tcopy(k, h):
        jj = j if h == 0 else sib
        src = target.at[
            pl.ds(pl.multiple_of(jj * rows, rows), rows), pl.ds(pl.multiple_of(nq[k] * gq, gq), gq)
        ]
        i = k * 2 + h
        return remote(
            src, tbuf.at[h, pl.ds((k) * rows, rows), :], t_s.at[i], t_r.at[i], (nbr[k], jj)
        )

    def wcols(way, u):
        u = u if way == 0 else (u + 4) % 8
        return pl.ds(u * cc, cc)

    def wrows(p):
        return pl.ds(p * rows, rows)

    def wown(way, u):
        to, ss, rs = ((1, wx_s, wx_r), (2, wy_s, wy_r))[way]
        at = wcols(way, u)
        return remote(
            raw.at[wrows(0), at], raw.at[wrows(to), at], ss.at[u], rs.at[u], (nbr[to], j)
        )

    def wpass(way, m):
        to, ss, rs = ((1, wx_s, wx_r), (2, wy_s, wy_r))[way]
        at = wcols(1 - way, m)
        return remote(
            raw.at[wrows(3 - to), at], raw.at[wrows(3), at], ss.at[8 + m], rs.at[8 + m], (nbr[to], j)
        )

    def wsib(p, i, at):
        return remote(wbuf.at[0, wrows(p), at], wbuf.at[1, wrows(p), at], wd_s.at[i], wd_r.at[i], here)

    every = pl.ds(0, cells)
    def small_wait(k):
        remote(small.at[nbr[k]], small.at[nbr[k]], sm_s.at[k], sm_r.at[k], here).wait_recv()

    small_wait(1)
    smalls(3).start()
    ea[3].start()
    for u in range(8):
        wown(0, u).start()
        wown(1, u).start()

    def small_hop(s):
        @pl.when(z >= s)
        def _():
            zsmall(0, z - s).wait_recv()

            @pl.when(has_right)
            def _():
                zsmall(0, z - s).start()

        @pl.when(z + s <= nz - 1)
        def _():
            zsmall(1, z + s).wait_recv()

            @pl.when(has_left)
            def _():
                zsmall(1, z + s).start()

    def gated(p, at):
        wbuf[0, wrows(p), at] = (gateb[0:1, at] * raw[wrows(p), at].astype(f32)).astype(bf16)

    def gates():
        for o in range(nspot):
            for h in range(cd // 128):
                g = jax.nn.sigmoid(small[o, h : h + 1, :])
                gateb[:, o * cd + h * 128 : o * cd + (h + 1) * 128] = jnp.broadcast_to(g, (8, 128))

        @pl.loop(0, 8)
        def _(u):
            gated(0, pl.ds(pl.multiple_of(u * cc, cc), cc))

        wsib(0, 0, every).start()
        massb[pl.ds(me, 1), :, :] = dot_nt(jnp.ones((8, cells), bf16), wbuf[0, 0:rows, :])[None]

    tlist = [(0, 1)] + [(k, h) for k in (3, 1, 2) for h in (0, 1)]

    def target_start():
        for k in range(GROUP):
            esib(nbr[k]).wait_recv()
        for k, h in tlist:
            tcopy(k, h).start()

    def plane_start():
        small_wait(2)
        small_wait(3)

        @pl.when(has_right)
        def _():
            zsmall(0, z).start()

        @pl.when(has_left)
        def _():
            zsmall(1, z).start()

    def along(s, k):
        if s == 0:
            remote(eblock(0, nbr[k]), eblock(0, nbr[k]), ea_s.at[k], ea_r.at[k], here).wait_recv()
            spread(nbr[k])
            return

        @pl.when(z >= s)
        def _():
            o = nbr[k] - GROUP * s
            ezwait(o)

            @pl.when(has_right)
            def _():
                zsend(0, o).start()

            esib(o).start()

        @pl.when(z + s <= nz - 1)
        def _():
            o = nbr[k] + GROUP * s
            ezwait(o)

            @pl.when(has_left)
            def _():
                zsend(1, o).start()

            esib(o).start()

    def pass_on(m):
        wown(0, m).wait_recv()
        wown(1, m).wait_recv()
        wpass(0, m).start()
        wpass(1, m).start()

    def gate_pieces(first, last):
        for u in range(first, last):
            if u >= 4:
                wown(0, u).wait_recv()
                wown(1, u).wait_recv()
            gated(1, wcols(0, u))
            gated(2, wcols(1, u))

    along(0, 1)
    along(0, 2)
    along(1, 0)
    plane_start()
    along(1, 1)
    pass_on(0)
    along(0, 3)
    along(1, 2)
    pass_on(1)
    along(2, 0)
    small_hop(1)
    pass_on(2)
    along(1, 3)
    pass_on(3)
    target_start()
    along(2, 1)
    small_hop(2)
    along(2, 2)
    along(3, 0)
    along(2, 3)
    small_hop(3)
    gates()
    gate_pieces(0, 8)
    wsib(1, 1, every).start()
    wsib(2, 2, every).start()

    early, late = slice(0, 3 * rows), slice(3 * rows, 4 * rows)
    pc = GROUP * cd
    kb = min(pc, cc)

    def project(at, span, first):
        for h in range(2):
            v = jnp.dot(wbuf[0, span, at], ebuf[h, at, :], preferred_element_type=f32)
            to = (span, slice(h * gq, (h + 1) * gq))
            if first:
                pbuf[to] = v
            else:
                pbuf[to] += v

    def project_plane(at, first):
        for k in range(GROUP):
            if not first:
                esib(at * GROUP + k).wait_recv()
        for i in range(pc // kb):
            project(pl.ds(pl.multiple_of(at * pc + i * kb, kb), kb), early, first and i == 0)

    def project_from(s):
        @pl.when(z >= s)
        def _():
            project_plane(z - s, False)

        @pl.when(z + s <= nz - 1)
        def _():
            project_plane(z + s, False)

    project_plane(z, True)
    project_from(1)
    project_from(2)
    along(3, 1)
    along(3, 2)
    along(3, 3)
    project_from(3)

    def moment(i, p, values, first):
        by_gene = jnp.sum(values, axis=0, keepdims=True)
        if first:
            stat_s[0, i] = by_gene
        else:
            stat_s[0, i] += by_gene
        stat_s[1, i, :, p * rows : (p + 1) * rows] = lanes_to_row(values)

    def squares(p):
        v = pbuf[p * rows : (p + 1) * rows, :]
        moment(0, p, v * v, p == 0)

    def with_target(p, first):
        span = slice(p * rows, (p + 1) * rows)
        t = jnp.concatenate([tbuf[h, span, :].astype(f32) for h in range(2)], axis=1)
        moment(1, p, pbuf[span, :] * t, first)
        moment(2, p, t * t, first)

    def stat(k, late):
        at = pl.ds(1, 2) if late else pl.ds(0, 1)
        i = 2 * k + late
        src, dev = (stat_s.at[0, at], here) if k == 0 else (stat_s.at[1, at], (nbr[k], j))
        return remote(src, stat_r.at[k, at], st_s.at[i], st_r.at[i], dev)

    for p in (0, 1, 2):
        squares(p)
    pair(0).wait_recv()
    kept = jnp.maximum(kept_mine + jnp.sum(pair_r[0, 0:1, gq : gq + 1]), 1.0)
    weight = jnp.concatenate([mine_mask, pair_r[0, 0:1, 0:gq]], axis=1) / kept / SLIDES

    def gather(buf, r, ss, rs):
        return remote(buf.at[me], buf.at[me], ss.at[r], rs.at[r], ((me + r) % nspot, j))

    def gather_start(buf, ss, rs):
        @pl.loop(1, nspot)
        def _(r):
            gather(buf, r, ss, rs).start()

    def gather_wait(buf, ss, rs):
        @pl.loop(1, nspot)
        def _(r):
            o = (me + nspot - r) % nspot
            remote(buf.at[o], buf.at[o], ss.at[r], rs.at[r], here).wait_recv()

    def gather_sent(buf, ss, rs):
        @pl.loop(1, nspot)
        def _(r):
            gather(buf, r, ss, rs).wait_send()

    gather_start(massb, ma_s, ma_r)

    for m in range(4):
        wpass(0, m).wait_recv()
        wpass(1, m).wait_recv()
        for way in (0, 1):
            at = wcols(1 - way, m)
            gated(3, at)
            project(at, late, m == 0 and way == 0)
    wsib(3, 3, every).start()
    squares(3)
    for k in (3, 1, 2, 0):
        stat(k, 0).start()
    tcopy(0, 1).wait_recv()
    with_target(0, True)
    for k in (3, 1, 2):
        tcopy(k, 0).wait_recv()
        tcopy(k, 1).wait_recv()
        with_target(k, False)
    for k in (3, 1, 2, 0):
        stat(k, 1).start()

    for n in (0, 1):
        stat(0, n).wait_recv()
    order = (slice(gq, 2 * gq), slice(0, gq))
    pred_sq, dots, truth_sq = (
        jnp.concatenate([stat_r[0, i, :, c] for c in order], axis=1) + stat_s[0, i] for i in range(3)
    )
    slide_a = lax.rsqrt(pred_sq + eps_norm)
    slide_b = lax.rsqrt(truth_sq + eps_norm)
    coef_t = -weight * slide_a * slide_b
    coef_p = weight * dots * slide_a**3 * slide_b
    cos_gene = (dots * slide_a * slide_b)[:, 0:gq]

    for k in (1, 2, 3):
        for n in (0, 1):
            stat(k, n).wait_recv()
    spot = []
    for i in range(3):
        parts = []
        for k in range(GROUP):
            v = stat_s[1, i, :, k * rows : (k + 1) * rows]
            there = [stat_r[m, i, :, (k ^ m) * rows : ((k ^ m) + 1) * rows] for m in (1, 2, 3)]
            parts.append((v + there[0]) + (there[1] + there[2]))
        spot.append(jnp.concatenate(parts, axis=1))
    spot_pp, spot_dot, spot_tt = spot
    spot_a = lax.rsqrt(spot_pp + eps_norm)
    spot_b = lax.rsqrt(spot_tt + eps_norm)
    cos_spot = (spot_dot * spot_a * spot_b)[:, 0:rows]
    col_t = column(-(spot_a * spot_b) / spots_all, grp)
    col_p = column(spot_dot * spot_a**3 * spot_b / spots_all, grp)

    for g in range(2 * gq // 128):
        at = slice(g * 128, (g + 1) * 128)
        t = tbuf[g * 128 // gq, :, (g * 128) % gq : (g * 128) % gq + 128].astype(f32)
        dpb[:, at] = ((coef_t[:, at] + col_t) * t + (coef_p[:, at] + col_p) * pbuf[:, at]).astype(bf16)
    dps_copy = remote(dpb.at[:, pl.ds(gq, gq)], dps, dp_s.at[0], dp_r.at[0], here)
    dps_copy.start()

    def xcopy(c):
        return remote(sendx.at[c], recvx.at[c], x_s.at[c], x_r.at[c], (nbr[1], j))

    def ycopy(c):
        return remote(sendy.at[c], recvy.at[c], y_s.at[c], y_r.at[c], (nbr[2], j))

    def x2copy(c):
        return remote(send2x.at[c], recv2x.at[c], x2_s.at[c], x2_r.at[c], (nbr[1], j))

    def y2copy(c):
        return remote(send2y.at[c], recv2y.at[c], y2_s.at[c], y2_r.at[c], (nbr[2], j))

    def weight_grad(at):
        return dot_nt(dpb[:, 0:gq], ebuf[0, at, :]) + dot_nt(dpb[:, gq : 2 * gq], ebuf[1, at, :])

    def dsend_to(way, o):
        if way == 0:
            return remote(dsend.at[o], dright.at[o], dr_s.at[o], dr_r.at[o], (me + GROUP, j))
        return remote(dsend.at[o], dleft.at[o], dl_s.at[o], dl_r.at[o], (me - GROUP, j))

    up = z // (nz // 2)

    def weight_chunk(c):
        lo_at = pl.ds(pl.multiple_of(c * cc, cc), cc)
        d = weight_grad(lo_at)
        gwr[:, lo_at] = d[0:rows]
        sendx[c, 0:rows] = d[rows : 2 * rows].astype(bf16)
        sendx[c, rows : 2 * rows] = d[3 * rows : 4 * rows].astype(bf16)
        held[0, :, lo_at] = d[2 * rows : 3 * rows]
        xcopy(c).start()
        hi_at = pl.ds(pl.multiple_of(half + c * cc, cc), cc)
        d = weight_grad(hi_at)
        gwr[:, hi_at] = d[0:rows]
        sendy[c, 0:rows] = d[3 * rows : 4 * rows].astype(bf16)
        sendy[c, rows : 2 * rows] = d[2 * rows : 3 * rows].astype(bf16)
        held[1, :, lo_at] = d[rows : 2 * rows]
        ycopy(c).start()

    def expr_block(k, u):
        kx, ky = k % 2, k // 2
        kq = (x + kx - 2 * x * kx) + 2 * (y + ky - 2 * y * ky)
        to = up * u + (1 - up) * (nz - 1 - u)
        o = to * GROUP + kq
        at = pl.ds(pl.multiple_of(o * cd, cd), cd)
        v = jnp.dot(dpt[:, 0:grp], wbuf[0, :, at], preferred_element_type=f32) + jnp.dot(
            dpt[:, grp : 2 * grp], wbuf[1, :, at], preferred_element_type=f32
        )
        grad[o] = v

        @pl.when((z == 0) & (to > 0))
        def _():
            dsend[o] = v.astype(bf16)
            dsend_to(0, o).start()

        @pl.when((z == nz - 1) & (to < nz - 1))
        def _():
            dsend[o] = v.astype(bf16)
            dsend_to(1, o).start()

    @pl.loop(0, GROUP + nz - 1)
    def _(w):
        @pl.when(w < 4)
        def _():
            weight_chunk(w)

        @pl.when(w == 0)
        def _():
            dpt[:, 0:grp] = jnp.transpose(dpb[:, 0:gq].astype(f32)).astype(bf16)
            for k in range(GROUP):
                wsib(k, k, every).wait_recv()
            dps_copy.wait_recv()
            dpt[:, grp : 2 * grp] = jnp.transpose(dps[...].astype(f32)).astype(bf16)

        @pl.loop(0, nz)
        def _(u):
            @pl.when((w >= u) & (w - u < GROUP))
            def _():
                expr_block(GROUP - 1 - (w - u), u)

    def chain(hops, u, k):
        @pl.when((z == hops) & (z < nz - 1 - u))
        def _():
            o = nbr[k] + GROUP * (nz - 1 - u - z)
            dsend_to(0, o).wait_recv()
            dsend[o] = (grad[o] + dright[o].astype(f32)).astype(bf16)
            dsend_to(0, o).start()

        @pl.when((nz - 1 - z == hops) & (z > u))
        def _():
            o = nbr[k] - GROUP * (z - u)
            dsend_to(1, o).wait_recv()
            dsend[o] = (grad[o] + dleft[o].astype(f32)).astype(bf16)
            dsend_to(1, o).start()

    mine_cols = pl.ds(pl.multiple_of(q * gq, gq), gq)

    def fin(k):
        return remote(fins.at[k - 1], gexpr.at[:, mine_cols], fn_s.at[k], fn_r.at[k], (nbr[k], j))

    def fin_wait(k):
        remote(fins.at[k - 1], gexpr.at[:, pl.ds(pl.multiple_of(nq[k] * gq, gq), gq)],
               fn_s.at[k], fn_r.at[k], here).wait_recv()

    def finish(k):
        o = nbr[k]

        @pl.when(has_left)
        def _():
            dsend_to(0, o).wait_recv()
            grad[o] += dright[o].astype(f32)

        @pl.when(has_right)
        def _():
            dsend_to(1, o).wait_recv()
            grad[o] += dleft[o].astype(f32)

        v = jnp.transpose(grad[o]).astype(bf16)
        if k:
            fins[k - 1] = v
            fin(k).start()
        else:
            gexpr[:, mine_cols] = v

    def relay(c):
        lo_at = pl.ds(c * cc, cc)
        xcopy(c).wait_recv()
        send2y[c] = (held[0, :, lo_at] + recvx[c, rows : 2 * rows].astype(f32)).astype(bf16)
        y2copy(c).start()
        ycopy(c).wait_recv()
        send2x[c] = (held[1, :, lo_at] + recvy[c, 0:rows].astype(f32)).astype(bf16)
        x2copy(c).start()
        gwr[:, lo_at] += recvx[c, 0:rows].astype(f32)
        gwr[:, pl.ds(half + c * cc, cc)] += recvy[c, rows : 2 * rows].astype(f32)

    def fcopy(o):
        return remote(fsend.at[o], frecv.at[me], fi_s.at[o], fi_r.at[me], (o, j))

    def whole(c, gm):
        for base, got, pieces in ((0, y2copy, recv2y), (half, x2copy, recv2x)):
            got(c).wait_recv()
            start = base + c * cc
            at = slice(start, start + cc)
            p = probs[:, at]
            gw = gwr[:, at] + pieces[c].astype(f32) + jnp.concatenate([gm] * (cc // 128), axis=1)
            part = jnp.sum(gw * p.astype(bf16).astype(f32), axis=0, keepdims=True)
            for i in range(cc // cd):
                o = start // cd + i
                fsend[o, 0:1] = part[:, i * cd : (i + 1) * cd]
                fsend[o, 1:2] = loss_part

                @pl.when(me != o)
                def _():
                    fcopy(o).start()

            gp = (gateb[0:1, at] * gw).astype(bf16)
            gpb[:, at] = gp
            v = fold(p * gp.astype(f32))
            if c == 0 and base == 0:
                rowsum[...] = v
            else:
                rowsum[...] += v

    def mass_parts():
        gather_wait(massb, ma_s, ma_r)
        count_total = jnp.zeros((1, 128), f32)
        gate_sum = jnp.zeros((1, 128), f32)
        for o in range(nspot):
            count_total = count_total + small[o, 2:3, :] + small[o, 3:4, :]
        for o in range(cells // 128):
            gate_sum = gate_sum + gateb[0:1, o * 128 : (o + 1) * 128]
        count_total = jnp.sum(count_total)
        gate_total = jnp.sum(gate_sum)
        mass_sum = jnp.zeros((1, 128), f32)
        kl_sum = jnp.zeros((1, 128), f32)
        share_sum = jnp.zeros((1, 128), f32)
        for o in range(nspot):
            m = massb[o, 0:1, :]
            share = jnp.where(j == 0, small[o, 2:3, :], small[o, 3:4, :]) / count_total
            mass_sum = mass_sum + m
            share_sum = share_sum + share
            kl_sum = kl_sum + share * (jnp.log(share) - jnp.log(m))
        pair_s[1, 0:1, 0:128] = mass_sum
        pair_s[1, 1:2, 0:128] = kl_sum
        pair_s[1, 2:3, 0:128] = share_sum
        pair(1).start()
        return count_total, gate_total, mass_sum, kl_sum, share_sum

    def mass_totals(count_total, gate_total, mass_sum, kl_sum, share_sum):
        pair(1).wait_recv()
        mass_total = jnp.sum(mass_sum + pair_r[1, 0:1, 0:128])
        kl_all = jnp.sum(kl_sum + pair_r[1, 1:2, 0:128])
        share_all = jnp.sum(share_sum + pair_r[1, 2:3, 0:128])
        log_total = jnp.sum(jnp.log(jnp.full((1, 128), mass_total))[:, 0:1])
        excess = gate_total / count_total - 1.0
        my_dens = small[pl.ds(me, 1), pl.ds(2 + j, 1), :].reshape(1, 128)
        my_mass = massb[pl.ds(me, 1), 0:1, :].reshape(1, 128)
        gm_row = (1.0 / mass_total - my_dens / count_total / my_mass).astype(bf16).astype(f32)
        return kl_all + share_all * log_total + excess * excess, excess, column(gm_row, rows)

    def forward_sent():
        for c in ea.values():
            c.wait_send()
        for k, h in tlist:
            tcopy(k, h).wait_send()
        for k in (1, 2, 3):
            smalls(k).wait_send()
        for way in (0, 1):
            for u in range(8):
                wown(way, u).wait_send()
            for m in range(4):
                wpass(way, m).wait_send()
        for k in range(GROUP):
            wsib(k, k, every).wait_send()
        for i in range(4):
            stat(i, 0).wait_send()
            stat(i, 1).wait_send()
        dps_copy.wait_send()

    def along_sent():
        @pl.loop(0, nspot)
        def _(o):
            esib(o).wait_send()
            at = o // GROUP

            @pl.when(has_right & (at <= z))
            def _():
                zsend(0, o).wait_send()

            @pl.when(has_left & (at >= z))
            def _():
                zsend(1, o).wait_send()

        @pl.loop(0, nz)
        def _(at):
            @pl.when(has_right & (at <= z))
            def _():
                zsmall(0, at).wait_send()

            @pl.when(has_left & (at >= z))
            def _():
                zsmall(1, at).wait_send()

    relay(0)
    chain(1, 0, 3)
    chain(1, 1, 3)
    totals = mass_parts()
    chain(1, 0, 2)
    rest, excess, gm = mass_totals(*totals)
    relay(1)
    chain(2, 0, 3)
    forward_sent()
    chain(2, 0, 2)
    chain(1, 1, 2)
    relay(2)
    chain(1, 0, 1)
    along_sent()
    gather_sent(massb, ma_s, ma_r)
    relay(3)
    finish(3)
    finish(2)
    chain(2, 0, 1)
    chain(1, 1, 1)
    gene_part = jnp.sum(mine_mask * cos_gene / kept)
    loss_part = jnp.broadcast_to(-gene_part / SLIDES - jnp.sum(cos_spot) / spots_all, (1, cd))
    whole(0, gm)
    chain(1, 0, 0)
    whole(1, gm)
    finish(1)
    chain(2, 0, 0)
    chain(1, 1, 0)
    whole(2, gm)
    whole(3, gm)

    frecv[pl.ds(me, 1)] = fsend[pl.ds(me, 1)]

    def others(act):
        @pl.loop(0, nspot)
        def _(o):
            @pl.when(o != me)
            def _():
                act(o)

    tot_o[...] = jnp.broadcast_to(jnp.sum(rowsum[...], axis=1, keepdims=True), (rows, 128))
    finish(0)
    others(lambda o: remote(fsend.at[o], frecv.at[o], fi_s.at[o], fi_r.at[o], here).wait_recv())
    ftotal = frecv[0]
    for o in range(1, nspot):
        ftotal = ftotal + frecv[o]
    pair_s[2, 0:2, 0:cd] = ftotal
    pair(2).start()
    count_total = totals[0]
    my_gate = jax.nn.sigmoid(filt[...])

    others(lambda o: fcopy(o).wait_send())
    for k in range(1, GROUP):
        fin(k).wait_send()

    @pl.loop(0, 4)
    def _(c):
        xcopy(c).wait_send()
        ycopy(c).wait_send()
        x2copy(c).wait_send()
        y2copy(c).wait_send()

    @pl.loop(0, nspot)
    def _(o):
        at = o // GROUP

        @pl.when(has_right & (at > z))
        def _():
            dsend_to(0, o).wait_send()

        @pl.when(has_left & (at < z))
        def _():
            dsend_to(1, o).wait_send()

    for i in range(3):
        pair(i).wait_send()
    pair(2).wait_recv()
    fsum = ftotal + pair_r[2, 0:2, 0:cd]
    last_o[cd // 128 : cd // 128 + 1, :] = fsum[1:2, 0:128] + rest
    fsum = fsum[0:1] + 2.0 * excess / count_total
    for h in range(cd // 128):
        g = my_gate[h : h + 1, :]
        last_o[h : h + 1, :] = fsum[:, h * 128 : (h + 1) * 128] * g * (1.0 - g)
    for k in (3, 2, 1):
        fin_wait(k)
    ge_o[...] = gexpr[...]


def finish_kernel(probs, gp, tot, ge, last, gl_o, ge_o, loss_o, gf_o, gl, gx, loss, out_s):
    f32 = jnp.float32
    parts = 4
    cc = probs.shape[1] // parts
    copies = []

    def send(src, dst):
        copies.append(pltpu.make_async_copy(src, dst, out_s.at[len(copies)]))
        copies[-1].start()

    gx[...] = ge[...].astype(f32)
    send(gx, ge_o)
    n = gf_o.shape[0]
    loss[...] = last[n : n + 1, 0:1]
    send(last.at[pl.ds(0, n)], gf_o)
    send(loss, loss_o)
    for i in range(parts):
        for c in range(i * cc, (i + 1) * cc, 128):
            at = slice(c, c + 128)
            gl[:, at] = probs[:, at] * (gp[:, at].astype(f32) - tot[...])
        at = pl.ds(i * cc, cc)
        send(gl.at[:, at], gl_o.at[:, at])
    for c in copies:
        c.wait()


def grouped(logits, filt, expr, target, gene_mask, density):
    f32, bf16, i32 = jnp.float32, jnp.bfloat16, jnp.int32
    nspot = lax.axis_size("spot")
    rows, cells = logits.shape
    cd, half = expr.shape
    gq = half // GROUP
    grp = GROUP * rows
    hc = cells // 2
    cc = hc // 4
    nz = nspot // GROUP
    wide = max(2 * gq, grp, cd, 128)

    def vmem(*shape, dtype=f32):
        return pltpu.VMEM(shape, dtype)

    def dma(*shape):
        return pltpu.SemaphoreType.DMA(shape)

    buffers = [
        vmem(rows, cells, dtype=bf16), vmem(cd // 128, 128), vmem(*gene_mask.shape, dtype=i32),
        vmem(2 * rows // 128, 128, dtype=i32),
        vmem(8, cells), vmem(grp, cells, dtype=bf16), vmem(2, grp, cells, dtype=bf16),
        vmem(2, cells, gq, dtype=bf16),
        vmem(2, grp, gq, dtype=bf16), vmem(grp, 2 * gq), vmem(grp, 2 * gq, dtype=bf16),
        vmem(grp, gq, dtype=bf16), vmem(gq, 2 * grp, dtype=bf16),
        vmem(nspot, 8, 128), vmem(nspot, 8, 128),
        vmem(4, 8, wide), vmem(4, 8, wide), vmem(2, 3, 1, wide), vmem(4, 3, 1, wide),
        vmem(4, 2 * rows, cc, dtype=bf16), vmem(4, 2 * rows, cc, dtype=bf16),
        vmem(4, 2 * rows, cc, dtype=bf16), vmem(4, 2 * rows, cc, dtype=bf16),
        vmem(4, rows, cc, dtype=bf16), vmem(4, rows, cc, dtype=bf16),
        vmem(4, rows, cc, dtype=bf16), vmem(4, rows, cc, dtype=bf16),
        vmem(rows, cells), vmem(2, rows, hc), vmem(rows, 128),
        vmem(nspot, gq, cd), vmem(nspot, gq, cd, dtype=bf16),
        vmem(nspot, gq, cd, dtype=bf16), vmem(nspot, gq, cd, dtype=bf16),
        vmem(3, cd, gq, dtype=bf16), vmem(cd, half, dtype=bf16),
        vmem(nspot, 2, cd), vmem(nspot, 2, cd),
    ]
    sems = [
        dma(6), dma(4), dma(4), dma(2, nspot), dma(nspot), dma(nspot), dma(nspot),
        dma(12), dma(12), dma(12), dma(12), dma(4), dma(4), dma(8), dma(8),
        dma(4), dma(4), dma(2, nz), dma(nz), dma(nspot), dma(nspot),
        dma(nspot), dma(nspot),
        dma(4), dma(4), dma(8), dma(8),
        dma(4), dma(4), dma(4), dma(4), dma(4), dma(4), dma(4), dma(4),
        dma(nspot), dma(nspot), dma(nspot), dma(nspot), dma(4), dma(4), dma(1), dma(1),
    ]
    v, a = pl.BlockSpec(memory_space=pltpu.VMEM), pl.BlockSpec(memory_space=pl.ANY)
    shape = jax.ShapeDtypeStruct
    fparts = (cd // 128, 128)
    given = (logits, filt.reshape(-1, 128), expr, target, gene_mask, density.reshape(-1, 128))
    probs, gp, tot, last, grad_expr = pl.pallas_call(
        functools.partial(group_kernel, nspot),
        out_shape=[
            vmem(rows, cells),
            vmem(rows, cells, dtype=bf16),
            vmem(rows, 128),
            vmem(8, 128),
            vmem(cd, half, dtype=bf16),
        ],
        in_specs=[a] * 6,
        out_specs=[v] * 5,
        scratch_shapes=buffers + sems,
        compiler_params=pltpu.CompilerParams(
            collective_id=0, has_side_effects=True, vmem_limit_bytes=VMEM_BYTES
        ),
        name="group_step",
    )(*(pltpu.with_memory_space_constraint(g, pltpu.HBM) for g in given))
    grad_logits, grad_expr, loss, grad_filt = pl.pallas_call(
        finish_kernel,
        out_shape=[shape((rows, cells), f32), shape((cd, half), f32), shape((1, 1), f32), shape(fparts, f32)],
        in_specs=[v] * 5,
        out_specs=[a] * 4,
        scratch_shapes=[vmem(rows, cells), vmem(cd, half), vmem(1, 1), dma(7)],
        compiler_params=pltpu.CompilerParams(vmem_limit_bytes=LAST_BYTES),
        name="finish_step",
    )(probs, gp, tot, grad_expr, last)
    return (loss.reshape(()), grad_logits, grad_filt.reshape(-1), grad_expr)


def fits(logits, filt, expr):
    nspot = lax.axis_size("spot")
    rows, cells = logits.shape
    held = cells * (expr.shape[1] // GROUP) * 2 * 2 + 2 * GROUP * rows * cells * 2
    return (
        nspot == GROUP * SLIDES
        and lax.axis_size("gene") == 2
        and rows == 128
        and filt.shape[0] == 256
        and held <= 16 << 20
    )


def per_device(logits, filt, expr, target, gene_mask, density):
    plan = grouped if fits(logits, filt, expr) else streamed
    return plan(logits, filt, expr, target, gene_mask, density)


def solution(mesh):
    in_specs = (
        P(("spot", "gene"), None),
        P("spot"),
        P("spot", "gene"),
        P("spot", "gene"),
        P(None, "gene"),
        P("spot"),
    )
    out_specs = (P(), P(("spot", "gene"), None), P("spot"), P("spot", "gene"))
    return jax.shard_map(
        per_device, mesh=mesh, in_specs=in_specs, out_specs=out_specs, check_vma=False
    )
```

```python
import functools

import jax
import jax.numpy as jnp
from jax import lax
from jax.experimental import pallas as pl
from jax.experimental.pallas import tpu as pltpu
from jax.sharding import PartitionSpec as P

SPOTS = 4096
SLIDES = 4


eps_norm = 1e-06


def slide_moments(onehot, pred, truth):
    hi = lax.Precision.HIGHEST
    return jnp.stack(
        [
            jnp.dot(onehot.T, pred * truth, precision=hi),
            jnp.dot(onehot.T, pred * pred, precision=hi),
            jnp.dot(onehot.T, truth * truth, precision=hi),
        ]
    )


def spot_moments(pred, truth):
    return jnp.stack(
        [
            jnp.sum(pred * truth, axis=1),
            jnp.sum(pred * pred, axis=1),
            jnp.sum(truth * truth, axis=1),
        ]
    )


def cosine_parts(slide_stats):
    dots = slide_stats[0]
    slide_a = lax.rsqrt(slide_stats[1] + eps_norm)
    slide_b = lax.rsqrt(slide_stats[2] + eps_norm)
    return (dots, slide_a, slide_b, dots * slide_a * slide_b)


def pred_gradient(onehot, weight_slide, dots, slide_a, slide_b, spot_stats, pred, truth):
    hi = lax.Precision.HIGHEST
    spot_a = lax.rsqrt(spot_stats[1] + eps_norm)
    spot_b = lax.rsqrt(spot_stats[2] + eps_norm)
    coef_truth = -weight_slide * slide_a * slide_b
    coef_pred = weight_slide * dots * slide_a**3 * slide_b
    grad_pred = (
        jnp.dot(onehot, coef_truth, precision=hi) * truth
        + jnp.dot(onehot, coef_pred, precision=hi) * pred
    )
    grad_pred = (
        grad_pred
        + (
            -(spot_a * spot_b)[:, None] * truth
            + (spot_stats[0] * spot_a**3 * spot_b)[:, None] * pred
        )
        / SPOTS
    )
    return (grad_pred, spot_stats[0] * spot_a * spot_b)


def streamed(logits, filt, expr, target, gene_mask, density):
    f32 = jnp.float32
    bf16 = jnp.bfloat16
    nspot = lax.axis_size("spot")
    ngene = lax.axis_size("gene")
    spot_dev = logits.shape[0]
    cells = logits.shape[1]
    cell_dev = filt.shape[0]
    owned = target.shape[0]
    half = target.shape[1]
    spots_all = owned * nspot
    slide_len = SPOTS // SLIDES
    scores = logits.astype(f32)
    shifted = jnp.exp(scores - jnp.max(scores, axis=1, keepdims=True))
    probs = shifted / jnp.sum(shifted, axis=1, keepdims=True)
    moved = lax.all_to_all(probs.astype(bf16), "spot", split_axis=1, concat_axis=0, tiled=True)
    paired = lax.all_gather(moved.reshape(nspot, 1, spot_dev, cell_dev), "gene", axis=1, tiled=True)
    paired = paired.reshape(spots_all, cell_dev)
    gate = jax.nn.sigmoid(filt)
    weighted = (paired.astype(f32) * gate[None, :]).astype(bf16)
    partial_pred = jnp.dot(weighted, expr, preferred_element_type=f32)
    partial_mass = jnp.sum(weighted.astype(f32), axis=1)
    gate_part = jnp.sum(gate)
    maskf = gene_mask.astype(f32)
    mask_part = jnp.sum(maskf, axis=1)
    pred_three, mass_two = (
        lax.psum_scatter(
            partial_pred.reshape(nspot, owned, half), "spot", scatter_dimension=0, tiled=True
        ),
        lax.psum_scatter(
            partial_mass.reshape(nspot, owned), "spot", scatter_dimension=0, tiled=True
        ),
    )
    pred = pred_three.reshape(owned, half)
    mass = mass_two.reshape(owned)
    truth = target.astype(f32)
    dens = density.astype(f32)
    spot_ids = lax.axis_index("spot") * owned + jnp.arange(owned, dtype=jnp.int32)
    onehot = (
        spot_ids[:, None] // slide_len == jnp.arange(SLIDES, dtype=jnp.int32)[None, :]
    ).astype(f32)
    slide_stats, mass_total, gate_total, count_total = lax.psum(
        (slide_moments(onehot, pred, truth), jnp.sum(mass), gate_part, jnp.sum(dens)), "spot"
    )
    dots, slide_a, slide_b, cos_gene = cosine_parts(slide_stats)
    spot_stats, kept_genes, gene_numer = lax.psum(
        (spot_moments(pred, truth), mask_part, jnp.sum(maskf * cos_gene, axis=1)), "gene"
    )
    genes_kept = jnp.maximum(kept_genes, 1.0)
    weight_slide = maskf / genes_kept[:, None] / SLIDES
    grad_pred, cos_spot = pred_gradient(
        onehot, weight_slide, dots, slide_a, slide_b, spot_stats, pred, truth
    )
    share = dens / count_total
    kl_local = jnp.sum(share * (jnp.log(share) - jnp.log(mass) + jnp.log(mass_total)))
    cos_total, kl_total = lax.psum((jnp.sum(cos_spot), kl_local), "spot")
    grad_mass = 1.0 / mass_total - share / mass
    spread_three, spread_two = (
        lax.all_gather(grad_pred.astype(bf16).reshape(1, owned, half), "spot", axis=0, tiled=True),
        lax.all_gather(grad_mass.astype(bf16).reshape(1, owned), "spot", axis=0, tiled=True),
    )
    spread_pred = spread_three.reshape(spots_all, half)
    spread_mass = spread_two.reshape(spots_all)
    gene_term = jnp.mean(gene_numer / genes_kept)
    excess = gate_total / count_total - 1.0
    loss = -gene_term - cos_total / SPOTS + kl_total + excess * excess
    grad_expr = lax.dot_general(
        weighted, spread_pred, (((0,), (0,)), ((), ())), preferred_element_type=f32
    )
    first_half = (lax.axis_index("gene") == 0).astype(f32)
    grad_weighted = lax.dot_general(
        spread_pred, expr, (((1,), (1,)), ((), ())), preferred_element_type=f32
    )
    grad_weighted = grad_weighted + first_half * spread_mass.astype(f32)[:, None]
    filter_part = jnp.sum(grad_weighted * paired.astype(f32), axis=0)
    filter_total = lax.psum(filter_part, "gene")
    grad_filt = (filter_total + 2.0 * excess / count_total) * gate * (1.0 - gate)
    terms = (grad_weighted * gate[None, :]).reshape(nspot, ngene, spot_dev, cell_dev)
    moved_back = lax.all_to_all(terms, "spot", split_axis=0, concat_axis=3, tiled=True)
    folded = lax.psum_scatter(moved_back, "gene", scatter_dimension=1, tiled=True)
    rounded = lax.optimization_barrier(folded.reshape(spot_dev, cells).astype(bf16))
    grad_probs = rounded.astype(f32)
    grad_logits = probs * (grad_probs - jnp.sum(probs * grad_probs, axis=1, keepdims=True))
    return (loss, grad_logits, grad_filt, grad_expr)


GROUP = 4
PIECE = 128
MESH = pl.DeviceIdType.MESH
VMEM_BYTES = 44 << 20
LAST_BYTES = 16 << 20


def remote(src, dst, send, recv, dev):
    return pltpu.make_async_remote_copy(
        src_ref=src, dst_ref=dst, send_sem=send, recv_sem=recv, device_id=dev, device_id_type=MESH
    )


def dot_nt(a, b):
    return lax.dot_general(a, b, (((1,), (1,)), ((), ())), preferred_element_type=jnp.float32)


def column(row, length):
    return jnp.transpose(jnp.broadcast_to(row, (128, length)))


def fold(values):
    total = values[:, 0:128]
    for i in range(1, values.shape[1] // 128):
        total = total + values[:, i * 128 : (i + 1) * 128]
    return total


def group_kernel(
    nspot, logits_h, filt_h, expr, target, mask_h, dens_h,
    probs, gpb, tot_o, last_o, ge_o,
    logits, filt, mask, dens, rawq, wraw, wg, wt, ebuf, tbuf, gcol, small, pfin, ahead,
    psx, prx, psy, pry, ps2x, pr2x, ps2y, pr2y, hx, hy, massp, massr, statg, statr, acc, spots, spotr,
    dpa, grad, dsend, dright, dleft, dwo, dws, dwr, gps, gpr, rowsum, tile_s, tile_r, tz, gms, gmr, gmcol,
    fsend, frecv, pair_s, pair_r,
    hello, lc, zs_s, zs_r, ez_s, ez_r, w_s, w_r, wd_s, wd_r, pr_s, pr_r,
    px_s, px_r, py_s, py_r, p2x_s, p2x_r, p2y_s, p2y_r, ms_s, ms_r, st_s, st_r, ag_s, ag_r,
    dr_s, dr_r, dl_s, dl_r, dw_s, dw_r, gp_s, gp_r, tl_s, tl_r, tz_s, tz_r, gm_s, gm_r, fz_s, fz_r,
):
    f32, bf16 = jnp.float32, jnp.bfloat16
    rows, cells = probs.shape
    cd, genes = expr.shape
    nz = nspot // GROUP
    np_ = genes // PIECE
    grp = GROUP * rows
    mine = cells // GROUP
    spots_all = nspot * 2 * rows
    me, j = lax.axis_index("spot"), lax.axis_index("gene")
    sib = 1 - j
    z, q = me // GROUP, me % GROUP
    x, y = q % 2, q // 2
    nbr = [me, me + 1 - 2 * x, me + 2 - 4 * y, me + 3 - 2 * x - 4 * y]
    nq = [n % GROUP for n in nbr]
    here = (me, sib)
    has_right, has_left = z < nz - 1, z > 0
    ends = (z == 0, z == nz - 1)
    chip = [(n, j) for n in nbr]
    beside = ((me + GROUP, j), (me - GROUP, j))

    def at_k(k, h=0):
        return pl.ds(h * grp + k * rows, rows)

    def piece(g):
        return pl.ds(g * PIECE, PIECE)

    def half_of(buf, r, g):
        return buf.at[g // 2, r, pl.ds(g % 2 * PIECE, PIECE)]

    def seg(p):
        return pl.ds(pl.multiple_of(p * cd, cd), cd)

    barrier = pltpu.get_barrier_semaphore()

    def greet(dev):
        pl.semaphore_signal(barrier, inc=1, device_id=dev, device_id_type=MESH)

    greet(chip[1])
    greet(chip[2])

    @pl.when(has_right)
    def _():
        greet(beside[0])

    @pl.when(has_left)
    def _():
        greet(beside[1])

    greet(here)
    loads = [pltpu.make_async_copy(logits_h, logits, lc.at[0])]
    loads += [
        pltpu.make_async_copy(s, d, lc.at[1 + i])
        for i, (s, d) in enumerate(((filt_h, filt), (mask_h, mask), (dens_h, dens)))
    ]
    loads += [
        pltpu.make_async_copy(
            expr.at[:, pl.ds(i * 2 * PIECE, 2 * PIECE)], ebuf.at[i, seg(z), :], lc.at[4 + i]
        )
        for i in range(np_ // 2)
    ]
    loads += [
        pltpu.make_async_copy(
            target.at[pl.ds(pl.multiple_of(c * rows, rows), rows)],
            tbuf.at[pl.ds(i * rows, rows)],
            lc.at[4 + np_ // 2 + i],
        )
        for i, c in enumerate((j, sib))
    ]
    for c in loads:
        c.start()
    loads[0].wait()

    step = 32

    @pl.loop(0, rows // step)
    def _(i):
        at = pl.ds(pl.multiple_of(i * step, step), step)
        s = logits[at, :].astype(f32)
        e = jnp.exp(s - jnp.max(s, axis=1, keepdims=True))
        p = e * (1.0 / jnp.sum(e, axis=1, keepdims=True))
        probs[at, :] = p
        for o in range(nspot):
            c = o // GROUP * cd
            rawq[o % GROUP, at, c : c + cd] = p[:, o * cd : (o + 1) * cd].astype(bf16)

    for c in loads[1:]:
        c.wait()
    small[pl.ds(z, 1), 0 : cd // 128, :] = filt[...][None]
    maskf = mask[pl.ds(z, 1), :].astype(f32)
    kept_mine = jnp.sum(maskf)
    pair_s[0] = jnp.full((8, 2 * rows), kept_mine)
    pl.semaphore_wait(barrier, 3 + has_right.astype(jnp.int32) + has_left.astype(jnp.int32))

    def zsmall(way, p):
        return remote(small.at[p], small.at[p], zs_s.at[way, p], zs_r.at[p], beside[way])

    def zsend(way, p, g):
        u = half_of(ebuf, seg(p), g)
        return remote(u, u, ez_s.at[way, p, g], ez_r.at[p, g], beside[way])

    def both(make):
        @pl.when(has_right)
        def _():
            make(0).start()

        @pl.when(has_left)
        def _():
            make(1).start()

    def hop(s, make):
        @pl.when(z >= s)
        def _():
            make(0, z - s).wait_recv()

            @pl.when(has_right)
            def _():
                make(0, z - s).start()

        @pl.when(z + s <= nz - 1)
        def _():
            make(1, z + s).wait_recv()

            @pl.when(has_left)
            def _():
                make(1, z + s).start()

    def own(g):
        if g < np_:
            both(lambda way: zsend(way, z, g))

    def along(s, g):
        if 0 <= g < np_:
            hop(s, lambda way, p: zsend(way, p, g))

    both(lambda way: zsmall(way, z))
    own(0)
    own(1)

    def wcopy(k):
        return remote(rawq.at[nq[k]], wraw.at[at_k(k)], w_s.at[k], w_r.at[k], chip[k])

    def wsib(k):
        return remote(wraw.at[at_k(k)], wraw.at[at_k(k, 1)], wd_s.at[k], wd_r.at[k], here)

    def pair(i):
        return remote(pair_s.at[i], pair_r.at[i], pr_s.at[i], pr_r.at[i], here)

    wcopy(1).start()
    wcopy(2).start()
    pl.semaphore_signal(hello, inc=1, device_id=chip[1], device_id_type=MESH)
    wraw[at_k(0), :] = rawq[pl.ds(q, 1)].reshape(rows, mine)
    wsib(0).start()
    pair(0).start()
    pl.semaphore_wait(hello, 1)
    wcopy(3).start()

    def gated(k, h):
        r = at_k(k, h)
        for c in range(0, mine, 512):
            at = pl.ds(c, 512)
            wg[r, at] = (gcol[0:1, at] * wraw[r, at].astype(f32)).astype(bf16)

    def turned(k, h):
        r = at_k(k, h)
        for c in range(0, mine, 512):
            at = pl.ds(c, 512)
            wt[at, r] = jnp.transpose(wg[r, at].astype(f32)).astype(bf16)

    def arrive(k):
        wcopy(k).wait_recv()
        wsib(k).start()
        gated(k, 0)

    def arrive_sib(k):
        wsib(k).wait_recv()
        gated(k, 1)

    first, second = pl.ds(0, rows), pl.ds(rows, rows)

    def pxcopy(g, n):
        h = (first, second)[n]
        return remote(psx.at[g, h], prx.at[g, h], px_s.at[n, g], px_r.at[n, g], chip[1])

    def pycopy(g, n):
        h = (first, second)[n]
        return remote(psy.at[g, h], pry.at[g, h], py_s.at[n, g], py_r.at[n, g], chip[2])

    def p2xcopy(g):
        return remote(ps2x.at[g], pr2x.at[g], p2x_s.at[g], p2x_r.at[g], chip[1])

    def p2ycopy(g):
        return remote(ps2y.at[g], pr2y.at[g], p2y_s.at[g], p2y_r.at[g], chip[2])

    def piece_of(g, at):
        return ebuf[g // 2, at, g % 2 * PIECE : (g % 2 + 1) * PIECE]

    def project(g):
        share(g, jnp.dot(wg[...], piece_of(g, pl.ds(0, mine)), preferred_element_type=f32))

    far = (1 - z // (nz // 2)) * (nz - 1)
    near = pl.ds(pl.multiple_of(z // (nz // 2) * cd, cd), mine - cd)

    def project_ahead(g):
        ahead[...] = jnp.dot(wg[:, near], piece_of(g, near), preferred_element_type=f32)

    def project_last(g):
        share(g, ahead[...] + jnp.dot(wg[:, seg(far)], piece_of(g, seg(far)), preferred_element_type=f32))

    def share(g, v):
        def part(k, h):
            s = h * grp + k * rows
            return v[s : s + rows]

        psx[g, second] = part(3, 0).astype(bf16)
        pxcopy(g, 1).start()
        psy[g, second] = part(3, 1).astype(bf16)
        pycopy(g, 1).start()
        psx[g, first] = part(1, 0).astype(bf16)
        pxcopy(g, 0).start()
        psy[g, first] = part(2, 1).astype(bf16)
        pycopy(g, 0).start()
        hx[g] = part(2, 0)
        hy[g] = part(1, 1)
        pfin[first, piece(g)] = part(0, 0)
        pfin[second, piece(g)] = part(0, 1)

    def relay(g):
        pxcopy(g, 1).wait_recv()
        ps2y[g] = (hx[g] + prx[g, second].astype(f32)).astype(bf16)
        p2ycopy(g).start()
        pycopy(g, 1).wait_recv()
        ps2x[g] = (hy[g] + pry[g, second].astype(f32)).astype(bf16)
        p2xcopy(g).start()

    def whole(g):
        at = piece(g)
        pxcopy(g, 0).wait_recv()
        pycopy(g, 0).wait_recv()
        p2ycopy(g).wait_recv()
        p2xcopy(g).wait_recv()
        pfin[first, at] += prx[g, first].astype(f32) + pr2y[g].astype(f32)
        pfin[second, at] += pry[g, first].astype(f32) + pr2x[g].astype(f32)
        p = pfin[:, at]
        t = tbuf[:, at].astype(f32)
        for i, v in enumerate((p * p, p * t, t * t)):
            statg[i, :, at] = jnp.sum(v, axis=0, keepdims=True)
            acc[i] += v

    parts = (pl.ds(0, (np_ - 2) * PIECE), pl.ds((np_ - 2) * PIECE, 2 * PIECE))

    def stat(k, n):
        i = 2 * k + n
        return remote(
            statg.at[:, :, parts[n]], statr.at[k, :, :, parts[n]], st_s.at[i], st_r.at[i], chip[k]
        )

    def gates():
        for p in range(nz):
            for h in range(cd // 128):
                g = jax.nn.sigmoid(small[p, h : h + 1, :])
                c = p * cd + h * 128
                gcol[:, c : c + 128] = jnp.broadcast_to(g, (8, 128))

    def mass_copy(k):
        return remote(massp.at[k], massr.at[k], ms_s.at[k], ms_r.at[k], chip[k])

    def masses():
        m = dot_nt(jnp.ones((8, mine), bf16), wg[...])
        for k in range(GROUP):
            for h in range(2):
                s = h * grp + k * rows
                massp[k, h : h + 1, :] = m[0:1, s : s + rows]
            if k:
                mass_copy(k).start()

    acc[...] = jnp.zeros_like(acc)
    hop(1, zsmall)
    along(1, 0)
    own(2)
    hop(2, zsmall)
    along(1, 1)
    along(2, 0)
    own(3)
    hop(3, zsmall)
    gates()
    gated(0, 0)
    arrive(1)
    arrive(2)
    arrive_sib(0)
    along(1, 2)
    along(2, 1)
    own(4)
    arrive_sib(1)
    arrive_sib(2)
    for k in range(3):
        turned(k, 0)
    arrive(3)
    arrive_sib(3)
    along(3, 0)
    project(0)
    for s in range(3, np_ + 2):
        along(1, s)
        along(2, s - 1)
        own(s + 2)
        if s == np_ + 1:
            relay(s - 3)
        along(3, s - 2)
        if s < np_ + 1:
            project(s - 2)
        else:
            project_last(s - 2)
        if s == 4:
            masses()
        if s == 5:
            for k in range(3):
                turned(k, 1)
        if s == 6:
            turned(3, 0)
            turned(3, 1)
        if s < np_ + 1:
            relay(s - 3)
        if s == np_:
            project_ahead(np_ - 1)
        if s > 4:
            whole(s - 5)
    whole(np_ - 3)
    for k in (3, 1, 2):
        stat(k, 0).start()
    pair(0).wait_recv()
    kept = jnp.maximum(kept_mine + jnp.sum(pair_r[0, 0:1, 0:1]), 1.0)
    weight = maskf / kept / SLIDES
    relay(np_ - 1)
    whole(np_ - 2)
    whole(np_ - 1)
    for k in (3, 1, 2):
        stat(k, 1).start()

    for i in range(3):
        spots[i] = jnp.sum(jnp.transpose(acc[i]), axis=0, keepdims=True)
    spot_copy = remote(spots, spotr, pr_s.at[4], pr_r.at[4], here)
    spot_copy.start()

    def slide_sums(n):
        for k in (1, 2, 3):
            stat(k, n).wait_recv()
        at = parts[n]
        pred_sq, dots, truth_sq = (
            (statg[i, :, at] + statr[1, i, :, at]) + (statr[2, i, :, at] + statr[3, i, :, at])
            for i in range(3)
        )
        slide_a = lax.rsqrt(pred_sq + eps_norm)
        slide_b = lax.rsqrt(truth_sq + eps_norm)
        w = weight[:, at.start : at.start + at.size]
        return (
            -w * slide_a * slide_b,
            w * dots * slide_a**3 * slide_b,
            w * (dots * slide_a * slide_b),
        )

    coefs = [slide_sums(0), None]
    spot_copy.wait_recv()
    spot_pp, spot_dot, spot_tt = (
        spots[i] + jnp.concatenate([spotr[i, :, rows : 2 * rows], spotr[i, :, 0:rows]], axis=1)
        for i in range(3)
    )
    spot_a = lax.rsqrt(spot_pp + eps_norm)
    spot_b = lax.rsqrt(spot_tt + eps_norm)
    col_t = column(-(spot_a * spot_b) / spots_all, 2 * rows)
    col_p = column(spot_dot * spot_a**3 * spot_b / spots_all, 2 * rows)

    def agcopy(i, g):
        src, dst, to = (
            (at_k(0), at_k(1), 1), (at_k(0, 1), at_k(1, 1), 1), (at_k(0, 1), at_k(2, 1), 2),
            (at_k(0), at_k(2), 2), (at_k(1), at_k(3), 2), (at_k(2, 1), at_k(3, 1), 1),
        )[i]
        return remote(half_of(dpa, src, g), half_of(dpa, dst, g), ag_s.at[i, g], ag_r.at[i, g], chip[to])

    def give(g):
        n = 0 if g < np_ - 2 else 1
        if n and coefs[1] is None:
            coefs[1] = slide_sums(1)
        c = g * PIECE - parts[n].start
        c_t, c_p = (v[:, c : c + PIECE] for v in coefs[n][0:2])
        at = piece(g)
        d = ((c_t + col_t) * tbuf[:, at].astype(f32) + (c_p + col_p) * pfin[:, at]).astype(bf16)
        lanes = pl.ds(g % 2 * PIECE, PIECE)
        dpa[g // 2, at_k(0), lanes] = d[0:rows]
        dpa[g // 2, at_k(0, 1), lanes] = d[rows : 2 * rows]
        for i in range(4):
            agcopy(i, g).start()

    def give_on(g):
        agcopy(0, g).wait_recv()
        agcopy(4, g).start()
        agcopy(2, g).wait_recv()
        agcopy(5, g).start()

    def dcopy(way, p, g):
        if way == 0:
            return remote(dsend.at[p, g], dright.at[p, g], dr_s.at[p, g], dr_r.at[p, g], beside[0])
        return remote(dsend.at[p, g], dleft.at[p, g], dl_s.at[p, g], dl_r.at[p, g], beside[1])

    def expr_grad_first():
        for i in (1, 3, 4, 5):
            agcopy(i, 0).wait_recv()
        up = z // (nz // 2)

        @pl.loop(0, nz)
        def _(u):
            p = up * u + (1 - up) * (nz - 1 - u)
            v = jnp.dot(wt[seg(p), :], dpa[0, :, 0:PIECE], preferred_element_type=f32)
            grad[p, :, 0:PIECE] = v

            @pl.when((ends[0] | ends[1]) & (p != z))
            def _():
                dsend[p, 0] = v.astype(bf16)

            @pl.when(ends[0] & (p != z))
            def _():
                dcopy(0, p, 0).start()

            @pl.when(ends[1] & (p != z))
            def _():
                dcopy(1, p, 0).start()

    def expr_grad(g):
        for i in (1, 3, 4, 5):
            agcopy(i, g).wait_recv()
        lanes = slice(g % 2 * PIECE, (g % 2 + 1) * PIECE)
        v = jnp.dot(wt[...], dpa[g // 2, :, lanes], preferred_element_type=f32)
        for p in range(nz):
            grad[p, :, piece(g)] = v[p * cd : (p + 1) * cd]

        @pl.when(ends[0])
        def _():
            for p in range(1, nz):
                dsend[p, g] = v[p * cd : (p + 1) * cd].astype(bf16)

        @pl.when(ends[1])
        def _():
            for p in range(nz - 1):
                dsend[p, g] = v[p * cd : (p + 1) * cd].astype(bf16)

    def start_from_ends(u, g):
        if not 0 <= g < np_:
            return

        @pl.when(ends[0])
        def _():
            dcopy(0, nz - 1 - u, g).start()

        @pl.when(ends[1])
        def _():
            dcopy(1, u, g).start()

    def starts(*pieces):
        for u, g in pieces:
            start_from_ends(u, g)

    def chain(hops, u, g):
        if nz - 1 - u > hops:

            @pl.when(z == hops)
            def _():
                p = nz - 1 - u
                dcopy(0, p, g).wait_recv()
                dsend[p, g] = (grad[p, :, piece(g)] + dright[p, g].astype(f32)).astype(bf16)
                dcopy(0, p, g).start()

            @pl.when(nz - 1 - z == hops)
            def _():
                dcopy(1, u, g).wait_recv()
                dsend[u, g] = (grad[u, :, piece(g)] + dleft[u, g].astype(f32)).astype(bf16)
                dcopy(1, u, g).start()

    def finish(g):
        at = piece(g)
        ge_o[:, at] = grad[pl.ds(z, 1), :, at].reshape(cd, PIECE)

        @pl.when(has_left)
        def _():
            dcopy(0, z, g).wait_recv()
            ge_o[:, at] += dright[pl.ds(z, 1), g].reshape(cd, PIECE).astype(f32)

        @pl.when(has_right)
        def _():
            dcopy(1, z, g).wait_recv()
            ge_o[:, at] += dleft[pl.ds(z, 1), g].reshape(cd, PIECE).astype(f32)

    def tile_copy(k):
        return remote(tile_s, tile_r.at[k], tl_s.at[k], tl_r.at[k], chip[k])

    def zcopy(buf, src, r, ss, rs):
        to = (z + r) % nz
        return remote(buf.at[src], buf.at[z], ss.at[r], rs.at[r], (to * GROUP + q, j))

    def zcopy_wait(buf, r, ss, rs):
        o = (z + nz - r) % nz
        remote(buf.at[o], buf.at[o], ss.at[r], rs.at[r], here).wait_recv()

    def chip_masses():
        for k in (1, 2, 3):
            mass_copy(k).wait_recv()
        return (massp[0, 0:2] + massr[1, 0:2]) + (massr[2, 0:2] + massr[3, 0:2])

    def own_dens():
        d = dens[...].astype(f32)
        return jnp.where(j == 0, d, jnp.concatenate([d[1:2], d[0:1]], axis=0))

    def tile_start():
        mass, d = chip_masses(), own_dens()
        gene = fold(coefs[0][2]) + fold(coefs[1][2])
        cos = fold(spot_dot * spot_a * spot_b)
        tile_s[0:1] = -2.0 / GROUP * gene - cos / spots_all
        tile_s[1:2] = d[0:1] + d[1:2]
        f = jax.nn.sigmoid(filt[...])
        tile_s[2:3] = f[0:1] + f[1:2]
        tile_s[3:4] = mass[0:1] + mass[1:2]
        kl = d * (jnp.log(d) - jnp.log(mass))
        tile_s[4:5] = kl[0:1] + kl[1:2]
        tile_s[5:8] = jnp.zeros((3, 128), f32)
        for k in (3, 1, 2):
            tile_copy(k).start()
        return mass, d

    def tile_along():
        for k in (1, 2, 3):
            tile_copy(k).wait_recv()
        tz[pl.ds(z, 1)] = ((tile_s[...] + tile_r[1]) + (tile_r[2] + tile_r[3]))[None]
        for r in range(1, nz):
            zcopy(tz, z, r, tz_s, tz_r).start()

    def gm_copy(k):
        return remote(gms, gmr.at[k], gm_s.at[k], gm_r.at[k], chip[k])

    def totals(mass, d):
        for r in range(1, nz):
            zcopy_wait(tz, r, tz_s, tz_r)
        t = tz[0]
        for p in range(1, nz):
            t = t + tz[p]
        loss_part, count, gate, mass_total, kl = (jnp.sum(t[i : i + 1]) for i in range(5))
        logs = jnp.log(jnp.where(lax.broadcasted_iota(jnp.int32, (1, 128), 1) == 0, count, mass_total))
        log_count, log_mass = jnp.sum(logs[:, 0:1]), jnp.sum(logs[:, 1:2])
        excess = gate / count - 1.0
        gms[...] = jnp.zeros_like(gms)
        gms[0:2] = (1.0 / mass_total - d / count / mass).astype(bf16).astype(f32)
        for k in (3, 1, 2):
            gm_copy(k).start()
        pair_s[1] = jnp.full((8, 2 * rows), loss_part + kl / count - log_count + log_mass + excess * excess)
        pair(1).start()
        return 2.0 * excess / count

    def mass_columns():
        gmcol[at_k(0), :] = column(gms[0:1], rows)
        for k in (1, 2, 3):
            gm_copy(k).wait_recv()
            gmcol[at_k(k), :] = column(gmr[k, 0:1], rows)

    def dwcopy(p):
        return remote(dws.at[p], dwr.at[p], dw_s.at[p], dw_r.at[p], here)

    def weight_grad(p):
        cs = slice(p * cd, (p + 1) * cd)

        def rows_of(h):
            d = dot_nt(dpa[0, h * grp : (h + 1) * grp, :], ebuf[0, cs, :])
            for c in range(1, np_ // 2):
                d = d + dot_nt(dpa[c, h * grp : (h + 1) * grp, :], ebuf[c, cs, :])
            return d

        dws[p] = rows_of(1)
        dwcopy(p).start()
        dwo[p] = rows_of(0)

    def gpcopy(k, p):
        return remote(gps.at[p, at_k(k)], gpr.at[k, p], gp_s.at[k, p], gp_r.at[k, p], chip[k])

    def give_back(p):
        dwcopy(p).wait_recv()
        cs = pl.ds(p * cd, cd)
        total = jnp.zeros((1, cd), f32)
        for k in (3, 1, 2, 0):
            r = at_k(k)
            gm = gmcol[r, :]
            gw = dwo[p, r] + dwr[p, r] + jnp.concatenate([gm] * (cd // 128), axis=1)
            total = total + jnp.sum(gw * wraw[r, cs].astype(f32), axis=0, keepdims=True)
            gps[p, r] = (gcol[0:1, cs] * gw).astype(bf16)
            if k:
                gpcopy(k, p).start()
        fsend[p] = total

    def filter_along():
        frecv[pl.ds(z, 1)] = fsend[pl.ds(z, 1)]
        for r in range(1, nz):
            to = (z + r) % nz
            remote(fsend.at[to], frecv.at[z], fz_s.at[r], fz_r.at[r], (to * GROUP + q, j)).start()

    def take(k, p, start=False):
        if k:
            gpcopy(k, p).wait_recv()
            v = gpr[k, p]
        else:
            v = gps[p, at_k(0)]
        at = pl.ds(pl.multiple_of((p * GROUP + nq[k]) * cd, cd), cd)
        gpb[:, at] = v
        s = fold(probs[:, at] * v.astype(f32))
        if start:
            rowsum[...] = s
        else:
            rowsum[...] += s

    def sent_first():
        for k in (1, 2, 3):
            wcopy(k).wait_send()
            mass_copy(k).wait_send()
            for n in (0, 1):
                stat(k, n).wait_send()
        for k in range(GROUP):
            wsib(k).wait_send()
        pair(0).wait_send()
        spot_copy.wait_send()

        @pl.loop(0, np_)
        def _(g):
            for c in (pxcopy, pycopy):
                c(g, 0).wait_send()
                c(g, 1).wait_send()
            p2xcopy(g).wait_send()
            p2ycopy(g).wait_send()

    def sent_along():
        @pl.loop(0, nz)
        def _(p):
            @pl.when(has_right & (p <= z))
            def _():
                zsmall(0, p).wait_send()
                for g in range(np_):
                    zsend(0, p, g).wait_send()

            @pl.when(has_left & (p >= z))
            def _():
                zsmall(1, p).wait_send()
                for g in range(np_):
                    zsend(1, p, g).wait_send()

    def sent_back():
        for g in range(np_):
            for i in range(6):
                agcopy(i, g).wait_send()

    def sent_last():
        for k in (1, 2, 3):
            tile_copy(k).wait_send()
            gm_copy(k).wait_send()
            for p in range(nz):
                gpcopy(k, p).wait_send()
        for r in range(1, nz):
            zcopy(tz, z, r, tz_s, tz_r).wait_send()
            zcopy(fsend, z, r, fz_s, fz_r).wait_send()
        for p in range(nz):
            dwcopy(p).wait_send()
        for i in (1, 2):
            pair(i).wait_send()

    def sent_sums():
        @pl.loop(0, nz)
        def _(p):
            @pl.when(has_right & (p > z))
            def _():
                for g in range(np_):
                    dcopy(0, p, g).wait_send()

            @pl.when(has_left & (p < z))
            def _():
                for g in range(np_):
                    dcopy(1, p, g).wait_send()

    give(0)
    give(1)
    coefs[1] = slide_sums(1)
    mass, d = tile_start()
    give_on(0)
    give(2)
    give_on(1)
    give(3)
    expr_grad_first()
    give_on(2)
    give(4)
    tile_along()
    expr_grad(1)
    starts((0, 1), (1, 1), (2, 1))
    give_on(3)
    give(5)
    chain(1, 0, 0)
    give_on(4)
    expr_grad(2)
    starts((0, 2), (1, 2))
    chain(1, 1, 0)
    give(6)
    give_on(5)
    expr_grad(3)
    starts((0, 3), (1, 3))
    chain(1, 0, 1)
    chain(2, 0, 0)
    give(7)
    give_on(6)
    chain(1, 1, 1)
    expr_grad(4)
    starts((0, 4), (2, 2), (1, 4))
    push = totals(mass, d)
    give_on(7)
    chain(2, 0, 1)
    chain(1, 0, 2)
    expr_grad(5)
    starts((0, 5), (2, 3), (1, 5))
    finish(0)
    chain(1, 1, 2)
    expr_grad(6)
    starts((0, 6), (2, 4))
    chain(1, 0, 3)
    mass_columns()
    expr_grad(7)
    starts((0, 7), (1, 6), (1, 7))
    finish(1)
    chain(2, 0, 2)
    chain(1, 1, 3)
    weight_grad(0)
    chain(1, 0, 4)
    chain(2, 0, 3)
    weight_grad(1)
    give_back(0)
    finish(2)
    chain(1, 1, 4)
    weight_grad(2)
    give_back(1)
    chain(2, 0, 4)
    chain(1, 0, 5)
    weight_grad(3)
    give_back(2)
    finish(3)
    give_back(3)
    filter_along()
    starts((2, 5), (2, 6), (2, 7))
    chain(1, 1, 5)
    chain(2, 0, 5)
    take(0, 0, True)
    for p in range(1, nz):
        take(0, p)
    chain(1, 0, 6)
    sent_first()
    finish(4)
    chain(1, 0, 7)
    for k in (1, 2, 3):
        take(k, 0)
    sent_along()
    chain(2, 0, 6)
    chain(1, 1, 6)
    for k in (1, 2, 3):
        take(k, 1)
    chain(1, 1, 7)
    sent_back()
    chain(2, 0, 7)
    for k in (1, 2, 3):
        take(k, 2)
    finish(5)
    for r in range(1, nz):
        zcopy_wait(frecv, r, fz_s, fz_r)
    ftotal = frecv[0]
    for p in range(1, nz):
        ftotal = ftotal + frecv[p]
    pair_s[2, 0:1, 0:cd] = ftotal
    pair(2).start()
    for k in (1, 2, 3):
        take(k, 3)
    tot_o[...] = jnp.broadcast_to(jnp.sum(rowsum[...], axis=1, keepdims=True), (rows, 128))
    sent_last()
    finish(6)
    pair(1).wait_recv()
    pair(2).wait_recv()
    my_gate = jax.nn.sigmoid(filt[...])
    fsum = ftotal + pair_r[2, 0:1, 0:cd] + push
    for h in range(cd // 128):
        g = my_gate[h : h + 1, :]
        last_o[h : h + 1, :] = fsum[:, h * 128 : (h + 1) * 128] * g * (1.0 - g)
    last_o[cd // 128 : cd // 128 + 1, :] = 0.5 * (pair_s[1, 0:1, 0:128] + pair_r[1, 0:1, 0:128])
    finish(7)
    sent_sums()


def finish_kernel(probs, gp, tot, ge, last, gl_o, ge_o, loss_o, gf_o, gl, loss, out_s):
    f32 = jnp.float32
    parts = 4
    cc = probs.shape[1] // parts
    copies = []

    def send(src, dst):
        copies.append(pltpu.make_async_copy(src, dst, out_s.at[len(copies)]))
        copies[-1].start()

    send(ge, ge_o)
    n = gf_o.shape[0]
    loss[...] = last[n : n + 1, 0:1]
    send(last.at[pl.ds(0, n)], gf_o)
    send(loss, loss_o)
    for i in range(parts):
        for c in range(i * cc, (i + 1) * cc, 128):
            at = slice(c, c + 128)
            gl[:, at] = probs[:, at] * (gp[:, at].astype(f32) - tot[...])
        at = pl.ds(i * cc, cc)
        send(gl.at[:, at], gl_o.at[:, at])
    for c in copies:
        c.wait()


def grouped(logits, filt, expr, target, gene_mask, density):
    f32, bf16, i32 = jnp.float32, jnp.bfloat16, jnp.int32
    nspot = lax.axis_size("spot")
    rows, cells = logits.shape
    cd, genes = expr.shape
    nz = nspot // GROUP
    n = genes // PIECE
    grp = GROUP * rows
    mine = cells // GROUP
    spots = 2 * rows

    def vmem(*shape, dtype=f32):
        return pltpu.VMEM(shape, dtype)

    def dma(*shape):
        return pltpu.SemaphoreType.DMA(shape)

    def low(*shape):
        return pltpu.VMEM(shape, bf16)

    buffers = [
        low(rows, cells), vmem(cd // 128, 128), vmem(*gene_mask.shape, dtype=i32), vmem(spots // 128, 128, dtype=i32),
        low(GROUP, rows, mine), low(2 * grp, mine), low(2 * grp, mine), low(mine, 2 * grp),
        low(n // 2, mine, 2 * PIECE), low(spots, genes), vmem(8, mine), vmem(nz, 8, 128), vmem(spots, genes),
        vmem(2 * grp, PIECE),
        low(n, 2 * rows, PIECE), low(n, 2 * rows, PIECE), low(n, 2 * rows, PIECE), low(n, 2 * rows, PIECE),
        low(n, rows, PIECE), low(n, rows, PIECE), low(n, rows, PIECE), low(n, rows, PIECE),
        vmem(n, rows, PIECE), vmem(n, rows, PIECE), vmem(GROUP, 8, 128), vmem(GROUP, 8, 128),
        vmem(3, 1, genes), vmem(GROUP, 3, 1, genes), vmem(3, spots, PIECE), vmem(3, 1, spots), vmem(3, 1, spots),
        low(n // 2, 2 * grp, 2 * PIECE), vmem(nz, cd, genes),
        low(nz, n, cd, PIECE), low(nz, n, cd, PIECE), low(nz, n, cd, PIECE),
        vmem(nz, grp, cd), vmem(nz, grp, cd), vmem(nz, grp, cd), low(nz, grp, cd), low(GROUP, nz, rows, cd),
        vmem(rows, 128), vmem(8, 128), vmem(GROUP, 8, 128), vmem(nz, 8, 128), vmem(8, 128), vmem(GROUP, 8, 128),
        vmem(grp, 128), vmem(nz, 1, cd), vmem(nz, 1, cd), vmem(3, 8, spots), vmem(3, 8, spots),
    ]
    sems = [
        pltpu.SemaphoreType.REGULAR, dma(4 + n // 2 + 2), dma(2, nz), dma(nz), dma(2, nz, n), dma(nz, n),
        dma(4), dma(4), dma(4), dma(4), dma(5), dma(5),
        dma(2, n), dma(2, n), dma(2, n), dma(2, n), dma(n), dma(n), dma(n), dma(n),
        dma(4), dma(4), dma(8), dma(8), dma(6, n), dma(6, n),
        dma(nz, n), dma(nz, n), dma(nz, n), dma(nz, n), dma(nz), dma(nz), dma(4, nz), dma(4, nz),
        dma(4), dma(4), dma(nz), dma(nz), dma(4), dma(4), dma(nz), dma(nz),
    ]
    v, a = pl.BlockSpec(memory_space=pltpu.VMEM), pl.BlockSpec(memory_space=pl.ANY)
    shape = jax.ShapeDtypeStruct
    fparts = (cd // 128, 128)
    given = (logits, filt.reshape(-1, 128), expr, target, gene_mask, density.reshape(-1, 128))
    probs, gp, tot, last, grad_expr = pl.pallas_call(
        functools.partial(group_kernel, nspot),
        out_shape=[vmem(rows, cells), low(rows, cells), vmem(rows, 128), vmem(8, 128), vmem(cd, genes)],
        in_specs=[a] * 6,
        out_specs=[v] * 5,
        scratch_shapes=buffers + sems,
        compiler_params=pltpu.CompilerParams(
            collective_id=0, has_side_effects=True, vmem_limit_bytes=VMEM_BYTES
        ),
        name="group_step",
    )(*(pltpu.with_memory_space_constraint(g, pltpu.HBM) for g in given))
    grad_logits, grad_expr, loss, grad_filt = pl.pallas_call(
        finish_kernel,
        out_shape=[shape((rows, cells), f32), shape((cd, genes), f32), shape((1, 1), f32), shape(fparts, f32)],
        in_specs=[v] * 5,
        out_specs=[a] * 4,
        scratch_shapes=[vmem(rows, cells), vmem(1, 1), dma(7)],
        compiler_params=pltpu.CompilerParams(vmem_limit_bytes=LAST_BYTES),
        name="finish_step",
    )(probs, gp, tot, grad_expr, last)
    return (loss.reshape(()), grad_logits, grad_filt.reshape(-1), grad_expr)


def fits(logits, filt, expr):
    nspot = lax.axis_size("spot")
    rows, cells = logits.shape
    sizes = (rows, cells, filt.shape[0], expr.shape[1])
    return (
        nspot == GROUP * SLIDES and lax.axis_size("gene") == 2 and sizes == (128, 4096, 256, 1024)
    )


def per_device(logits, filt, expr, target, gene_mask, density):
    plan = grouped if fits(logits, filt, expr) else streamed
    return plan(logits, filt, expr, target, gene_mask, density)


def solution(mesh):
    in_specs = (
        P(("spot", "gene"), None),
        P("spot"),
        P("spot", "gene"),
        P("spot", "gene"),
        P(None, "gene"),
        P("spot"),
    )
    out_specs = (P(), P(("spot", "gene"), None), P("spot"), P("spot", "gene"))
    return jax.shard_map(
        per_device, mesh=mesh, in_specs=in_specs, out_specs=out_specs, check_vma=False
    )
```

```python
import functools

import jax
import jax.numpy as jnp
from jax import lax
from jax.experimental import pallas as pl
from jax.experimental.pallas import tpu as pltpu
from jax.sharding import PartitionSpec as P

SPOTS = 4096
SLIDES = 4


eps_norm = 1e-06


def slide_moments(onehot, pred, truth):
    hi = lax.Precision.HIGHEST
    return jnp.stack(
        [
            jnp.dot(onehot.T, pred * truth, precision=hi),
            jnp.dot(onehot.T, pred * pred, precision=hi),
            jnp.dot(onehot.T, truth * truth, precision=hi),
        ]
    )


def spot_moments(pred, truth):
    return jnp.stack(
        [
            jnp.sum(pred * truth, axis=1),
            jnp.sum(pred * pred, axis=1),
            jnp.sum(truth * truth, axis=1),
        ]
    )


def cosine_parts(slide_stats):
    dots = slide_stats[0]
    slide_a = lax.rsqrt(slide_stats[1] + eps_norm)
    slide_b = lax.rsqrt(slide_stats[2] + eps_norm)
    return (dots, slide_a, slide_b, dots * slide_a * slide_b)


def pred_gradient(onehot, weight_slide, dots, slide_a, slide_b, spot_stats, pred, truth):
    hi = lax.Precision.HIGHEST
    spot_a = lax.rsqrt(spot_stats[1] + eps_norm)
    spot_b = lax.rsqrt(spot_stats[2] + eps_norm)
    coef_truth = -weight_slide * slide_a * slide_b
    coef_pred = weight_slide * dots * slide_a**3 * slide_b
    grad_pred = (
        jnp.dot(onehot, coef_truth, precision=hi) * truth
        + jnp.dot(onehot, coef_pred, precision=hi) * pred
    )
    grad_pred = (
        grad_pred
        + (
            -(spot_a * spot_b)[:, None] * truth
            + (spot_stats[0] * spot_a**3 * spot_b)[:, None] * pred
        )
        / SPOTS
    )
    return (grad_pred, spot_stats[0] * spot_a * spot_b)


def streamed(logits, filt, expr, target, gene_mask, density):
    f32 = jnp.float32
    bf16 = jnp.bfloat16
    nspot = lax.axis_size("spot")
    ngene = lax.axis_size("gene")
    spot_dev = logits.shape[0]
    cells = logits.shape[1]
    cell_dev = filt.shape[0]
    owned = target.shape[0]
    half = target.shape[1]
    spots_all = owned * nspot
    slide_len = SPOTS // SLIDES
    scores = logits.astype(f32)
    shifted = jnp.exp(scores - jnp.max(scores, axis=1, keepdims=True))
    probs = shifted / jnp.sum(shifted, axis=1, keepdims=True)
    moved = lax.all_to_all(probs.astype(bf16), "spot", split_axis=1, concat_axis=0, tiled=True)
    paired = lax.all_gather(moved.reshape(nspot, 1, spot_dev, cell_dev), "gene", axis=1, tiled=True)
    paired = paired.reshape(spots_all, cell_dev)
    gate = jax.nn.sigmoid(filt)
    weighted = (paired.astype(f32) * gate[None, :]).astype(bf16)
    partial_pred = jnp.dot(weighted, expr, preferred_element_type=f32)
    partial_mass = jnp.sum(weighted.astype(f32), axis=1)
    gate_part = jnp.sum(gate)
    maskf = gene_mask.astype(f32)
    mask_part = jnp.sum(maskf, axis=1)
    pred_three, mass_two = (
        lax.psum_scatter(
            partial_pred.reshape(nspot, owned, half), "spot", scatter_dimension=0, tiled=True
        ),
        lax.psum_scatter(
            partial_mass.reshape(nspot, owned), "spot", scatter_dimension=0, tiled=True
        ),
    )
    pred = pred_three.reshape(owned, half)
    mass = mass_two.reshape(owned)
    truth = target.astype(f32)
    dens = density.astype(f32)
    spot_ids = lax.axis_index("spot") * owned + jnp.arange(owned, dtype=jnp.int32)
    onehot = (
        spot_ids[:, None] // slide_len == jnp.arange(SLIDES, dtype=jnp.int32)[None, :]
    ).astype(f32)
    slide_stats, mass_total, gate_total, count_total = lax.psum(
        (slide_moments(onehot, pred, truth), jnp.sum(mass), gate_part, jnp.sum(dens)), "spot"
    )
    dots, slide_a, slide_b, cos_gene = cosine_parts(slide_stats)
    spot_stats, kept_genes, gene_numer = lax.psum(
        (spot_moments(pred, truth), mask_part, jnp.sum(maskf * cos_gene, axis=1)), "gene"
    )
    genes_kept = jnp.maximum(kept_genes, 1.0)
    weight_slide = maskf / genes_kept[:, None] / SLIDES
    grad_pred, cos_spot = pred_gradient(
        onehot, weight_slide, dots, slide_a, slide_b, spot_stats, pred, truth
    )
    share = dens / count_total
    kl_local = jnp.sum(share * (jnp.log(share) - jnp.log(mass) + jnp.log(mass_total)))
    cos_total, kl_total = lax.psum((jnp.sum(cos_spot), kl_local), "spot")
    grad_mass = 1.0 / mass_total - share / mass
    spread_three, spread_two = (
        lax.all_gather(grad_pred.astype(bf16).reshape(1, owned, half), "spot", axis=0, tiled=True),
        lax.all_gather(grad_mass.astype(bf16).reshape(1, owned), "spot", axis=0, tiled=True),
    )
    spread_pred = spread_three.reshape(spots_all, half)
    spread_mass = spread_two.reshape(spots_all)
    gene_term = jnp.mean(gene_numer / genes_kept)
    excess = gate_total / count_total - 1.0
    loss = -gene_term - cos_total / SPOTS + kl_total + excess * excess
    grad_expr = lax.dot_general(
        weighted, spread_pred, (((0,), (0,)), ((), ())), preferred_element_type=f32
    )
    first_half = (lax.axis_index("gene") == 0).astype(f32)
    grad_weighted = lax.dot_general(
        spread_pred, expr, (((1,), (1,)), ((), ())), preferred_element_type=f32
    )
    grad_weighted = grad_weighted + first_half * spread_mass.astype(f32)[:, None]
    filter_part = jnp.sum(grad_weighted * paired.astype(f32), axis=0)
    filter_total = lax.psum(filter_part, "gene")
    grad_filt = (filter_total + 2.0 * excess / count_total) * gate * (1.0 - gate)
    terms = (grad_weighted * gate[None, :]).reshape(nspot, ngene, spot_dev, cell_dev)
    moved_back = lax.all_to_all(terms, "spot", split_axis=0, concat_axis=3, tiled=True)
    folded = lax.psum_scatter(moved_back, "gene", scatter_dimension=1, tiled=True)
    rounded = lax.optimization_barrier(folded.reshape(spot_dev, cells).astype(bf16))
    grad_probs = rounded.astype(f32)
    grad_logits = probs * (grad_probs - jnp.sum(probs * grad_probs, axis=1, keepdims=True))
    return (loss, grad_logits, grad_filt, grad_expr)


GROUP = 4
PIECE = 128
MESH = pl.DeviceIdType.MESH
VMEM_BYTES = 44 << 20
LAST_BYTES = 16 << 20


def remote(src, dst, send, recv, dev):
    return pltpu.make_async_remote_copy(
        src_ref=src, dst_ref=dst, send_sem=send, recv_sem=recv, device_id=dev, device_id_type=MESH
    )


def dot_nt(a, b):
    return lax.dot_general(a, b, (((1,), (1,)), ((), ())), preferred_element_type=jnp.float32)


def column(row, length):
    return jnp.transpose(jnp.broadcast_to(row, (128, length)))


def fold(values):
    total = values[:, 0:128]
    for i in range(1, values.shape[1] // 128):
        total = total + values[:, i * 128 : (i + 1) * 128]
    return total


def group_kernel(
    nspot, logits_h, filt_h, expr, target, mask_h, dens_h,
    probs, gpb, tot_o, last_o, ge_o,
    logits, filt, mask, dens, rawq, wraw, wg, wt, ebuf, tbuf, gcol, small, pfin, ahead,
    psx, prx, psy, pry, ps2x, pr2x, ps2y, pr2y, hx, hy, massp, massr, statg, statr, acc, spots, spotr, tlead, plead,
    dpa, grad, dsend, dright, dleft, dwo, dws, dwr, gps, gpr, rowsum, tile_s, tile_r, tz, gms, gmr, gmcol,
    fsend, frecv, pair_s, pair_r,
    hello, lc, zs_s, zs_r, ez_s, ez_r, w_s, w_r, wd_s, wd_r, pr_s, pr_r,
    px_s, px_r, py_s, py_r, p2x_s, p2x_r, p2y_s, p2y_r, ms_s, ms_r, st_s, st_r, ld_s, ld_r, sp_s, sp_r, ag_s, ag_r,
    dr_s, dr_r, dl_s, dl_r, dw_s, dw_r, gp_s, gp_r, tl_s, tl_r, tz_s, tz_r, gm_s, gm_r, fz_s, fz_r,
):
    f32, bf16 = jnp.float32, jnp.bfloat16
    rows, cells = probs.shape
    cd, genes = expr.shape
    nz = nspot // GROUP
    np_ = genes // PIECE
    grp = GROUP * rows
    mine = cells // GROUP
    spots_all = nspot * 2 * rows
    me, j = lax.axis_index("spot"), lax.axis_index("gene")
    sib = 1 - j
    z, q = me // GROUP, me % GROUP
    x, y = q % 2, q // 2
    nbr = [me, me + 1 - 2 * x, me + 2 - 4 * y, me + 3 - 2 * x - 4 * y]
    nq = [n % GROUP for n in nbr]
    here = (me, sib)
    has_right, has_left = z < nz - 1, z > 0
    ends = (z == 0, z == nz - 1)
    chip = [(n, j) for n in nbr]
    beside = ((me + GROUP, j), (me - GROUP, j))

    def at_k(k, h=0):
        return pl.ds(h * grp + k * rows, rows)

    def piece(g):
        return pl.ds(g * PIECE, PIECE)

    def half_of(buf, r, g):
        return buf.at[g // 2, r, pl.ds(g % 2 * PIECE, PIECE)]

    def seg(p):
        return pl.ds(pl.multiple_of(p * cd, cd), cd)

    barrier = pltpu.get_barrier_semaphore()

    def greet(dev):
        pl.semaphore_signal(barrier, inc=1, device_id=dev, device_id_type=MESH)

    greet(chip[1])
    greet(chip[2])

    @pl.when(has_right)
    def _():
        greet(beside[0])

    @pl.when(has_left)
    def _():
        greet(beside[1])

    greet(here)
    loads = [pltpu.make_async_copy(logits_h, logits, lc.at[0])]
    loads += [
        pltpu.make_async_copy(s, d, lc.at[1 + i])
        for i, (s, d) in enumerate(((filt_h, filt), (mask_h, mask), (dens_h, dens)))
    ]
    loads += [
        pltpu.make_async_copy(
            expr.at[:, pl.ds(i * 2 * PIECE, 2 * PIECE)], ebuf.at[i, seg(z), :], lc.at[4 + i]
        )
        for i in range(np_ // 2)
    ]
    loads += [
        pltpu.make_async_copy(
            target.at[pl.ds(pl.multiple_of(c * rows, rows), rows)],
            tbuf.at[pl.ds(i * rows, rows)],
            lc.at[4 + np_ // 2 + i],
        )
        for i, c in enumerate((j, sib))
    ]
    for c in loads:
        c.start()
    loads[0].wait()

    step = 32

    @pl.loop(0, rows // step)
    def _(i):
        at = pl.ds(pl.multiple_of(i * step, step), step)
        s = logits[at, :].astype(f32)
        e = jnp.exp(s - jnp.max(s, axis=1, keepdims=True))
        p = e * (1.0 / jnp.sum(e, axis=1, keepdims=True))
        probs[at, :] = p
        for o in range(nspot):
            c = o // GROUP * cd
            rawq[o % GROUP, at, c : c + cd] = p[:, o * cd : (o + 1) * cd].astype(bf16)

    for c in loads[1:]:
        c.wait()
    small[pl.ds(z, 1), 0 : cd // 128, :] = filt[...][None]
    maskf = mask[pl.ds(z, 1), :].astype(f32)
    kept_mine = jnp.sum(maskf)
    pair_s[0] = jnp.full((8, 2 * rows), kept_mine)
    pl.semaphore_wait(barrier, 3 + has_right.astype(jnp.int32) + has_left.astype(jnp.int32))

    def zsmall(way, p):
        return remote(small.at[p], small.at[p], zs_s.at[way, p], zs_r.at[p], beside[way])

    def zsend(way, p, g):
        u = half_of(ebuf, seg(p), g)
        return remote(u, u, ez_s.at[way, p, g], ez_r.at[p, g], beside[way])

    def both(make):
        @pl.when(has_right)
        def _():
            make(0).start()

        @pl.when(has_left)
        def _():
            make(1).start()

    def hop(s, make):
        @pl.when(z >= s)
        def _():
            make(0, z - s).wait_recv()

            @pl.when(has_right)
            def _():
                make(0, z - s).start()

        @pl.when(z + s <= nz - 1)
        def _():
            make(1, z + s).wait_recv()

            @pl.when(has_left)
            def _():
                make(1, z + s).start()

    def own(g):
        if g < np_:
            both(lambda way: zsend(way, z, g))

    def along(s, g):
        if 0 <= g < np_:
            hop(s, lambda way, p: zsend(way, p, g))

    both(lambda way: zsmall(way, z))
    own(0)
    own(1)

    def wcopy(k):
        return remote(rawq.at[nq[k]], wraw.at[at_k(k)], w_s.at[k], w_r.at[k], chip[k])

    def wsib(k):
        return remote(wraw.at[at_k(k)], wraw.at[at_k(k, 1)], wd_s.at[k], wd_r.at[k], here)

    def pair(i):
        return remote(pair_s.at[i], pair_r.at[i], pr_s.at[i], pr_r.at[i], here)

    def lead_copy(buf, i, k, h):
        r = at_k(0, h)
        return remote(buf.at[r], buf.at[at_k(k, h)], ld_s.at[i, k, h], ld_r.at[i, k, h], chip[k])

    def lead(buf, i, values):
        for h in range(2):
            buf[at_k(0, h), :] = values[h * rows : (h + 1) * rows]
        for k in (3, 1, 2):
            for h in range(2):
                lead_copy(buf, i, k, h).start()

    def lead_wait(buf, i):
        for k in (1, 2, 3):
            for h in range(2):
                lead_copy(buf, i, k, h).wait_recv()

    wcopy(1).start()
    wcopy(2).start()
    pl.semaphore_signal(hello, inc=1, device_id=chip[1], device_id_type=MESH)
    wraw[at_k(0), :] = rawq[pl.ds(q, 1)].reshape(rows, mine)
    wsib(0).start()
    pair(0).start()
    pl.semaphore_wait(hello, 1)
    wcopy(3).start()

    def gated(k, h):
        r = at_k(k, h)
        for c in range(0, mine, 512):
            at = pl.ds(c, 512)
            wg[r, at] = (gcol[0:1, at] * wraw[r, at].astype(f32)).astype(bf16)

    def turned(k, h):
        r = at_k(k, h)
        for c in range(0, mine, 512):
            at = pl.ds(c, 512)
            wt[at, r] = jnp.transpose(wg[r, at].astype(f32)).astype(bf16)

    def arrive(k):
        wcopy(k).wait_recv()
        wsib(k).start()
        gated(k, 0)

    def arrive_sib(k):
        wsib(k).wait_recv()
        gated(k, 1)

    first, second = pl.ds(0, rows), pl.ds(rows, rows)

    def pxcopy(g, n):
        h = (first, second)[n]
        return remote(psx.at[g, h], prx.at[g, h], px_s.at[n, g], px_r.at[n, g], chip[1])

    def pycopy(g, n):
        h = (first, second)[n]
        return remote(psy.at[g, h], pry.at[g, h], py_s.at[n, g], py_r.at[n, g], chip[2])

    def p2xcopy(g):
        return remote(ps2x.at[g], pr2x.at[g], p2x_s.at[g], p2x_r.at[g], chip[1])

    def p2ycopy(g):
        return remote(ps2y.at[g], pr2y.at[g], p2y_s.at[g], p2y_r.at[g], chip[2])

    def piece_of(g, at):
        return ebuf[g // 2, at, g % 2 * PIECE : (g % 2 + 1) * PIECE]

    def project(g):
        share(g, jnp.dot(wg[...], piece_of(g, pl.ds(0, mine)), preferred_element_type=f32))

    far = (1 - z // (nz // 2)) * (nz - 1)
    near = pl.ds(pl.multiple_of(z // (nz // 2) * cd, cd), mine - cd)

    def project_ahead():
        ahead[...] = jnp.dot(wg[:, near], ebuf[np_ // 2 - 1, near, :], preferred_element_type=f32)

    def project_last(g):
        v = jnp.dot(wg[:, seg(far)], piece_of(g, seg(far)), preferred_element_type=f32)
        share(g, ahead[:, g % 2 * PIECE : (g % 2 + 1) * PIECE] + v)

    def share(g, v):
        def part(k, h):
            s = h * grp + k * rows
            return v[s : s + rows]

        psx[g, second] = part(3, 0).astype(bf16)
        pxcopy(g, 1).start()
        psy[g, second] = part(3, 1).astype(bf16)
        pycopy(g, 1).start()
        psx[g, first] = part(1, 0).astype(bf16)
        pxcopy(g, 0).start()
        psy[g, first] = part(2, 1).astype(bf16)
        pycopy(g, 0).start()
        hx[g] = part(2, 0)
        hy[g] = part(1, 1)
        pfin[first, piece(g)] = part(0, 0)
        pfin[second, piece(g)] = part(0, 1)

    def relay(g):
        pxcopy(g, 1).wait_recv()
        ps2y[g] = (hx[g] + prx[g, second].astype(f32)).astype(bf16)
        p2ycopy(g).start()
        pycopy(g, 1).wait_recv()
        ps2x[g] = (hy[g] + pry[g, second].astype(f32)).astype(bf16)
        p2xcopy(g).start()

    def whole(g):
        at = piece(g)
        pxcopy(g, 0).wait_recv()
        pycopy(g, 0).wait_recv()
        p2ycopy(g).wait_recv()
        p2xcopy(g).wait_recv()
        pfin[first, at] += prx[g, first].astype(f32) + pr2y[g].astype(f32)
        pfin[second, at] += pry[g, first].astype(f32) + pr2x[g].astype(f32)
        p = pfin[:, at]
        t = tbuf[:, at].astype(f32)
        for i, v in enumerate((p * p, p * t, t * t)):
            statg[i, :, at] = jnp.sum(v, axis=0, keepdims=True)
            acc[i] += v

    parts = (pl.ds(0, (np_ - 2) * PIECE), pl.ds((np_ - 2) * PIECE, 2 * PIECE))

    def stat(k, n):
        i = 2 * k + n
        return remote(
            statg.at[:, :, parts[n]], statr.at[k, :, :, parts[n]], st_s.at[i], st_r.at[i], chip[k]
        )

    def gates():
        for p in range(nz):
            for h in range(cd // 128):
                g = jax.nn.sigmoid(small[p, h : h + 1, :])
                c = p * cd + h * 128
                gcol[:, c : c + 128] = jnp.broadcast_to(g, (8, 128))

    def mass_copy(k):
        return remote(massp.at[k], massr.at[k], ms_s.at[k], ms_r.at[k], chip[k])

    def masses():
        m = dot_nt(jnp.ones((8, mine), bf16), wg[...])
        for k in range(GROUP):
            for h in range(2):
                s = h * grp + k * rows
                massp[k, h : h + 1, :] = m[0:1, s : s + rows]
            if k:
                mass_copy(k).start()

    acc[...] = jnp.zeros_like(acc)
    hop(1, zsmall)
    along(1, 0)
    own(2)
    hop(2, zsmall)
    along(1, 1)
    along(2, 0)
    own(3)
    hop(3, zsmall)
    gates()
    gated(0, 0)
    arrive(1)
    arrive(2)
    arrive_sib(0)
    along(1, 2)
    along(2, 1)
    own(4)
    arrive_sib(1)
    arrive_sib(2)
    for k in range(3):
        turned(k, 0)
    arrive(3)
    arrive_sib(3)
    along(3, 0)
    project(0)
    for s in range(3, np_ + 2):
        along(1, s)
        along(2, s - 1)
        own(s + 2)
        if s == np_:
            project_ahead()
        along(3, s - 2)
        if s < np_:
            project(s - 2)
        else:
            project_last(s - 2)
        if s == 4:
            masses()
        if s == 5:
            for k in range(3):
                turned(k, 1)
        if s == 6:
            turned(3, 0)
            turned(3, 1)
        relay(s - 3)
        if s == 4:
            lead(tlead, 0, tbuf[:, 0:PIECE])
        if s > 4:
            whole(s - 5)
        if s == 5:
            lead(plead, 1, pfin[:, 0:PIECE].astype(bf16))
    whole(np_ - 3)
    for k in (3, 1, 2):
        stat(k, 0).start()
    pair(0).wait_recv()
    kept = jnp.maximum(kept_mine + jnp.sum(pair_r[0, 0:1, 0:1]), 1.0)
    weight = maskf / kept / SLIDES
    relay(np_ - 1)
    whole(np_ - 2)
    whole(np_ - 1)
    for k in (3, 1, 2):
        stat(k, 1).start()

    for i in range(3):
        spots[i] = jnp.sum(jnp.transpose(acc[i]), axis=0, keepdims=True)
    def spot_copy(k, h):
        i = 2 * k + h
        dev = (nbr[k], sib) if h else chip[k]
        return remote(spots, spotr.at[h, k], sp_s.at[i], sp_r.at[i], dev)

    others = [(k, h) for k in (3, 1, 2, 0) for h in (1, 0) if k or h]
    for k, h in others:
        spot_copy(k, h).start()

    def slide_sums(n):
        for k in (1, 2, 3):
            stat(k, n).wait_recv()
        at = parts[n]
        pred_sq, dots, truth_sq = (
            (statg[i, :, at] + statr[1, i, :, at]) + (statr[2, i, :, at] + statr[3, i, :, at])
            for i in range(3)
        )
        slide_a = lax.rsqrt(pred_sq + eps_norm)
        slide_b = lax.rsqrt(truth_sq + eps_norm)
        w = weight[:, at.start : at.start + at.size]
        return (
            -w * slide_a * slide_b,
            w * dots * slide_a**3 * slide_b,
            w * (dots * slide_a * slide_b),
        )

    coefs = [slide_sums(0), None]

    def spot_coefs(k):
        if k:
            spot_copy(k, 0).wait_recv()
        spot_copy(k, 1).wait_recv()
        pp, dot, tt = (
            (spotr[0, k, i] if k else spots[i])
            + jnp.concatenate([spotr[1, k, i, :, rows : 2 * rows], spotr[1, k, i, :, 0:rows]], axis=1)
            for i in range(3)
        )
        a, b = lax.rsqrt(pp + eps_norm), lax.rsqrt(tt + eps_norm)
        return (
            column(-(a * b) / spots_all, 2 * rows),
            column(dot * a**3 * b / spots_all, 2 * rows),
            dot * a * b,
        )

    col_t, col_p, cos_spot = spot_coefs(0)

    def agcopy(i, g):
        src, dst, to = (
            (at_k(0), at_k(1), 1), (at_k(0, 1), at_k(1, 1), 1), (at_k(0, 1), at_k(2, 1), 2),
            (at_k(0), at_k(2), 2), (at_k(1), at_k(3), 2), (at_k(2, 1), at_k(3, 1), 1),
        )[i]
        return remote(half_of(dpa, src, g), half_of(dpa, dst, g), ag_s.at[i, g], ag_r.at[i, g], chip[to])

    def give(g):
        n = 0 if g < np_ - 2 else 1
        if n and coefs[1] is None:
            coefs[1] = slide_sums(1)
        c = g * PIECE - parts[n].start
        c_t, c_p = (v[:, c : c + PIECE] for v in coefs[n][0:2])
        at = piece(g)
        d = ((c_t + col_t) * tbuf[:, at].astype(f32) + (c_p + col_p) * pfin[:, at]).astype(bf16)
        lanes = pl.ds(g % 2 * PIECE, PIECE)
        dpa[g // 2, at_k(0), lanes] = d[0:rows]
        dpa[g // 2, at_k(0, 1), lanes] = d[rows : 2 * rows]
        for i in range(4):
            agcopy(i, g).start()

    def lead_grad():
        lead_wait(tlead, 0)
        lead_wait(plead, 1)
        c_t, c_p = (v[:, 0:PIECE] for v in coefs[0][0:2])
        for k in (0, 1, 2, 3):
            t, p = (col_t, col_p) if k == 0 else spot_coefs(k)[0:2]
            for h in range(2):
                r, m = at_k(k, h), slice(h * rows, (h + 1) * rows)
                d = (c_t + t[m]) * tlead[r, :].astype(f32) + (c_p + p[m]) * plead[r, :].astype(f32)
                dpa[0, r, 0:PIECE] = d.astype(bf16)

    def give_on(g):
        agcopy(0, g).wait_recv()
        agcopy(4, g).start()
        agcopy(2, g).wait_recv()
        agcopy(5, g).start()

    def dcopy(way, p, g):
        if way == 0:
            return remote(dsend.at[p, g], dright.at[p, g], dr_s.at[p, g], dr_r.at[p, g], beside[0])
        return remote(dsend.at[p, g], dleft.at[p, g], dl_s.at[p, g], dl_r.at[p, g], beside[1])

    def expr_grad_first():
        up = z // (nz // 2)

        @pl.loop(0, nz)
        def _(u):
            p = up * u + (1 - up) * (nz - 1 - u)
            v = jnp.dot(wt[seg(p), :], dpa[0, :, 0:PIECE], preferred_element_type=f32)
            grad[p, :, 0:PIECE] = v

            @pl.when((ends[0] | ends[1]) & (p != z))
            def _():
                dsend[p, 0] = v.astype(bf16)

            @pl.when(ends[0] & (p != z))
            def _():
                dcopy(0, p, 0).start()

            @pl.when(ends[1] & (p != z))
            def _():
                dcopy(1, p, 0).start()

    def expr_grad(g):
        for i in (1, 3, 4, 5):
            agcopy(i, g).wait_recv()
        lanes = slice(g % 2 * PIECE, (g % 2 + 1) * PIECE)
        v = jnp.dot(wt[...], dpa[g // 2, :, lanes], preferred_element_type=f32)
        for p in range(nz):
            grad[p, :, piece(g)] = v[p * cd : (p + 1) * cd]

        @pl.when(ends[0])
        def _():
            for p in range(1, nz):
                dsend[p, g] = v[p * cd : (p + 1) * cd].astype(bf16)

        @pl.when(ends[1])
        def _():
            for p in range(nz - 1):
                dsend[p, g] = v[p * cd : (p + 1) * cd].astype(bf16)

    def start_from_ends(u, g):
        if not 0 <= g < np_:
            return

        @pl.when(ends[0])
        def _():
            dcopy(0, nz - 1 - u, g).start()

        @pl.when(ends[1])
        def _():
            dcopy(1, u, g).start()

    def starts(*pieces):
        for u, g in pieces:
            start_from_ends(u, g)

    def chain(hops, u, g):
        if nz - 1 - u > hops:

            @pl.when(z == hops)
            def _():
                p = nz - 1 - u
                dcopy(0, p, g).wait_recv()
                dsend[p, g] = (grad[p, :, piece(g)] + dright[p, g].astype(f32)).astype(bf16)
                dcopy(0, p, g).start()

            @pl.when(nz - 1 - z == hops)
            def _():
                dcopy(1, u, g).wait_recv()
                dsend[u, g] = (grad[u, :, piece(g)] + dleft[u, g].astype(f32)).astype(bf16)
                dcopy(1, u, g).start()

    def finish(g):
        at = piece(g)
        ge_o[:, at] = grad[pl.ds(z, 1), :, at].reshape(cd, PIECE)

        @pl.when(has_left)
        def _():
            dcopy(0, z, g).wait_recv()
            ge_o[:, at] += dright[pl.ds(z, 1), g].reshape(cd, PIECE).astype(f32)

        @pl.when(has_right)
        def _():
            dcopy(1, z, g).wait_recv()
            ge_o[:, at] += dleft[pl.ds(z, 1), g].reshape(cd, PIECE).astype(f32)

    def tile_copy(k):
        return remote(tile_s, tile_r.at[k], tl_s.at[k], tl_r.at[k], chip[k])

    def zcopy(buf, src, r, ss, rs):
        to = (z + r) % nz
        return remote(buf.at[src], buf.at[z], ss.at[r], rs.at[r], (to * GROUP + q, j))

    def zcopy_wait(buf, r, ss, rs):
        o = (z + nz - r) % nz
        remote(buf.at[o], buf.at[o], ss.at[r], rs.at[r], here).wait_recv()

    def chip_masses():
        for k in (1, 2, 3):
            mass_copy(k).wait_recv()
        return (massp[0, 0:2] + massr[1, 0:2]) + (massr[2, 0:2] + massr[3, 0:2])

    def own_dens():
        d = dens[...].astype(f32)
        return jnp.where(j == 0, d, jnp.concatenate([d[1:2], d[0:1]], axis=0))

    def tile_start():
        mass, d = chip_masses(), own_dens()
        gene = fold(coefs[0][2]) + fold(coefs[1][2])
        cos = fold(cos_spot)
        tile_s[0:1] = -2.0 / GROUP * gene - cos / spots_all
        tile_s[1:2] = d[0:1] + d[1:2]
        f = jax.nn.sigmoid(filt[...])
        tile_s[2:3] = f[0:1] + f[1:2]
        tile_s[3:4] = mass[0:1] + mass[1:2]
        kl = d * (jnp.log(d) - jnp.log(mass))
        tile_s[4:5] = kl[0:1] + kl[1:2]
        tile_s[5:8] = jnp.zeros((3, 128), f32)
        for k in (3, 1, 2):
            tile_copy(k).start()
        return mass, d

    def tile_along():
        for k in (1, 2, 3):
            tile_copy(k).wait_recv()
        tz[pl.ds(z, 1)] = ((tile_s[...] + tile_r[1]) + (tile_r[2] + tile_r[3]))[None]
        for r in range(1, nz):
            zcopy(tz, z, r, tz_s, tz_r).start()

    def gm_copy(k):
        return remote(gms, gmr.at[k], gm_s.at[k], gm_r.at[k], chip[k])

    def totals(mass, d):
        for r in range(1, nz):
            zcopy_wait(tz, r, tz_s, tz_r)
        t = tz[0]
        for p in range(1, nz):
            t = t + tz[p]
        loss_part, count, gate, mass_total, kl = (jnp.sum(t[i : i + 1]) for i in range(5))
        logs = jnp.log(jnp.where(lax.broadcasted_iota(jnp.int32, (1, 128), 1) == 0, count, mass_total))
        log_count, log_mass = jnp.sum(logs[:, 0:1]), jnp.sum(logs[:, 1:2])
        excess = gate / count - 1.0
        gms[...] = jnp.zeros_like(gms)
        gms[0:2] = (1.0 / mass_total - d / count / mass).astype(bf16).astype(f32)
        for k in (3, 1, 2):
            gm_copy(k).start()
        pair_s[1] = jnp.full((8, 2 * rows), loss_part + kl / count - log_count + log_mass + excess * excess)
        pair(1).start()
        return 2.0 * excess / count

    def mass_columns():
        gmcol[at_k(0), :] = column(gms[0:1], rows)
        for k in (1, 2, 3):
            gm_copy(k).wait_recv()
            gmcol[at_k(k), :] = column(gmr[k, 0:1], rows)

    def dwcopy(p):
        return remote(dws.at[p], dwr.at[p], dw_s.at[p], dw_r.at[p], here)

    def weight_grad(p):
        cs = slice(p * cd, (p + 1) * cd)

        def rows_of(h):
            d = dot_nt(dpa[0, h * grp : (h + 1) * grp, :], ebuf[0, cs, :])
            for c in range(1, np_ // 2):
                d = d + dot_nt(dpa[c, h * grp : (h + 1) * grp, :], ebuf[c, cs, :])
            return d

        dws[p] = rows_of(1)
        dwcopy(p).start()
        dwo[p] = rows_of(0)

    def gpcopy(k, p):
        return remote(gps.at[p, at_k(k)], gpr.at[k, p], gp_s.at[k, p], gp_r.at[k, p], chip[k])

    def give_back(p):
        dwcopy(p).wait_recv()
        cs = pl.ds(p * cd, cd)
        total = jnp.zeros((1, cd), f32)
        for k in (3, 1, 2, 0):
            r = at_k(k)
            gm = gmcol[r, :]
            gw = dwo[p, r] + dwr[p, r] + jnp.concatenate([gm] * (cd // 128), axis=1)
            total = total + jnp.sum(gw * wraw[r, cs].astype(f32), axis=0, keepdims=True)
            gps[p, r] = (gcol[0:1, cs] * gw).astype(bf16)
            if k:
                gpcopy(k, p).start()
        fsend[p] = total

    def filter_along():
        frecv[pl.ds(z, 1)] = fsend[pl.ds(z, 1)]
        for r in range(1, nz):
            to = (z + r) % nz
            remote(fsend.at[to], frecv.at[z], fz_s.at[r], fz_r.at[r], (to * GROUP + q, j)).start()

    def take(k, p, start=False):
        if k:
            gpcopy(k, p).wait_recv()
            v = gpr[k, p]
        else:
            v = gps[p, at_k(0)]
        at = pl.ds(pl.multiple_of((p * GROUP + nq[k]) * cd, cd), cd)
        gpb[:, at] = v
        s = fold(probs[:, at] * v.astype(f32))
        if start:
            rowsum[...] = s
        else:
            rowsum[...] += s

    def sent_first():
        for k in (1, 2, 3):
            wcopy(k).wait_send()
            mass_copy(k).wait_send()
            for n in (0, 1):
                stat(k, n).wait_send()
        for k in range(GROUP):
            wsib(k).wait_send()
        pair(0).wait_send()
        for k, h in others:
            spot_copy(k, h).wait_send()
        for k in (1, 2, 3):
            for h in range(2):
                lead_copy(tlead, 0, k, h).wait_send()
                lead_copy(plead, 1, k, h).wait_send()

        @pl.loop(0, np_)
        def _(g):
            for c in (pxcopy, pycopy):
                c(g, 0).wait_send()
                c(g, 1).wait_send()
            p2xcopy(g).wait_send()
            p2ycopy(g).wait_send()

    def sent_along():
        @pl.loop(0, nz)
        def _(p):
            @pl.when(has_right & (p <= z))
            def _():
                zsmall(0, p).wait_send()
                for g in range(np_):
                    zsend(0, p, g).wait_send()

            @pl.when(has_left & (p >= z))
            def _():
                zsmall(1, p).wait_send()
                for g in range(np_):
                    zsend(1, p, g).wait_send()

    def sent_back():
        for g in range(1, np_):
            for i in range(6):
                agcopy(i, g).wait_send()

    def sent_last():
        for k in (1, 2, 3):
            tile_copy(k).wait_send()
            gm_copy(k).wait_send()
            for p in range(nz):
                gpcopy(k, p).wait_send()
        for r in range(1, nz):
            zcopy(tz, z, r, tz_s, tz_r).wait_send()
            zcopy(fsend, z, r, fz_s, fz_r).wait_send()
        for p in range(nz):
            dwcopy(p).wait_send()
        for i in (1, 2):
            pair(i).wait_send()

    def sent_sums():
        @pl.loop(0, nz)
        def _(p):
            @pl.when(has_right & (p > z))
            def _():
                for g in range(np_):
                    dcopy(0, p, g).wait_send()

            @pl.when(has_left & (p < z))
            def _():
                for g in range(np_):
                    dcopy(1, p, g).wait_send()

    give(1)
    give(2)
    coefs[1] = slide_sums(1)
    mass, d = tile_start()
    lead_grad()
    expr_grad_first()
    give_on(1)
    give(3)
    give_on(2)
    give(4)
    tile_along()
    expr_grad(1)
    starts((0, 1), (1, 1), (2, 1))
    give_on(3)
    give(5)
    chain(1, 0, 0)
    give_on(4)
    expr_grad(2)
    starts((0, 2), (1, 2))
    chain(1, 1, 0)
    give(6)
    give_on(5)
    expr_grad(3)
    starts((0, 3), (1, 3))
    chain(1, 0, 1)
    chain(2, 0, 0)
    give(7)
    give_on(6)
    chain(1, 1, 1)
    expr_grad(4)
    starts((0, 4), (1, 4), (2, 2))
    push = totals(mass, d)
    give_on(7)
    chain(2, 0, 1)
    chain(1, 0, 2)
    expr_grad(5)
    starts((0, 5), (1, 5))
    finish(0)
    chain(1, 1, 2)
    expr_grad(6)
    starts((0, 6), (1, 6))
    chain(1, 0, 3)
    finish(1)
    mass_columns()
    expr_grad(7)
    starts((0, 7), (2, 3), (1, 7))
    chain(2, 0, 2)
    chain(1, 1, 3)
    weight_grad(0)
    chain(1, 0, 4)
    chain(2, 0, 3)
    weight_grad(1)
    give_back(0)
    chain(1, 1, 4)
    finish(2)
    weight_grad(2)
    give_back(1)
    chain(2, 0, 4)
    chain(1, 0, 5)
    weight_grad(3)
    give_back(2)
    chain(1, 1, 5)
    give_back(3)
    filter_along()
    starts((2, 4), (2, 5), (2, 6), (2, 7))
    chain(1, 0, 6)
    take(0, 0, True)
    for p in range(1, nz):
        take(0, p)
    chain(2, 0, 5)
    chain(1, 1, 6)
    sent_first()
    chain(1, 0, 7)
    for k in (1, 2, 3):
        take(k, 0)
    sent_along()
    chain(2, 0, 6)
    finish(3)
    for k in (1, 2, 3):
        take(k, 1)
    chain(1, 1, 7)
    sent_back()
    chain(2, 0, 7)
    finish(4)
    for k in (1, 2, 3):
        take(k, 2)
    finish(5)
    for r in range(1, nz):
        zcopy_wait(frecv, r, fz_s, fz_r)
    ftotal = frecv[0]
    for p in range(1, nz):
        ftotal = ftotal + frecv[p]
    pair_s[2, 0:1, 0:cd] = ftotal
    pair(2).start()
    for k in (1, 2, 3):
        take(k, 3)
    tot_o[...] = jnp.broadcast_to(jnp.sum(rowsum[...], axis=1, keepdims=True), (rows, 128))
    sent_last()
    finish(6)
    pair(1).wait_recv()
    pair(2).wait_recv()
    my_gate = jax.nn.sigmoid(filt[...])
    fsum = ftotal + pair_r[2, 0:1, 0:cd] + push
    for h in range(cd // 128):
        g = my_gate[h : h + 1, :]
        last_o[h : h + 1, :] = fsum[:, h * 128 : (h + 1) * 128] * g * (1.0 - g)
    last_o[cd // 128 : cd // 128 + 1, :] = 0.5 * (pair_s[1, 0:1, 0:128] + pair_r[1, 0:1, 0:128])
    finish(7)
    sent_sums()


def finish_kernel(probs, gp, tot, ge, last, gl_o, ge_o, loss_o, gf_o, gl, loss, out_s):
    f32 = jnp.float32
    parts = 4
    cc = probs.shape[1] // parts
    copies = []

    def send(src, dst):
        copies.append(pltpu.make_async_copy(src, dst, out_s.at[len(copies)]))
        copies[-1].start()

    send(ge, ge_o)
    n = gf_o.shape[0]
    loss[...] = last[n : n + 1, 0:1]
    send(last.at[pl.ds(0, n)], gf_o)
    send(loss, loss_o)
    for i in range(parts):
        for c in range(i * cc, (i + 1) * cc, 128):
            at = slice(c, c + 128)
            gl[:, at] = probs[:, at] * (gp[:, at].astype(f32) - tot[...])
        at = pl.ds(i * cc, cc)
        send(gl.at[:, at], gl_o.at[:, at])
    for c in copies:
        c.wait()


def grouped(logits, filt, expr, target, gene_mask, density):
    f32, bf16, i32 = jnp.float32, jnp.bfloat16, jnp.int32
    nspot = lax.axis_size("spot")
    rows, cells = logits.shape
    cd, genes = expr.shape
    nz = nspot // GROUP
    n = genes // PIECE
    grp = GROUP * rows
    mine = cells // GROUP
    spots = 2 * rows

    def vmem(*shape, dtype=f32):
        return pltpu.VMEM(shape, dtype)

    def dma(*shape):
        return pltpu.SemaphoreType.DMA(shape)

    def low(*shape):
        return pltpu.VMEM(shape, bf16)

    buffers = [
        low(rows, cells), vmem(cd // 128, 128), vmem(*gene_mask.shape, dtype=i32), vmem(spots // 128, 128, dtype=i32),
        low(GROUP, rows, mine), low(2 * grp, mine), low(2 * grp, mine), low(mine, 2 * grp),
        low(n // 2, mine, 2 * PIECE), low(spots, genes), vmem(8, mine), vmem(nz, 8, 128), vmem(spots, genes),
        vmem(2 * grp, 2 * PIECE),
        low(n, 2 * rows, PIECE), low(n, 2 * rows, PIECE), low(n, 2 * rows, PIECE), low(n, 2 * rows, PIECE),
        low(n, rows, PIECE), low(n, rows, PIECE), low(n, rows, PIECE), low(n, rows, PIECE),
        vmem(n, rows, PIECE), vmem(n, rows, PIECE), vmem(GROUP, 8, 128), vmem(GROUP, 8, 128),
        vmem(3, 1, genes), vmem(GROUP, 3, 1, genes), vmem(3, spots, PIECE), vmem(3, 1, spots), vmem(2, GROUP, 3, 1, spots), low(2 * grp, PIECE), low(2 * grp, PIECE),
        low(n // 2, 2 * grp, 2 * PIECE), vmem(nz, cd, genes),
        low(nz, n, cd, PIECE), low(nz, n, cd, PIECE), low(nz, n, cd, PIECE),
        vmem(nz, grp, cd), vmem(nz, grp, cd), vmem(nz, grp, cd), low(nz, grp, cd), low(GROUP, nz, rows, cd),
        vmem(rows, 128), vmem(8, 128), vmem(GROUP, 8, 128), vmem(nz, 8, 128), vmem(8, 128), vmem(GROUP, 8, 128),
        vmem(grp, 128), vmem(nz, 1, cd), vmem(nz, 1, cd), vmem(3, 8, spots), vmem(3, 8, spots),
    ]
    sems = [
        pltpu.SemaphoreType.REGULAR, dma(4 + n // 2 + 2), dma(2, nz), dma(nz), dma(2, nz, n), dma(nz, n),
        dma(4), dma(4), dma(4), dma(4), dma(3), dma(3),
        dma(2, n), dma(2, n), dma(2, n), dma(2, n), dma(n), dma(n), dma(n), dma(n),
        dma(4), dma(4), dma(8), dma(8), dma(2, 4, 2), dma(2, 4, 2), dma(8), dma(8), dma(6, n), dma(6, n),
        dma(nz, n), dma(nz, n), dma(nz, n), dma(nz, n), dma(nz), dma(nz), dma(4, nz), dma(4, nz),
        dma(4), dma(4), dma(nz), dma(nz), dma(4), dma(4), dma(nz), dma(nz),
    ]
    v, a = pl.BlockSpec(memory_space=pltpu.VMEM), pl.BlockSpec(memory_space=pl.ANY)
    shape = jax.ShapeDtypeStruct
    fparts = (cd // 128, 128)
    given = (logits, filt.reshape(-1, 128), expr, target, gene_mask, density.reshape(-1, 128))
    probs, gp, tot, last, grad_expr = pl.pallas_call(
        functools.partial(group_kernel, nspot),
        out_shape=[vmem(rows, cells), low(rows, cells), vmem(rows, 128), vmem(8, 128), vmem(cd, genes)],
        in_specs=[a] * 6,
        out_specs=[v] * 5,
        scratch_shapes=buffers + sems,
        compiler_params=pltpu.CompilerParams(
            collective_id=0, has_side_effects=True, vmem_limit_bytes=VMEM_BYTES
        ),
        name="group_step",
    )(*(pltpu.with_memory_space_constraint(g, pltpu.HBM) for g in given))
    grad_logits, grad_expr, loss, grad_filt = pl.pallas_call(
        finish_kernel,
        out_shape=[shape((rows, cells), f32), shape((cd, genes), f32), shape((1, 1), f32), shape(fparts, f32)],
        in_specs=[v] * 5,
        out_specs=[a] * 4,
        scratch_shapes=[vmem(rows, cells), vmem(1, 1), dma(7)],
        compiler_params=pltpu.CompilerParams(vmem_limit_bytes=LAST_BYTES),
        name="finish_step",
    )(probs, gp, tot, grad_expr, last)
    return (loss.reshape(()), grad_logits, grad_filt.reshape(-1), grad_expr)


def fits(logits, filt, expr):
    nspot = lax.axis_size("spot")
    rows, cells = logits.shape
    sizes = (rows, cells, filt.shape[0], expr.shape[1])
    return (
        nspot == GROUP * SLIDES and lax.axis_size("gene") == 2 and sizes == (128, 4096, 256, 1024)
    )


def per_device(logits, filt, expr, target, gene_mask, density):
    plan = grouped if fits(logits, filt, expr) else streamed
    return plan(logits, filt, expr, target, gene_mask, density)


def solution(mesh):
    in_specs = (
        P(("spot", "gene"), None),
        P("spot"),
        P("spot", "gene"),
        P("spot", "gene"),
        P(None, "gene"),
        P("spot"),
    )
    out_specs = (P(), P(("spot", "gene"), None), P("spot"), P("spot", "gene"))
    return jax.shard_map(
        per_device, mesh=mesh, in_specs=in_specs, out_specs=out_specs, check_vma=False
    )
```

```python
import functools

import jax
import jax.numpy as jnp
from jax import lax
from jax.experimental import pallas as pl
from jax.experimental.pallas import tpu as pltpu
from jax.sharding import PartitionSpec as P

SPOTS = 4096
SLIDES = 4


eps_norm = 1e-06


def slide_moments(onehot, pred, truth):
    hi = lax.Precision.HIGHEST
    return jnp.stack(
        [
            jnp.dot(onehot.T, pred * truth, precision=hi),
            jnp.dot(onehot.T, pred * pred, precision=hi),
            jnp.dot(onehot.T, truth * truth, precision=hi),
        ]
    )


def spot_moments(pred, truth):
    return jnp.stack(
        [
            jnp.sum(pred * truth, axis=1),
            jnp.sum(pred * pred, axis=1),
            jnp.sum(truth * truth, axis=1),
        ]
    )


def cosine_parts(slide_stats):
    dots = slide_stats[0]
    slide_a = lax.rsqrt(slide_stats[1] + eps_norm)
    slide_b = lax.rsqrt(slide_stats[2] + eps_norm)
    return (dots, slide_a, slide_b, dots * slide_a * slide_b)


def pred_gradient(onehot, weight_slide, dots, slide_a, slide_b, spot_stats, pred, truth):
    hi = lax.Precision.HIGHEST
    spot_a = lax.rsqrt(spot_stats[1] + eps_norm)
    spot_b = lax.rsqrt(spot_stats[2] + eps_norm)
    coef_truth = -weight_slide * slide_a * slide_b
    coef_pred = weight_slide * dots * slide_a**3 * slide_b
    grad_pred = (
        jnp.dot(onehot, coef_truth, precision=hi) * truth
        + jnp.dot(onehot, coef_pred, precision=hi) * pred
    )
    grad_pred = (
        grad_pred
        + (
            -(spot_a * spot_b)[:, None] * truth
            + (spot_stats[0] * spot_a**3 * spot_b)[:, None] * pred
        )
        / SPOTS
    )
    return (grad_pred, spot_stats[0] * spot_a * spot_b)


def streamed(logits, filt, expr, target, gene_mask, density):
    f32 = jnp.float32
    bf16 = jnp.bfloat16
    nspot = lax.axis_size("spot")
    ngene = lax.axis_size("gene")
    spot_dev = logits.shape[0]
    cells = logits.shape[1]
    cell_dev = filt.shape[0]
    owned = target.shape[0]
    half = target.shape[1]
    spots_all = owned * nspot
    slide_len = SPOTS // SLIDES
    scores = logits.astype(f32)
    shifted = jnp.exp(scores - jnp.max(scores, axis=1, keepdims=True))
    probs = shifted / jnp.sum(shifted, axis=1, keepdims=True)
    moved = lax.all_to_all(probs.astype(bf16), "spot", split_axis=1, concat_axis=0, tiled=True)
    paired = lax.all_gather(moved.reshape(nspot, 1, spot_dev, cell_dev), "gene", axis=1, tiled=True)
    paired = paired.reshape(spots_all, cell_dev)
    gate = jax.nn.sigmoid(filt)
    weighted = (paired.astype(f32) * gate[None, :]).astype(bf16)
    partial_pred = jnp.dot(weighted, expr, preferred_element_type=f32)
    partial_mass = jnp.sum(weighted.astype(f32), axis=1)
    gate_part = jnp.sum(gate)
    maskf = gene_mask.astype(f32)
    mask_part = jnp.sum(maskf, axis=1)
    pred_three, mass_two = (
        lax.psum_scatter(
            partial_pred.reshape(nspot, owned, half), "spot", scatter_dimension=0, tiled=True
        ),
        lax.psum_scatter(
            partial_mass.reshape(nspot, owned), "spot", scatter_dimension=0, tiled=True
        ),
    )
    pred = pred_three.reshape(owned, half)
    mass = mass_two.reshape(owned)
    truth = target.astype(f32)
    dens = density.astype(f32)
    spot_ids = lax.axis_index("spot") * owned + jnp.arange(owned, dtype=jnp.int32)
    onehot = (
        spot_ids[:, None] // slide_len == jnp.arange(SLIDES, dtype=jnp.int32)[None, :]
    ).astype(f32)
    slide_stats, mass_total, gate_total, count_total = lax.psum(
        (slide_moments(onehot, pred, truth), jnp.sum(mass), gate_part, jnp.sum(dens)), "spot"
    )
    dots, slide_a, slide_b, cos_gene = cosine_parts(slide_stats)
    spot_stats, kept_genes, gene_numer = lax.psum(
        (spot_moments(pred, truth), mask_part, jnp.sum(maskf * cos_gene, axis=1)), "gene"
    )
    genes_kept = jnp.maximum(kept_genes, 1.0)
    weight_slide = maskf / genes_kept[:, None] / SLIDES
    grad_pred, cos_spot = pred_gradient(
        onehot, weight_slide, dots, slide_a, slide_b, spot_stats, pred, truth
    )
    share = dens / count_total
    kl_local = jnp.sum(share * (jnp.log(share) - jnp.log(mass) + jnp.log(mass_total)))
    cos_total, kl_total = lax.psum((jnp.sum(cos_spot), kl_local), "spot")
    grad_mass = 1.0 / mass_total - share / mass
    spread_three, spread_two = (
        lax.all_gather(grad_pred.astype(bf16).reshape(1, owned, half), "spot", axis=0, tiled=True),
        lax.all_gather(grad_mass.astype(bf16).reshape(1, owned), "spot", axis=0, tiled=True),
    )
    spread_pred = spread_three.reshape(spots_all, half)
    spread_mass = spread_two.reshape(spots_all)
    gene_term = jnp.mean(gene_numer / genes_kept)
    excess = gate_total / count_total - 1.0
    loss = -gene_term - cos_total / SPOTS + kl_total + excess * excess
    grad_expr = lax.dot_general(
        weighted, spread_pred, (((0,), (0,)), ((), ())), preferred_element_type=f32
    )
    first_half = (lax.axis_index("gene") == 0).astype(f32)
    grad_weighted = lax.dot_general(
        spread_pred, expr, (((1,), (1,)), ((), ())), preferred_element_type=f32
    )
    grad_weighted = grad_weighted + first_half * spread_mass.astype(f32)[:, None]
    filter_part = jnp.sum(grad_weighted * paired.astype(f32), axis=0)
    filter_total = lax.psum(filter_part, "gene")
    grad_filt = (filter_total + 2.0 * excess / count_total) * gate * (1.0 - gate)
    terms = (grad_weighted * gate[None, :]).reshape(nspot, ngene, spot_dev, cell_dev)
    moved_back = lax.all_to_all(terms, "spot", split_axis=0, concat_axis=3, tiled=True)
    folded = lax.psum_scatter(moved_back, "gene", scatter_dimension=1, tiled=True)
    rounded = lax.optimization_barrier(folded.reshape(spot_dev, cells).astype(bf16))
    grad_probs = rounded.astype(f32)
    grad_logits = probs * (grad_probs - jnp.sum(probs * grad_probs, axis=1, keepdims=True))
    return (loss, grad_logits, grad_filt, grad_expr)


GROUP = 4
PIECE = 128
MESH = pl.DeviceIdType.MESH
VMEM_BYTES = 44 << 20
LAST_BYTES = 16 << 20


def remote(src, dst, send, recv, dev):
    return pltpu.make_async_remote_copy(
        src_ref=src, dst_ref=dst, send_sem=send, recv_sem=recv, device_id=dev, device_id_type=MESH
    )


def dot_nt(a, b):
    return lax.dot_general(a, b, (((1,), (1,)), ((), ())), preferred_element_type=jnp.float32)


def column(row, length):
    return jnp.transpose(jnp.broadcast_to(row, (128, length)))


def fold(values):
    total = values[:, 0:128]
    for i in range(1, values.shape[1] // 128):
        total = total + values[:, i * 128 : (i + 1) * 128]
    return total


def group_kernel(
    nspot, logits_h, filt_h, expr, target, mask_h, dens_h,
    probs, gpb, tot_o, last_o, ge_o,
    logits, filt, mask, dens, rawq, wraw, wg, wt, ebuf, tbuf, gcol, small, pfin, ahead,
    psx, prx, psy, pry, ps2x, pr2x, ps2y, pr2y, hx, hy, massp, massr, statg, statr, acc, spots, spotr, tlead, plead,
    dpa, grad, dsend, dright, dleft, dwo, dws, dwr, gps, gpr, rowsum, tile_s, tile_r, tz, gms, gmr, gmcol,
    fsend, frecv, pair_s, pair_r,
    hello, lc, zs_s, zs_r, ez_s, ez_r, w_s, w_r, wd_s, wd_r, pr_s, pr_r,
    px_s, px_r, py_s, py_r, p2x_s, p2x_r, p2y_s, p2y_r, ms_s, ms_r, st_s, st_r, ld_s, ld_r, sp_s, sp_r, ag_s, ag_r,
    dr_s, dr_r, dl_s, dl_r, dw_s, dw_r, gp_s, gp_r, tl_s, tl_r, tz_s, tz_r, gm_s, gm_r, fz_s, fz_r,
):
    f32, bf16 = jnp.float32, jnp.bfloat16
    rows, cells = probs.shape
    cd, genes = expr.shape
    nz = nspot // GROUP
    np_ = genes // PIECE
    grp = GROUP * rows
    mine = cells // GROUP
    spots_all = nspot * 2 * rows
    me, j = lax.axis_index("spot"), lax.axis_index("gene")
    sib = 1 - j
    z, q = me // GROUP, me % GROUP
    x, y = q % 2, q // 2
    nbr = [me, me + 1 - 2 * x, me + 2 - 4 * y, me + 3 - 2 * x - 4 * y]
    nq = [n % GROUP for n in nbr]
    here = (me, sib)
    has_right, has_left = z < nz - 1, z > 0
    ends = (z == 0, z == nz - 1)
    chip = [(n, j) for n in nbr]
    beside = ((me + GROUP, j), (me - GROUP, j))

    def at_k(k, h=0):
        return pl.ds(h * grp + k * rows, rows)

    def piece(g):
        return pl.ds(g * PIECE, PIECE)

    def half_of(buf, r, g):
        return buf.at[g // 2, r, pl.ds(g % 2 * PIECE, PIECE)]

    def seg(p):
        return pl.ds(pl.multiple_of(p * cd, cd), cd)

    barrier = pltpu.get_barrier_semaphore()

    def greet(dev):
        pl.semaphore_signal(barrier, inc=1, device_id=dev, device_id_type=MESH)

    greet(chip[1])
    greet(chip[2])

    @pl.when(has_right)
    def _():
        greet(beside[0])

    @pl.when(has_left)
    def _():
        greet(beside[1])

    greet(here)
    loads = [pltpu.make_async_copy(logits_h, logits, lc.at[0])]
    loads += [
        pltpu.make_async_copy(s, d, lc.at[1 + i])
        for i, (s, d) in enumerate(((filt_h, filt), (mask_h, mask), (dens_h, dens)))
    ]
    loads += [
        pltpu.make_async_copy(
            expr.at[:, pl.ds(i * 2 * PIECE, 2 * PIECE)], ebuf.at[i, seg(z), :], lc.at[4 + i]
        )
        for i in range(np_ // 2)
    ]
    loads += [
        pltpu.make_async_copy(
            target.at[pl.ds(pl.multiple_of(c * rows, rows), rows)],
            tbuf.at[pl.ds(i * rows, rows)],
            lc.at[4 + np_ // 2 + i],
        )
        for i, c in enumerate((j, sib))
    ]
    for c in loads:
        c.start()
    for c in loads[1 : 4 + np_ // 2]:
        c.wait()
    small[pl.ds(z, 1), 0 : cd // 128, :] = filt[...][None]
    pl.semaphore_wait(barrier, 3 + has_right.astype(jnp.int32) + has_left.astype(jnp.int32))

    def zsmall(way, p):
        return remote(small.at[p], small.at[p], zs_s.at[way, p], zs_r.at[p], beside[way])

    def zsend(way, p, g):
        u = half_of(ebuf, seg(p), g)
        return remote(u, u, ez_s.at[way, p, g], ez_r.at[p, g], beside[way])

    def both(make):
        @pl.when(has_right)
        def _():
            make(0).start()

        @pl.when(has_left)
        def _():
            make(1).start()

    def hop(s, make):
        @pl.when(z >= s)
        def _():
            make(0, z - s).wait_recv()

            @pl.when(has_right)
            def _():
                make(0, z - s).start()

        @pl.when(z + s <= nz - 1)
        def _():
            make(1, z + s).wait_recv()

            @pl.when(has_left)
            def _():
                make(1, z + s).start()

    def own(g):
        if g < np_:
            both(lambda way: zsend(way, z, g))

    def along(s, g):
        if 0 <= g < np_:
            hop(s, lambda way, p: zsend(way, p, g))

    both(lambda way: zsmall(way, z))
    own(0)
    own(1)

    loads[0].wait()

    step = 32

    @pl.loop(0, rows // step)
    def _(i):
        at = pl.ds(pl.multiple_of(i * step, step), step)
        s = logits[at, :].astype(f32)
        e = jnp.exp(s - jnp.max(s, axis=1, keepdims=True))
        p = e * (1.0 / jnp.sum(e, axis=1, keepdims=True))
        probs[at, :] = p
        for o in range(nspot):
            c = o // GROUP * cd
            rawq[o % GROUP, at, c : c + cd] = p[:, o * cd : (o + 1) * cd].astype(bf16)

    for c in loads[4 + np_ // 2 :]:
        c.wait()
    maskf = mask[pl.ds(z, 1), :].astype(f32)
    kept_mine = jnp.sum(maskf)
    pair_s[0] = jnp.full((8, 2 * rows), kept_mine)

    def wcopy(k):
        return remote(rawq.at[nq[k]], wraw.at[at_k(k)], w_s.at[k], w_r.at[k], chip[k])

    def wsib(k):
        return remote(wraw.at[at_k(k)], wraw.at[at_k(k, 1)], wd_s.at[k], wd_r.at[k], here)

    def pair(i):
        return remote(pair_s.at[i], pair_r.at[i], pr_s.at[i], pr_r.at[i], here)

    def lead_copy(buf, i, k, h):
        r = at_k(0, h)
        return remote(buf.at[r], buf.at[at_k(k, h)], ld_s.at[i, k, h], ld_r.at[i, k, h], chip[k])

    def lead(buf, i, values):
        for h in range(2):
            buf[at_k(0, h), :] = values[h * rows : (h + 1) * rows]
        for k in (3, 1, 2):
            for h in range(2):
                lead_copy(buf, i, k, h).start()

    def lead_wait(buf, i):
        for k in (1, 2, 3):
            for h in range(2):
                lead_copy(buf, i, k, h).wait_recv()

    wcopy(1).start()
    wcopy(2).start()
    pl.semaphore_signal(hello, inc=1, device_id=chip[1], device_id_type=MESH)
    wraw[at_k(0), :] = rawq[pl.ds(q, 1)].reshape(rows, mine)
    wsib(0).start()
    pair(0).start()
    pl.semaphore_wait(hello, 1)
    wcopy(3).start()

    def gated(k, h):
        r = at_k(k, h)
        for c in range(0, mine, 512):
            at = pl.ds(c, 512)
            wg[r, at] = (gcol[0:1, at] * wraw[r, at].astype(f32)).astype(bf16)

    def turned(k, h):
        r = at_k(k, h)
        for c in range(0, mine, 512):
            at = pl.ds(c, 512)
            wt[at, r] = jnp.transpose(wg[r, at].astype(f32)).astype(bf16)

    def arrive(k):
        wcopy(k).wait_recv()
        wsib(k).start()
        gated(k, 0)

    def arrive_sib(k):
        wsib(k).wait_recv()
        gated(k, 1)

    first, second = pl.ds(0, rows), pl.ds(rows, rows)

    def pxcopy(g, n):
        h = (first, second)[n]
        return remote(psx.at[g, h], prx.at[g, h], px_s.at[n, g], px_r.at[n, g], chip[1])

    def pycopy(g, n):
        h = (first, second)[n]
        return remote(psy.at[g, h], pry.at[g, h], py_s.at[n, g], py_r.at[n, g], chip[2])

    def p2xcopy(g):
        return remote(ps2x.at[g], pr2x.at[g], p2x_s.at[g], p2x_r.at[g], chip[1])

    def p2ycopy(g):
        return remote(ps2y.at[g], pr2y.at[g], p2y_s.at[g], p2y_r.at[g], chip[2])

    def piece_of(g, at):
        return ebuf[g // 2, at, g % 2 * PIECE : (g % 2 + 1) * PIECE]

    def project(g):
        share(g, jnp.dot(wg[...], piece_of(g, pl.ds(0, mine)), preferred_element_type=f32))

    far = (1 - z // (nz // 2)) * (nz - 1)
    near = pl.ds(pl.multiple_of(z // (nz // 2) * cd, cd), mine - cd)

    def project_ahead():
        ahead[...] = jnp.dot(wg[:, near], ebuf[np_ // 2 - 1, near, :], preferred_element_type=f32)

    def project_last(g):
        v = jnp.dot(wg[:, seg(far)], piece_of(g, seg(far)), preferred_element_type=f32)
        share(g, ahead[:, g % 2 * PIECE : (g % 2 + 1) * PIECE] + v)

    def share(g, v):
        def part(k, h):
            s = h * grp + k * rows
            return v[s : s + rows]

        psx[g, second] = part(3, 0).astype(bf16)
        pxcopy(g, 1).start()
        psy[g, second] = part(3, 1).astype(bf16)
        pycopy(g, 1).start()
        psx[g, first] = part(1, 0).astype(bf16)
        pxcopy(g, 0).start()
        psy[g, first] = part(2, 1).astype(bf16)
        pycopy(g, 0).start()
        hx[g] = part(2, 0)
        hy[g] = part(1, 1)
        pfin[first, piece(g)] = part(0, 0)
        pfin[second, piece(g)] = part(0, 1)

    def relay(g):
        pxcopy(g, 1).wait_recv()
        ps2y[g] = (hx[g] + prx[g, second].astype(f32)).astype(bf16)
        p2ycopy(g).start()
        pycopy(g, 1).wait_recv()
        ps2x[g] = (hy[g] + pry[g, second].astype(f32)).astype(bf16)
        p2xcopy(g).start()

    def whole(g):
        at = piece(g)
        pxcopy(g, 0).wait_recv()
        pycopy(g, 0).wait_recv()
        p2ycopy(g).wait_recv()
        p2xcopy(g).wait_recv()
        pfin[first, at] += prx[g, first].astype(f32) + pr2y[g].astype(f32)
        pfin[second, at] += pry[g, first].astype(f32) + pr2x[g].astype(f32)
        p = pfin[:, at]
        t = tbuf[:, at].astype(f32)
        for i, v in enumerate((p * p, p * t, t * t)):
            statg[i, :, at] = jnp.sum(v, axis=0, keepdims=True)
            acc[i] += v

    parts = (pl.ds(0, (np_ - 2) * PIECE), pl.ds((np_ - 2) * PIECE, 2 * PIECE))

    def stat(k, n):
        i = 2 * k + n
        return remote(
            statg.at[:, :, parts[n]], statr.at[k, :, :, parts[n]], st_s.at[i], st_r.at[i], chip[k]
        )

    def gates():
        for p in range(nz):
            for h in range(cd // 128):
                g = jax.nn.sigmoid(small[p, h : h + 1, :])
                c = p * cd + h * 128
                gcol[:, c : c + 128] = jnp.broadcast_to(g, (8, 128))

    def mass_copy(k):
        return remote(massp.at[k], massr.at[k], ms_s.at[k], ms_r.at[k], chip[k])

    def masses():
        m = dot_nt(jnp.ones((8, mine), bf16), wg[...])
        for k in range(GROUP):
            for h in range(2):
                s = h * grp + k * rows
                massp[k, h : h + 1, :] = m[0:1, s : s + rows]
            if k:
                mass_copy(k).start()

    acc[...] = jnp.zeros_like(acc)
    hop(1, zsmall)
    along(1, 0)
    own(2)
    hop(2, zsmall)
    along(1, 1)
    along(2, 0)
    own(3)
    hop(3, zsmall)
    gates()
    gated(0, 0)
    arrive(1)
    arrive(2)
    arrive_sib(0)
    along(1, 2)
    along(2, 1)
    own(4)
    arrive_sib(1)
    arrive_sib(2)
    for k in range(3):
        turned(k, 0)
    arrive(3)
    arrive_sib(3)
    along(3, 0)
    project(0)
    for s in range(3, np_ + 2):
        along(1, s)
        along(2, s - 1)
        own(s + 2)
        if s == np_:
            project_ahead()
        along(3, s - 2)
        if s < np_:
            project(s - 2)
        else:
            project_last(s - 2)
        if s == 4:
            masses()
        if s == 5:
            for k in range(3):
                turned(k, 1)
        if s == 6:
            turned(3, 0)
            turned(3, 1)
        relay(s - 3)
        if s == 4:
            lead(tlead, 0, tbuf[:, 0:PIECE])
        if s > 4:
            whole(s - 5)
        if s == 5:
            lead(plead, 1, pfin[:, 0:PIECE].astype(bf16))
    whole(np_ - 3)
    for k in (3, 1, 2):
        stat(k, 0).start()
    pair(0).wait_recv()
    kept = jnp.maximum(kept_mine + jnp.sum(pair_r[0, 0:1, 0:1]), 1.0)
    weight = maskf / kept / SLIDES
    relay(np_ - 1)
    whole(np_ - 2)
    whole(np_ - 1)
    for k in (3, 1, 2):
        stat(k, 1).start()

    for i in range(3):
        spots[i] = jnp.sum(jnp.transpose(acc[i]), axis=0, keepdims=True)
    def spot_copy(k, h):
        i = 2 * k + h
        dev = (nbr[k], sib) if h else chip[k]
        return remote(spots, spotr.at[h, k], sp_s.at[i], sp_r.at[i], dev)

    others = [(k, h) for k in (3, 1, 2, 0) for h in (1, 0) if k or h]
    for k, h in others:
        spot_copy(k, h).start()

    def slide_sums(n):
        for k in (1, 2, 3):
            stat(k, n).wait_recv()
        at = parts[n]
        pred_sq, dots, truth_sq = (
            (statg[i, :, at] + statr[1, i, :, at]) + (statr[2, i, :, at] + statr[3, i, :, at])
            for i in range(3)
        )
        slide_a = lax.rsqrt(pred_sq + eps_norm)
        slide_b = lax.rsqrt(truth_sq + eps_norm)
        w = weight[:, at.start : at.start + at.size]
        return (
            -w * slide_a * slide_b,
            w * dots * slide_a**3 * slide_b,
            w * (dots * slide_a * slide_b),
        )

    coefs = [slide_sums(0), None]

    def spot_coefs(k):
        if k:
            spot_copy(k, 0).wait_recv()
        spot_copy(k, 1).wait_recv()
        pp, dot, tt = (
            (spotr[0, k, i] if k else spots[i])
            + jnp.concatenate([spotr[1, k, i, :, rows : 2 * rows], spotr[1, k, i, :, 0:rows]], axis=1)
            for i in range(3)
        )
        a, b = lax.rsqrt(pp + eps_norm), lax.rsqrt(tt + eps_norm)
        return (
            column(-(a * b) / spots_all, 2 * rows),
            column(dot * a**3 * b / spots_all, 2 * rows),
            dot * a * b,
        )

    col_t, col_p, cos_spot = spot_coefs(0)

    def agcopy(i, g):
        src, dst, to = (
            (at_k(0), at_k(1), 1), (at_k(0, 1), at_k(1, 1), 1), (at_k(0, 1), at_k(2, 1), 2),
            (at_k(0), at_k(2), 2), (at_k(1), at_k(3), 2), (at_k(2, 1), at_k(3, 1), 1),
        )[i]
        return remote(half_of(dpa, src, g), half_of(dpa, dst, g), ag_s.at[i, g], ag_r.at[i, g], chip[to])

    def give(g):
        n = 0 if g < np_ - 2 else 1
        if n and coefs[1] is None:
            coefs[1] = slide_sums(1)
        c = g * PIECE - parts[n].start
        c_t, c_p = (v[:, c : c + PIECE] for v in coefs[n][0:2])
        at = piece(g)
        d = ((c_t + col_t) * tbuf[:, at].astype(f32) + (c_p + col_p) * pfin[:, at]).astype(bf16)
        lanes = pl.ds(g % 2 * PIECE, PIECE)
        dpa[g // 2, at_k(0), lanes] = d[0:rows]
        dpa[g // 2, at_k(0, 1), lanes] = d[rows : 2 * rows]
        for i in range(4):
            agcopy(i, g).start()

    def lead_grad():
        lead_wait(tlead, 0)
        lead_wait(plead, 1)
        c_t, c_p = (v[:, 0:PIECE] for v in coefs[0][0:2])
        for k in (0, 1, 2, 3):
            t, p = (col_t, col_p) if k == 0 else spot_coefs(k)[0:2]
            for h in range(2):
                r, m = at_k(k, h), slice(h * rows, (h + 1) * rows)
                d = (c_t + t[m]) * tlead[r, :].astype(f32) + (c_p + p[m]) * plead[r, :].astype(f32)
                dpa[0, r, 0:PIECE] = d.astype(bf16)

    def give_on(g):
        agcopy(0, g).wait_recv()
        agcopy(4, g).start()
        agcopy(2, g).wait_recv()
        agcopy(5, g).start()

    def dcopy(way, p, g):
        if way == 0:
            return remote(dsend.at[p, g], dright.at[p, g], dr_s.at[p, g], dr_r.at[p, g], beside[0])
        return remote(dsend.at[p, g], dleft.at[p, g], dl_s.at[p, g], dl_r.at[p, g], beside[1])

    def expr_grad_first():
        up = z // (nz // 2)

        @pl.loop(0, nz)
        def _(u):
            p = up * u + (1 - up) * (nz - 1 - u)
            v = jnp.dot(wt[seg(p), :], dpa[0, :, 0:PIECE], preferred_element_type=f32)
            grad[p, :, 0:PIECE] = v

            @pl.when((ends[0] | ends[1]) & (p != z))
            def _():
                dsend[p, 0] = v.astype(bf16)

            @pl.when(ends[0] & (p != z))
            def _():
                dcopy(0, p, 0).start()

            @pl.when(ends[1] & (p != z))
            def _():
                dcopy(1, p, 0).start()

    def expr_grad(g):
        for i in (1, 3, 4, 5):
            agcopy(i, g).wait_recv()
        lanes = slice(g % 2 * PIECE, (g % 2 + 1) * PIECE)
        v = jnp.dot(wt[...], dpa[g // 2, :, lanes], preferred_element_type=f32)
        for p in range(nz):
            grad[p, :, piece(g)] = v[p * cd : (p + 1) * cd]

        @pl.when(ends[0])
        def _():
            for p in range(1, nz):
                dsend[p, g] = v[p * cd : (p + 1) * cd].astype(bf16)

        @pl.when(ends[1])
        def _():
            for p in range(nz - 1):
                dsend[p, g] = v[p * cd : (p + 1) * cd].astype(bf16)

    def start_from_ends(u, g):
        if not 0 <= g < np_:
            return

        @pl.when(ends[0])
        def _():
            dcopy(0, nz - 1 - u, g).start()

        @pl.when(ends[1])
        def _():
            dcopy(1, u, g).start()

    def starts(*pieces):
        for u, g in pieces:
            start_from_ends(u, g)

    def chain(hops, u, g):
        if nz - 1 - u > hops:

            @pl.when(z == hops)
            def _():
                p = nz - 1 - u
                dcopy(0, p, g).wait_recv()
                dsend[p, g] = (grad[p, :, piece(g)] + dright[p, g].astype(f32)).astype(bf16)
                dcopy(0, p, g).start()

            @pl.when(nz - 1 - z == hops)
            def _():
                dcopy(1, u, g).wait_recv()
                dsend[u, g] = (grad[u, :, piece(g)] + dleft[u, g].astype(f32)).astype(bf16)
                dcopy(1, u, g).start()

    def finish(g):
        at = piece(g)
        ge_o[:, at] = grad[pl.ds(z, 1), :, at].reshape(cd, PIECE)

        @pl.when(has_left)
        def _():
            dcopy(0, z, g).wait_recv()
            ge_o[:, at] += dright[pl.ds(z, 1), g].reshape(cd, PIECE).astype(f32)

        @pl.when(has_right)
        def _():
            dcopy(1, z, g).wait_recv()
            ge_o[:, at] += dleft[pl.ds(z, 1), g].reshape(cd, PIECE).astype(f32)

    def tile_copy(k):
        return remote(tile_s, tile_r.at[k], tl_s.at[k], tl_r.at[k], chip[k])

    def zcopy(buf, src, r, ss, rs):
        to = (z + r) % nz
        return remote(buf.at[src], buf.at[z], ss.at[r], rs.at[r], (to * GROUP + q, j))

    def zcopy_wait(buf, r, ss, rs):
        o = (z + nz - r) % nz
        remote(buf.at[o], buf.at[o], ss.at[r], rs.at[r], here).wait_recv()

    def chip_masses():
        for k in (1, 2, 3):
            mass_copy(k).wait_recv()
        return (massp[0, 0:2] + massr[1, 0:2]) + (massr[2, 0:2] + massr[3, 0:2])

    def own_dens():
        d = dens[...].astype(f32)
        return jnp.where(j == 0, d, jnp.concatenate([d[1:2], d[0:1]], axis=0))

    def tile_start():
        mass, d = chip_masses(), own_dens()
        gene = fold(coefs[0][2]) + fold(coefs[1][2])
        cos = fold(cos_spot)
        tile_s[0:1] = -2.0 / GROUP * gene - cos / spots_all
        tile_s[1:2] = d[0:1] + d[1:2]
        f = jax.nn.sigmoid(filt[...])
        tile_s[2:3] = f[0:1] + f[1:2]
        tile_s[3:4] = mass[0:1] + mass[1:2]
        kl = d * (jnp.log(d) - jnp.log(mass))
        tile_s[4:5] = kl[0:1] + kl[1:2]
        tile_s[5:8] = jnp.zeros((3, 128), f32)
        for k in (3, 1, 2):
            tile_copy(k).start()
        return mass, d

    def tile_along():
        for k in (1, 2, 3):
            tile_copy(k).wait_recv()
        tz[pl.ds(z, 1)] = ((tile_s[...] + tile_r[1]) + (tile_r[2] + tile_r[3]))[None]
        for r in range(1, nz):
            zcopy(tz, z, r, tz_s, tz_r).start()

    def gm_copy(k):
        return remote(gms, gmr.at[k], gm_s.at[k], gm_r.at[k], chip[k])

    def totals(mass, d):
        for r in range(1, nz):
            zcopy_wait(tz, r, tz_s, tz_r)
        t = tz[0]
        for p in range(1, nz):
            t = t + tz[p]
        loss_part, count, gate, mass_total, kl = (jnp.sum(t[i : i + 1]) for i in range(5))
        logs = jnp.log(jnp.where(lax.broadcasted_iota(jnp.int32, (1, 128), 1) == 0, count, mass_total))
        log_count, log_mass = jnp.sum(logs[:, 0:1]), jnp.sum(logs[:, 1:2])
        excess = gate / count - 1.0
        gms[...] = jnp.zeros_like(gms)
        gms[0:2] = (1.0 / mass_total - d / count / mass).astype(bf16).astype(f32)
        for k in (3, 1, 2):
            gm_copy(k).start()
        pair_s[1] = jnp.full((8, 2 * rows), loss_part + kl / count - log_count + log_mass + excess * excess)
        pair(1).start()
        return 2.0 * excess / count

    def mass_columns():
        gmcol[at_k(0), :] = column(gms[0:1], rows)
        for k in (1, 2, 3):
            gm_copy(k).wait_recv()
            gmcol[at_k(k), :] = column(gmr[k, 0:1], rows)

    def dwcopy(p):
        return remote(dws.at[p], dwr.at[p], dw_s.at[p], dw_r.at[p], here)

    def weight_grad(p):
        cs = slice(p * cd, (p + 1) * cd)

        def rows_of(h):
            d = dot_nt(dpa[0, h * grp : (h + 1) * grp, :], ebuf[0, cs, :])
            for c in range(1, np_ // 2):
                d = d + dot_nt(dpa[c, h * grp : (h + 1) * grp, :], ebuf[c, cs, :])
            return d

        dws[p] = rows_of(1)
        dwcopy(p).start()
        dwo[p] = rows_of(0)

    def gpcopy(k, p):
        return remote(gps.at[p, at_k(k)], gpr.at[k, p], gp_s.at[k, p], gp_r.at[k, p], chip[k])

    def give_back(p):
        dwcopy(p).wait_recv()
        cs = pl.ds(p * cd, cd)
        total = jnp.zeros((1, cd), f32)
        for k in (3, 1, 2, 0):
            r = at_k(k)
            gm = gmcol[r, :]
            gw = dwo[p, r] + dwr[p, r] + jnp.concatenate([gm] * (cd // 128), axis=1)
            total = total + jnp.sum(gw * wraw[r, cs].astype(f32), axis=0, keepdims=True)
            gps[p, r] = (gcol[0:1, cs] * gw).astype(bf16)
            if k:
                gpcopy(k, p).start()
        fsend[p] = total

    def filter_along():
        frecv[pl.ds(z, 1)] = fsend[pl.ds(z, 1)]
        for r in range(1, nz):
            to = (z + r) % nz
            remote(fsend.at[to], frecv.at[z], fz_s.at[r], fz_r.at[r], (to * GROUP + q, j)).start()

    def take(k, p, start=False):
        if k:
            gpcopy(k, p).wait_recv()
            v = gpr[k, p]
        else:
            v = gps[p, at_k(0)]
        at = pl.ds(pl.multiple_of((p * GROUP + nq[k]) * cd, cd), cd)
        gpb[:, at] = v
        s = fold(probs[:, at] * v.astype(f32))
        if start:
            rowsum[...] = s
        else:
            rowsum[...] += s

    def sent_first():
        for k in (1, 2, 3):
            wcopy(k).wait_send()
            mass_copy(k).wait_send()
            for n in (0, 1):
                stat(k, n).wait_send()
        for k in range(GROUP):
            wsib(k).wait_send()
        pair(0).wait_send()
        for k, h in others:
            spot_copy(k, h).wait_send()
        for k in (1, 2, 3):
            for h in range(2):
                lead_copy(tlead, 0, k, h).wait_send()
                lead_copy(plead, 1, k, h).wait_send()

        @pl.loop(0, np_)
        def _(g):
            for c in (pxcopy, pycopy):
                c(g, 0).wait_send()
                c(g, 1).wait_send()
            p2xcopy(g).wait_send()
            p2ycopy(g).wait_send()

    def sent_along():
        @pl.loop(0, nz)
        def _(p):
            @pl.when(has_right & (p <= z))
            def _():
                zsmall(0, p).wait_send()
                for g in range(np_):
                    zsend(0, p, g).wait_send()

            @pl.when(has_left & (p >= z))
            def _():
                zsmall(1, p).wait_send()
                for g in range(np_):
                    zsend(1, p, g).wait_send()

    def sent_back():
        for g in range(1, np_):
            for i in range(6):
                agcopy(i, g).wait_send()

    def sent_last():
        for k in (1, 2, 3):
            tile_copy(k).wait_send()
            gm_copy(k).wait_send()
            for p in range(nz):
                gpcopy(k, p).wait_send()
        for r in range(1, nz):
            zcopy(tz, z, r, tz_s, tz_r).wait_send()
            zcopy(fsend, z, r, fz_s, fz_r).wait_send()
        for p in range(nz):
            dwcopy(p).wait_send()
        for i in (1, 2):
            pair(i).wait_send()

    def sent_sums():
        @pl.loop(0, nz)
        def _(p):
            @pl.when(has_right & (p > z))
            def _():
                for g in range(np_):
                    dcopy(0, p, g).wait_send()

            @pl.when(has_left & (p < z))
            def _():
                for g in range(np_):
                    dcopy(1, p, g).wait_send()

    give(1)
    give(2)
    coefs[1] = slide_sums(1)
    mass, d = tile_start()
    lead_grad()
    expr_grad_first()
    give_on(1)
    give(3)
    give_on(2)
    give(4)
    tile_along()
    expr_grad(1)
    starts((0, 1), (1, 1), (2, 1))
    give_on(3)
    give(5)
    chain(1, 0, 0)
    give_on(4)
    expr_grad(2)
    starts((0, 2), (1, 2))
    chain(1, 1, 0)
    give(6)
    give_on(5)
    expr_grad(3)
    starts((0, 3))
    chain(1, 0, 1)
    chain(2, 0, 0)
    give(7)
    give_on(6)
    chain(1, 1, 1)
    expr_grad(4)
    starts((0, 4), (1, 3))
    push = totals(mass, d)
    give_on(7)
    chain(2, 0, 1)
    chain(1, 0, 2)
    expr_grad(5)
    starts((0, 5), (1, 4))
    finish(0)
    chain(1, 1, 2)
    expr_grad(6)
    starts((0, 6))
    chain(1, 0, 3)
    finish(1)
    mass_columns()
    chain(2, 0, 2)
    expr_grad(7)
    starts((0, 7), (1, 5), (2, 2), (1, 6), (2, 3), (1, 7))
    chain(1, 0, 4)
    chain(1, 1, 3)
    weight_grad(0)
    chain(2, 0, 3)
    chain(1, 0, 5)
    weight_grad(1)
    chain(2, 0, 4)
    give_back(0)
    chain(1, 1, 4)
    weight_grad(2)
    chain(1, 0, 6)
    give_back(1)
    chain(2, 0, 5)
    weight_grad(3)
    chain(1, 0, 7)
    give_back(2)
    chain(1, 1, 5)
    give_back(3)
    filter_along()
    starts((2, 4), (2, 5), (2, 6), (2, 7))
    chain(2, 0, 6)
    finish(2)
    take(0, 0, True)
    for p in range(1, nz):
        take(0, p)
    chain(2, 0, 7)
    chain(1, 1, 6)
    for k in (1, 2, 3):
        take(k, 0)
    finish(3)
    sent_first()
    chain(1, 1, 7)
    for k in (1, 2, 3):
        take(k, 1)
    sent_along()
    finish(4)
    for k in (1, 2, 3):
        take(k, 2)
    sent_back()
    finish(5)
    for r in range(1, nz):
        zcopy_wait(frecv, r, fz_s, fz_r)
    ftotal = frecv[0]
    for p in range(1, nz):
        ftotal = ftotal + frecv[p]
    pair_s[2, 0:1, 0:cd] = ftotal
    pair(2).start()
    for k in (1, 2, 3):
        take(k, 3)
    tot_o[...] = jnp.broadcast_to(jnp.sum(rowsum[...], axis=1, keepdims=True), (rows, 128))
    sent_last()
    finish(6)
    pair(1).wait_recv()
    pair(2).wait_recv()
    my_gate = jax.nn.sigmoid(filt[...])
    fsum = ftotal + pair_r[2, 0:1, 0:cd] + push
    for h in range(cd // 128):
        g = my_gate[h : h + 1, :]
        last_o[h : h + 1, :] = fsum[:, h * 128 : (h + 1) * 128] * g * (1.0 - g)
    last_o[cd // 128 : cd // 128 + 1, :] = 0.5 * (pair_s[1, 0:1, 0:128] + pair_r[1, 0:1, 0:128])
    finish(7)
    sent_sums()


def finish_kernel(probs, gp, tot, ge, last, gl_o, ge_o, loss_o, gf_o, gl, loss, out_s):
    f32 = jnp.float32
    parts = 4
    cc = probs.shape[1] // parts
    copies = []

    def send(src, dst):
        copies.append(pltpu.make_async_copy(src, dst, out_s.at[len(copies)]))
        copies[-1].start()

    send(ge, ge_o)
    n = gf_o.shape[0]
    loss[...] = last[n : n + 1, 0:1]
    send(last.at[pl.ds(0, n)], gf_o)
    send(loss, loss_o)
    for i in range(parts):
        for c in range(i * cc, (i + 1) * cc, 128):
            at = slice(c, c + 128)
            gl[:, at] = probs[:, at] * (gp[:, at].astype(f32) - tot[...])
        at = pl.ds(i * cc, cc)
        send(gl.at[:, at], gl_o.at[:, at])
    for c in copies:
        c.wait()


def grouped(logits, filt, expr, target, gene_mask, density):
    f32, bf16, i32 = jnp.float32, jnp.bfloat16, jnp.int32
    nspot = lax.axis_size("spot")
    rows, cells = logits.shape
    cd, genes = expr.shape
    nz = nspot // GROUP
    n = genes // PIECE
    grp = GROUP * rows
    mine = cells // GROUP
    spots = 2 * rows

    def vmem(*shape, dtype=f32):
        return pltpu.VMEM(shape, dtype)

    def dma(*shape):
        return pltpu.SemaphoreType.DMA(shape)

    def low(*shape):
        return pltpu.VMEM(shape, bf16)

    buffers = [
        low(rows, cells), vmem(cd // 128, 128), vmem(*gene_mask.shape, dtype=i32), vmem(spots // 128, 128, dtype=i32),
        low(GROUP, rows, mine), low(2 * grp, mine), low(2 * grp, mine), low(mine, 2 * grp),
        low(n // 2, mine, 2 * PIECE), low(spots, genes), vmem(8, mine), vmem(nz, 8, 128), vmem(spots, genes),
        vmem(2 * grp, 2 * PIECE),
        low(n, 2 * rows, PIECE), low(n, 2 * rows, PIECE), low(n, 2 * rows, PIECE), low(n, 2 * rows, PIECE),
        low(n, rows, PIECE), low(n, rows, PIECE), low(n, rows, PIECE), low(n, rows, PIECE),
        vmem(n, rows, PIECE), vmem(n, rows, PIECE), vmem(GROUP, 8, 128), vmem(GROUP, 8, 128),
        vmem(3, 1, genes), vmem(GROUP, 3, 1, genes), vmem(3, spots, PIECE), vmem(3, 1, spots), vmem(2, GROUP, 3, 1, spots), low(2 * grp, PIECE), low(2 * grp, PIECE),
        low(n // 2, 2 * grp, 2 * PIECE), vmem(nz, cd, genes),
        low(nz, n, cd, PIECE), low(nz, n, cd, PIECE), low(nz, n, cd, PIECE),
        vmem(nz, grp, cd), vmem(nz, grp, cd), vmem(nz, grp, cd), low(nz, grp, cd), low(GROUP, nz, rows, cd),
        vmem(rows, 128), vmem(8, 128), vmem(GROUP, 8, 128), vmem(nz, 8, 128), vmem(8, 128), vmem(GROUP, 8, 128),
        vmem(grp, 128), vmem(nz, 1, cd), vmem(nz, 1, cd), vmem(3, 8, spots), vmem(3, 8, spots),
    ]
    sems = [
        pltpu.SemaphoreType.REGULAR, dma(4 + n // 2 + 2), dma(2, nz), dma(nz), dma(2, nz, n), dma(nz, n),
        dma(4), dma(4), dma(4), dma(4), dma(3), dma(3),
        dma(2, n), dma(2, n), dma(2, n), dma(2, n), dma(n), dma(n), dma(n), dma(n),
        dma(4), dma(4), dma(8), dma(8), dma(2, 4, 2), dma(2, 4, 2), dma(8), dma(8), dma(6, n), dma(6, n),
        dma(nz, n), dma(nz, n), dma(nz, n), dma(nz, n), dma(nz), dma(nz), dma(4, nz), dma(4, nz),
        dma(4), dma(4), dma(nz), dma(nz), dma(4), dma(4), dma(nz), dma(nz),
    ]
    v, a = pl.BlockSpec(memory_space=pltpu.VMEM), pl.BlockSpec(memory_space=pl.ANY)
    shape = jax.ShapeDtypeStruct
    fparts = (cd // 128, 128)
    given = (logits, filt.reshape(-1, 128), expr, target, gene_mask, density.reshape(-1, 128))
    probs, gp, tot, last, grad_expr = pl.pallas_call(
        functools.partial(group_kernel, nspot),
        out_shape=[vmem(rows, cells), low(rows, cells), vmem(rows, 128), vmem(8, 128), vmem(cd, genes)],
        in_specs=[a] * 6,
        out_specs=[v] * 5,
        scratch_shapes=buffers + sems,
        compiler_params=pltpu.CompilerParams(
            collective_id=0, has_side_effects=True, vmem_limit_bytes=VMEM_BYTES
        ),
        name="group_step",
    )(*(pltpu.with_memory_space_constraint(g, pltpu.HBM) for g in given))
    grad_logits, grad_expr, loss, grad_filt = pl.pallas_call(
        finish_kernel,
        out_shape=[shape((rows, cells), f32), shape((cd, genes), f32), shape((1, 1), f32), shape(fparts, f32)],
        in_specs=[v] * 5,
        out_specs=[a] * 4,
        scratch_shapes=[vmem(rows, cells), vmem(1, 1), dma(7)],
        compiler_params=pltpu.CompilerParams(vmem_limit_bytes=LAST_BYTES),
        name="finish_step",
    )(probs, gp, tot, grad_expr, last)
    return (loss.reshape(()), grad_logits, grad_filt.reshape(-1), grad_expr)


def fits(logits, filt, expr):
    nspot = lax.axis_size("spot")
    rows, cells = logits.shape
    sizes = (rows, cells, filt.shape[0], expr.shape[1])
    return (
        nspot == GROUP * SLIDES and lax.axis_size("gene") == 2 and sizes == (128, 4096, 256, 1024)
    )


def per_device(logits, filt, expr, target, gene_mask, density):
    plan = grouped if fits(logits, filt, expr) else streamed
    return plan(logits, filt, expr, target, gene_mask, density)


def solution(mesh):
    in_specs = (
        P(("spot", "gene"), None),
        P("spot"),
        P("spot", "gene"),
        P("spot", "gene"),
        P(None, "gene"),
        P("spot"),
    )
    out_specs = (P(), P(("spot", "gene"), None), P("spot"), P("spot", "gene"))
    return jax.shard_map(
        per_device, mesh=mesh, in_specs=in_specs, out_specs=out_specs, check_vma=False
    )
```

```python
import functools

import jax
import jax.numpy as jnp
from jax import lax
from jax.experimental import pallas as pl
from jax.experimental.pallas import tpu as pltpu
from jax.sharding import PartitionSpec as P

SPOTS = 4096
SLIDES = 4


eps_norm = 1e-06


def slide_moments(onehot, pred, truth):
    hi = lax.Precision.HIGHEST
    return jnp.stack(
        [
            jnp.dot(onehot.T, pred * truth, precision=hi),
            jnp.dot(onehot.T, pred * pred, precision=hi),
            jnp.dot(onehot.T, truth * truth, precision=hi),
        ]
    )


def spot_moments(pred, truth):
    return jnp.stack(
        [
            jnp.sum(pred * truth, axis=1),
            jnp.sum(pred * pred, axis=1),
            jnp.sum(truth * truth, axis=1),
        ]
    )


def cosine_parts(slide_stats):
    dots = slide_stats[0]
    slide_a = lax.rsqrt(slide_stats[1] + eps_norm)
    slide_b = lax.rsqrt(slide_stats[2] + eps_norm)
    return (dots, slide_a, slide_b, dots * slide_a * slide_b)


def pred_gradient(onehot, weight_slide, dots, slide_a, slide_b, spot_stats, pred, truth):
    hi = lax.Precision.HIGHEST
    spot_a = lax.rsqrt(spot_stats[1] + eps_norm)
    spot_b = lax.rsqrt(spot_stats[2] + eps_norm)
    coef_truth = -weight_slide * slide_a * slide_b
    coef_pred = weight_slide * dots * slide_a**3 * slide_b
    grad_pred = (
        jnp.dot(onehot, coef_truth, precision=hi) * truth
        + jnp.dot(onehot, coef_pred, precision=hi) * pred
    )
    grad_pred = (
        grad_pred
        + (
            -(spot_a * spot_b)[:, None] * truth
            + (spot_stats[0] * spot_a**3 * spot_b)[:, None] * pred
        )
        / SPOTS
    )
    return (grad_pred, spot_stats[0] * spot_a * spot_b)


def streamed(logits, filt, expr, target, gene_mask, density):
    f32 = jnp.float32
    bf16 = jnp.bfloat16
    nspot = lax.axis_size("spot")
    ngene = lax.axis_size("gene")
    spot_dev = logits.shape[0]
    cells = logits.shape[1]
    cell_dev = filt.shape[0]
    owned = target.shape[0]
    half = target.shape[1]
    spots_all = owned * nspot
    slide_len = SPOTS // SLIDES
    scores = logits.astype(f32)
    shifted = jnp.exp(scores - jnp.max(scores, axis=1, keepdims=True))
    probs = shifted / jnp.sum(shifted, axis=1, keepdims=True)
    moved = lax.all_to_all(probs.astype(bf16), "spot", split_axis=1, concat_axis=0, tiled=True)
    paired = lax.all_gather(moved.reshape(nspot, 1, spot_dev, cell_dev), "gene", axis=1, tiled=True)
    paired = paired.reshape(spots_all, cell_dev)
    gate = jax.nn.sigmoid(filt)
    weighted = (paired.astype(f32) * gate[None, :]).astype(bf16)
    partial_pred = jnp.dot(weighted, expr, preferred_element_type=f32)
    partial_mass = jnp.sum(weighted.astype(f32), axis=1)
    gate_part = jnp.sum(gate)
    maskf = gene_mask.astype(f32)
    mask_part = jnp.sum(maskf, axis=1)
    pred_three, mass_two = (
        lax.psum_scatter(
            partial_pred.reshape(nspot, owned, half), "spot", scatter_dimension=0, tiled=True
        ),
        lax.psum_scatter(
            partial_mass.reshape(nspot, owned), "spot", scatter_dimension=0, tiled=True
        ),
    )
    pred = pred_three.reshape(owned, half)
    mass = mass_two.reshape(owned)
    truth = target.astype(f32)
    dens = density.astype(f32)
    spot_ids = lax.axis_index("spot") * owned + jnp.arange(owned, dtype=jnp.int32)
    onehot = (
        spot_ids[:, None] // slide_len == jnp.arange(SLIDES, dtype=jnp.int32)[None, :]
    ).astype(f32)
    slide_stats, mass_total, gate_total, count_total = lax.psum(
        (slide_moments(onehot, pred, truth), jnp.sum(mass), gate_part, jnp.sum(dens)), "spot"
    )
    dots, slide_a, slide_b, cos_gene = cosine_parts(slide_stats)
    spot_stats, kept_genes, gene_numer = lax.psum(
        (spot_moments(pred, truth), mask_part, jnp.sum(maskf * cos_gene, axis=1)), "gene"
    )
    genes_kept = jnp.maximum(kept_genes, 1.0)
    weight_slide = maskf / genes_kept[:, None] / SLIDES
    grad_pred, cos_spot = pred_gradient(
        onehot, weight_slide, dots, slide_a, slide_b, spot_stats, pred, truth
    )
    share = dens / count_total
    kl_local = jnp.sum(share * (jnp.log(share) - jnp.log(mass) + jnp.log(mass_total)))
    cos_total, kl_total = lax.psum((jnp.sum(cos_spot), kl_local), "spot")
    grad_mass = 1.0 / mass_total - share / mass
    spread_three, spread_two = (
        lax.all_gather(grad_pred.astype(bf16).reshape(1, owned, half), "spot", axis=0, tiled=True),
        lax.all_gather(grad_mass.astype(bf16).reshape(1, owned), "spot", axis=0, tiled=True),
    )
    spread_pred = spread_three.reshape(spots_all, half)
    spread_mass = spread_two.reshape(spots_all)
    gene_term = jnp.mean(gene_numer / genes_kept)
    excess = gate_total / count_total - 1.0
    loss = -gene_term - cos_total / SPOTS + kl_total + excess * excess
    grad_expr = lax.dot_general(
        weighted, spread_pred, (((0,), (0,)), ((), ())), preferred_element_type=f32
    )
    first_half = (lax.axis_index("gene") == 0).astype(f32)
    grad_weighted = lax.dot_general(
        spread_pred, expr, (((1,), (1,)), ((), ())), preferred_element_type=f32
    )
    grad_weighted = grad_weighted + first_half * spread_mass.astype(f32)[:, None]
    filter_part = jnp.sum(grad_weighted * paired.astype(f32), axis=0)
    filter_total = lax.psum(filter_part, "gene")
    grad_filt = (filter_total + 2.0 * excess / count_total) * gate * (1.0 - gate)
    terms = (grad_weighted * gate[None, :]).reshape(nspot, ngene, spot_dev, cell_dev)
    moved_back = lax.all_to_all(terms, "spot", split_axis=0, concat_axis=3, tiled=True)
    folded = lax.psum_scatter(moved_back, "gene", scatter_dimension=1, tiled=True)
    rounded = lax.optimization_barrier(folded.reshape(spot_dev, cells).astype(bf16))
    grad_probs = rounded.astype(f32)
    grad_logits = probs * (grad_probs - jnp.sum(probs * grad_probs, axis=1, keepdims=True))
    return (loss, grad_logits, grad_filt, grad_expr)


GROUP = 4
PIECE = 128
MESH = pl.DeviceIdType.MESH
VMEM_BYTES = 44 << 20
LAST_BYTES = 16 << 20


def remote(src, dst, send, recv, dev):
    return pltpu.make_async_remote_copy(
        src_ref=src, dst_ref=dst, send_sem=send, recv_sem=recv, device_id=dev, device_id_type=MESH
    )


def dot_nt(a, b):
    return lax.dot_general(a, b, (((1,), (1,)), ((), ())), preferred_element_type=jnp.float32)


def column(row, length):
    return jnp.transpose(jnp.broadcast_to(row, (128, length)))


def fold(values):
    total = values[:, 0:128]
    for i in range(1, values.shape[1] // 128):
        total = total + values[:, i * 128 : (i + 1) * 128]
    return total


def group_kernel(
    nspot, logits_h, filt_h, expr, target, mask_h, dens_h,
    probs, gpb, tot_o, last_o, ge_o,
    logits, filt, mask, dens, rawq, wraw, wg, wt, ebuf, tbuf, gcol, small, pfin, ahead,
    psx, prx, psy, pry, ps2x, pr2x, ps2y, pr2y, hx, hy, massp, massr, statg, statr, acc, spots, spotr, tlead, plead, tturn, pturn, dturn, coefrow,
    dpa, grad, dsend, dright, dleft, dwo, dws, dwr, gps, gpr, rowsum, tile_s, tile_r, tz, gms, gmr, gmcol,
    fsend, frecv, pair_s, pair_r,
    hello, lc, zs_s, zs_r, ez_s, ez_r, w_s, w_r, wd_s, wd_r, pr_s, pr_r,
    px_s, px_r, py_s, py_r, p2x_s, p2x_r, p2y_s, p2y_r, ms_s, ms_r, st_s, st_r, ld_s, ld_r, sp_s, sp_r, ag_s, ag_r,
    dr_s, dr_r, dl_s, dl_r, dw_s, dw_r, gp_s, gp_r, tl_s, tl_r, tz_s, tz_r, gm_s, gm_r, fz_s, fz_r,
):
    f32, bf16 = jnp.float32, jnp.bfloat16
    rows, cells = probs.shape
    cd, genes = expr.shape
    nz = nspot // GROUP
    np_ = genes // PIECE
    grp = GROUP * rows
    mine = cells // GROUP
    spots_all = nspot * 2 * rows
    me, j = lax.axis_index("spot"), lax.axis_index("gene")
    sib = 1 - j
    z, q = me // GROUP, me % GROUP
    x, y = q % 2, q // 2
    nbr = [me, me + 1 - 2 * x, me + 2 - 4 * y, me + 3 - 2 * x - 4 * y]
    nq = [n % GROUP for n in nbr]
    here = (me, sib)
    has_right, has_left = z < nz - 1, z > 0
    ends = (z == 0, z == nz - 1)
    chip = [(n, j) for n in nbr]
    beside = ((me + GROUP, j), (me - GROUP, j))

    def at_k(k, h=0):
        return pl.ds(h * grp + k * rows, rows)

    def piece(g):
        return pl.ds(g * PIECE, PIECE)

    def half_of(buf, r, g):
        return buf.at[g // 2, r, pl.ds(g % 2 * PIECE, PIECE)]

    def seg(p):
        return pl.ds(pl.multiple_of(p * cd, cd), cd)

    barrier = pltpu.get_barrier_semaphore()

    def greet(dev):
        pl.semaphore_signal(barrier, inc=1, device_id=dev, device_id_type=MESH)

    greet(chip[1])
    greet(chip[2])

    @pl.when(has_right)
    def _():
        greet(beside[0])

    @pl.when(has_left)
    def _():
        greet(beside[1])

    greet(here)
    loads = [pltpu.make_async_copy(logits_h, logits, lc.at[0])]
    loads += [
        pltpu.make_async_copy(s, d, lc.at[1 + i])
        for i, (s, d) in enumerate(((filt_h, filt), (mask_h, mask), (dens_h, dens)))
    ]
    loads += [
        pltpu.make_async_copy(
            expr.at[:, pl.ds(i * 2 * PIECE, 2 * PIECE)], ebuf.at[i, seg(z), :], lc.at[4 + i]
        )
        for i in range(np_ // 2)
    ]
    loads += [
        pltpu.make_async_copy(
            target.at[pl.ds(pl.multiple_of(c * rows, rows), rows)],
            tbuf.at[pl.ds(i * rows, rows)],
            lc.at[4 + np_ // 2 + i],
        )
        for i, c in enumerate((j, sib))
    ]
    for c in loads:
        c.start()
    for c in loads[1 : 4 + np_ // 2]:
        c.wait()
    small[pl.ds(z, 1), 0 : cd // 128, :] = filt[...][None]
    pl.semaphore_wait(barrier, 3 + has_right.astype(jnp.int32) + has_left.astype(jnp.int32))

    def zsmall(way, p):
        return remote(small.at[p], small.at[p], zs_s.at[way, p], zs_r.at[p], beside[way])

    def zsend(way, p, g):
        u = half_of(ebuf, seg(p), g)
        return remote(u, u, ez_s.at[way, p, g], ez_r.at[p, g], beside[way])

    def both(make):
        @pl.when(has_right)
        def _():
            make(0).start()

        @pl.when(has_left)
        def _():
            make(1).start()

    def hop(s, make):
        @pl.when(z >= s)
        def _():
            make(0, z - s).wait_recv()

            @pl.when(has_right)
            def _():
                make(0, z - s).start()

        @pl.when(z + s <= nz - 1)
        def _():
            make(1, z + s).wait_recv()

            @pl.when(has_left)
            def _():
                make(1, z + s).start()

    def own(g):
        if g < np_:
            both(lambda way: zsend(way, z, g))

    def passes(s, g):
        if not 0 <= g < np_:
            return

        @pl.when((z >= s) & has_right)
        def _():
            zsend(0, z - s, g).wait_recv()
            zsend(0, z - s, g).start()

        @pl.when((z + s <= nz - 1) & has_left)
        def _():
            zsend(1, z + s, g).wait_recv()
            zsend(1, z + s, g).start()

    def ends_here(s, g):
        if not 0 <= g < np_:
            return

        @pl.when((z >= s) & ends[1])
        def _():
            zsend(0, z - s, g).wait_recv()

        @pl.when((z + s <= nz - 1) & ends[0])
        def _():
            zsend(1, z + s, g).wait_recv()

    both(lambda way: zsmall(way, z))
    for g in range(4):
        own(g)

    loads[0].wait()

    step = 32

    @pl.loop(0, rows // step)
    def _(i):
        at = pl.ds(pl.multiple_of(i * step, step), step)
        s = logits[at, :].astype(f32)
        e = jnp.exp(s - jnp.max(s, axis=1, keepdims=True))
        p = e * (1.0 / jnp.sum(e, axis=1, keepdims=True))
        probs[at, :] = p
        for o in range(nspot):
            c = o // GROUP * cd
            rawq[o % GROUP, at, c : c + cd] = p[:, o * cd : (o + 1) * cd].astype(bf16)

    for c in loads[4 + np_ // 2 :]:
        c.wait()
    maskf = mask[pl.ds(z, 1), :].astype(f32)
    kept_mine = jnp.sum(maskf)
    pair_s[0] = jnp.full((8, 2 * rows), kept_mine)

    def wcopy(k):
        return remote(rawq.at[nq[k]], wraw.at[at_k(k)], w_s.at[k], w_r.at[k], chip[k])

    def wsib(k):
        return remote(wraw.at[at_k(k)], wraw.at[at_k(k, 1)], wd_s.at[k], wd_r.at[k], here)

    def pair(i):
        return remote(pair_s.at[i], pair_r.at[i], pr_s.at[i], pr_r.at[i], here)

    def lead_copy(buf, i, k, h):
        r = at_k(0, h)
        return remote(buf.at[r], buf.at[at_k(k, h)], ld_s.at[i, k, h], ld_r.at[i, k, h], chip[k])

    def lead(buf, i, values):
        for h in range(2):
            buf[at_k(0, h), :] = values[h * rows : (h + 1) * rows]
        for k in (3, 1, 2):
            for h in range(2):
                lead_copy(buf, i, k, h).start()

    def lead_turned(buf, i, out):
        lead_wait(buf, i)
        for c in range(0, 2 * grp, rows):
            out[:, c : c + rows] = jnp.transpose(buf[c : c + rows, :].astype(f32))

    def lead_wait(buf, i):
        for k in (1, 2, 3):
            for h in range(2):
                lead_copy(buf, i, k, h).wait_recv()

    wcopy(1).start()
    wcopy(2).start()
    pl.semaphore_signal(hello, inc=1, device_id=chip[1], device_id_type=MESH)
    wraw[at_k(0), :] = rawq[pl.ds(q, 1)].reshape(rows, mine)
    wsib(0).start()
    pair(0).start()
    pl.semaphore_wait(hello, 1)
    wcopy(3).start()

    def gated(k, h):
        r = at_k(k, h)
        for c in range(0, mine, 512):
            at = pl.ds(c, 512)
            wg[r, at] = (gcol[0:1, at] * wraw[r, at].astype(f32)).astype(bf16)

    def turned(k, h):
        r = at_k(k, h)
        for c in range(0, mine, 512):
            at = pl.ds(c, 512)
            wt[at, r] = jnp.transpose(wg[r, at].astype(f32)).astype(bf16)

    def arrive(k):
        wcopy(k).wait_recv()
        wsib(k).start()
        gated(k, 0)

    def arrive_sib(k):
        wsib(k).wait_recv()
        gated(k, 1)

    first, second = pl.ds(0, rows), pl.ds(rows, rows)

    def pxcopy(g, n):
        h = (first, second)[n]
        return remote(psx.at[g, h], prx.at[g, h], px_s.at[n, g], px_r.at[n, g], chip[1])

    def pycopy(g, n):
        h = (first, second)[n]
        return remote(psy.at[g, h], pry.at[g, h], py_s.at[n, g], py_r.at[n, g], chip[2])

    def p2xcopy(g):
        return remote(ps2x.at[g], pr2x.at[g], p2x_s.at[g], p2x_r.at[g], chip[1])

    def p2ycopy(g):
        return remote(ps2y.at[g], pr2y.at[g], p2y_s.at[g], p2y_r.at[g], chip[2])

    def piece_of(g, at):
        return ebuf[g // 2, at, g % 2 * PIECE : (g % 2 + 1) * PIECE]

    def project(g):
        share(g, jnp.dot(wg[...], piece_of(g, pl.ds(0, mine)), preferred_element_type=f32))

    far = (1 - z // (nz // 2)) * (nz - 1)
    near = pl.ds(pl.multiple_of(z // (nz // 2) * cd, cd), mine - cd)

    def project_ahead():
        ahead[...] = jnp.dot(wg[:, near], ebuf[np_ // 2 - 1, near, :], preferred_element_type=f32)

    def project_last(g):
        v = jnp.dot(wg[:, seg(far)], piece_of(g, seg(far)), preferred_element_type=f32)
        share(g, ahead[:, g % 2 * PIECE : (g % 2 + 1) * PIECE] + v)

    def share(g, v):
        def part(k, h):
            s = h * grp + k * rows
            return v[s : s + rows]

        psx[g, second] = part(3, 0).astype(bf16)
        pxcopy(g, 1).start()
        psy[g, second] = part(3, 1).astype(bf16)
        pycopy(g, 1).start()
        psx[g, first] = part(1, 0).astype(bf16)
        pxcopy(g, 0).start()
        psy[g, first] = part(2, 1).astype(bf16)
        pycopy(g, 0).start()
        hx[g] = part(2, 0)
        hy[g] = part(1, 1)
        pfin[first, piece(g)] = part(0, 0)
        pfin[second, piece(g)] = part(0, 1)

    def relay(g):
        pxcopy(g, 1).wait_recv()
        ps2y[g] = (hx[g] + prx[g, second].astype(f32)).astype(bf16)
        p2ycopy(g).start()
        pycopy(g, 1).wait_recv()
        ps2x[g] = (hy[g] + pry[g, second].astype(f32)).astype(bf16)
        p2xcopy(g).start()

    def whole(g):
        at = piece(g)
        pxcopy(g, 0).wait_recv()
        pycopy(g, 0).wait_recv()
        p2ycopy(g).wait_recv()
        p2xcopy(g).wait_recv()
        pfin[first, at] += prx[g, first].astype(f32) + pr2y[g].astype(f32)
        pfin[second, at] += pry[g, first].astype(f32) + pr2x[g].astype(f32)
        p = pfin[:, at]
        t = tbuf[:, at].astype(f32)
        for i, v in enumerate((p * p, p * t, t * t)):
            statg[i, :, at] = jnp.sum(v, axis=0, keepdims=True)
            acc[i] += v

    parts = (pl.ds(0, (np_ - 2) * PIECE), pl.ds((np_ - 2) * PIECE, 2 * PIECE))

    def stat(k, n):
        i = 2 * k + n
        return remote(
            statg.at[:, :, parts[n]], statr.at[k, :, :, parts[n]], st_s.at[i], st_r.at[i], chip[k]
        )

    def gates():
        for p in range(nz):
            for h in range(cd // 128):
                g = jax.nn.sigmoid(small[p, h : h + 1, :])
                c = p * cd + h * 128
                gcol[:, c : c + 128] = jnp.broadcast_to(g, (8, 128))

    def mass_copy(k):
        return remote(massp.at[k], massr.at[k], ms_s.at[k], ms_r.at[k], chip[k])

    def masses():
        m = dot_nt(jnp.ones((8, mine), bf16), wg[...])
        for k in range(GROUP):
            for h in range(2):
                s = h * grp + k * rows
                massp[k, h : h + 1, :] = m[0:1, s : s + rows]
            if k:
                mass_copy(k).start()

    acc[...] = jnp.zeros_like(acc)
    hop(1, zsmall)
    passes(1, 0)
    hop(2, zsmall)
    passes(1, 1)
    passes(2, 0)
    hop(3, zsmall)
    gates()
    gated(0, 0)
    arrive(1)
    arrive(2)
    arrive_sib(0)
    passes(1, 2)
    passes(2, 1)
    own(4)
    lead(tlead, 0, tbuf[:, 0:PIECE])
    arrive_sib(1)
    arrive_sib(2)
    for k in range(3):
        turned(k, 0)
    passes(1, 3)
    passes(2, 2)
    own(5)
    arrive(3)
    arrive_sib(3)
    passes(1, 4)
    passes(2, 3)
    own(6)
    for n in (1, 2, 3):
        ends_here(n, 0)
    project(0)
    for s in range(3, np_ + 2):
        passes(1, s + 2)
        passes(2, s + 1)
        own(s + 4)
        if s < np_ + 1:
            for n in (1, 2):
                ends_here(n, s - 2)
        if s == np_:
            for n in (1, 2):
                ends_here(n, np_ - 1)
            project_ahead()
        ends_here(3, s - 2)
        if s < np_:
            project(s - 2)
        else:
            project_last(s - 2)
        if s == 4:
            masses()
        if s == 5:
            for k in range(3):
                turned(k, 1)
        if s == 6:
            turned(3, 0)
            turned(3, 1)
            lead_turned(tlead, 0, tturn)
        relay(s - 3)
        if s > 4:
            whole(s - 5)
        if s == 5:
            lead(plead, 1, pfin[:, 0:PIECE].astype(bf16))
    whole(np_ - 3)
    lead_turned(plead, 1, pturn)
    for k in (3, 1, 2):
        stat(k, 0).start()
    pair(0).wait_recv()
    kept = jnp.maximum(kept_mine + jnp.sum(pair_r[0, 0:1, 0:1]), 1.0)
    weight = maskf / kept / SLIDES
    relay(np_ - 1)
    whole(np_ - 2)
    whole(np_ - 1)
    for k in (3, 1, 2):
        stat(k, 1).start()

    for i in range(3):
        spots[i] = jnp.sum(jnp.transpose(acc[i]), axis=0, keepdims=True)
    def spot_copy(k, h):
        i = 2 * k + h
        dev = (nbr[k], sib) if h else chip[k]
        return remote(spots, spotr.at[h, k], sp_s.at[i], sp_r.at[i], dev)

    others = [(k, h) for k in (3, 1, 2, 0) for h in (1, 0) if k or h]
    for k, h in others:
        spot_copy(k, h).start()

    def slide_sums(n):
        for k in (1, 2, 3):
            stat(k, n).wait_recv()
        at = parts[n]
        pred_sq, dots, truth_sq = (
            (statg[i, :, at] + statr[1, i, :, at]) + (statr[2, i, :, at] + statr[3, i, :, at])
            for i in range(3)
        )
        slide_a = lax.rsqrt(pred_sq + eps_norm)
        slide_b = lax.rsqrt(truth_sq + eps_norm)
        w = weight[:, at.start : at.start + at.size]
        return (
            -w * slide_a * slide_b,
            w * dots * slide_a**3 * slide_b,
            w * (dots * slide_a * slide_b),
        )

    coefs = [slide_sums(0), None]

    def spot_coefs(k):
        if k:
            spot_copy(k, 0).wait_recv()
        spot_copy(k, 1).wait_recv()
        pp, dot, tt = (
            (spotr[0, k, i] if k else spots[i])
            + jnp.concatenate([spotr[1, k, i, :, rows : 2 * rows], spotr[1, k, i, :, 0:rows]], axis=1)
            for i in range(3)
        )
        a, b = lax.rsqrt(pp + eps_norm), lax.rsqrt(tt + eps_norm)
        t, p = -(a * b) / spots_all, dot * a**3 * b / spots_all
        for h in range(2):
            c = h * grp + k * rows
            coefrow[0:1, c : c + rows] = t[:, h * rows : (h + 1) * rows]
            coefrow[1:2, c : c + rows] = p[:, h * rows : (h + 1) * rows]
        return t, p, dot * a * b

    lead_t, lead_p = (column(v[:, 0:PIECE], PIECE) for v in coefs[0][0:2])
    row_t, row_p, cos_spot = spot_coefs(0)
    col_t, col_p = column(row_t, 2 * rows), column(row_p, 2 * rows)

    def agcopy(i, g):
        src, dst, to = (
            (at_k(0), at_k(1), 1), (at_k(0, 1), at_k(1, 1), 1), (at_k(0, 1), at_k(2, 1), 2),
            (at_k(0), at_k(2), 2), (at_k(1), at_k(3), 2), (at_k(2, 1), at_k(3, 1), 1),
        )[i]
        return remote(half_of(dpa, src, g), half_of(dpa, dst, g), ag_s.at[i, g], ag_r.at[i, g], chip[to])

    def give(g):
        n = 0 if g < np_ - 2 else 1
        if n and coefs[1] is None:
            coefs[1] = slide_sums(1)
        c = g * PIECE - parts[n].start
        c_t, c_p = (v[:, c : c + PIECE] for v in coefs[n][0:2])
        at = piece(g)
        d = ((c_t + col_t) * tbuf[:, at].astype(f32) + (c_p + col_p) * pfin[:, at]).astype(bf16)
        lanes = pl.ds(g % 2 * PIECE, PIECE)
        dpa[g // 2, at_k(0), lanes] = d[0:rows]
        dpa[g // 2, at_k(0, 1), lanes] = d[rows : 2 * rows]
        for i in range(4):
            agcopy(i, g).start()

    def lead_grad():
        for k in (1, 2, 3):
            spot_coefs(k)
        for c in range(0, 2 * grp, 128):
            at = slice(c, c + 128)
            d = (lead_t + coefrow[0:1, at]) * tturn[:, at] + (lead_p + coefrow[1:2, at]) * pturn[:, at]
            dturn[:, at] = d.astype(bf16)

    def lead_back():
        for c in range(0, 2 * grp, rows):
            dpa[0, c : c + rows, 0:PIECE] = jnp.transpose(dturn[:, c : c + rows].astype(f32)).astype(bf16)

    def give_on(g):
        agcopy(0, g).wait_recv()
        agcopy(4, g).start()
        agcopy(2, g).wait_recv()
        agcopy(5, g).start()

    def dcopy(way, p, g):
        if way == 0:
            return remote(dsend.at[p, g], dright.at[p, g], dr_s.at[p, g], dr_r.at[p, g], beside[0])
        return remote(dsend.at[p, g], dleft.at[p, g], dl_s.at[p, g], dl_r.at[p, g], beside[1])

    def expr_grad_first():
        up = z // (nz // 2)

        @pl.loop(0, nz)
        def _(u):
            p = up * u + (1 - up) * (nz - 1 - u)
            v = dot_nt(wt[seg(p), :], dturn[...])
            grad[p, :, 0:PIECE] = v

            @pl.when((ends[0] | ends[1]) & (p != z))
            def _():
                dsend[p, 0] = v.astype(bf16)

            @pl.when(ends[0] & (p != z))
            def _():
                dcopy(0, p, 0).start()

            @pl.when(ends[1] & (p != z))
            def _():
                dcopy(1, p, 0).start()

            @pl.when(u == 0)
            def _():
                give_on(1)

    def expr_grad(g, wait=True):
        if wait:
            for i in (1, 3, 4, 5):
                agcopy(i, g).wait_recv()
        lanes = slice(g % 2 * PIECE, (g % 2 + 1) * PIECE)
        v = jnp.dot(wt[...], dpa[g // 2, :, lanes], preferred_element_type=f32)
        for p in range(nz):
            grad[p, :, piece(g)] = v[p * cd : (p + 1) * cd]

        @pl.when(ends[0])
        def _():
            for p in range(1, nz):
                dsend[p, g] = v[p * cd : (p + 1) * cd].astype(bf16)

        @pl.when(ends[1])
        def _():
            for p in range(nz - 1):
                dsend[p, g] = v[p * cd : (p + 1) * cd].astype(bf16)

    def start_from_ends(u, g):
        if not 0 <= g < np_:
            return

        @pl.when(ends[0])
        def _():
            dcopy(0, nz - 1 - u, g).start()

        @pl.when(ends[1])
        def _():
            dcopy(1, u, g).start()

    def starts(*pieces):
        for u, g in pieces:
            start_from_ends(u, g)

    def chain(hops, u, g):
        if nz - 1 - u > hops:

            @pl.when(z == hops)
            def _():
                p = nz - 1 - u
                dcopy(0, p, g).wait_recv()
                dsend[p, g] = (grad[p, :, piece(g)] + dright[p, g].astype(f32)).astype(bf16)
                dcopy(0, p, g).start()

            @pl.when(nz - 1 - z == hops)
            def _():
                dcopy(1, u, g).wait_recv()
                dsend[u, g] = (grad[u, :, piece(g)] + dleft[u, g].astype(f32)).astype(bf16)
                dcopy(1, u, g).start()

    def finish(g):
        at = piece(g)
        ge_o[:, at] = grad[pl.ds(z, 1), :, at].reshape(cd, PIECE)

        @pl.when(has_left)
        def _():
            dcopy(0, z, g).wait_recv()
            ge_o[:, at] += dright[pl.ds(z, 1), g].reshape(cd, PIECE).astype(f32)

        @pl.when(has_right)
        def _():
            dcopy(1, z, g).wait_recv()
            ge_o[:, at] += dleft[pl.ds(z, 1), g].reshape(cd, PIECE).astype(f32)

    def tile_copy(k):
        return remote(tile_s, tile_r.at[k], tl_s.at[k], tl_r.at[k], chip[k])

    def zcopy(buf, src, r, ss, rs):
        to = (z + r) % nz
        return remote(buf.at[src], buf.at[z], ss.at[r], rs.at[r], (to * GROUP + q, j))

    def zcopy_wait(buf, r, ss, rs):
        o = (z + nz - r) % nz
        remote(buf.at[o], buf.at[o], ss.at[r], rs.at[r], here).wait_recv()

    def chip_masses():
        for k in (1, 2, 3):
            mass_copy(k).wait_recv()
        return (massp[0, 0:2] + massr[1, 0:2]) + (massr[2, 0:2] + massr[3, 0:2])

    def own_dens():
        d = dens[...].astype(f32)
        return jnp.where(j == 0, d, jnp.concatenate([d[1:2], d[0:1]], axis=0))

    def tile_start():
        mass, d = chip_masses(), own_dens()
        gene = fold(coefs[0][2]) + fold(coefs[1][2])
        cos = fold(cos_spot)
        tile_s[0:1] = -2.0 / GROUP * gene - cos / spots_all
        tile_s[1:2] = d[0:1] + d[1:2]
        f = jax.nn.sigmoid(filt[...])
        tile_s[2:3] = f[0:1] + f[1:2]
        tile_s[3:4] = mass[0:1] + mass[1:2]
        kl = d * (jnp.log(d) - jnp.log(mass))
        tile_s[4:5] = kl[0:1] + kl[1:2]
        tile_s[5:8] = jnp.zeros((3, 128), f32)
        for k in (3, 1, 2):
            tile_copy(k).start()
        return mass, d

    def tile_along():
        for k in (1, 2, 3):
            tile_copy(k).wait_recv()
        tz[pl.ds(z, 1)] = ((tile_s[...] + tile_r[1]) + (tile_r[2] + tile_r[3]))[None]
        for r in range(1, nz):
            zcopy(tz, z, r, tz_s, tz_r).start()

    def gm_copy(k):
        return remote(gms, gmr.at[k], gm_s.at[k], gm_r.at[k], chip[k])

    def totals(mass, d):
        for r in range(1, nz):
            zcopy_wait(tz, r, tz_s, tz_r)
        t = tz[0]
        for p in range(1, nz):
            t = t + tz[p]
        loss_part, count, gate, mass_total, kl = (jnp.sum(t[i : i + 1]) for i in range(5))
        logs = jnp.log(jnp.where(lax.broadcasted_iota(jnp.int32, (1, 128), 1) == 0, count, mass_total))
        log_count, log_mass = jnp.sum(logs[:, 0:1]), jnp.sum(logs[:, 1:2])
        excess = gate / count - 1.0
        gms[...] = jnp.zeros_like(gms)
        gms[0:2] = (1.0 / mass_total - d / count / mass).astype(bf16).astype(f32)
        for k in (3, 1, 2):
            gm_copy(k).start()
        pair_s[1] = jnp.full((8, 2 * rows), loss_part + kl / count - log_count + log_mass + excess * excess)
        pair(1).start()
        return 2.0 * excess / count

    def mass_columns():
        gmcol[at_k(0), :] = column(gms[0:1], rows)
        for k in (1, 2, 3):
            gm_copy(k).wait_recv()
            gmcol[at_k(k), :] = column(gmr[k, 0:1], rows)

    def dwcopy(p):
        return remote(dws.at[p], dwr.at[p], dw_s.at[p], dw_r.at[p], here)

    def weight_grad(p):
        cs = slice(p * cd, (p + 1) * cd)

        def rows_of(h):
            d = dot_nt(dpa[0, h * grp : (h + 1) * grp, :], ebuf[0, cs, :])
            for c in range(1, np_ // 2):
                d = d + dot_nt(dpa[c, h * grp : (h + 1) * grp, :], ebuf[c, cs, :])
            return d

        dws[p] = rows_of(1)
        dwcopy(p).start()
        dwo[p] = rows_of(0)

    def gpcopy(k, p):
        return remote(gps.at[p, at_k(k)], gpr.at[k, p], gp_s.at[k, p], gp_r.at[k, p], chip[k])

    def give_back(p):
        dwcopy(p).wait_recv()
        cs = pl.ds(p * cd, cd)
        total = jnp.zeros((1, cd), f32)
        for k in (3, 1, 2, 0):
            r = at_k(k)
            gm = gmcol[r, :]
            gw = dwo[p, r] + dwr[p, r] + jnp.concatenate([gm] * (cd // 128), axis=1)
            total = total + jnp.sum(gw * wraw[r, cs].astype(f32), axis=0, keepdims=True)
            gps[p, r] = (gcol[0:1, cs] * gw).astype(bf16)
            if k:
                gpcopy(k, p).start()
        fsend[p] = total

    def filter_along():
        frecv[pl.ds(z, 1)] = fsend[pl.ds(z, 1)]
        for r in range(1, nz):
            to = (z + r) % nz
            remote(fsend.at[to], frecv.at[z], fz_s.at[r], fz_r.at[r], (to * GROUP + q, j)).start()

    def take(k, p, start=False):
        if k:
            gpcopy(k, p).wait_recv()
            v = gpr[k, p]
        else:
            v = gps[p, at_k(0)]
        at = pl.ds(pl.multiple_of((p * GROUP + nq[k]) * cd, cd), cd)
        gpb[:, at] = v
        s = fold(probs[:, at] * v.astype(f32))
        if start:
            rowsum[...] = s
        else:
            rowsum[...] += s

    def sent_first():
        for k in (1, 2, 3):
            wcopy(k).wait_send()
            mass_copy(k).wait_send()
            for n in (0, 1):
                stat(k, n).wait_send()
        for k in range(GROUP):
            wsib(k).wait_send()
        pair(0).wait_send()
        for k, h in others:
            spot_copy(k, h).wait_send()
        for k in (1, 2, 3):
            for h in range(2):
                lead_copy(tlead, 0, k, h).wait_send()
                lead_copy(plead, 1, k, h).wait_send()

        @pl.loop(0, np_)
        def _(g):
            for c in (pxcopy, pycopy):
                c(g, 0).wait_send()
                c(g, 1).wait_send()
            p2xcopy(g).wait_send()
            p2ycopy(g).wait_send()

    def sent_along():
        @pl.loop(0, nz)
        def _(p):
            @pl.when(has_right & (p <= z))
            def _():
                zsmall(0, p).wait_send()
                for g in range(np_):
                    zsend(0, p, g).wait_send()

            @pl.when(has_left & (p >= z))
            def _():
                zsmall(1, p).wait_send()
                for g in range(np_):
                    zsend(1, p, g).wait_send()

    def sent_back():
        for g in range(1, np_):
            for i in range(6):
                agcopy(i, g).wait_send()

    def sent_last():
        for k in (1, 2, 3):
            tile_copy(k).wait_send()
            gm_copy(k).wait_send()
            for p in range(nz):
                gpcopy(k, p).wait_send()
        for r in range(1, nz):
            zcopy(tz, z, r, tz_s, tz_r).wait_send()
            zcopy(fsend, z, r, fz_s, fz_r).wait_send()
        for p in range(nz):
            dwcopy(p).wait_send()
        for i in (1, 2):
            pair(i).wait_send()

    def sent_sums():
        @pl.loop(0, nz)
        def _(p):
            @pl.when(has_right & (p > z))
            def _():
                for g in range(np_):
                    dcopy(0, p, g).wait_send()

            @pl.when(has_left & (p < z))
            def _():
                for g in range(np_):
                    dcopy(1, p, g).wait_send()

    give(1)
    give(2)
    coefs[1] = slide_sums(1)
    mass, d = tile_start()
    lead_grad()
    expr_grad_first()
    lead_back()
    give_on(2)
    give(3)
    give(4)
    tile_along()
    expr_grad(1)
    starts((0, 1), (1, 1), (2, 1))
    chain(1, 0, 0)
    give_on(3)
    give(5)
    chain(1, 1, 0)
    give_on(4)
    give(6)
    expr_grad(2)
    starts((0, 2), (1, 2))
    chain(2, 0, 0)
    chain(1, 0, 1)
    give_on(5)
    give(7)
    expr_grad(3)
    starts((0, 3))
    chain(1, 1, 1)
    give_on(6)
    expr_grad(4)
    starts((0, 4), (1, 3))
    push = totals(mass, d)
    chain(2, 0, 1)
    chain(1, 0, 2)
    give_on(7)
    expr_grad(5)
    starts((0, 5), (1, 4))
    finish(0)
    chain(1, 1, 2)
    expr_grad(6)
    starts((0, 6), (1, 5))
    chain(1, 0, 3)
    for i in (1, 3, 4, 5):
        agcopy(i, np_ - 1).wait_recv()
    weight_grad(0)
    chain(2, 0, 2)
    chain(1, 0, 4)
    weight_grad(1)
    finish(1)
    mass_columns()
    give_back(0)
    chain(1, 1, 3)
    expr_grad(7, False)
    starts((0, 7), (2, 2), (1, 6), (2, 3), (1, 7))
    chain(2, 0, 3)
    chain(1, 0, 5)
    weight_grad(2)
    give_back(1)
    chain(2, 0, 4)
    chain(1, 1, 4)
    weight_grad(3)
    give_back(2)
    chain(1, 0, 6)
    give_back(3)
    filter_along()
    starts((2, 4), (2, 5), (2, 6), (2, 7))
    chain(1, 1, 5)
    take(0, 0, True)
    for p in range(1, nz):
        take(0, p)
    chain(2, 0, 5)
    chain(1, 0, 7)
    sent_first()
    chain(2, 0, 6)
    finish(2)
    for k in (1, 2, 3):
        take(k, 0)
    chain(1, 1, 6)
    chain(2, 0, 7)
    for k in (1, 2, 3):
        take(k, 1)
    finish(3)
    sent_along()
    chain(1, 1, 7)
    for k in (1, 2, 3):
        take(k, 2)
    finish(4)
    sent_back()
    finish(5)
    for r in range(1, nz):
        zcopy_wait(frecv, r, fz_s, fz_r)
    ftotal = frecv[0]
    for p in range(1, nz):
        ftotal = ftotal + frecv[p]
    pair_s[2, 0:1, 0:cd] = ftotal
    pair(2).start()
    for k in (1, 2, 3):
        take(k, 3)
    tot_o[...] = jnp.broadcast_to(jnp.sum(rowsum[...], axis=1, keepdims=True), (rows, 128))
    sent_last()
    finish(6)
    pair(1).wait_recv()
    pair(2).wait_recv()
    my_gate = jax.nn.sigmoid(filt[...])
    fsum = ftotal + pair_r[2, 0:1, 0:cd] + push
    for h in range(cd // 128):
        g = my_gate[h : h + 1, :]
        last_o[h : h + 1, :] = fsum[:, h * 128 : (h + 1) * 128] * g * (1.0 - g)
    last_o[cd // 128 : cd // 128 + 1, :] = 0.5 * (pair_s[1, 0:1, 0:128] + pair_r[1, 0:1, 0:128])
    finish(7)
    sent_sums()


def finish_kernel(probs, gp, tot, ge, last, gl_o, ge_o, loss_o, gf_o, gl, loss, out_s):
    f32 = jnp.float32
    parts = 4
    cc = probs.shape[1] // parts
    copies = []

    def send(src, dst):
        copies.append(pltpu.make_async_copy(src, dst, out_s.at[len(copies)]))
        copies[-1].start()

    send(ge, ge_o)
    n = gf_o.shape[0]
    loss[...] = last[n : n + 1, 0:1]
    send(last.at[pl.ds(0, n)], gf_o)
    send(loss, loss_o)
    for i in range(parts):
        for c in range(i * cc, (i + 1) * cc, 128):
            at = slice(c, c + 128)
            gl[:, at] = probs[:, at] * (gp[:, at].astype(f32) - tot[...])
        at = pl.ds(i * cc, cc)
        send(gl.at[:, at], gl_o.at[:, at])
    for c in copies:
        c.wait()


def grouped(logits, filt, expr, target, gene_mask, density):
    f32, bf16, i32 = jnp.float32, jnp.bfloat16, jnp.int32
    nspot = lax.axis_size("spot")
    rows, cells = logits.shape
    cd, genes = expr.shape
    nz = nspot // GROUP
    n = genes // PIECE
    grp = GROUP * rows
    mine = cells // GROUP
    spots = 2 * rows

    def vmem(*shape, dtype=f32):
        return pltpu.VMEM(shape, dtype)

    def dma(*shape):
        return pltpu.SemaphoreType.DMA(shape)

    def low(*shape):
        return pltpu.VMEM(shape, bf16)

    buffers = [
        low(rows, cells), vmem(cd // 128, 128), vmem(*gene_mask.shape, dtype=i32), vmem(spots // 128, 128, dtype=i32),
        low(GROUP, rows, mine), low(2 * grp, mine), low(2 * grp, mine), low(mine, 2 * grp),
        low(n // 2, mine, 2 * PIECE), low(spots, genes), vmem(8, mine), vmem(nz, 8, 128), vmem(spots, genes),
        vmem(2 * grp, 2 * PIECE),
        low(n, 2 * rows, PIECE), low(n, 2 * rows, PIECE), low(n, 2 * rows, PIECE), low(n, 2 * rows, PIECE),
        low(n, rows, PIECE), low(n, rows, PIECE), low(n, rows, PIECE), low(n, rows, PIECE),
        vmem(n, rows, PIECE), vmem(n, rows, PIECE), vmem(GROUP, 8, 128), vmem(GROUP, 8, 128),
        vmem(3, 1, genes), vmem(GROUP, 3, 1, genes), vmem(3, spots, PIECE), vmem(3, 1, spots), vmem(2, GROUP, 3, 1, spots), low(2 * grp, PIECE), low(2 * grp, PIECE),
        vmem(PIECE, 2 * grp), vmem(PIECE, 2 * grp), low(PIECE, 2 * grp), vmem(2, 2 * grp),
        low(n // 2, 2 * grp, 2 * PIECE), vmem(nz, cd, genes),
        low(nz, n, cd, PIECE), low(nz, n, cd, PIECE), low(nz, n, cd, PIECE),
        vmem(nz, grp, cd), vmem(nz, grp, cd), vmem(nz, grp, cd), low(nz, grp, cd), low(GROUP, nz, rows, cd),
        vmem(rows, 128), vmem(8, 128), vmem(GROUP, 8, 128), vmem(nz, 8, 128), vmem(8, 128), vmem(GROUP, 8, 128),
        vmem(grp, 128), vmem(nz, 1, cd), vmem(nz, 1, cd), vmem(3, 8, spots), vmem(3, 8, spots),
    ]
    sems = [
        pltpu.SemaphoreType.REGULAR, dma(4 + n // 2 + 2), dma(2, nz), dma(nz), dma(2, nz, n), dma(nz, n),
        dma(4), dma(4), dma(4), dma(4), dma(3), dma(3),
        dma(2, n), dma(2, n), dma(2, n), dma(2, n), dma(n), dma(n), dma(n), dma(n),
        dma(4), dma(4), dma(8), dma(8), dma(2, 4, 2), dma(2, 4, 2), dma(8), dma(8), dma(6, n), dma(6, n),
        dma(nz, n), dma(nz, n), dma(nz, n), dma(nz, n), dma(nz), dma(nz), dma(4, nz), dma(4, nz),
        dma(4), dma(4), dma(nz), dma(nz), dma(4), dma(4), dma(nz), dma(nz),
    ]
    v, a = pl.BlockSpec(memory_space=pltpu.VMEM), pl.BlockSpec(memory_space=pl.ANY)
    shape = jax.ShapeDtypeStruct
    fparts = (cd // 128, 128)
    given = (logits, filt.reshape(-1, 128), expr, target, gene_mask, density.reshape(-1, 128))
    probs, gp, tot, last, grad_expr = pl.pallas_call(
        functools.partial(group_kernel, nspot),
        out_shape=[vmem(rows, cells), low(rows, cells), vmem(rows, 128), vmem(8, 128), vmem(cd, genes)],
        in_specs=[a] * 6,
        out_specs=[v] * 5,
        scratch_shapes=buffers + sems,
        compiler_params=pltpu.CompilerParams(
            collective_id=0, has_side_effects=True, vmem_limit_bytes=VMEM_BYTES
        ),
        name="group_step",
    )(*(pltpu.with_memory_space_constraint(g, pltpu.HBM) for g in given))
    grad_logits, grad_expr, loss, grad_filt = pl.pallas_call(
        finish_kernel,
        out_shape=[shape((rows, cells), f32), shape((cd, genes), f32), shape((1, 1), f32), shape(fparts, f32)],
        in_specs=[v] * 5,
        out_specs=[a] * 4,
        scratch_shapes=[vmem(rows, cells), vmem(1, 1), dma(7)],
        compiler_params=pltpu.CompilerParams(vmem_limit_bytes=LAST_BYTES),
        name="finish_step",
    )(probs, gp, tot, grad_expr, last)
    return (loss.reshape(()), grad_logits, grad_filt.reshape(-1), grad_expr)


def fits(logits, filt, expr):
    nspot = lax.axis_size("spot")
    rows, cells = logits.shape
    sizes = (rows, cells, filt.shape[0], expr.shape[1])
    return (
        nspot == GROUP * SLIDES and lax.axis_size("gene") == 2 and sizes == (128, 4096, 256, 1024)
    )


def per_device(logits, filt, expr, target, gene_mask, density):
    plan = grouped if fits(logits, filt, expr) else streamed
    return plan(logits, filt, expr, target, gene_mask, density)


def solution(mesh):
    in_specs = (
        P(("spot", "gene"), None),
        P("spot"),
        P("spot", "gene"),
        P("spot", "gene"),
        P(None, "gene"),
        P("spot"),
    )
    out_specs = (P(), P(("spot", "gene"), None), P("spot"), P("spot", "gene"))
    return jax.shard_map(
        per_device, mesh=mesh, in_specs=in_specs, out_specs=out_specs, check_vma=False
    )
```

```python
import functools

import jax
import jax.numpy as jnp
from jax import lax
from jax.experimental import pallas as pl
from jax.experimental.pallas import tpu as pltpu
from jax.sharding import PartitionSpec as P

SPOTS = 4096
SLIDES = 4


eps_norm = 1e-06


def slide_moments(onehot, pred, truth):
    hi = lax.Precision.HIGHEST
    return jnp.stack(
        [
            jnp.dot(onehot.T, pred * truth, precision=hi),
            jnp.dot(onehot.T, pred * pred, precision=hi),
            jnp.dot(onehot.T, truth * truth, precision=hi),
        ]
    )


def spot_moments(pred, truth):
    return jnp.stack(
        [
            jnp.sum(pred * truth, axis=1),
            jnp.sum(pred * pred, axis=1),
            jnp.sum(truth * truth, axis=1),
        ]
    )


def cosine_parts(slide_stats):
    dots = slide_stats[0]
    slide_a = lax.rsqrt(slide_stats[1] + eps_norm)
    slide_b = lax.rsqrt(slide_stats[2] + eps_norm)
    return (dots, slide_a, slide_b, dots * slide_a * slide_b)


def pred_gradient(onehot, weight_slide, dots, slide_a, slide_b, spot_stats, pred, truth):
    hi = lax.Precision.HIGHEST
    spot_a = lax.rsqrt(spot_stats[1] + eps_norm)
    spot_b = lax.rsqrt(spot_stats[2] + eps_norm)
    coef_truth = -weight_slide * slide_a * slide_b
    coef_pred = weight_slide * dots * slide_a**3 * slide_b
    grad_pred = (
        jnp.dot(onehot, coef_truth, precision=hi) * truth
        + jnp.dot(onehot, coef_pred, precision=hi) * pred
    )
    grad_pred = (
        grad_pred
        + (
            -(spot_a * spot_b)[:, None] * truth
            + (spot_stats[0] * spot_a**3 * spot_b)[:, None] * pred
        )
        / SPOTS
    )
    return (grad_pred, spot_stats[0] * spot_a * spot_b)


def streamed(logits, filt, expr, target, gene_mask, density):
    f32 = jnp.float32
    bf16 = jnp.bfloat16
    nspot = lax.axis_size("spot")
    ngene = lax.axis_size("gene")
    spot_dev = logits.shape[0]
    cells = logits.shape[1]
    cell_dev = filt.shape[0]
    owned = target.shape[0]
    half = target.shape[1]
    spots_all = owned * nspot
    slide_len = SPOTS // SLIDES
    scores = logits.astype(f32)
    shifted = jnp.exp(scores - jnp.max(scores, axis=1, keepdims=True))
    probs = shifted / jnp.sum(shifted, axis=1, keepdims=True)
    moved = lax.all_to_all(probs.astype(bf16), "spot", split_axis=1, concat_axis=0, tiled=True)
    paired = lax.all_gather(moved.reshape(nspot, 1, spot_dev, cell_dev), "gene", axis=1, tiled=True)
    paired = paired.reshape(spots_all, cell_dev)
    gate = jax.nn.sigmoid(filt)
    weighted = (paired.astype(f32) * gate[None, :]).astype(bf16)
    partial_pred = jnp.dot(weighted, expr, preferred_element_type=f32)
    partial_mass = jnp.sum(weighted.astype(f32), axis=1)
    gate_part = jnp.sum(gate)
    maskf = gene_mask.astype(f32)
    mask_part = jnp.sum(maskf, axis=1)
    pred_three, mass_two = (
        lax.psum_scatter(
            partial_pred.reshape(nspot, owned, half), "spot", scatter_dimension=0, tiled=True
        ),
        lax.psum_scatter(
            partial_mass.reshape(nspot, owned), "spot", scatter_dimension=0, tiled=True
        ),
    )
    pred = pred_three.reshape(owned, half)
    mass = mass_two.reshape(owned)
    truth = target.astype(f32)
    dens = density.astype(f32)
    spot_ids = lax.axis_index("spot") * owned + jnp.arange(owned, dtype=jnp.int32)
    onehot = (
        spot_ids[:, None] // slide_len == jnp.arange(SLIDES, dtype=jnp.int32)[None, :]
    ).astype(f32)
    slide_stats, mass_total, gate_total, count_total = lax.psum(
        (slide_moments(onehot, pred, truth), jnp.sum(mass), gate_part, jnp.sum(dens)), "spot"
    )
    dots, slide_a, slide_b, cos_gene = cosine_parts(slide_stats)
    spot_stats, kept_genes, gene_numer = lax.psum(
        (spot_moments(pred, truth), mask_part, jnp.sum(maskf * cos_gene, axis=1)), "gene"
    )
    genes_kept = jnp.maximum(kept_genes, 1.0)
    weight_slide = maskf / genes_kept[:, None] / SLIDES
    grad_pred, cos_spot = pred_gradient(
        onehot, weight_slide, dots, slide_a, slide_b, spot_stats, pred, truth
    )
    share = dens / count_total
    kl_local = jnp.sum(share * (jnp.log(share) - jnp.log(mass) + jnp.log(mass_total)))
    cos_total, kl_total = lax.psum((jnp.sum(cos_spot), kl_local), "spot")
    grad_mass = 1.0 / mass_total - share / mass
    spread_three, spread_two = (
        lax.all_gather(grad_pred.astype(bf16).reshape(1, owned, half), "spot", axis=0, tiled=True),
        lax.all_gather(grad_mass.astype(bf16).reshape(1, owned), "spot", axis=0, tiled=True),
    )
    spread_pred = spread_three.reshape(spots_all, half)
    spread_mass = spread_two.reshape(spots_all)
    gene_term = jnp.mean(gene_numer / genes_kept)
    excess = gate_total / count_total - 1.0
    loss = -gene_term - cos_total / SPOTS + kl_total + excess * excess
    grad_expr = lax.dot_general(
        weighted, spread_pred, (((0,), (0,)), ((), ())), preferred_element_type=f32
    )
    first_half = (lax.axis_index("gene") == 0).astype(f32)
    grad_weighted = lax.dot_general(
        spread_pred, expr, (((1,), (1,)), ((), ())), preferred_element_type=f32
    )
    grad_weighted = grad_weighted + first_half * spread_mass.astype(f32)[:, None]
    filter_part = jnp.sum(grad_weighted * paired.astype(f32), axis=0)
    filter_total = lax.psum(filter_part, "gene")
    grad_filt = (filter_total + 2.0 * excess / count_total) * gate * (1.0 - gate)
    terms = (grad_weighted * gate[None, :]).reshape(nspot, ngene, spot_dev, cell_dev)
    moved_back = lax.all_to_all(terms, "spot", split_axis=0, concat_axis=3, tiled=True)
    folded = lax.psum_scatter(moved_back, "gene", scatter_dimension=1, tiled=True)
    rounded = lax.optimization_barrier(folded.reshape(spot_dev, cells).astype(bf16))
    grad_probs = rounded.astype(f32)
    grad_logits = probs * (grad_probs - jnp.sum(probs * grad_probs, axis=1, keepdims=True))
    return (loss, grad_logits, grad_filt, grad_expr)


GROUP = 4
PIECE = 128
MESH = pl.DeviceIdType.MESH
PAIRS = (4, 6,)
VMEM_BYTES = 44 << 20
LAST_BYTES = 16 << 20


def remote(src, dst, send, recv, dev):
    return pltpu.make_async_remote_copy(
        src_ref=src, dst_ref=dst, send_sem=send, recv_sem=recv, device_id=dev, device_id_type=MESH
    )


def dot_nt(a, b):
    return lax.dot_general(a, b, (((1,), (1,)), ((), ())), preferred_element_type=jnp.float32)


def column(row, length):
    return jnp.transpose(jnp.broadcast_to(row, (128, length)))


def fold(values):
    total = values[:, 0:128]
    for i in range(1, values.shape[1] // 128):
        total = total + values[:, i * 128 : (i + 1) * 128]
    return total


def group_kernel(
    nspot, logits_h, filt_h, expr, target, mask_h, dens_h,
    probs, gpb, tot_o, last_o, ge_o,
    logits, filt, mask, dens, rawq, wraw, wg, wt, ebuf, tbuf, gcol, small, pfin, ahead,
    psx, prx, psy, pry, ps2x, pr2x, ps2y, pr2y, hx, hy, massp, massr, statg, statr, acc, spots, spotr, tlead, plead, tturn, pturn, dturn, coefrow,
    dpa, grad, dsend, dright, dleft, dwo, dws, dwr, gps, gpr, rowsum, tile_s, tile_r, tz, gms, gmr, gmcol,
    fsend, frecv, pair_s, pair_r,
    hello, lc, zs_s, zs_r, ez_s, ez_r, w_s, w_r, wd_s, wd_r, pr_s, pr_r,
    px_s, px_r, py_s, py_r, p2x_s, p2x_r, p2y_s, p2y_r, ms_s, ms_r, st_s, st_r, ld_s, ld_r, sp_s, sp_r, ag_s, ag_r,
    dr_s, dr_r, dl_s, dl_r, dw_s, dw_r, gp_s, gp_r, tl_s, tl_r, tz_s, tz_r, gm_s, gm_r, fz_s, fz_r,
):
    f32, bf16 = jnp.float32, jnp.bfloat16
    rows, cells = probs.shape
    cd, genes = expr.shape
    nz = nspot // GROUP
    np_ = genes // PIECE
    grp = GROUP * rows
    mine = cells // GROUP
    spots_all = nspot * 2 * rows
    me, j = lax.axis_index("spot"), lax.axis_index("gene")
    sib = 1 - j
    z, q = me // GROUP, me % GROUP
    x, y = q % 2, q // 2
    nbr = [me, me + 1 - 2 * x, me + 2 - 4 * y, me + 3 - 2 * x - 4 * y]
    nq = [n % GROUP for n in nbr]
    here = (me, sib)
    has_right, has_left = z < nz - 1, z > 0
    ends = (z == 0, z == nz - 1)
    chip = [(n, j) for n in nbr]
    beside = ((me + GROUP, j), (me - GROUP, j))

    def at_k(k, h=0):
        return pl.ds(h * grp + k * rows, rows)

    def piece(g):
        return pl.ds(g * PIECE, PIECE)

    def half_of(buf, r, g):
        return buf.at[g // 2, r, pl.ds(g % 2 * PIECE, PIECE)]

    def seg(p):
        return pl.ds(pl.multiple_of(p * cd, cd), cd)

    barrier = pltpu.get_barrier_semaphore()

    def greet(dev):
        pl.semaphore_signal(barrier, inc=1, device_id=dev, device_id_type=MESH)

    greet(chip[1])
    greet(chip[2])

    @pl.when(has_right)
    def _():
        greet(beside[0])

    @pl.when(has_left)
    def _():
        greet(beside[1])

    greet(here)
    loads = [pltpu.make_async_copy(logits_h, logits, lc.at[0])]
    loads += [
        pltpu.make_async_copy(s, d, lc.at[1 + i])
        for i, (s, d) in enumerate(((filt_h, filt), (mask_h, mask), (dens_h, dens)))
    ]
    loads += [
        pltpu.make_async_copy(
            expr.at[:, pl.ds(i * 2 * PIECE, 2 * PIECE)], ebuf.at[i, seg(z), :], lc.at[4 + i]
        )
        for i in range(np_ // 2)
    ]
    loads += [
        pltpu.make_async_copy(
            target.at[pl.ds(pl.multiple_of(c * rows, rows), rows)],
            tbuf.at[pl.ds(i * rows, rows)],
            lc.at[4 + np_ // 2 + i],
        )
        for i, c in enumerate((j, sib))
    ]
    for c in loads:
        c.start()
    for c in loads[1 : 4 + np_ // 2]:
        c.wait()
    small[pl.ds(z, 1), 0 : cd // 128, :] = filt[...][None]
    pl.semaphore_wait(barrier, 3 + has_right.astype(jnp.int32) + has_left.astype(jnp.int32))

    def zsmall(way, p):
        return remote(small.at[p], small.at[p], zs_s.at[way, p], zs_r.at[p], beside[way])

    def zsend(way, p, g):
        u = half_of(ebuf, seg(p), g)
        return remote(u, u, ez_s.at[way, p, g], ez_r.at[p, g], beside[way])

    def both(make):
        @pl.when(has_right)
        def _():
            make(0).start()

        @pl.when(has_left)
        def _():
            make(1).start()

    def hop(s, make):
        @pl.when(z >= s)
        def _():
            make(0, z - s).wait_recv()

            @pl.when(has_right)
            def _():
                make(0, z - s).start()

        @pl.when(z + s <= nz - 1)
        def _():
            make(1, z + s).wait_recv()

            @pl.when(has_left)
            def _():
                make(1, z + s).start()

    def own(g):
        if g < np_:
            both(lambda way: zsend(way, z, g))

    def passes(s, g):
        if not 0 <= g < np_:
            return

        @pl.when((z >= s) & has_right)
        def _():
            zsend(0, z - s, g).wait_recv()
            zsend(0, z - s, g).start()

        @pl.when((z + s <= nz - 1) & has_left)
        def _():
            zsend(1, z + s, g).wait_recv()
            zsend(1, z + s, g).start()

    def ends_here(s, g):
        if not 0 <= g < np_:
            return

        @pl.when((z >= s) & ends[1])
        def _():
            zsend(0, z - s, g).wait_recv()

        @pl.when((z + s <= nz - 1) & ends[0])
        def _():
            zsend(1, z + s, g).wait_recv()

    both(lambda way: zsmall(way, z))
    for g in range(4):
        own(g)

    loads[0].wait()

    step = 32

    @pl.loop(0, rows // step)
    def _(i):
        at = pl.ds(pl.multiple_of(i * step, step), step)
        s = logits[at, :].astype(f32)
        e = jnp.exp(s - jnp.max(s, axis=1, keepdims=True))
        p = e * (1.0 / jnp.sum(e, axis=1, keepdims=True))
        probs[at, :] = p
        for o in range(nspot):
            c = o // GROUP * cd
            rawq[o % GROUP, at, c : c + cd] = p[:, o * cd : (o + 1) * cd].astype(bf16)

    for c in loads[4 + np_ // 2 :]:
        c.wait()
    maskf = mask[pl.ds(z, 1), :].astype(f32)
    kept_mine = jnp.sum(maskf)
    pair_s[0] = jnp.full((8, 2 * rows), kept_mine)

    def wcopy(k):
        return remote(rawq.at[nq[k]], wraw.at[at_k(k)], w_s.at[k], w_r.at[k], chip[k])

    def wsib(k):
        return remote(wraw.at[at_k(k)], wraw.at[at_k(k, 1)], wd_s.at[k], wd_r.at[k], here)

    def pair(i):
        return remote(pair_s.at[i], pair_r.at[i], pr_s.at[i], pr_r.at[i], here)

    def lead_copy(buf, i, k, h):
        r = at_k(0, h)
        return remote(buf.at[r], buf.at[at_k(k, h)], ld_s.at[i, k, h], ld_r.at[i, k, h], chip[k])

    def lead(buf, i, values):
        for h in range(2):
            buf[at_k(0, h), :] = values[h * rows : (h + 1) * rows]
        for k in (3, 1, 2):
            for h in range(2):
                lead_copy(buf, i, k, h).start()

    def lead_turned(buf, i, out):
        lead_wait(buf, i)
        for c in range(0, 2 * grp, rows):
            out[:, c : c + rows] = jnp.transpose(buf[c : c + rows, :].astype(f32))

    def lead_wait(buf, i):
        for k in (1, 2, 3):
            for h in range(2):
                lead_copy(buf, i, k, h).wait_recv()

    wcopy(1).start()
    wcopy(2).start()
    pl.semaphore_signal(hello, inc=1, device_id=chip[1], device_id_type=MESH)
    wraw[at_k(0), :] = rawq[pl.ds(q, 1)].reshape(rows, mine)
    wsib(0).start()
    pair(0).start()
    pl.semaphore_wait(hello, 1)
    wcopy(3).start()

    def gated(k, h):
        r = at_k(k, h)
        for c in range(0, mine, 512):
            at = pl.ds(c, 512)
            wg[r, at] = (gcol[0:1, at] * wraw[r, at].astype(f32)).astype(bf16)

    def turned(k, h):
        r = at_k(k, h)
        for c in range(0, mine, 512):
            at = pl.ds(c, 512)
            wt[at, r] = jnp.transpose(wg[r, at].astype(f32)).astype(bf16)

    def arrive(k):
        wcopy(k).wait_recv()
        wsib(k).start()
        gated(k, 0)

    def arrive_sib(k):
        wsib(k).wait_recv()
        gated(k, 1)

    first, second = pl.ds(0, rows), pl.ds(rows, rows)

    def pxcopy(g, n):
        h = (first, second)[n]
        return remote(psx.at[g, h], prx.at[g, h], px_s.at[n, g], px_r.at[n, g], chip[1])

    def pycopy(g, n):
        h = (first, second)[n]
        return remote(psy.at[g, h], pry.at[g, h], py_s.at[n, g], py_r.at[n, g], chip[2])

    def p2xcopy(g):
        return remote(ps2x.at[g], pr2x.at[g], p2x_s.at[g], p2x_r.at[g], chip[1])

    def p2ycopy(g):
        return remote(ps2y.at[g], pr2y.at[g], p2y_s.at[g], p2y_r.at[g], chip[2])

    def piece_of(g, at):
        return ebuf[g // 2, at, g % 2 * PIECE : (g % 2 + 1) * PIECE]

    def project(g):
        share(g, jnp.dot(wg[...], piece_of(g, pl.ds(0, mine)), preferred_element_type=f32))

    far = (1 - z // (nz // 2)) * (nz - 1)
    near = pl.ds(pl.multiple_of(z // (nz // 2) * cd, cd), mine - cd)

    def project_ahead(g):
        ahead[...] = jnp.dot(wg[:, near], ebuf[g // 2, near, :], preferred_element_type=f32)

    def project_last(g):
        e = piece_of(g, seg(far))
        lanes = pl.ds(g % 2 * PIECE, PIECE)

        def rows_of(r):
            return ahead[r, lanes] + jnp.dot(wg[r, seg(far)], e, preferred_element_type=f32)

        relayed = [rows_of(at_k(3, h)) for h in range(2)]
        psx[g, second] = relayed[0].astype(bf16)
        pxcopy(g, 1).start()
        psy[g, second] = relayed[1].astype(bf16)
        pycopy(g, 1).start()
        rest = [rows_of(pl.ds(h * grp, 3 * rows)) for h in range(2)]
        share_rest(g, lambda k, h: rest[h][k * rows : (k + 1) * rows])

    def share(g, v):
        def part(k, h):
            s = h * grp + k * rows
            return v[s : s + rows]

        psx[g, second] = part(3, 0).astype(bf16)
        pxcopy(g, 1).start()
        psy[g, second] = part(3, 1).astype(bf16)
        pycopy(g, 1).start()
        share_rest(g, part)

    def share_rest(g, part):
        psx[g, first] = part(1, 0).astype(bf16)
        pxcopy(g, 0).start()
        psy[g, first] = part(2, 1).astype(bf16)
        pycopy(g, 0).start()
        hx[g] = part(2, 0)
        hy[g] = part(1, 1)
        pfin[first, piece(g)] = part(0, 0)
        pfin[second, piece(g)] = part(0, 1)

    def relay(g):
        pxcopy(g, 1).wait_recv()
        ps2y[g] = (hx[g] + prx[g, second].astype(f32)).astype(bf16)
        p2ycopy(g).start()
        pycopy(g, 1).wait_recv()
        ps2x[g] = (hy[g] + pry[g, second].astype(f32)).astype(bf16)
        p2xcopy(g).start()

    def whole(g):
        at = piece(g)
        pxcopy(g, 0).wait_recv()
        pycopy(g, 0).wait_recv()
        p2ycopy(g).wait_recv()
        p2xcopy(g).wait_recv()
        pfin[first, at] += prx[g, first].astype(f32) + pr2y[g].astype(f32)
        pfin[second, at] += pry[g, first].astype(f32) + pr2x[g].astype(f32)
        p = pfin[:, at]
        t = tbuf[:, at].astype(f32)
        for i, v in enumerate((p * p, p * t, t * t)):
            statg[i, :, at] = jnp.sum(v, axis=0, keepdims=True)
            acc[i] += v

    parts = (pl.ds(0, (np_ - 2) * PIECE), pl.ds((np_ - 2) * PIECE, 2 * PIECE))

    def stat(k, n):
        i = 2 * k + n
        return remote(
            statg.at[:, :, parts[n]], statr.at[k, :, :, parts[n]], st_s.at[i], st_r.at[i], chip[k]
        )

    def gates():
        for p in range(nz):
            for h in range(cd // 128):
                g = jax.nn.sigmoid(small[p, h : h + 1, :])
                c = p * cd + h * 128
                gcol[:, c : c + 128] = jnp.broadcast_to(g, (8, 128))

    def mass_copy(k):
        return remote(massp.at[k], massr.at[k], ms_s.at[k], ms_r.at[k], chip[k])

    def masses():
        m = dot_nt(jnp.ones((8, mine), bf16), wg[...])
        for k in range(GROUP):
            for h in range(2):
                s = h * grp + k * rows
                massp[k, h : h + 1, :] = m[0:1, s : s + rows]
            if k:
                mass_copy(k).start()

    acc[...] = jnp.zeros_like(acc)
    hop(1, zsmall)
    passes(1, 0)
    hop(2, zsmall)
    passes(1, 1)
    passes(2, 0)
    hop(3, zsmall)
    gates()
    gated(0, 0)
    arrive(1)
    arrive(2)
    arrive_sib(0)
    passes(1, 2)
    passes(2, 1)
    own(4)
    lead(tlead, 0, tbuf[:, 0:PIECE])
    arrive_sib(1)
    arrive_sib(2)
    for k in range(3):
        turned(k, 0)
    passes(1, 3)
    passes(2, 2)
    own(5)
    arrive(3)
    arrive_sib(3)
    passes(1, 4)
    passes(2, 3)
    own(6)
    for n in (1, 2, 3):
        ends_here(n, 0)
    project(0)
    for s in range(3, np_ + 2):
        passes(1, s + 2)
        passes(2, s + 1)
        own(s + 4)
        g = s - 2
        if g in PAIRS:
            for n in (1, 2):
                ends_here(n, g)
                ends_here(n, g + 1)
            project_ahead(g)
        elif g - 1 not in PAIRS:
            for n in (1, 2):
                ends_here(n, g)
        ends_here(3, g)
        if g in PAIRS or g - 1 in PAIRS:
            project_last(g)
        else:
            project(g)
        if s == 4:
            masses()
        if s == 5:
            for k in range(3):
                turned(k, 1)
        if s == 6:
            turned(3, 0)
            turned(3, 1)
            lead_turned(tlead, 0, tturn)
        relay(s - 3)
        if s > 4:
            whole(s - 5)
        if s == 5:
            lead(plead, 1, pfin[:, 0:PIECE].astype(bf16))
    whole(np_ - 3)
    lead_turned(plead, 1, pturn)
    for k in (3, 1, 2):
        stat(k, 0).start()
    pair(0).wait_recv()
    kept = jnp.maximum(kept_mine + jnp.sum(pair_r[0, 0:1, 0:1]), 1.0)
    weight = maskf / kept / SLIDES
    relay(np_ - 1)
    whole(np_ - 2)
    whole(np_ - 1)
    for k in (3, 1, 2):
        stat(k, 1).start()

    for i in range(3):
        spots[i] = jnp.sum(jnp.transpose(acc[i]), axis=0, keepdims=True)
    def spot_copy(k, h):
        i = 2 * k + h
        dev = (nbr[k], sib) if h else chip[k]
        return remote(spots, spotr.at[h, k], sp_s.at[i], sp_r.at[i], dev)

    others = [(k, h) for k in (3, 1, 2, 0) for h in (1, 0) if k or h]
    for k, h in others:
        spot_copy(k, h).start()

    def slide_sums(n):
        for k in (1, 2, 3):
            stat(k, n).wait_recv()
        at = parts[n]
        pred_sq, dots, truth_sq = (
            (statg[i, :, at] + statr[1, i, :, at]) + (statr[2, i, :, at] + statr[3, i, :, at])
            for i in range(3)
        )
        slide_a = lax.rsqrt(pred_sq + eps_norm)
        slide_b = lax.rsqrt(truth_sq + eps_norm)
        w = weight[:, at.start : at.start + at.size]
        return (
            -w * slide_a * slide_b,
            w * dots * slide_a**3 * slide_b,
            w * (dots * slide_a * slide_b),
        )

    coefs = [slide_sums(0), None]

    def spot_coefs(k):
        if k:
            spot_copy(k, 0).wait_recv()
        spot_copy(k, 1).wait_recv()
        pp, dot, tt = (
            (spotr[0, k, i] if k else spots[i])
            + jnp.concatenate([spotr[1, k, i, :, rows : 2 * rows], spotr[1, k, i, :, 0:rows]], axis=1)
            for i in range(3)
        )
        a, b = lax.rsqrt(pp + eps_norm), lax.rsqrt(tt + eps_norm)
        t, p = -(a * b) / spots_all, dot * a**3 * b / spots_all
        for h in range(2):
            c = h * grp + k * rows
            coefrow[0:1, c : c + rows] = t[:, h * rows : (h + 1) * rows]
            coefrow[1:2, c : c + rows] = p[:, h * rows : (h + 1) * rows]
        return t, p, dot * a * b

    lead_t, lead_p = (column(v[:, 0:PIECE], PIECE) for v in coefs[0][0:2])
    row_t, row_p, cos_spot = spot_coefs(0)
    col_t, col_p = column(row_t, 2 * rows), column(row_p, 2 * rows)

    def agcopy(i, g):
        src, dst, to = (
            (at_k(0), at_k(1), 1), (at_k(0, 1), at_k(1, 1), 1), (at_k(0, 1), at_k(2, 1), 2),
            (at_k(0), at_k(2), 2), (at_k(1), at_k(3), 2), (at_k(2, 1), at_k(3, 1), 1),
        )[i]
        return remote(half_of(dpa, src, g), half_of(dpa, dst, g), ag_s.at[i, g], ag_r.at[i, g], chip[to])

    def give(g):
        n = 0 if g < np_ - 2 else 1
        if n and coefs[1] is None:
            coefs[1] = slide_sums(1)
        c = g * PIECE - parts[n].start
        c_t, c_p = (v[:, c : c + PIECE] for v in coefs[n][0:2])
        at = piece(g)
        d = ((c_t + col_t) * tbuf[:, at].astype(f32) + (c_p + col_p) * pfin[:, at]).astype(bf16)
        lanes = pl.ds(g % 2 * PIECE, PIECE)
        dpa[g // 2, at_k(0), lanes] = d[0:rows]
        dpa[g // 2, at_k(0, 1), lanes] = d[rows : 2 * rows]
        for i in range(4):
            agcopy(i, g).start()

    def lead_grad():
        for k in (1, 2, 3):
            spot_coefs(k)
        for c in range(0, 2 * grp, 128):
            at = slice(c, c + 128)
            d = (lead_t + coefrow[0:1, at]) * tturn[:, at] + (lead_p + coefrow[1:2, at]) * pturn[:, at]
            dturn[:, at] = d.astype(bf16)

    def lead_back():
        for c in range(0, 2 * grp, rows):
            dpa[0, c : c + rows, 0:PIECE] = jnp.transpose(dturn[:, c : c + rows].astype(f32)).astype(bf16)

    def give_on(g):
        agcopy(0, g).wait_recv()
        agcopy(4, g).start()
        agcopy(2, g).wait_recv()
        agcopy(5, g).start()

    def dcopy(way, p, g):
        if way == 0:
            return remote(dsend.at[p, g], dright.at[p, g], dr_s.at[p, g], dr_r.at[p, g], beside[0])
        return remote(dsend.at[p, g], dleft.at[p, g], dl_s.at[p, g], dl_r.at[p, g], beside[1])

    def expr_grad_first():
        up = z // (nz // 2)

        @pl.loop(0, nz)
        def _(u):
            p = up * u + (1 - up) * (nz - 1 - u)
            v = dot_nt(wt[seg(p), :], dturn[...])
            grad[p, :, 0:PIECE] = v

            @pl.when((ends[0] | ends[1]) & (p != z))
            def _():
                dsend[p, 0] = v.astype(bf16)

            @pl.when(ends[0] & (p != z))
            def _():
                dcopy(0, p, 0).start()

            @pl.when(ends[1] & (p != z))
            def _():
                dcopy(1, p, 0).start()

            @pl.when(u == 0)
            def _():
                give_on(1)

    def expr_grad(g, wait=True):
        if wait:
            for i in (1, 3, 4, 5):
                agcopy(i, g).wait_recv()
        lanes = slice(g % 2 * PIECE, (g % 2 + 1) * PIECE)
        v = jnp.dot(wt[...], dpa[g // 2, :, lanes], preferred_element_type=f32)
        for p in range(nz):
            grad[p, :, piece(g)] = v[p * cd : (p + 1) * cd]

        @pl.when(ends[0])
        def _():
            for p in range(1, nz):
                dsend[p, g] = v[p * cd : (p + 1) * cd].astype(bf16)

        @pl.when(ends[1])
        def _():
            for p in range(nz - 1):
                dsend[p, g] = v[p * cd : (p + 1) * cd].astype(bf16)

    def start_from_ends(u, g):
        if not 0 <= g < np_:
            return

        @pl.when(ends[0])
        def _():
            dcopy(0, nz - 1 - u, g).start()

        @pl.when(ends[1])
        def _():
            dcopy(1, u, g).start()

    def starts(*pieces):
        for u, g in pieces:
            start_from_ends(u, g)

    def chain(hops, u, g):
        if nz - 1 - u > hops:

            @pl.when(z == hops)
            def _():
                p = nz - 1 - u
                dcopy(0, p, g).wait_recv()
                dsend[p, g] = (grad[p, :, piece(g)] + dright[p, g].astype(f32)).astype(bf16)
                dcopy(0, p, g).start()

            @pl.when(nz - 1 - z == hops)
            def _():
                dcopy(1, u, g).wait_recv()
                dsend[u, g] = (grad[u, :, piece(g)] + dleft[u, g].astype(f32)).astype(bf16)
                dcopy(1, u, g).start()

    def finish(g):
        at = piece(g)
        ge_o[:, at] = grad[pl.ds(z, 1), :, at].reshape(cd, PIECE)

        @pl.when(has_left)
        def _():
            dcopy(0, z, g).wait_recv()
            ge_o[:, at] += dright[pl.ds(z, 1), g].reshape(cd, PIECE).astype(f32)

        @pl.when(has_right)
        def _():
            dcopy(1, z, g).wait_recv()
            ge_o[:, at] += dleft[pl.ds(z, 1), g].reshape(cd, PIECE).astype(f32)

    def tile_copy(k):
        return remote(tile_s, tile_r.at[k], tl_s.at[k], tl_r.at[k], chip[k])

    def zcopy(buf, src, r, ss, rs):
        to = (z + r) % nz
        return remote(buf.at[src], buf.at[z], ss.at[r], rs.at[r], (to * GROUP + q, j))

    def zcopy_wait(buf, r, ss, rs):
        o = (z + nz - r) % nz
        remote(buf.at[o], buf.at[o], ss.at[r], rs.at[r], here).wait_recv()

    def chip_masses():
        for k in (1, 2, 3):
            mass_copy(k).wait_recv()
        return (massp[0, 0:2] + massr[1, 0:2]) + (massr[2, 0:2] + massr[3, 0:2])

    def own_dens():
        d = dens[...].astype(f32)
        return jnp.where(j == 0, d, jnp.concatenate([d[1:2], d[0:1]], axis=0))

    def tile_start():
        mass, d = chip_masses(), own_dens()
        gene = fold(coefs[0][2]) + fold(coefs[1][2])
        cos = fold(cos_spot)
        tile_s[0:1] = -2.0 / GROUP * gene - cos / spots_all
        tile_s[1:2] = d[0:1] + d[1:2]
        f = jax.nn.sigmoid(filt[...])
        tile_s[2:3] = f[0:1] + f[1:2]
        tile_s[3:4] = mass[0:1] + mass[1:2]
        kl = d * (jnp.log(d) - jnp.log(mass))
        tile_s[4:5] = kl[0:1] + kl[1:2]
        tile_s[5:8] = jnp.zeros((3, 128), f32)
        for k in (3, 1, 2):
            tile_copy(k).start()
        return mass, d

    def tile_along():
        for k in (1, 2, 3):
            tile_copy(k).wait_recv()
        tz[pl.ds(z, 1)] = ((tile_s[...] + tile_r[1]) + (tile_r[2] + tile_r[3]))[None]
        for r in range(1, nz):
            zcopy(tz, z, r, tz_s, tz_r).start()

    def gm_copy(k):
        return remote(gms, gmr.at[k], gm_s.at[k], gm_r.at[k], chip[k])

    def totals(mass, d):
        for r in range(1, nz):
            zcopy_wait(tz, r, tz_s, tz_r)
        t = tz[0]
        for p in range(1, nz):
            t = t + tz[p]
        loss_part, count, gate, mass_total, kl = (jnp.sum(t[i : i + 1]) for i in range(5))
        logs = jnp.log(jnp.where(lax.broadcasted_iota(jnp.int32, (1, 128), 1) == 0, count, mass_total))
        log_count, log_mass = jnp.sum(logs[:, 0:1]), jnp.sum(logs[:, 1:2])
        excess = gate / count - 1.0
        gms[...] = jnp.zeros_like(gms)
        gms[0:2] = (1.0 / mass_total - d / count / mass).astype(bf16).astype(f32)
        for k in (3, 1, 2):
            gm_copy(k).start()
        pair_s[1] = jnp.full((8, 2 * rows), loss_part + kl / count - log_count + log_mass + excess * excess)
        pair(1).start()
        return 2.0 * excess / count

    def mass_columns():
        gmcol[at_k(0), :] = column(gms[0:1], rows)
        for k in (1, 2, 3):
            gm_copy(k).wait_recv()
            gmcol[at_k(k), :] = column(gmr[k, 0:1], rows)

    def dwcopy(p):
        return remote(dws.at[p], dwr.at[p], dw_s.at[p], dw_r.at[p], here)

    def weight_grad(p):
        cs = slice(p * cd, (p + 1) * cd)

        def rows_of(h):
            d = dot_nt(dpa[0, h * grp : (h + 1) * grp, :], ebuf[0, cs, :])
            for c in range(1, np_ // 2):
                d = d + dot_nt(dpa[c, h * grp : (h + 1) * grp, :], ebuf[c, cs, :])
            return d

        dws[p] = rows_of(1)
        dwcopy(p).start()
        dwo[p] = rows_of(0)

    def gpcopy(k, p):
        return remote(gps.at[p, at_k(k)], gpr.at[k, p], gp_s.at[k, p], gp_r.at[k, p], chip[k])

    def give_back(p):
        dwcopy(p).wait_recv()
        cs = pl.ds(p * cd, cd)
        total = jnp.zeros((1, cd), f32)
        for k in (3, 1, 2, 0):
            r = at_k(k)
            gm = gmcol[r, :]
            gw = dwo[p, r] + dwr[p, r] + jnp.concatenate([gm] * (cd // 128), axis=1)
            total = total + jnp.sum(gw * wraw[r, cs].astype(f32), axis=0, keepdims=True)
            gps[p, r] = (gcol[0:1, cs] * gw).astype(bf16)
            if k:
                gpcopy(k, p).start()
        fsend[p] = total

    def filter_along():
        frecv[pl.ds(z, 1)] = fsend[pl.ds(z, 1)]
        for r in range(1, nz):
            to = (z + r) % nz
            remote(fsend.at[to], frecv.at[z], fz_s.at[r], fz_r.at[r], (to * GROUP + q, j)).start()

    def take(k, p, start=False):
        if k:
            gpcopy(k, p).wait_recv()
            v = gpr[k, p]
        else:
            v = gps[p, at_k(0)]
        at = pl.ds(pl.multiple_of((p * GROUP + nq[k]) * cd, cd), cd)
        gpb[:, at] = v
        s = fold(probs[:, at] * v.astype(f32))
        if start:
            rowsum[...] = s
        else:
            rowsum[...] += s

    def sent_first():
        for k in (1, 2, 3):
            wcopy(k).wait_send()
            mass_copy(k).wait_send()
            for n in (0, 1):
                stat(k, n).wait_send()
        for k in range(GROUP):
            wsib(k).wait_send()
        pair(0).wait_send()
        for k, h in others:
            spot_copy(k, h).wait_send()
        for k in (1, 2, 3):
            for h in range(2):
                lead_copy(tlead, 0, k, h).wait_send()
                lead_copy(plead, 1, k, h).wait_send()

        @pl.loop(0, np_)
        def _(g):
            for c in (pxcopy, pycopy):
                c(g, 0).wait_send()
                c(g, 1).wait_send()
            p2xcopy(g).wait_send()
            p2ycopy(g).wait_send()

    def sent_along():
        @pl.loop(0, nz)
        def _(p):
            @pl.when(has_right & (p <= z))
            def _():
                zsmall(0, p).wait_send()
                for g in range(np_):
                    zsend(0, p, g).wait_send()

            @pl.when(has_left & (p >= z))
            def _():
                zsmall(1, p).wait_send()
                for g in range(np_):
                    zsend(1, p, g).wait_send()

    def sent_back():
        for g in range(1, np_):
            for i in range(6):
                agcopy(i, g).wait_send()

    def sent_last():
        for k in (1, 2, 3):
            tile_copy(k).wait_send()
            gm_copy(k).wait_send()
            for p in range(nz):
                gpcopy(k, p).wait_send()
        for r in range(1, nz):
            zcopy(tz, z, r, tz_s, tz_r).wait_send()
            zcopy(fsend, z, r, fz_s, fz_r).wait_send()
        for p in range(nz):
            dwcopy(p).wait_send()
        for i in (1, 2):
            pair(i).wait_send()

    def sent_sums():
        @pl.loop(0, nz)
        def _(p):
            @pl.when(has_right & (p > z))
            def _():
                for g in range(np_):
                    dcopy(0, p, g).wait_send()

            @pl.when(has_left & (p < z))
            def _():
                for g in range(np_):
                    dcopy(1, p, g).wait_send()

    give(1)
    give(2)
    coefs[1] = slide_sums(1)
    mass, d = tile_start()
    lead_grad()
    expr_grad_first()
    give_on(2)
    give(3)
    give(4)
    tile_along()
    expr_grad(1)
    starts((0, 1), (1, 1), (2, 1))
    chain(1, 0, 0)
    give_on(3)
    give(5)
    chain(1, 1, 0)
    give_on(4)
    give(6)
    expr_grad(2)
    starts((0, 2), (1, 2))
    chain(2, 0, 0)
    chain(1, 0, 1)
    give_on(5)
    give(7)
    expr_grad(3)
    starts((0, 3))
    chain(1, 1, 1)
    give_on(6)
    expr_grad(4)
    starts((0, 4), (1, 3))
    push = totals(mass, d)
    lead_back()
    chain(2, 0, 1)
    chain(1, 0, 2)
    give_on(7)
    expr_grad(5)
    starts((0, 5), (1, 4))
    finish(0)
    chain(1, 1, 2)
    expr_grad(6)
    starts((0, 6), (1, 5))
    chain(1, 0, 3)
    for i in (1, 3, 4, 5):
        agcopy(i, np_ - 1).wait_recv()
    weight_grad(0)
    chain(2, 0, 2)
    chain(1, 0, 4)
    weight_grad(1)
    finish(1)
    mass_columns()
    give_back(0)
    chain(1, 1, 3)
    expr_grad(7, False)
    starts((0, 7), (2, 2), (1, 6), (2, 3), (1, 7))
    chain(2, 0, 3)
    chain(1, 0, 5)
    weight_grad(2)
    give_back(1)
    chain(2, 0, 4)
    chain(1, 1, 4)
    weight_grad(3)
    give_back(2)
    chain(1, 0, 6)
    give_back(3)
    filter_along()
    starts((2, 4), (2, 5), (2, 6), (2, 7))
    chain(1, 1, 5)
    take(0, 0, True)
    for p in range(1, nz):
        take(0, p)
    chain(2, 0, 5)
    chain(1, 0, 7)
    sent_first()
    chain(2, 0, 6)
    finish(2)
    for k in (1, 2, 3):
        take(k, 0)
    chain(1, 1, 6)
    chain(2, 0, 7)
    for k in (1, 2, 3):
        take(k, 1)
    finish(3)
    sent_along()
    chain(1, 1, 7)
    for k in (1, 2, 3):
        take(k, 2)
    finish(4)
    sent_back()
    finish(5)
    for r in range(1, nz):
        zcopy_wait(frecv, r, fz_s, fz_r)
    ftotal = frecv[0]
    for p in range(1, nz):
        ftotal = ftotal + frecv[p]
    pair_s[2, 0:1, 0:cd] = ftotal
    pair(2).start()
    for k in (1, 2, 3):
        take(k, 3)
    tot_o[...] = jnp.broadcast_to(jnp.sum(rowsum[...], axis=1, keepdims=True), (rows, 128))
    sent_last()
    finish(6)
    pair(1).wait_recv()
    pair(2).wait_recv()
    my_gate = jax.nn.sigmoid(filt[...])
    fsum = ftotal + pair_r[2, 0:1, 0:cd] + push
    for h in range(cd // 128):
        g = my_gate[h : h + 1, :]
        last_o[h : h + 1, :] = fsum[:, h * 128 : (h + 1) * 128] * g * (1.0 - g)
    last_o[cd // 128 : cd // 128 + 1, :] = 0.5 * (pair_s[1, 0:1, 0:128] + pair_r[1, 0:1, 0:128])
    finish(7)
    sent_sums()


def finish_kernel(probs, gp, tot, ge, last, gl_o, ge_o, loss_o, gf_o, gl, loss, out_s):
    f32 = jnp.float32
    parts = 4
    cc = probs.shape[1] // parts
    copies = []

    def send(src, dst):
        copies.append(pltpu.make_async_copy(src, dst, out_s.at[len(copies)]))
        copies[-1].start()

    send(ge, ge_o)
    n = gf_o.shape[0]
    loss[...] = last[n : n + 1, 0:1]
    send(last.at[pl.ds(0, n)], gf_o)
    send(loss, loss_o)
    for i in range(parts):
        for c in range(i * cc, (i + 1) * cc, 128):
            at = slice(c, c + 128)
            gl[:, at] = probs[:, at] * (gp[:, at].astype(f32) - tot[...])
        at = pl.ds(i * cc, cc)
        send(gl.at[:, at], gl_o.at[:, at])
    for c in copies:
        c.wait()


def grouped(logits, filt, expr, target, gene_mask, density):
    f32, bf16, i32 = jnp.float32, jnp.bfloat16, jnp.int32
    nspot = lax.axis_size("spot")
    rows, cells = logits.shape
    cd, genes = expr.shape
    nz = nspot // GROUP
    n = genes // PIECE
    grp = GROUP * rows
    mine = cells // GROUP
    spots = 2 * rows

    def vmem(*shape, dtype=f32):
        return pltpu.VMEM(shape, dtype)

    def dma(*shape):
        return pltpu.SemaphoreType.DMA(shape)

    def low(*shape):
        return pltpu.VMEM(shape, bf16)

    buffers = [
        low(rows, cells), vmem(cd // 128, 128), vmem(*gene_mask.shape, dtype=i32), vmem(spots // 128, 128, dtype=i32),
        low(GROUP, rows, mine), low(2 * grp, mine), low(2 * grp, mine), low(mine, 2 * grp),
        low(n // 2, mine, 2 * PIECE), low(spots, genes), vmem(8, mine), vmem(nz, 8, 128), vmem(spots, genes),
        vmem(2 * grp, 2 * PIECE),
        low(n, 2 * rows, PIECE), low(n, 2 * rows, PIECE), low(n, 2 * rows, PIECE), low(n, 2 * rows, PIECE),
        low(n, rows, PIECE), low(n, rows, PIECE), low(n, rows, PIECE), low(n, rows, PIECE),
        vmem(n, rows, PIECE), vmem(n, rows, PIECE), vmem(GROUP, 8, 128), vmem(GROUP, 8, 128),
        vmem(3, 1, genes), vmem(GROUP, 3, 1, genes), vmem(3, spots, PIECE), vmem(3, 1, spots), vmem(2, GROUP, 3, 1, spots), low(2 * grp, PIECE), low(2 * grp, PIECE),
        vmem(PIECE, 2 * grp), vmem(PIECE, 2 * grp), low(PIECE, 2 * grp), vmem(2, 2 * grp),
        low(n // 2, 2 * grp, 2 * PIECE), vmem(nz, cd, genes),
        low(nz, n, cd, PIECE), low(nz, n, cd, PIECE), low(nz, n, cd, PIECE),
        vmem(nz, grp, cd), vmem(nz, grp, cd), vmem(nz, grp, cd), low(nz, grp, cd), low(GROUP, nz, rows, cd),
        vmem(rows, 128), vmem(8, 128), vmem(GROUP, 8, 128), vmem(nz, 8, 128), vmem(8, 128), vmem(GROUP, 8, 128),
        vmem(grp, 128), vmem(nz, 1, cd), vmem(nz, 1, cd), vmem(3, 8, spots), vmem(3, 8, spots),
    ]
    sems = [
        pltpu.SemaphoreType.REGULAR, dma(4 + n // 2 + 2), dma(2, nz), dma(nz), dma(2, nz, n), dma(nz, n),
        dma(4), dma(4), dma(4), dma(4), dma(3), dma(3),
        dma(2, n), dma(2, n), dma(2, n), dma(2, n), dma(n), dma(n), dma(n), dma(n),
        dma(4), dma(4), dma(8), dma(8), dma(2, 4, 2), dma(2, 4, 2), dma(8), dma(8), dma(6, n), dma(6, n),
        dma(nz, n), dma(nz, n), dma(nz, n), dma(nz, n), dma(nz), dma(nz), dma(4, nz), dma(4, nz),
        dma(4), dma(4), dma(nz), dma(nz), dma(4), dma(4), dma(nz), dma(nz),
    ]
    v, a = pl.BlockSpec(memory_space=pltpu.VMEM), pl.BlockSpec(memory_space=pl.ANY)
    shape = jax.ShapeDtypeStruct
    fparts = (cd // 128, 128)
    given = (logits, filt.reshape(-1, 128), expr, target, gene_mask, density.reshape(-1, 128))
    probs, gp, tot, last, grad_expr = pl.pallas_call(
        functools.partial(group_kernel, nspot),
        out_shape=[vmem(rows, cells), low(rows, cells), vmem(rows, 128), vmem(8, 128), vmem(cd, genes)],
        in_specs=[a] * 6,
        out_specs=[v] * 5,
        scratch_shapes=buffers + sems,
        compiler_params=pltpu.CompilerParams(
            collective_id=0, has_side_effects=True, vmem_limit_bytes=VMEM_BYTES
        ),
        name="group_step",
    )(*(pltpu.with_memory_space_constraint(g, pltpu.HBM) for g in given))
    grad_logits, grad_expr, loss, grad_filt = pl.pallas_call(
        finish_kernel,
        out_shape=[shape((rows, cells), f32), shape((cd, genes), f32), shape((1, 1), f32), shape(fparts, f32)],
        in_specs=[v] * 5,
        out_specs=[a] * 4,
        scratch_shapes=[vmem(rows, cells), vmem(1, 1), dma(7)],
        compiler_params=pltpu.CompilerParams(vmem_limit_bytes=LAST_BYTES),
        name="finish_step",
    )(probs, gp, tot, grad_expr, last)
    return (loss.reshape(()), grad_logits, grad_filt.reshape(-1), grad_expr)


def fits(logits, filt, expr):
    nspot = lax.axis_size("spot")
    rows, cells = logits.shape
    sizes = (rows, cells, filt.shape[0], expr.shape[1])
    return (
        nspot == GROUP * SLIDES and lax.axis_size("gene") == 2 and sizes == (128, 4096, 256, 1024)
    )


def per_device(logits, filt, expr, target, gene_mask, density):
    plan = grouped if fits(logits, filt, expr) else streamed
    return plan(logits, filt, expr, target, gene_mask, density)


def solution(mesh):
    in_specs = (
        P(("spot", "gene"), None),
        P("spot"),
        P("spot", "gene"),
        P("spot", "gene"),
        P(None, "gene"),
        P("spot"),
    )
    out_specs = (P(), P(("spot", "gene"), None), P("spot"), P("spot", "gene"))
    return jax.shard_map(
        per_device, mesh=mesh, in_specs=in_specs, out_specs=out_specs, check_vma=False
    )
```

```python
import functools

import jax
import jax.numpy as jnp
from jax import lax
from jax.experimental import pallas as pl
from jax.experimental.pallas import tpu as pltpu
from jax.sharding import PartitionSpec as P

SPOTS = 4096
SLIDES = 4


eps_norm = 1e-06


def slide_moments(onehot, pred, truth):
    hi = lax.Precision.HIGHEST
    return jnp.stack(
        [
            jnp.dot(onehot.T, pred * truth, precision=hi),
            jnp.dot(onehot.T, pred * pred, precision=hi),
            jnp.dot(onehot.T, truth * truth, precision=hi),
        ]
    )


def spot_moments(pred, truth):
    return jnp.stack(
        [
            jnp.sum(pred * truth, axis=1),
            jnp.sum(pred * pred, axis=1),
            jnp.sum(truth * truth, axis=1),
        ]
    )


def cosine_parts(slide_stats):
    dots = slide_stats[0]
    slide_a = lax.rsqrt(slide_stats[1] + eps_norm)
    slide_b = lax.rsqrt(slide_stats[2] + eps_norm)
    return (dots, slide_a, slide_b, dots * slide_a * slide_b)


def pred_gradient(onehot, weight_slide, dots, slide_a, slide_b, spot_stats, pred, truth):
    hi = lax.Precision.HIGHEST
    spot_a = lax.rsqrt(spot_stats[1] + eps_norm)
    spot_b = lax.rsqrt(spot_stats[2] + eps_norm)
    coef_truth = -weight_slide * slide_a * slide_b
    coef_pred = weight_slide * dots * slide_a**3 * slide_b
    grad_pred = (
        jnp.dot(onehot, coef_truth, precision=hi) * truth
        + jnp.dot(onehot, coef_pred, precision=hi) * pred
    )
    grad_pred = (
        grad_pred
        + (
            -(spot_a * spot_b)[:, None] * truth
            + (spot_stats[0] * spot_a**3 * spot_b)[:, None] * pred
        )
        / SPOTS
    )
    return (grad_pred, spot_stats[0] * spot_a * spot_b)


def streamed(logits, filt, expr, target, gene_mask, density):
    f32 = jnp.float32
    bf16 = jnp.bfloat16
    nspot = lax.axis_size("spot")
    ngene = lax.axis_size("gene")
    spot_dev = logits.shape[0]
    cells = logits.shape[1]
    cell_dev = filt.shape[0]
    owned = target.shape[0]
    half = target.shape[1]
    spots_all = owned * nspot
    slide_len = SPOTS // SLIDES
    scores = logits.astype(f32)
    shifted = jnp.exp(scores - jnp.max(scores, axis=1, keepdims=True))
    probs = shifted / jnp.sum(shifted, axis=1, keepdims=True)
    moved = lax.all_to_all(probs.astype(bf16), "spot", split_axis=1, concat_axis=0, tiled=True)
    paired = lax.all_gather(moved.reshape(nspot, 1, spot_dev, cell_dev), "gene", axis=1, tiled=True)
    paired = paired.reshape(spots_all, cell_dev)
    gate = jax.nn.sigmoid(filt)
    weighted = (paired.astype(f32) * gate[None, :]).astype(bf16)
    partial_pred = jnp.dot(weighted, expr, preferred_element_type=f32)
    partial_mass = jnp.sum(weighted.astype(f32), axis=1)
    gate_part = jnp.sum(gate)
    maskf = gene_mask.astype(f32)
    mask_part = jnp.sum(maskf, axis=1)
    pred_three, mass_two = (
        lax.psum_scatter(
            partial_pred.reshape(nspot, owned, half), "spot", scatter_dimension=0, tiled=True
        ),
        lax.psum_scatter(
            partial_mass.reshape(nspot, owned), "spot", scatter_dimension=0, tiled=True
        ),
    )
    pred = pred_three.reshape(owned, half)
    mass = mass_two.reshape(owned)
    truth = target.astype(f32)
    dens = density.astype(f32)
    spot_ids = lax.axis_index("spot") * owned + jnp.arange(owned, dtype=jnp.int32)
    onehot = (
        spot_ids[:, None] // slide_len == jnp.arange(SLIDES, dtype=jnp.int32)[None, :]
    ).astype(f32)
    slide_stats, mass_total, gate_total, count_total = lax.psum(
        (slide_moments(onehot, pred, truth), jnp.sum(mass), gate_part, jnp.sum(dens)), "spot"
    )
    dots, slide_a, slide_b, cos_gene = cosine_parts(slide_stats)
    spot_stats, kept_genes, gene_numer = lax.psum(
        (spot_moments(pred, truth), mask_part, jnp.sum(maskf * cos_gene, axis=1)), "gene"
    )
    genes_kept = jnp.maximum(kept_genes, 1.0)
    weight_slide = maskf / genes_kept[:, None] / SLIDES
    grad_pred, cos_spot = pred_gradient(
        onehot, weight_slide, dots, slide_a, slide_b, spot_stats, pred, truth
    )
    share = dens / count_total
    kl_local = jnp.sum(share * (jnp.log(share) - jnp.log(mass) + jnp.log(mass_total)))
    cos_total, kl_total = lax.psum((jnp.sum(cos_spot), kl_local), "spot")
    grad_mass = 1.0 / mass_total - share / mass
    spread_three, spread_two = (
        lax.all_gather(grad_pred.astype(bf16).reshape(1, owned, half), "spot", axis=0, tiled=True),
        lax.all_gather(grad_mass.astype(bf16).reshape(1, owned), "spot", axis=0, tiled=True),
    )
    spread_pred = spread_three.reshape(spots_all, half)
    spread_mass = spread_two.reshape(spots_all)
    gene_term = jnp.mean(gene_numer / genes_kept)
    excess = gate_total / count_total - 1.0
    loss = -gene_term - cos_total / SPOTS + kl_total + excess * excess
    grad_expr = lax.dot_general(
        weighted, spread_pred, (((0,), (0,)), ((), ())), preferred_element_type=f32
    )
    first_half = (lax.axis_index("gene") == 0).astype(f32)
    grad_weighted = lax.dot_general(
        spread_pred, expr, (((1,), (1,)), ((), ())), preferred_element_type=f32
    )
    grad_weighted = grad_weighted + first_half * spread_mass.astype(f32)[:, None]
    filter_part = jnp.sum(grad_weighted * paired.astype(f32), axis=0)
    filter_total = lax.psum(filter_part, "gene")
    grad_filt = (filter_total + 2.0 * excess / count_total) * gate * (1.0 - gate)
    terms = (grad_weighted * gate[None, :]).reshape(nspot, ngene, spot_dev, cell_dev)
    moved_back = lax.all_to_all(terms, "spot", split_axis=0, concat_axis=3, tiled=True)
    folded = lax.psum_scatter(moved_back, "gene", scatter_dimension=1, tiled=True)
    rounded = lax.optimization_barrier(folded.reshape(spot_dev, cells).astype(bf16))
    grad_probs = rounded.astype(f32)
    grad_logits = probs * (grad_probs - jnp.sum(probs * grad_probs, axis=1, keepdims=True))
    return (loss, grad_logits, grad_filt, grad_expr)


GROUP = 4
PIECE = 128
MESH = pl.DeviceIdType.MESH
PAIRS = (4, 6,)
VMEM_BYTES = 44 << 20
LAST_BYTES = 16 << 20


def remote(src, dst, send, recv, dev):
    return pltpu.make_async_remote_copy(
        src_ref=src, dst_ref=dst, send_sem=send, recv_sem=recv, device_id=dev, device_id_type=MESH
    )


def dot_nt(a, b):
    return lax.dot_general(a, b, (((1,), (1,)), ((), ())), preferred_element_type=jnp.float32)


def column(row, length):
    return jnp.transpose(jnp.broadcast_to(row, (128, length)))


def fold(values):
    total = values[:, 0:128]
    for i in range(1, values.shape[1] // 128):
        total = total + values[:, i * 128 : (i + 1) * 128]
    return total


def group_kernel(
    nspot, logits_h, filt_h, expr, target, mask_h, dens_h,
    probs, gpb, tot_o, last_o, ge_o,
    logits, filt, mask, dens, rawq, wraw, wg, wt, ebuf, tbuf, gcol, small, pfin, ahead,
    psx, prx, psy, pry, ps2x, pr2x, ps2y, pr2y, hx, hy, massp, massr, statg, statr, acc, spots, spotr, tlead, plead, tturn, pturn, dturn, coefrow,
    dpa, grad, dsend, dright, dleft, dwo, dws, dwr, gps, gpr, rowsum, tile_s, tile_r, tz, gms, gmr, gmcol,
    fsend, frecv, pair_s, pair_r,
    hello, lc, zs_s, zs_r, ez_s, ez_r, w_s, w_r, wd_s, wd_r, pr_s, pr_r,
    px_s, px_r, py_s, py_r, p2x_s, p2x_r, p2y_s, p2y_r, ms_s, ms_r, st_s, st_r, ld_s, ld_r, sp_s, sp_r, ag_s, ag_r,
    dr_s, dr_r, dl_s, dl_r, dw_s, dw_r, gp_s, gp_r, tl_s, tl_r, tz_s, tz_r, gm_s, gm_r, fz_s, fz_r,
):
    f32, bf16 = jnp.float32, jnp.bfloat16
    rows, cells = probs.shape
    cd, genes = expr.shape
    nz = nspot // GROUP
    np_ = genes // PIECE
    grp = GROUP * rows
    mine = cells // GROUP
    spots_all = nspot * 2 * rows
    me, j = lax.axis_index("spot"), lax.axis_index("gene")
    sib = 1 - j
    z, q = me // GROUP, me % GROUP
    x, y = q % 2, q // 2
    nbr = [me, me + 1 - 2 * x, me + 2 - 4 * y, me + 3 - 2 * x - 4 * y]
    nq = [n % GROUP for n in nbr]
    here = (me, sib)
    has_right, has_left = z < nz - 1, z > 0
    ends = (z == 0, z == nz - 1)
    chip = [(n, j) for n in nbr]
    beside = ((me + GROUP, j), (me - GROUP, j))

    def at_k(k, h=0):
        return pl.ds(h * grp + k * rows, rows)

    def piece(g):
        return pl.ds(g * PIECE, PIECE)

    def half_of(buf, r, g):
        return buf.at[g // 2, r, pl.ds(g % 2 * PIECE, PIECE)]

    def seg(p):
        return pl.ds(pl.multiple_of(p * cd, cd), cd)

    barrier = pltpu.get_barrier_semaphore()

    def greet(dev):
        pl.semaphore_signal(barrier, inc=1, device_id=dev, device_id_type=MESH)

    greet(chip[1])
    greet(chip[2])

    @pl.when(has_right)
    def _():
        greet(beside[0])

    @pl.when(has_left)
    def _():
        greet(beside[1])

    greet(here)
    loads = [pltpu.make_async_copy(logits_h, logits, lc.at[0])]
    loads += [
        pltpu.make_async_copy(s, d, lc.at[1 + i])
        for i, (s, d) in enumerate(((filt_h, filt), (mask_h, mask), (dens_h, dens)))
    ]
    loads += [
        pltpu.make_async_copy(
            expr.at[:, pl.ds(i * 2 * PIECE, 2 * PIECE)], ebuf.at[i, seg(z), :], lc.at[4 + i]
        )
        for i in range(np_ // 2)
    ]
    loads += [
        pltpu.make_async_copy(
            target.at[pl.ds(pl.multiple_of(c * rows, rows), rows)],
            tbuf.at[pl.ds(i * rows, rows)],
            lc.at[4 + np_ // 2 + i],
        )
        for i, c in enumerate((j, sib))
    ]
    for c in loads:
        c.start()
    for c in loads[1 : 4 + np_ // 2]:
        c.wait()
    small[pl.ds(z, 1), 0 : cd // 128, :] = filt[...][None]
    pl.semaphore_wait(barrier, 3 + has_right.astype(jnp.int32) + has_left.astype(jnp.int32))

    def zsmall(way, p):
        return remote(small.at[p], small.at[p], zs_s.at[way, p], zs_r.at[p], beside[way])

    def zsend(way, p, g):
        u = half_of(ebuf, seg(p), g)
        return remote(u, u, ez_s.at[way, p, g], ez_r.at[p, g], beside[way])

    def both(make):
        @pl.when(has_right)
        def _():
            make(0).start()

        @pl.when(has_left)
        def _():
            make(1).start()

    def hop(s, make):
        @pl.when(z >= s)
        def _():
            make(0, z - s).wait_recv()

            @pl.when(has_right)
            def _():
                make(0, z - s).start()

        @pl.when(z + s <= nz - 1)
        def _():
            make(1, z + s).wait_recv()

            @pl.when(has_left)
            def _():
                make(1, z + s).start()

    def own(g):
        if g < np_:
            both(lambda way: zsend(way, z, g))

    def passes(s, g):
        if not 0 <= g < np_:
            return

        @pl.when((z >= s) & has_right)
        def _():
            zsend(0, z - s, g).wait_recv()
            zsend(0, z - s, g).start()

        @pl.when((z + s <= nz - 1) & has_left)
        def _():
            zsend(1, z + s, g).wait_recv()
            zsend(1, z + s, g).start()

    def ends_here(s, g):
        if not 0 <= g < np_:
            return

        @pl.when((z >= s) & ends[1])
        def _():
            zsend(0, z - s, g).wait_recv()

        @pl.when((z + s <= nz - 1) & ends[0])
        def _():
            zsend(1, z + s, g).wait_recv()

    both(lambda way: zsmall(way, z))
    for g in range(4):
        own(g)

    loads[0].wait()

    step = 32

    @pl.loop(0, rows // step)
    def _(i):
        at = pl.ds(pl.multiple_of(i * step, step), step)
        s = logits[at, :].astype(f32)
        e = jnp.exp(s - jnp.max(s, axis=1, keepdims=True))
        p = e * (1.0 / jnp.sum(e, axis=1, keepdims=True))
        probs[at, :] = p
        for o in range(nspot):
            c = o // GROUP * cd
            rawq[o % GROUP, at, c : c + cd] = p[:, o * cd : (o + 1) * cd].astype(bf16)

    for c in loads[4 + np_ // 2 :]:
        c.wait()
    maskf = mask[pl.ds(z, 1), :].astype(f32)
    kept_mine = jnp.sum(maskf)
    pair_s[0] = jnp.full((8, 2 * rows), kept_mine)

    def wcopy(k):
        return remote(rawq.at[nq[k]], wraw.at[at_k(k)], w_s.at[k], w_r.at[k], chip[k])

    def wsib(k):
        return remote(wraw.at[at_k(k)], wraw.at[at_k(k, 1)], wd_s.at[k], wd_r.at[k], here)

    def pair(i):
        return remote(pair_s.at[i], pair_r.at[i], pr_s.at[i], pr_r.at[i], here)

    def lead_copy(buf, i, k, h):
        r = at_k(0, h)
        return remote(buf.at[r], buf.at[at_k(k, h)], ld_s.at[i, k, h], ld_r.at[i, k, h], chip[k])

    def lead(buf, i, values):
        for h in range(2):
            buf[at_k(0, h), :] = values[h * rows : (h + 1) * rows]
        for k in (3, 1, 2):
            for h in range(2):
                lead_copy(buf, i, k, h).start()

    def lead_turned(buf, i, out):
        lead_wait(buf, i)
        for c in range(0, 2 * grp, rows):
            out[:, c : c + rows] = jnp.transpose(buf[c : c + rows, :].astype(f32))

    def lead_wait(buf, i):
        for k in (1, 2, 3):
            for h in range(2):
                lead_copy(buf, i, k, h).wait_recv()

    wcopy(1).start()
    wcopy(2).start()
    pl.semaphore_signal(hello, inc=1, device_id=chip[1], device_id_type=MESH)
    wraw[at_k(0), :] = rawq[pl.ds(q, 1)].reshape(rows, mine)
    wsib(0).start()
    pair(0).start()
    pl.semaphore_wait(hello, 1)
    wcopy(3).start()

    def gated(k, h):
        r = at_k(k, h)
        for c in range(0, mine, 512):
            at = pl.ds(c, 512)
            wg[r, at] = (gcol[0:1, at] * wraw[r, at].astype(f32)).astype(bf16)

    def turned(k, h):
        r = at_k(k, h)
        for c in range(0, mine, 512):
            at = pl.ds(c, 512)
            wt[at, r] = jnp.transpose(wg[r, at].astype(f32)).astype(bf16)

    def arrive(k):
        wcopy(k).wait_recv()
        wsib(k).start()
        gated(k, 0)

    def arrive_sib(k):
        wsib(k).wait_recv()
        gated(k, 1)

    first, second = pl.ds(0, rows), pl.ds(rows, rows)

    def pxcopy(g, n):
        h = (first, second)[n]
        return remote(psx.at[g, h], prx.at[g, h], px_s.at[n, g], px_r.at[n, g], chip[1])

    def pycopy(g, n):
        h = (first, second)[n]
        return remote(psy.at[g, h], pry.at[g, h], py_s.at[n, g], py_r.at[n, g], chip[2])

    def p2xcopy(g):
        return remote(ps2x.at[g], pr2x.at[g], p2x_s.at[g], p2x_r.at[g], chip[1])

    def p2ycopy(g):
        return remote(ps2y.at[g], pr2y.at[g], p2y_s.at[g], p2y_r.at[g], chip[2])

    def piece_of(g, at):
        return ebuf[g // 2, at, g % 2 * PIECE : (g % 2 + 1) * PIECE]

    def project(g):
        share(g, jnp.dot(wg[...], piece_of(g, pl.ds(0, mine)), preferred_element_type=f32))

    far = (1 - z // (nz // 2)) * (nz - 1)
    near = pl.ds(pl.multiple_of(z // (nz // 2) * cd, cd), mine - cd)

    def project_ahead(g):
        ahead[...] = jnp.dot(wg[:, near], ebuf[g // 2, near, :], preferred_element_type=f32)

    def project_last(g):
        e = piece_of(g, seg(far))
        lanes = pl.ds(g % 2 * PIECE, PIECE)

        def rows_of(r):
            return ahead[r, lanes] + jnp.dot(wg[r, seg(far)], e, preferred_element_type=f32)

        relayed = [rows_of(at_k(3, h)) for h in range(2)]
        psx[g, second] = relayed[0].astype(bf16)
        pxcopy(g, 1).start()
        psy[g, second] = relayed[1].astype(bf16)
        pycopy(g, 1).start()
        rest = [rows_of(pl.ds(h * grp, 3 * rows)) for h in range(2)]
        share_rest(g, lambda k, h: rest[h][k * rows : (k + 1) * rows])

    def share(g, v):
        def part(k, h):
            s = h * grp + k * rows
            return v[s : s + rows]

        psx[g, second] = part(3, 0).astype(bf16)
        pxcopy(g, 1).start()
        psy[g, second] = part(3, 1).astype(bf16)
        pycopy(g, 1).start()
        share_rest(g, part)

    def share_rest(g, part):
        psx[g, first] = part(1, 0).astype(bf16)
        pxcopy(g, 0).start()
        psy[g, first] = part(2, 1).astype(bf16)
        pycopy(g, 0).start()
        hx[g] = part(2, 0)
        hy[g] = part(1, 1)
        pfin[first, piece(g)] = part(0, 0)
        pfin[second, piece(g)] = part(0, 1)

    def relay(g):
        pxcopy(g, 1).wait_recv()
        ps2y[g] = (hx[g] + prx[g, second].astype(f32)).astype(bf16)
        p2ycopy(g).start()
        pycopy(g, 1).wait_recv()
        ps2x[g] = (hy[g] + pry[g, second].astype(f32)).astype(bf16)
        p2xcopy(g).start()

    def whole(g):
        at = piece(g)
        pxcopy(g, 0).wait_recv()
        pycopy(g, 0).wait_recv()
        p2ycopy(g).wait_recv()
        p2xcopy(g).wait_recv()
        pfin[first, at] += prx[g, first].astype(f32) + pr2y[g].astype(f32)
        pfin[second, at] += pry[g, first].astype(f32) + pr2x[g].astype(f32)
        p = pfin[:, at]
        t = tbuf[:, at].astype(f32)
        for i, v in enumerate((p * p, p * t)):
            statg[i, :, at] = jnp.sum(v, axis=0, keepdims=True)
            acc[i] += v

    def target_moments():
        for g in range(np_):
            t = tbuf[:, piece(g)].astype(f32)
            statg[2, :, piece(g)] = jnp.sum(t * t, axis=0, keepdims=True)
            acc[2] += t * t
        spots[2] = jnp.sum(jnp.transpose(acc[2]), axis=0, keepdims=True)

    parts = (pl.ds(0, (np_ - 2) * PIECE), pl.ds((np_ - 2) * PIECE, 2 * PIECE))

    def stat(k, n):
        i = 2 * k + n
        return remote(
            statg.at[:, :, parts[n]], statr.at[k, :, :, parts[n]], st_s.at[i], st_r.at[i], chip[k]
        )

    def gates():
        for p in range(nz):
            for h in range(cd // 128):
                g = jax.nn.sigmoid(small[p, h : h + 1, :])
                c = p * cd + h * 128
                gcol[:, c : c + 128] = jnp.broadcast_to(g, (8, 128))

    def mass_copy(k):
        return remote(massp.at[k], massr.at[k], ms_s.at[k], ms_r.at[k], chip[k])

    def masses():
        m = dot_nt(jnp.ones((8, mine), bf16), wg[...])
        for k in range(GROUP):
            for h in range(2):
                s = h * grp + k * rows
                massp[k, h : h + 1, :] = m[0:1, s : s + rows]
            if k:
                mass_copy(k).start()

    acc[...] = jnp.zeros_like(acc)
    hop(1, zsmall)
    passes(1, 0)
    hop(2, zsmall)
    passes(1, 1)
    passes(2, 0)
    hop(3, zsmall)
    gates()
    gated(0, 0)
    arrive(1)
    arrive(2)
    arrive_sib(0)
    passes(1, 2)
    passes(2, 1)
    own(4)
    lead(tlead, 0, tbuf[:, 0:PIECE])
    arrive_sib(1)
    arrive_sib(2)
    for k in range(3):
        turned(k, 0)
    passes(1, 3)
    passes(2, 2)
    own(5)
    target_moments()
    arrive(3)
    arrive_sib(3)
    passes(1, 4)
    passes(2, 3)
    own(6)
    for n in (1, 2, 3):
        ends_here(n, 0)
    project(0)
    for s in range(3, np_ + 2):
        passes(1, s + 2)
        passes(2, s + 1)
        own(s + 4)
        g = s - 2
        if g in PAIRS:
            for n in (1, 2):
                ends_here(n, g)
                ends_here(n, g + 1)
            project_ahead(g)
        elif g - 1 not in PAIRS:
            for n in (1, 2):
                ends_here(n, g)
        ends_here(3, g)
        if g in PAIRS or g - 1 in PAIRS:
            project_last(g)
        else:
            project(g)
        if s == 3:
            masses()
        if s == 5:
            for k in range(3):
                turned(k, 1)
        if s == 6:
            turned(3, 0)
            turned(3, 1)
            lead_turned(tlead, 0, tturn)
        relay(s - 3)
        if s > 4:
            whole(s - 5)
        if s == 5:
            lead(plead, 1, pfin[:, 0:PIECE].astype(bf16))
    whole(np_ - 3)
    lead_turned(plead, 1, pturn)
    for k in (3, 1, 2):
        stat(k, 0).start()
    pair(0).wait_recv()
    kept = jnp.maximum(kept_mine + jnp.sum(pair_r[0, 0:1, 0:1]), 1.0)
    weight = maskf / kept / SLIDES
    relay(np_ - 1)
    whole(np_ - 2)
    whole(np_ - 1)
    for k in (3, 1, 2):
        stat(k, 1).start()

    for i in range(2):
        spots[i] = jnp.sum(jnp.transpose(acc[i]), axis=0, keepdims=True)
    def spot_copy(k, h):
        i = 2 * k + h
        dev = (nbr[k], sib) if h else chip[k]
        return remote(spots, spotr.at[h, k], sp_s.at[i], sp_r.at[i], dev)

    others = [(k, h) for k in (3, 1, 2, 0) for h in (1, 0) if k or h]
    for k, h in others:
        spot_copy(k, h).start()

    def slide_sums(n):
        for k in (1, 2, 3):
            stat(k, n).wait_recv()
        at = parts[n]
        pred_sq, dots, truth_sq = (
            (statg[i, :, at] + statr[1, i, :, at]) + (statr[2, i, :, at] + statr[3, i, :, at])
            for i in range(3)
        )
        slide_a = lax.rsqrt(pred_sq + eps_norm)
        slide_b = lax.rsqrt(truth_sq + eps_norm)
        w = weight[:, at.start : at.start + at.size]
        return (
            -w * slide_a * slide_b,
            w * dots * slide_a**3 * slide_b,
            w * (dots * slide_a * slide_b),
        )

    coefs = [slide_sums(0), None]

    def spot_coefs(k):
        if k:
            spot_copy(k, 0).wait_recv()
        spot_copy(k, 1).wait_recv()
        pp, dot, tt = (
            (spotr[0, k, i] if k else spots[i])
            + jnp.concatenate([spotr[1, k, i, :, rows : 2 * rows], spotr[1, k, i, :, 0:rows]], axis=1)
            for i in range(3)
        )
        a, b = lax.rsqrt(pp + eps_norm), lax.rsqrt(tt + eps_norm)
        t, p = -(a * b) / spots_all, dot * a**3 * b / spots_all
        for h in range(2):
            c = h * grp + k * rows
            coefrow[0:1, c : c + rows] = t[:, h * rows : (h + 1) * rows]
            coefrow[1:2, c : c + rows] = p[:, h * rows : (h + 1) * rows]
        return t, p, dot * a * b

    lead_t, lead_p = (column(v[:, 0:PIECE], PIECE) for v in coefs[0][0:2])
    row_t, row_p, cos_spot = spot_coefs(0)
    col_t, col_p = column(row_t, 2 * rows), column(row_p, 2 * rows)

    def agcopy(i, g):
        src, dst, to = (
            (at_k(0), at_k(1), 1), (at_k(0, 1), at_k(1, 1), 1), (at_k(0, 1), at_k(2, 1), 2),
            (at_k(0), at_k(2), 2), (at_k(1), at_k(3), 2), (at_k(2, 1), at_k(3, 1), 1),
        )[i]
        return remote(half_of(dpa, src, g), half_of(dpa, dst, g), ag_s.at[i, g], ag_r.at[i, g], chip[to])

    def give(g):
        n = 0 if g < np_ - 2 else 1
        if n and coefs[1] is None:
            coefs[1] = slide_sums(1)
        c = g * PIECE - parts[n].start
        c_t, c_p = (v[:, c : c + PIECE] for v in coefs[n][0:2])
        at = piece(g)
        d = ((c_t + col_t) * tbuf[:, at].astype(f32) + (c_p + col_p) * pfin[:, at]).astype(bf16)
        lanes = pl.ds(g % 2 * PIECE, PIECE)
        dpa[g // 2, at_k(0), lanes] = d[0:rows]
        dpa[g // 2, at_k(0, 1), lanes] = d[rows : 2 * rows]
        for i in range(4):
            agcopy(i, g).start()

    def lead_grad():
        for k in (1, 2, 3):
            spot_coefs(k)
        for c in range(0, 2 * grp, 128):
            at = slice(c, c + 128)
            d = (lead_t + coefrow[0:1, at]) * tturn[:, at] + (lead_p + coefrow[1:2, at]) * pturn[:, at]
            dturn[:, at] = d.astype(bf16)

    def lead_back():
        for c in range(0, 2 * grp, rows):
            dpa[0, c : c + rows, 0:PIECE] = jnp.transpose(dturn[:, c : c + rows].astype(f32)).astype(bf16)

    def give_on(g):
        agcopy(0, g).wait_recv()
        agcopy(4, g).start()
        agcopy(2, g).wait_recv()
        agcopy(5, g).start()

    def dcopy(way, p, g):
        if way == 0:
            return remote(dsend.at[p, g], dright.at[p, g], dr_s.at[p, g], dr_r.at[p, g], beside[0])
        return remote(dsend.at[p, g], dleft.at[p, g], dl_s.at[p, g], dl_r.at[p, g], beside[1])

    def expr_grad_first():
        up = z // (nz // 2)

        @pl.loop(0, nz)
        def _(u):
            p = up * u + (1 - up) * (nz - 1 - u)
            v = dot_nt(wt[seg(p), :], dturn[...])
            grad[p, :, 0:PIECE] = v

            @pl.when((ends[0] | ends[1]) & (p != z))
            def _():
                dsend[p, 0] = v.astype(bf16)

            @pl.when(ends[0] & (p != z))
            def _():
                dcopy(0, p, 0).start()

            @pl.when(ends[1] & (p != z))
            def _():
                dcopy(1, p, 0).start()

            @pl.when(u == 0)
            def _():
                give_on(1)

    def expr_grad(g, wait=True):
        if wait:
            for i in (1, 3, 4, 5):
                agcopy(i, g).wait_recv()
        lanes = slice(g % 2 * PIECE, (g % 2 + 1) * PIECE)
        v = jnp.dot(wt[...], dpa[g // 2, :, lanes], preferred_element_type=f32)
        for p in range(nz):
            grad[p, :, piece(g)] = v[p * cd : (p + 1) * cd]

        @pl.when(ends[0])
        def _():
            for p in range(1, nz):
                dsend[p, g] = v[p * cd : (p + 1) * cd].astype(bf16)

        @pl.when(ends[1])
        def _():
            for p in range(nz - 1):
                dsend[p, g] = v[p * cd : (p + 1) * cd].astype(bf16)

    def start_from_ends(u, g):
        if not 0 <= g < np_:
            return

        @pl.when(ends[0])
        def _():
            dcopy(0, nz - 1 - u, g).start()

        @pl.when(ends[1])
        def _():
            dcopy(1, u, g).start()

    def starts(*pieces):
        for u, g in pieces:
            start_from_ends(u, g)

    def chain(hops, u, g):
        if nz - 1 - u > hops:

            @pl.when(z == hops)
            def _():
                p = nz - 1 - u
                dcopy(0, p, g).wait_recv()
                dsend[p, g] = (grad[p, :, piece(g)] + dright[p, g].astype(f32)).astype(bf16)
                dcopy(0, p, g).start()

            @pl.when(nz - 1 - z == hops)
            def _():
                dcopy(1, u, g).wait_recv()
                dsend[u, g] = (grad[u, :, piece(g)] + dleft[u, g].astype(f32)).astype(bf16)
                dcopy(1, u, g).start()

    def finish(g):
        at = piece(g)
        ge_o[:, at] = grad[pl.ds(z, 1), :, at].reshape(cd, PIECE)

        @pl.when(has_left)
        def _():
            dcopy(0, z, g).wait_recv()
            ge_o[:, at] += dright[pl.ds(z, 1), g].reshape(cd, PIECE).astype(f32)

        @pl.when(has_right)
        def _():
            dcopy(1, z, g).wait_recv()
            ge_o[:, at] += dleft[pl.ds(z, 1), g].reshape(cd, PIECE).astype(f32)

    def tile_copy(k):
        return remote(tile_s, tile_r.at[k], tl_s.at[k], tl_r.at[k], chip[k])

    def zcopy(buf, src, r, ss, rs):
        to = (z + r) % nz
        return remote(buf.at[src], buf.at[z], ss.at[r], rs.at[r], (to * GROUP + q, j))

    def zcopy_wait(buf, r, ss, rs):
        o = (z + nz - r) % nz
        remote(buf.at[o], buf.at[o], ss.at[r], rs.at[r], here).wait_recv()

    def chip_masses():
        for k in (1, 2, 3):
            mass_copy(k).wait_recv()
        return (massp[0, 0:2] + massr[1, 0:2]) + (massr[2, 0:2] + massr[3, 0:2])

    def own_dens():
        d = dens[...].astype(f32)
        return jnp.where(j == 0, d, jnp.concatenate([d[1:2], d[0:1]], axis=0))

    def tile_start():
        mass, d = chip_masses(), own_dens()
        gene = fold(coefs[0][2]) + fold(coefs[1][2])
        cos = fold(cos_spot)
        tile_s[0:1] = -2.0 / GROUP * gene - cos / spots_all
        tile_s[1:2] = d[0:1] + d[1:2]
        f = jax.nn.sigmoid(filt[...])
        tile_s[2:3] = f[0:1] + f[1:2]
        tile_s[3:4] = mass[0:1] + mass[1:2]
        kl = d * (jnp.log(d) - jnp.log(mass))
        tile_s[4:5] = kl[0:1] + kl[1:2]
        tile_s[5:8] = jnp.zeros((3, 128), f32)
        for k in (3, 1, 2):
            tile_copy(k).start()
        return mass, d

    def tile_along():
        for k in (1, 2, 3):
            tile_copy(k).wait_recv()
        tz[pl.ds(z, 1)] = ((tile_s[...] + tile_r[1]) + (tile_r[2] + tile_r[3]))[None]
        for r in range(1, nz):
            zcopy(tz, z, r, tz_s, tz_r).start()

    def gm_copy(k):
        return remote(gms, gmr.at[k], gm_s.at[k], gm_r.at[k], chip[k])

    def totals(mass, d):
        for r in range(1, nz):
            zcopy_wait(tz, r, tz_s, tz_r)
        t = tz[0]
        for p in range(1, nz):
            t = t + tz[p]
        loss_part, count, gate, mass_total, kl = (jnp.sum(t[i : i + 1]) for i in range(5))
        logs = jnp.log(jnp.where(lax.broadcasted_iota(jnp.int32, (1, 128), 1) == 0, count, mass_total))
        log_count, log_mass = jnp.sum(logs[:, 0:1]), jnp.sum(logs[:, 1:2])
        excess = gate / count - 1.0
        gms[...] = jnp.zeros_like(gms)
        gms[0:2] = (1.0 / mass_total - d / count / mass).astype(bf16).astype(f32)
        for k in (3, 1, 2):
            gm_copy(k).start()
        pair_s[1] = jnp.full((8, 2 * rows), loss_part + kl / count - log_count + log_mass + excess * excess)
        pair(1).start()
        return 2.0 * excess / count

    def mass_columns():
        gmcol[at_k(0), :] = column(gms[0:1], rows)
        for k in (1, 2, 3):
            gm_copy(k).wait_recv()
            gmcol[at_k(k), :] = column(gmr[k, 0:1], rows)

    def dwcopy(p):
        return remote(dws.at[p], dwr.at[p], dw_s.at[p], dw_r.at[p], here)

    def weight_grad(p):
        cs = slice(p * cd, (p + 1) * cd)

        def rows_of(h):
            d = dot_nt(dpa[0, h * grp : (h + 1) * grp, :], ebuf[0, cs, :])
            for c in range(1, np_ // 2):
                d = d + dot_nt(dpa[c, h * grp : (h + 1) * grp, :], ebuf[c, cs, :])
            return d

        dws[p] = rows_of(1)
        dwcopy(p).start()
        dwo[p] = rows_of(0)

    def gpcopy(k, p):
        return remote(gps.at[p, at_k(k)], gpr.at[k, p], gp_s.at[k, p], gp_r.at[k, p], chip[k])

    def give_back(p):
        dwcopy(p).wait_recv()
        cs = pl.ds(p * cd, cd)
        total = jnp.zeros((1, cd), f32)
        for k in (3, 1, 2, 0):
            r = at_k(k)
            gm = gmcol[r, :]
            gw = dwo[p, r] + dwr[p, r] + jnp.concatenate([gm] * (cd // 128), axis=1)
            total = total + jnp.sum(gw * wraw[r, cs].astype(f32), axis=0, keepdims=True)
            gps[p, r] = (gcol[0:1, cs] * gw).astype(bf16)
            if k:
                gpcopy(k, p).start()
        fsend[p] = total

    def filter_along():
        frecv[pl.ds(z, 1)] = fsend[pl.ds(z, 1)]
        for r in range(1, nz):
            to = (z + r) % nz
            remote(fsend.at[to], frecv.at[z], fz_s.at[r], fz_r.at[r], (to * GROUP + q, j)).start()

    def take(k, p, start=False):
        if k:
            gpcopy(k, p).wait_recv()
            v = gpr[k, p]
        else:
            v = gps[p, at_k(0)]
        at = pl.ds(pl.multiple_of((p * GROUP + nq[k]) * cd, cd), cd)
        gpb[:, at] = v
        s = fold(probs[:, at] * v.astype(f32))
        if start:
            rowsum[...] = s
        else:
            rowsum[...] += s

    def sent_first():
        for k in (1, 2, 3):
            wcopy(k).wait_send()
            mass_copy(k).wait_send()
            for n in (0, 1):
                stat(k, n).wait_send()
        for k in range(GROUP):
            wsib(k).wait_send()
        pair(0).wait_send()
        for k, h in others:
            spot_copy(k, h).wait_send()
        for k in (1, 2, 3):
            for h in range(2):
                lead_copy(tlead, 0, k, h).wait_send()
                lead_copy(plead, 1, k, h).wait_send()

        @pl.loop(0, np_)
        def _(g):
            for c in (pxcopy, pycopy):
                c(g, 0).wait_send()
                c(g, 1).wait_send()
            p2xcopy(g).wait_send()
            p2ycopy(g).wait_send()

    def sent_along():
        @pl.loop(0, nz)
        def _(p):
            @pl.when(has_right & (p <= z))
            def _():
                zsmall(0, p).wait_send()
                for g in range(np_):
                    zsend(0, p, g).wait_send()

            @pl.when(has_left & (p >= z))
            def _():
                zsmall(1, p).wait_send()
                for g in range(np_):
                    zsend(1, p, g).wait_send()

    def sent_back():
        for g in range(1, np_):
            for i in range(6):
                agcopy(i, g).wait_send()

    def sent_last():
        for k in (1, 2, 3):
            tile_copy(k).wait_send()
            gm_copy(k).wait_send()
            for p in range(nz):
                gpcopy(k, p).wait_send()
        for r in range(1, nz):
            zcopy(tz, z, r, tz_s, tz_r).wait_send()
            zcopy(fsend, z, r, fz_s, fz_r).wait_send()
        for p in range(nz):
            dwcopy(p).wait_send()
        for i in (1, 2):
            pair(i).wait_send()

    def sent_sums():
        @pl.loop(0, nz)
        def _(p):
            @pl.when(has_right & (p > z))
            def _():
                for g in range(np_):
                    dcopy(0, p, g).wait_send()

            @pl.when(has_left & (p < z))
            def _():
                for g in range(np_):
                    dcopy(1, p, g).wait_send()

    give(1)
    give(2)
    coefs[1] = slide_sums(1)
    mass, d = tile_start()
    lead_grad()
    expr_grad_first()
    give_on(2)
    give(3)
    give(4)
    tile_along()
    expr_grad(1)
    starts((0, 1), (1, 1), (2, 1))
    chain(1, 0, 0)
    give_on(3)
    give(5)
    chain(1, 1, 0)
    give_on(4)
    give(6)
    expr_grad(2)
    starts((0, 2), (1, 2))
    chain(2, 0, 0)
    chain(1, 0, 1)
    give_on(5)
    give(7)
    expr_grad(3)
    starts((0, 3))
    chain(1, 1, 1)
    give_on(6)
    expr_grad(4)
    starts((0, 4), (1, 3))
    push = totals(mass, d)
    lead_back()
    chain(2, 0, 1)
    chain(1, 0, 2)
    give_on(7)
    expr_grad(5)
    starts((0, 5), (1, 4))
    finish(0)
    chain(1, 1, 2)
    expr_grad(6)
    starts((0, 6), (1, 5))
    chain(1, 0, 3)
    for i in (1, 3, 4, 5):
        agcopy(i, np_ - 1).wait_recv()
    weight_grad(0)
    chain(2, 0, 2)
    chain(1, 0, 4)
    weight_grad(1)
    finish(1)
    mass_columns()
    give_back(0)
    chain(1, 1, 3)
    expr_grad(7, False)
    starts((0, 7), (2, 2), (1, 6), (2, 3), (1, 7))
    chain(2, 0, 3)
    chain(1, 0, 5)
    weight_grad(2)
    give_back(1)
    chain(2, 0, 4)
    chain(1, 1, 4)
    weight_grad(3)
    give_back(2)
    chain(1, 0, 6)
    give_back(3)
    filter_along()
    starts((2, 4), (2, 5), (2, 6), (2, 7))
    chain(1, 1, 5)
    take(0, 0, True)
    for p in range(1, nz):
        take(0, p)
    chain(2, 0, 5)
    chain(1, 0, 7)
    sent_first()
    chain(2, 0, 6)
    finish(2)
    for k in (1, 2, 3):
        take(k, 0)
    chain(1, 1, 6)
    chain(2, 0, 7)
    for k in (1, 2, 3):
        take(k, 1)
    finish(3)
    sent_along()
    chain(1, 1, 7)
    for k in (1, 2, 3):
        take(k, 2)
    finish(4)
    sent_back()
    finish(5)
    for r in range(1, nz):
        zcopy_wait(frecv, r, fz_s, fz_r)
    ftotal = frecv[0]
    for p in range(1, nz):
        ftotal = ftotal + frecv[p]
    pair_s[2, 0:1, 0:cd] = ftotal
    pair(2).start()
    for k in (1, 2, 3):
        take(k, 3)
    tot_o[...] = jnp.broadcast_to(jnp.sum(rowsum[...], axis=1, keepdims=True), (rows, 128))
    sent_last()
    finish(6)
    pair(1).wait_recv()
    pair(2).wait_recv()
    my_gate = jax.nn.sigmoid(filt[...])
    fsum = ftotal + pair_r[2, 0:1, 0:cd] + push
    for h in range(cd // 128):
        g = my_gate[h : h + 1, :]
        last_o[h : h + 1, :] = fsum[:, h * 128 : (h + 1) * 128] * g * (1.0 - g)
    last_o[cd // 128 : cd // 128 + 1, :] = 0.5 * (pair_s[1, 0:1, 0:128] + pair_r[1, 0:1, 0:128])
    finish(7)
    sent_sums()


def finish_kernel(probs, gp, tot, ge, last, gl_o, ge_o, loss_o, gf_o, gl, loss, out_s):
    f32 = jnp.float32
    parts = 4
    cc = probs.shape[1] // parts
    copies = []

    def send(src, dst):
        copies.append(pltpu.make_async_copy(src, dst, out_s.at[len(copies)]))
        copies[-1].start()

    send(ge, ge_o)
    n = gf_o.shape[0]
    loss[...] = last[n : n + 1, 0:1]
    send(last.at[pl.ds(0, n)], gf_o)
    send(loss, loss_o)
    for i in range(parts):
        for c in range(i * cc, (i + 1) * cc, 128):
            at = slice(c, c + 128)
            gl[:, at] = probs[:, at] * (gp[:, at].astype(f32) - tot[...])
        at = pl.ds(i * cc, cc)
        send(gl.at[:, at], gl_o.at[:, at])
    for c in copies:
        c.wait()


def grouped(logits, filt, expr, target, gene_mask, density):
    f32, bf16, i32 = jnp.float32, jnp.bfloat16, jnp.int32
    nspot = lax.axis_size("spot")
    rows, cells = logits.shape
    cd, genes = expr.shape
    nz = nspot // GROUP
    n = genes // PIECE
    grp = GROUP * rows
    mine = cells // GROUP
    spots = 2 * rows

    def vmem(*shape, dtype=f32):
        return pltpu.VMEM(shape, dtype)

    def dma(*shape):
        return pltpu.SemaphoreType.DMA(shape)

    def low(*shape):
        return pltpu.VMEM(shape, bf16)

    buffers = [
        low(rows, cells), vmem(cd // 128, 128), vmem(*gene_mask.shape, dtype=i32), vmem(spots // 128, 128, dtype=i32),
        low(GROUP, rows, mine), low(2 * grp, mine), low(2 * grp, mine), low(mine, 2 * grp),
        low(n // 2, mine, 2 * PIECE), low(spots, genes), vmem(8, mine), vmem(nz, 8, 128), vmem(spots, genes),
        vmem(2 * grp, 2 * PIECE),
        low(n, 2 * rows, PIECE), low(n, 2 * rows, PIECE), low(n, 2 * rows, PIECE), low(n, 2 * rows, PIECE),
        low(n, rows, PIECE), low(n, rows, PIECE), low(n, rows, PIECE), low(n, rows, PIECE),
        vmem(n, rows, PIECE), vmem(n, rows, PIECE), vmem(GROUP, 8, 128), vmem(GROUP, 8, 128),
        vmem(3, 1, genes), vmem(GROUP, 3, 1, genes), vmem(3, spots, PIECE), vmem(3, 1, spots), vmem(2, GROUP, 3, 1, spots), low(2 * grp, PIECE), low(2 * grp, PIECE),
        vmem(PIECE, 2 * grp), vmem(PIECE, 2 * grp), low(PIECE, 2 * grp), vmem(2, 2 * grp),
        low(n // 2, 2 * grp, 2 * PIECE), vmem(nz, cd, genes),
        low(nz, n, cd, PIECE), low(nz, n, cd, PIECE), low(nz, n, cd, PIECE),
        vmem(nz, grp, cd), vmem(nz, grp, cd), vmem(nz, grp, cd), low(nz, grp, cd), low(GROUP, nz, rows, cd),
        vmem(rows, 128), vmem(8, 128), vmem(GROUP, 8, 128), vmem(nz, 8, 128), vmem(8, 128), vmem(GROUP, 8, 128),
        vmem(grp, 128), vmem(nz, 1, cd), vmem(nz, 1, cd), vmem(3, 8, spots), vmem(3, 8, spots),
    ]
    sems = [
        pltpu.SemaphoreType.REGULAR, dma(4 + n // 2 + 2), dma(2, nz), dma(nz), dma(2, nz, n), dma(nz, n),
        dma(4), dma(4), dma(4), dma(4), dma(3), dma(3),
        dma(2, n), dma(2, n), dma(2, n), dma(2, n), dma(n), dma(n), dma(n), dma(n),
        dma(4), dma(4), dma(8), dma(8), dma(2, 4, 2), dma(2, 4, 2), dma(8), dma(8), dma(6, n), dma(6, n),
        dma(nz, n), dma(nz, n), dma(nz, n), dma(nz, n), dma(nz), dma(nz), dma(4, nz), dma(4, nz),
        dma(4), dma(4), dma(nz), dma(nz), dma(4), dma(4), dma(nz), dma(nz),
    ]
    v, a = pl.BlockSpec(memory_space=pltpu.VMEM), pl.BlockSpec(memory_space=pl.ANY)
    shape = jax.ShapeDtypeStruct
    fparts = (cd // 128, 128)
    given = (logits, filt.reshape(-1, 128), expr, target, gene_mask, density.reshape(-1, 128))
    probs, gp, tot, last, grad_expr = pl.pallas_call(
        functools.partial(group_kernel, nspot),
        out_shape=[vmem(rows, cells), low(rows, cells), vmem(rows, 128), vmem(8, 128), vmem(cd, genes)],
        in_specs=[a] * 6,
        out_specs=[v] * 5,
        scratch_shapes=buffers + sems,
        compiler_params=pltpu.CompilerParams(
            collective_id=0, has_side_effects=True, vmem_limit_bytes=VMEM_BYTES
        ),
        name="group_step",
    )(*(pltpu.with_memory_space_constraint(g, pltpu.HBM) for g in given))
    grad_logits, grad_expr, loss, grad_filt = pl.pallas_call(
        finish_kernel,
        out_shape=[shape((rows, cells), f32), shape((cd, genes), f32), shape((1, 1), f32), shape(fparts, f32)],
        in_specs=[v] * 5,
        out_specs=[a] * 4,
        scratch_shapes=[vmem(rows, cells), vmem(1, 1), dma(7)],
        compiler_params=pltpu.CompilerParams(vmem_limit_bytes=LAST_BYTES),
        name="finish_step",
    )(probs, gp, tot, grad_expr, last)
    return (loss.reshape(()), grad_logits, grad_filt.reshape(-1), grad_expr)


def fits(logits, filt, expr):
    nspot = lax.axis_size("spot")
    rows, cells = logits.shape
    sizes = (rows, cells, filt.shape[0], expr.shape[1])
    return (
        nspot == GROUP * SLIDES and lax.axis_size("gene") == 2 and sizes == (128, 4096, 256, 1024)
    )


def per_device(logits, filt, expr, target, gene_mask, density):
    plan = grouped if fits(logits, filt, expr) else streamed
    return plan(logits, filt, expr, target, gene_mask, density)


def solution(mesh):
    in_specs = (
        P(("spot", "gene"), None),
        P("spot"),
        P("spot", "gene"),
        P("spot", "gene"),
        P(None, "gene"),
        P("spot"),
    )
    out_specs = (P(), P(("spot", "gene"), None), P("spot"), P("spot", "gene"))
    return jax.shard_map(
        per_device, mesh=mesh, in_specs=in_specs, out_specs=out_specs, check_vma=False
    )
```
